32 devices in a mesh: sp: 8 (over z, y), ch: 4 (over x, core).
Axes of the slice: x: 2, y: 2, z: 4, core: 2. Of those that a mesh axis runs over, the one named last changes fastest.
Arguments:
- inputs: bfloat16 [8, 37, 37, 256], P('sp', None, None, 'ch'), may hold values from -6 to 6
- cotangent: bfloat16 [8, 19, 19, 728], P('sp', None, None, 'ch'), may hold values from -6 to 6
- kernel_entry: bfloat16 [3, 3, 256], P(None, None, 'ch'), may hold values from -2 to 2
- kernels: bfloat16 [4, 3, 3, 728], P(None, None, None, 'ch'), may hold values from -2 to 2
- project_entry: bfloat16 [2, 728, 256], P(None, 'ch'), may hold values from -0.375 to 0.375
- projects: bfloat16 [4, 728, 728], P(None, 'ch'), may hold values from -0.21875 to 0.21875
- bn_gains: float32 [6, 728], P(None, 'ch'), may hold values from 0.1 to 1.9
- bn_biases: float32 [6, 728], P(None, 'ch'), may hold values from -3 to 3
- run_means: float32 [6, 728], P(None, 'ch'), may hold values from -3 to 3
- run_vars: float32 [6, 728], P(None, 'ch'), may hold values from 0.5 to 2
Outputs:
- output: float32 [8, 19, 19, 728], P('sp', None, None, 'ch')
- grad_inputs: float32 [8, 37, 37, 256], P('sp', None, None, 'ch')
- grad_kernel_entry: float32 [3, 3, 256], P(None, None, 'ch')
- grad_kernels: float32 [4, 3, 3, 728], P(None, None, None, 'ch')
- grad_project_entry: float32 [2, 728, 256], P(None, 'ch')
- grad_projects: float32 [4, 728, 728], P(None, 'ch')
- grad_gains: float32 [6, 728], P(None, 'ch')
- grad_biases: float32 [6, 728], P(None, 'ch')
- new_means: float32 [6, 728], P(None, 'ch')
- new_vars: float32 [6, 728], P(None, 'ch')
The draws below stay inside these ranges and needn't reach their ends.
All inputs are finite; a program needn't handle non-finite values.
Results may differ from the reference program's by a relative error of at most 0.03.
Values may be sent and summed in bfloat16 or wider, within the bound.
A program may use at most 128 MiB of HBM per device.

```python
import math
import jax
import jax.numpy as jnp
from jax import lax

CHAN_IN = 256
CHAN = 728
ROWS = 37
COLS = 37
IMAGES = 8
OUT_ROWS = 19
OUT_COLS = 19


def shard_levels(key, shape, cuts, least, high):
    def one(axis_at, blocks):
        draws = jax.random.uniform(jax.random.fold_in(jax.random.fold_in(key, 6), axis_at), (blocks,), jnp.float32, least / len(cuts), high / len(cuts))
        return jnp.repeat(jnp.exp(draws), shape[axis_at] // blocks).reshape((-1,) + (1,) * (len(shape) - axis_at - 1))

    loudness = one(*cuts[0])
    for cut in cuts[1:]:
        loudness = loudness * one(*cut)
    return loudness


def normal_values(own_key, shape, width, bound, pieces=(), kind=jnp.bfloat16):
    entries = jax.random.normal(own_key, shape, jnp.float32) * width
    if len(pieces) > 0:
        entries = shard_levels(own_key, shape, pieces, -0.22, 0.18) * entries
    return jnp.clip(entries, min=-bound, max=bound).astype(kind)


def setup_inputs(seed: int = 0) -> dict:
    seeds = jax.random.split(jax.random.key(seed), 11)
    inputs = normal_values(seeds[0], (IMAGES, ROWS, COLS, CHAN_IN), 1.0, 6.0, ((0, 8), (3, 4)))
    cotangent = normal_values(seeds[1], (IMAGES, OUT_ROWS, OUT_COLS, CHAN), 1.0, 6.0, ((0, 8), (3, 4)))
    kernel_entry = normal_values(seeds[2], (3, 3, CHAN_IN), 9 ** -0.5, 2.0, ((2, 4),))
    kernels = normal_values(seeds[3], (4, 3, 3, CHAN), 9 ** -0.5, 2.0, ((3, 4),))
    project_entry = normal_values(seeds[4], (2, CHAN, CHAN_IN), CHAN_IN ** -0.5, 0.375, ((1, 4),))
    projects = normal_values(seeds[5], (4, CHAN, CHAN), CHAN ** -0.5, 0.21875, ((1, 4),))
    bn_gains = jnp.clip(1.0 + 0.18 * jax.random.normal(seeds[6], (6, CHAN), jnp.float32), 0.1, 1.9)
    bn_biases = normal_values(seeds[7], (6, CHAN), 0.5, 3.0, ((1, 4),), jnp.float32)
    run_means = normal_values(seeds[8], (6, CHAN), 0.5, 3.0, ((1, 4),), jnp.float32)
    run_vars = jnp.clip(jnp.exp(math.log(2.0) - 1.3862944 * jax.random.uniform(seeds[9], (6, CHAN), jnp.float32) ** shard_levels(seeds[9], (6, CHAN), ((1, 4),), -0.2, 0.2)), 0.5, 2.0)
    return dict(inputs=inputs, cotangent=cotangent, kernel_entry=kernel_entry, kernels=kernels, project_entry=project_entry, projects=projects, bn_gains=bn_gains, bn_biases=bn_biases, run_means=run_means, run_vars=run_vars)


EPSILON = 0.001
MOMENTUM = 0.5

@jax.custom_vjp
def low(v):
    return lax.optimization_barrier(v.astype(jnp.bfloat16)).astype(jnp.float32)

@jax.custom_vjp
def low_back(v):
    return v

def low_keep(v):
    return (low(v), None)

def low_pass(kept, grad):
    return (grad,)

def back_keep(v):
    return (v, None)

def back_low(kept, grad):
    return (low(grad),)
low.defvjp(low_keep, low_pass)
low_back.defvjp(back_keep, back_low)

def depthwise(source, kernel):
    height, breadth = (source.shape[1], source.shape[2])
    padded = jnp.pad(source, ((0, 0), (1, 1), (1, 1), (0, 0)))
    summed = jnp.zeros(source.shape, jnp.float32)
    for u in range(3):
        for v in range(3):
            summed = summed + kernel[u, v] * padded[:, u:u + height, v:v + breadth, :]
    return summed

def pointwise(source, weight):
    return jnp.einsum('bhwc,dc->bhwd', source, weight, precision=lax.Precision.HIGHEST)

def batch_norm(before, gain_row, bias_row):
    pixels = before.shape[0] * before.shape[1] * before.shape[2]
    average = lax.optimization_barrier(jnp.sum(before, axis=(0, 1, 2))) / pixels
    variance = lax.optimization_barrier(jnp.sum(before * before, axis=(0, 1, 2))) / pixels - average * average
    scaled = (before - average) * lax.rsqrt(variance + EPSILON)
    return (scaled * gain_row + bias_row, average, variance)

def separable(hidden, kernel, weight):
    active = low(jax.nn.silu(hidden))
    spread = low_back(low(depthwise(active, kernel)))
    return low_back(pointwise(spread, weight))

def average_pool(source):
    out_rows = (source.shape[1] + 1) // 2
    out_cols = (source.shape[2] + 1) // 2
    padded = jnp.pad(source, ((0, 0), (1, 1), (1, 1), (0, 0)))
    summed = jnp.zeros((source.shape[0], out_rows, out_cols, source.shape[3]), jnp.float32)
    for u in range(3):
        for v in range(3):
            summed = summed + padded[:, u:u + 2 * out_rows:2, v:v + 2 * out_cols:2, :]
    return summed / 9.0

def forward(inputs, kernel_entry, kernels, project_entry, projects, bn_gains, bn_biases):
    averages = []
    variances = []

    def norm_layer(before, index):
        normed, average, variance = batch_norm(before, bn_gains[index], bn_biases[index])
        averages.append(average)
        variances.append(variance)
        return normed
    normed_one = norm_layer(separable(inputs, kernel_entry, project_entry[0]), 0)
    normed_two = norm_layer(separable(normed_one, kernels[0], projects[0]), 1)
    pre_side = low_back(pointwise(inputs[:, ::2, ::2, :], project_entry[1]))
    merged = average_pool(normed_two) + norm_layer(pre_side, 2)
    hidden = merged
    for i in range(3):
        hidden = norm_layer(separable(hidden, kernels[1 + i], projects[1 + i]), 3 + i)
    return (merged + hidden, (jnp.stack(averages), jnp.stack(variances)))

def reference(inputs, cotangent, kernel_entry, kernels, project_entry, projects, bn_gains, bn_biases, run_means, run_vars):
    floats = tuple((record.astype(jnp.float32) for record in (inputs, kernel_entry, kernels, project_entry, projects)))
    output, pullback, moments = jax.vjp(forward, *floats, bn_gains, bn_biases, has_aux=True)
    gradients = pullback(cotangent.astype(jnp.float32))
    averages, variances = moments
    count_large = float(IMAGES * ROWS * COLS)
    count_small = float(IMAGES * OUT_ROWS * OUT_COLS)
    counts = jnp.array([count_large, count_large] + [count_small] * 4, jnp.float32)[:, None]
    new_means = (1.0 - MOMENTUM) * run_means + MOMENTUM * averages
    new_vars = (1.0 - MOMENTUM) * run_vars + MOMENTUM * variances * counts / (counts - 1.0)
    return (output, gradients[0], gradients[1], gradients[2], gradients[3], gradients[4], gradients[5], gradients[6], new_means, new_vars)
```

```python
import math
import types

import jax
import jax.numpy as jnp
from jax import lax
from jax.experimental import pallas as pl
from jax.experimental.pallas import tpu as pltpu
from jax.sharding import PartitionSpec as P

MESH = pl.DeviceIdType.MESH
EPSILON = 0.001
MOMENTUM = 0.5
LANE = 128
HALF = 64
F32 = jnp.float32
BF16 = jnp.bfloat16


def round_up(value, step):
    return -(-value // step) * step


def aligned(index, step):
    return pl.multiple_of(index, step)


def sigmoid(values):
    return 0.5 * jnp.tanh(0.5 * values) + 0.5


def dot(left, right, dims=(1, 0), precision=None):
    return lax.dot_general(
        left,
        right,
        (((dims[0],), (dims[1],)), ((), ())),
        precision=precision,
        preferred_element_type=F32,
    )


def fold(value):
    return jnp.sum(value.reshape(value.shape[0] // 8, 8, value.shape[1]), axis=0)


def geometry(mesh_shape, inputs, cotangent, project_entry, projects):
    geo = types.SimpleNamespace()
    geo.n_sp, geo.n_ch = mesh_shape["sp"], mesh_shape["ch"]
    geo.bands = geo.n_ch // 2
    geo.group = geo.n_sp * geo.bands
    _, geo.hl, geo.wl, geo.ci = inputs.shape
    _, geo.hs, geo.ws, geo.cc = cotangent.shape
    geo.cin, geo.chan = project_entry.shape[2], projects.shape[2]
    geo.wide = round_up(geo.chan, 2 * LANE)
    geo.half = geo.wide // 2
    geo.shard = geo.wide // geo.n_ch
    geo.tiles = geo.half // LANE
    geo.pl_, geo.ps = round_up(geo.wl + 1, 8), round_up(geo.ws + 1, 8)
    geo.bs = 2 * math.ceil(geo.hs / (2 * geo.bands))
    geo.bl = 2 * geo.bs
    geo.rs, geo.rl = geo.bs + 2, geo.bl + 2
    geo.na = 2 * math.ceil(geo.rl / 4)
    geo.nb = geo.rl - geo.na
    geo.ka = geo.na * geo.pl_
    geo.kb = geo.nb * geo.pl_
    geo.full = geo.n_ch * LANE
    geo.count_large = float(geo.n_sp * geo.hl * geo.wl)
    geo.count_small = float(geo.n_sp * geo.hs * geo.ws)
    return geo


IN_NAMES = [
    "inputs",
    "cotangent",
    "kernel_entry",
    "kernels",
    "project_entry",
    "projects",
    "bn_gains",
    "bn_biases",
    "run_means",
    "run_vars",
]
OUT_NAMES = [
    "o_out",
    "o_gin",
    "o_dke",
    "o_dw",
    "o_dwe",
    "o_dk",
    "o_gains",
    "o_biases",
    "o_means",
    "o_vars",
]


def scratch_table(g):
    dma, vm = pltpu.SemaphoreType.DMA, pltpu.VMEM
    small, large = g.rs * g.ps, g.rl * g.pl_
    cp_rows = (g.bands * g.bl + 2) * g.pl_
    x = g.bands
    return dict(
        x32=vm((cp_rows, LANE), F32),
        a1=vm((cp_rows + 2 * g.pl_, LANE), F32),
        s1=vm((cp_rows, LANE), F32),
        s1pk=vm((x, g.ka, LANE), BF16),
        s1full=vm((g.ka, g.full), BF16),
        sidepk=vm((x, small, LANE), BF16),
        sidefull=vm((small, g.full), BF16),
        sidecp=vm(((x * g.bs + 2) * g.ps, LANE), F32),
        parloc=vm((56, 2 * LANE), F32),
        parx=vm((x, 56, g.half), F32),
        par=vm((56, g.half), F32),
        place=vm((g.wide, g.wide), BF16),
        place_in=vm((2, g.cin, g.full), BF16),
        wpad=vm((g.shard, g.wide), BF16),
        w=vm((4, g.half, g.wide), BF16),
        we=vm((2, g.half, g.cin), BF16),
        wp=vm((3, g.half, g.full), BF16),
        cotpad=vm(((x * g.bs + 2) * g.ps, 2 * LANE), F32),
        cotx=vm(((x * g.bs + 2) * g.ps, g.half), BF16),
        cots=vm((x, small, g.half), BF16),
        cot=vm((small, g.half), F32),
        p1=vm((large, g.half), F32),
        a2=vm((large, g.half), F32),
        s2=vm((g.bl * g.pl_, g.wide), BF16),
        p2=vm((large + 3 * g.pl_, g.half), F32),
        tmp=vm((g.tiles, 48, LANE), F32),
        poolraw=vm((small, g.half), F32),
        pside=vm((small, g.half), F32),
        hid=vm((3, small, g.half), F32),
        act=vm((3, small, g.half), F32),
        sm=vm((3, g.bs * g.ps, g.wide), BF16),
        pm=vm((3, small, g.half), F32),
        gb=vm((3, small, g.half), F32),
        gt=vm((3, small, g.half), F32),
        gs=vm((small, g.half), F32),
        rsend=vm((3, small, g.half), BF16),
        rrecv=vm((3, small, g.half), BF16),
        gside=vm((small, g.half), BF16),
        gt2=vm((large, g.half), F32),
        rsend2=vm((large, g.half), BF16),
        rrecv2=vm((large, g.half), BF16),
        gs2=vm((large, g.half), F32),
        gb1=vm((large, g.half), F32),
        g1=vm((large, g.half), BF16),
        essend=vm((g.ka, x * LANE), BF16),
        esrecv=vm((g.ka, x * LANE), BF16),
        essum=vm((x, g.ka, LANE), BF16),
        esr=vm((x, g.ka, LANE), BF16),
        sdsend=vm((small, x * LANE), BF16),
        sdrecv=vm((small, x * LANE), BF16),
        sdsum=vm((x, small, LANE), BF16),
        sdr=vm((x, small, LANE), BF16),
        gs1=vm((cp_rows, LANE), F32),
        outx=vm((x, g.bs * g.ps, 2 * LANE), BF16),
        outs=vm((x, g.bs * g.ps, 2 * LANE), BF16),
        outf=vm((g.bs * g.ps, 2 * LANE), F32),
        dws=vm((4, g.half, g.wide), BF16),
        dwr=vm((4, x, g.shard, g.wide), BF16),
        dwes=vm((2, g.half, g.cin), BF16),
        dwer=vm((2, x, g.shard, g.cin), BF16),
        dk=vm((40, g.half), F32),
        dkx=vm((x, 40, g.half), F32),
        dke=vm((g.n_sp, 16, LANE), F32),
        vec=vm((56, g.half), F32),
        ar2=vm((5, g.group, 2, g.half), F32),
        ar4=vm((4, g.group, 4, g.half), F32),
        ar_ss=dma((9,)),
        ar_rs=dma((9,)),
        s1_ss=dma((2 * g.n_ch,)),
        s1_rs=dma((g.n_ch,)),
        sd_ss=dma((2 * g.n_ch,)),
        sd_rs=dma((g.n_ch,)),
        par_ss=dma((x,)),
        par_rs=dma((x,)),
        we_ss=dma((2, x)),
        we_rs=dma((2, x)),
        w_ss=dma((4, x)),
        w_rs=dma((4, x)),
        cot_ss=dma((x,)),
        cot_rs=dma((x,)),
        sm_ss=dma((4,)),
        sm_rs=dma((4,)),
        r_ss=dma((4,)),
        r_rs=dma((4,)),
        halo_ss=dma((7, 2)),
        halo_rs=dma((7, 2)),
        es_ss=dma((2,)),
        es_rs=dma((2,)),
        esx_ss=dma((2, x)),
        esx_rs=dma((2, x)),
        out_ss=dma((x,)),
        out_rs=dma((x,)),
        dw_ss=dma((6, x)),
        dw_rs=dma((6, x)),
        dk_ss=dma((x,)),
        dk_rs=dma((x,)),
        dke_ss=dma((1,)),
        dke_rs=dma((1,)),
    )


def make_kernel(g, scratch_names):
    n_bands, half, shard, tiles = g.bands, g.half, g.shard, g.tiles
    pitch, pitch_s = g.pl_, g.ps
    small, large = g.rs * g.ps, g.rl * g.pl_
    AVG, VAR, T1, T0, INV, ALPHA, BETA, KAPPA, LAM = (6 * k for k in range(9))
    counts = (g.count_large, g.count_large) + (g.count_small,) * 4

    def kernel(*refs):
        r = types.SimpleNamespace(**dict(zip(IN_NAMES + OUT_NAMES + scratch_names, refs)))
        s = lax.axis_index("sp")
        ch = lax.axis_index("ch")
        x = ch // 2
        c = lax.rem(ch, 2)
        me = s * n_bands + x
        sends = []

        def copy_to(src, dst, send, recv, s_, x_, c_):
            cp = pltpu.make_async_remote_copy(
                src_ref=src,
                dst_ref=dst,
                send_sem=send,
                recv_sem=recv,
                device_id=(s_, x_ * 2 + c_),
                device_id_type=MESH,
            )
            cp.start()
            sends.append(cp.wait_send)

        def landed(ref, sem):
            pltpu.make_async_copy(ref, ref, sem).wait()

        def other_band(k):
            return lax.rem(x + k, n_bands)

        def edge_copy(src_up, dst_up, src_down, dst_down, e):
            up = pltpu.make_async_remote_copy(
                src_up, dst_up, r.halo_ss.at[e, 0], r.halo_rs.at[e, 0],
                device_id=(s, (x - 1) * 2 + c), device_id_type=MESH)
            down = pltpu.make_async_remote_copy(
                src_down, dst_down, r.halo_ss.at[e, 1], r.halo_rs.at[e, 1],
                device_id=(s, (x + 1) * 2 + c), device_id_type=MESH)

            @pl.when(x > 0)
            def _():
                up.start()

            @pl.when(x < n_bands - 1)
            def _():
                down.start()

            def finish():
                @pl.when(x < n_bands - 1)
                def _():
                    landed(dst_up, r.halo_rs.at[e, 0])

                @pl.when(x > 0)
                def _():
                    landed(dst_down, r.halo_rs.at[e, 1])

            def sent():
                @pl.when(x > 0)
                def _():
                    up.wait_send()

                @pl.when(x < n_bands - 1)
                def _():
                    down.wait_send()

            sends.append(sent)
            return finish

        def edges(ref, e):
            first, last = pl.ds(pitch_s, pitch_s), pl.ds(g.bs * pitch_s, pitch_s)
            return edge_copy(
                ref.at[first], ref.at[pl.ds((g.bs + 1) * pitch_s, pitch_s)],
                ref.at[last], ref.at[pl.ds(0, pitch_s)], e)

        def sum_start(buf, at, e, rows):
            for k, row in enumerate(rows):
                buf[at, me, k : k + 1, :] = row

            def send(k, _):
                to = lax.rem(me + k, g.group)
                pltpu.make_async_remote_copy(
                    buf.at[at, me], buf.at[at, me], r.ar_ss.at[e], r.ar_rs.at[e],
                    device_id=(to // n_bands, lax.rem(to, n_bands) * 2 + c),
                    device_id_type=MESH).start()
                return 0

            lax.fori_loop(1, g.group, send, 0, unroll=g.group <= 16)

        def sum_finish(buf, at, e):
            block = buf.at[at, pl.ds(0, g.group - 1)]
            landed(block, r.ar_rs.at[e])
            sends.append(lambda: landed(block, r.ar_ss.at[e]))
            total = buf[at, 0]
            for k in range(1, g.group):
                total = total + buf[at, k]
            return total

        def fill(ref, start, rows):
            ref[pl.ds(start, rows)] = jnp.zeros((rows,) + ref.shape[1:], ref.dtype)

        def fill_all(ref, step):
            def one(i, _):
                ref[pl.ds(aligned(i * step, 8), step)] = jnp.zeros(
                    (step,) + ref.shape[1:], ref.dtype)
                return 0

            lax.fori_loop(0, ref.shape[0] // step, one, 0)

        def lane(t):
            return pl.ds(t * LANE, LANE)

        def col_mask(width, breadth):
            at = lax.broadcasted_iota(jnp.int32, (width, LANE), 0)
            return jnp.where(at < breadth, 1.0, 0.0).astype(F32)

        def row_ok(row, height):
            return jnp.where((row >= 0) & (row < height), 1.0, 0.0).astype(F32)

        mask_l, mask_s = col_mask(pitch, g.wl), col_mask(pitch_s, g.ws)

        def vrow(kind, layer, t):
            return r.vec[kind + layer : kind + layer + 1, lane(t)]

        def taps_of(base, t):
            return [
                [r.par[base + 3 * u + v : base + 3 * u + v + 1, lane(t)] for v in range(3)]
                for u in range(3)
            ]

        def flip(taps):
            return [[taps[2 - u][2 - v] for v in range(3)] for u in range(3)]

        def conv_row(rows, taps):
            width = rows[0].shape[0]
            side = [
                rows[0] * taps[0][v] + rows[1] * taps[1][v] + rows[2] * taps[2][v]
                for v in range(3)
            ]
            return side[1] + pltpu.roll(side[0], 1, 0) + pltpu.roll(side[2], width - 1, 0)

        def store_moments(layer, total, square):
            n = counts[layer]
            average = total / n
            variance = square / n - average * average
            inverse = lax.rsqrt(variance + EPSILON)
            alpha = inverse * r.par[layer : layer + 1, :]
            r.vec[AVG + layer : AVG + layer + 1, :] = average
            r.vec[VAR + layer : VAR + layer + 1, :] = variance
            r.vec[INV + layer : INV + layer + 1, :] = inverse
            r.vec[ALPHA + layer : ALPHA + layer + 1, :] = alpha
            r.vec[BETA + layer : BETA + layer + 1, :] = (
                r.par[6 + layer : 7 + layer, :] - average * alpha)

        def store_back(layer, total, product):
            n = counts[layer]
            average = r.vec[AVG + layer : AVG + layer + 1, :]
            inverse = r.vec[INV + layer : INV + layer + 1, :]
            alpha = r.vec[ALPHA + layer : ALPHA + layer + 1, :]
            scaled = inverse * (product - average * total)
            r.vec[T0 + layer : T0 + layer + 1, :] = total
            r.vec[T1 + layer : T1 + layer + 1, :] = scaled
            kappa = -alpha * inverse * scaled / n
            r.vec[KAPPA + layer : KAPPA + layer + 1, :] = kappa
            r.vec[LAM + layer : LAM + layer + 1, :] = -alpha * total / n - kappa * average

        def rowsum(value):
            return jnp.sum(value, axis=0, keepdims=True)

        fill_all(r.x32, pitch)
        fill_all(r.a1, pitch)
        fill_all(r.s1, pitch)
        fill_all(r.cotpad, pitch_s)
        fill_all(r.sidecp, pitch_s)
        fill(r.parloc, 0, 56)
        fill_all(r.wpad, 16)
        fill(r.tmp, 0, tiles)
        fill(r.p2, 0, 3 * pitch)
        fill(r.p2, (g.bl + 3) * pitch, 2 * pitch)
        fill(r.gb1, 0, pitch)
        fill(r.gb1, (g.bl + 1) * pitch, pitch)
        fill(r.dk, 0, 40)
        for i in range(3):
            for ref in (r.pm, r.gb):
                ref[i, 0:pitch_s] = jnp.zeros((pitch_s, half), F32)
                ref[i, (g.bs + 1) * pitch_s : small] = jnp.zeros((pitch_s, half), F32)
        for k in range(g.n_sp):
            r.dke[k] = jnp.zeros((16, LANE), F32)

        barrier = pltpu.get_barrier_semaphore()

        def greet(k, _):
            to = lax.rem(me + k, g.group)
            pl.semaphore_signal(
                barrier, inc=1,
                device_id=(to // n_bands, lax.rem(to, n_bands) * 2 + c),
                device_id_type=MESH)
            return 0

        lax.fori_loop(1, g.group, greet, 0)
        pl.semaphore_signal(
            barrier, inc=1, device_id=(s, x * 2 + 1 - c), device_id_type=MESH)

        def entry_silu(row, _):
            value = r.inputs[0, row].astype(F32)
            r.x32[pl.ds(aligned((row + 1) * pitch, 8), g.wl), 0 : g.ci] = value
            r.a1[pl.ds(aligned((row + 2) * pitch, 8), g.wl), 0 : g.ci] = value * sigmoid(value)
            return 0

        lax.fori_loop(0, g.hl, entry_silu, 0)
        r.parloc[0:6, 0 : g.cc] = r.bn_gains[...]
        r.parloc[6:12, 0 : g.cc] = r.bn_biases[...]
        for q in range(4):
            for u in range(3):
                at = 16 + 9 * q + 3 * u
                r.parloc[at : at + 3, 0 : g.cc] = r.kernels[q, u].astype(F32)
        taps_in = [
            [r.kernel_entry[u].astype(F32)[v : v + 1, :] for v in range(3)] for u in range(3)
        ]
        pad_in = jnp.zeros((1, LANE - g.ci), F32)
        taps_in = [[jnp.concatenate([k, pad_in], axis=1) for k in row] for row in taps_in]

        def entry_conv(row, _):
            rows = [
                r.a1[pl.ds(aligned((row + 1 + u) * pitch, 8), pitch), :] for u in range(3)
            ]
            r.s1[pl.ds(aligned((row + 1) * pitch, 8), pitch), :] = (
                conv_row(rows, taps_in) * mask_l)
            return 0

        lax.fori_loop(0, g.hl, entry_conv, 0)
        for b in range(n_bands):
            for k in range(g.na // 2):
                packed = r.s1[(b * g.bl + 2 * k) * pitch : (b * g.bl + 2 * k + 2) * pitch, :]
                if 2 * k < g.nb:
                    at = (b * g.bl + g.na + 2 * k) * pitch
                    packed = packed + pltpu.roll(r.s1[at : at + 2 * pitch, :], HALF, 1)
                r.s1pk[b, 2 * k * pitch : (2 * k + 2) * pitch, :] = packed.astype(BF16)
        for e in range(2):
            r.wpad[0 : g.cc, 0 : g.cin] = r.project_entry[e]
            r.we[e, pl.ds(aligned(x * shard, 16), shard), :] = r.wpad[:, 0 : g.cin]

        pl.semaphore_wait(barrier, g.group)
        tile = c * n_bands + x

        def full_lanes(t):
            return pl.ds(aligned(t * LANE, LANE), LANE)

        for k in range(1, n_bands):
            b = other_band(k)
            copy_to(r.s1pk.at[b], r.s1full.at[:, full_lanes(tile)],
                    r.s1_ss.at[k], r.s1_rs.at[tile], s, b, c)
        copy_to(r.s1pk.at[x], r.s1full.at[:, full_lanes(tile)],
                r.s1_ss.at[0], r.s1_rs.at[tile], s, x, 1 - c)
        r.s1full[:, full_lanes(tile)] = r.s1pk[x]
        for k in range(1, n_bands):
            mine = r.we.at[0, pl.ds(aligned(x * shard, 16), shard)]
            copy_to(mine, mine, r.we_ss.at[0, k], r.we_rs.at[0, x], s, other_band(k), c)

        spot = lax.broadcasted_iota(jnp.int32, (2 * LANE, half), 1) - x * shard
        pick = jnp.where(
            (spot == lax.broadcasted_iota(jnp.int32, (2 * LANE, half), 0)) & (spot < g.cc),
            1.0, 0.0).astype(F32)
        r.parx[x] = dot(r.parloc[...], pick, precision=lax.Precision.HIGHEST)
        for k in range(1, n_bands):
            copy_to(r.parx.at[x], r.parx.at[x], r.par_ss.at[k], r.par_rs.at[x],
                    s, other_band(k), c)

        r.sidecp[...] = jnp.zeros_like(r.sidecp)

        def side_row(row, _):
            at = aligned((2 * row + 1) * pitch, 8)
            r.sidecp[pl.ds(aligned((row + 1) * pitch_s, 8), g.ws), :] = r.x32[
                pl.ds(at, g.ws, stride=2), :]
            return 0

        lax.fori_loop(0, g.hs, side_row, 0)
        for b in range(n_bands):
            r.sidepk[b] = r.sidecp[b * g.bs * pitch_s : b * g.bs * pitch_s + small, :].astype(BF16)
        for k in range(1, n_bands):
            b = other_band(k)
            copy_to(r.sidepk.at[b], r.sidefull.at[:, full_lanes(tile)],
                    r.sd_ss.at[k], r.sd_rs.at[tile], s, b, c)
        copy_to(r.sidepk.at[x], r.sidefull.at[:, full_lanes(tile)],
                r.sd_ss.at[0], r.sd_rs.at[tile], s, x, 1 - c)
        r.sidefull[:, full_lanes(tile)] = r.sidepk[x]
        for k in range(1, n_bands):
            mine = r.we.at[1, pl.ds(aligned(x * shard, 16), shard)]
            copy_to(mine, mine, r.we_ss.at[1, k], r.we_rs.at[1, x], s, other_band(k), c)

        for k in range(1, n_bands):
            t = c * n_bands + other_band(k)
            landed(r.s1full.at[:, full_lanes(t)], r.s1_rs.at[t])
            copy_to(r.s1full.at[:, full_lanes(t)], r.s1full.at[:, full_lanes(t)],
                    r.s1_ss.at[g.n_ch + k], r.s1_rs.at[t], s, x, 1 - c)

        def channel_place(rows, k0, cols, cut, offset):
            k_at = k0 + lax.broadcasted_iota(jnp.int32, (rows, cols), 0)
            p_at = lax.broadcasted_iota(jnp.int32, (rows, cols), 1)
            want = k_at + offset(0)
            for j in range(1, g.n_ch):
                jump = offset(j) - offset(j - 1)
                want = want + jnp.where(k_at >= j * cut, jump, 0)
            return jnp.where(want == p_at, 1.0, 0.0).astype(BF16)

        def offset_wide(j):
            return (j % 2) * half + (j // 2) * shard - j * g.cc

        def offset_in(j):
            return ((j % 2) * n_bands + j // 2) * LANE - j * g.ci

        r.place_in[0] = channel_place(g.cin, 0, g.full, g.ci, offset_in)
        r.place_in[1] = channel_place(
            g.cin, 0, g.full, g.ci, lambda j: offset_in(j) + HALF)
        for k in range(1, n_bands):
            b = other_band(k)
            landed(r.we.at[0, pl.ds(aligned(b * shard, 16), shard)], r.we_rs.at[0, b])
        for a in range(2):
            r.wp[a] = dot(r.we[0], r.place_in[a]).astype(BF16)

        def place_rows(k, _):
            at = aligned(k * 64, 64)
            r.place[pl.ds(at, 64), :] = channel_place(64, at, g.wide, g.cc, offset_wide)
            return 0

        lax.fori_loop(0, g.wide // 64, place_rows, 0)
        fill_all(r.wpad, 16)

        def weight_prepare(q):
            r.wpad[0 : g.cc, 0 : g.chan] = r.projects[q]
            r.w[q, pl.ds(aligned(x * shard, 16), shard), :] = dot(
                r.wpad[...], r.place[...]).astype(BF16)
            for k in range(1, n_bands):
                mine = r.w.at[q, pl.ds(aligned(x * shard, 16), shard)]
                copy_to(mine, mine, r.w_ss.at[q, k], r.w_rs.at[q, x], s, other_band(k), c)

        def weight_landed(q):
            for k in range(1, n_bands):
                b = other_band(k)
                landed(r.w.at[q, pl.ds(aligned(b * shard, 16), shard)], r.w_rs.at[q, b])

        for k in range(n_bands):
            t = (1 - c) * n_bands + k
            landed(r.s1full.at[:, full_lanes(t)], r.s1_rs.at[t])
        r.p1[0 : g.ka, :] = dot(r.s1full[...], r.wp[0], (1, 1))
        r.p1[g.ka : large, :] = dot(r.s1full[0 : g.kb, :], r.wp[1], (1, 1))

        def moments(ref, first, rows, width):
            out = [[], []]
            for t in range(tiles):
                def one(k, carry):
                    v = ref[pl.ds(aligned((first + k) * width, 8), width), lane(t)]
                    return (carry[0] + fold(v), carry[1] + fold(v * v))

                zero = jnp.zeros((8, LANE), F32)
                total, square = lax.fori_loop(0, rows, one, (zero, zero))
                out[0].append(rowsum(total))
                out[1].append(rowsum(square))
            return [jnp.concatenate(o, axis=1) for o in out]

        sum_start(r.ar2, 0, 0, moments(r.p1, 1, g.bl, pitch))
        weight_prepare(0)
        for k in range(1, n_bands):
            b = other_band(k)
            landed(r.parx.at[b], r.par_rs.at[b])
        total = r.parx[0]
        for b in range(1, n_bands):
            total = total + r.parx[b]
        r.par[...] = total
        for k in range(1, n_bands):
            t = c * n_bands + other_band(k)
            landed(r.sidefull.at[:, full_lanes(t)], r.sd_rs.at[t])
            copy_to(r.sidefull.at[:, full_lanes(t)], r.sidefull.at[:, full_lanes(t)],
                    r.sd_ss.at[g.n_ch + k], r.sd_rs.at[t], s, x, 1 - c)
        total = sum_finish(r.ar2, 0, 0)
        store_moments(0, total[0:1], total[1:2])

        for t in range(tiles):
            alpha, beta = vrow(ALPHA, 0, t), vrow(BETA, 0, t)

            def one(k, _):
                at = pl.ds(aligned(k * pitch, 8), pitch)
                h = r.p1[at, lane(t)] * alpha + beta
                ok = mask_l * row_ok(x * g.bl + k - 1, g.hl)
                r.a2[at, lane(t)] = h * sigmoid(h) * ok
                return 0

            lax.fori_loop(0, g.rl, one, 0)
        mine_lanes = aligned(c * half, LANE)
        their_lanes = aligned((1 - c) * half, LANE)

        def own_tile(t):
            return pl.ds(aligned(c * half + t * LANE, LANE), LANE)

        def conv_pairs(source, base, target, row0, rows, height, width, mask):
            for t in range(tiles):
                taps = taps_of(base, t)

                def one(k, _):
                    block = [
                        source[pl.ds(aligned((2 * k + u) * width, 8), width), lane(t)]
                        for u in range(4)
                    ]
                    out = [
                        conv_row(block[j : j + 3], taps) * (mask * row_ok(row0 + 2 * k + j, height))
                        for j in range(2)
                    ]
                    target[pl.ds(aligned(k * 2 * width, 16), 2 * width), own_tile(t)] = (
                        jnp.concatenate(out, axis=0).astype(BF16))
                    return 0

                lax.fori_loop(0, rows // 2, one, 0)

        conv_pairs(r.a2, 16, r.s2, x * g.bl, g.bl, g.hl, pitch, mask_l)

        def swap_start(ref, e):
            mine = ref.at[:, pl.ds(mine_lanes, half)]
            copy_to(mine, mine, r.sm_ss.at[e], r.sm_rs.at[e], s, x, 1 - c)

        def swap_landed(ref, e):
            landed(ref.at[:, pl.ds(their_lanes, half)], r.sm_rs.at[e])

        swap_start(r.s2, 0)
        weight_landed(0)
        rows_all = g.bl * pitch
        step = rows_all // 2
        for k in range(2):
            rows = pl.ds(k * step, step)
            r.p2[3 * pitch + k * step : 3 * pitch + (k + 1) * step, :] = dot(
                r.s2[rows, pl.ds(mine_lanes, half)], r.w[0, :, pl.ds(mine_lanes, half)], (1, 1))
        swap_landed(r.s2, 0)
        for k in range(2):
            rows = pl.ds(k * step, step)
            at = slice(3 * pitch + k * step, 3 * pitch + (k + 1) * step)
            r.p2[at, :] = r.p2[at, :] + dot(
                r.s2[rows, pl.ds(their_lanes, half)], r.w[0, :, pl.ds(their_lanes, half)], (1, 1))
        edges_done = edge_copy(
            r.p2.at[pl.ds(3 * pitch, 2 * pitch)],
            r.p2.at[pl.ds((g.bl + 3) * pitch, 2 * pitch)],
            r.p2.at[pl.ds(g.bl * pitch, 3 * pitch)],
            r.p2.at[pl.ds(0, 3 * pitch)], 0)

        for k in range(1, n_bands):
            b = other_band(k)
            landed(r.we.at[1, pl.ds(aligned(b * shard, 16), shard)], r.we_rs.at[1, b])
        r.wp[2] = dot(r.we[1], r.place_in[0]).astype(BF16)
        for k in range(n_bands):
            t = (1 - c) * n_bands + k
            landed(r.sidefull.at[:, full_lanes(t)], r.sd_rs.at[t])
        r.pside[...] = dot(r.sidefull[...], r.wp[2], (1, 1))
        sum_start(r.ar4, 0, 1,
                  moments(r.p2, 3, g.bl, pitch) + moments(r.pside, 1, g.bs, pitch_s))

        def cot_row(row, _):
            r.cotpad[pl.ds(aligned((row + 1) * pitch_s, 8), g.ws), 0 : g.cc] = (
                r.cotangent[0, row].astype(F32))
            return 0

        lax.fori_loop(0, g.hs, cot_row, 0)
        r.cotx[...] = dot(r.cotpad[...].astype(BF16), pick.astype(BF16)).astype(BF16)
        for k in range(1, n_bands):
            b = other_band(k)
            copy_to(r.cotx.at[pl.ds(aligned(b * g.bs * pitch_s, 16), small)], r.cots.at[x],
                    r.cot_ss.at[k], r.cot_rs.at[x], s, b, c)
        r.cots[x] = r.cotx[pl.ds(aligned(x * g.bs * pitch_s, 16), small), :]
        weight_prepare(1)

        edges_done()
        for t in range(tiles):
            def one(k, _):
                v = (r.p2[pl.ds(aligned(2 * k * pitch, 8), pitch), lane(t)]
                     + r.p2[pl.ds(aligned((2 * k + 1) * pitch, 8), pitch), lane(t)]
                     + r.p2[pl.ds(aligned((2 * k + 2) * pitch, 8), pitch), lane(t)])
                r.tmp[t, 0:pitch, :] = v + pltpu.roll(v, 1, 0) + pltpu.roll(v, pitch - 1, 0)
                r.poolraw[pl.ds(aligned(k * pitch_s, 8), pitch_s), lane(t)] = r.tmp[
                    t, pl.ds(0, pitch_s, stride=2), :]
                return 0

            lax.fori_loop(0, g.rs, one, 0)
        total = sum_finish(r.ar4, 0, 1)
        store_moments(1, total[0:1], total[1:2])
        store_moments(2, total[2:3], total[3:4])

        at_col = lax.broadcasted_iota(jnp.int32, (pitch_s, LANE), 0)
        col_count = mask_s * (
            1.0
            + jnp.where(at_col > 0, 1.0, 0.0)
            + jnp.where(2 * at_col + 1 < g.wl, 1.0, 0.0)) * (1.0 / 9.0)

        def window_count(row):
            inside = jnp.where(row > 0, 1.0, 0.0) + jnp.where(2 * row + 1 < g.hl, 1.0, 0.0) + 1.0
            return col_count * (inside.astype(F32) * row_ok(row, g.hs))

        for t in range(tiles):
            alpha, beta = vrow(ALPHA, 1, t) * (1.0 / 9.0), vrow(BETA, 1, t)
            alpha_2, beta_2 = vrow(ALPHA, 2, t), vrow(BETA, 2, t)

            def one(k, _):
                at = pl.ds(aligned(k * pitch_s, 8), pitch_s)
                row = x * g.bs + k - 1
                ok = mask_s * row_ok(row, g.hs)
                h = (r.poolraw[at, lane(t)] * alpha + window_count(row) * beta
                     + r.pside[at, lane(t)] * alpha_2 + beta_2) * ok
                r.hid[0, at, lane(t)] = h
                r.act[0, at, lane(t)] = h * sigmoid(h)
                return 0

            lax.fori_loop(0, g.rs, one, 0)

        own_rows = slice(pitch_s, (g.bs + 1) * pitch_s)
        for i in range(3):
            if i > 0:
                for t in range(tiles):
                    alpha, beta = vrow(ALPHA, 2 + i, t), vrow(BETA, 2 + i, t)

                    def one(k, _):
                        at = pl.ds(aligned(k * pitch_s, 8), pitch_s)
                        ok = mask_s * row_ok(x * g.bs + k - 1, g.hs)
                        h = (r.pm[i - 1, at, lane(t)] * alpha + beta) * ok
                        r.hid[i, at, lane(t)] = h
                        r.act[i, at, lane(t)] = h * sigmoid(h)
                        return 0

                    lax.fori_loop(0, g.rs, one, 0)
            conv_pairs(r.act.at[i], 16 + 9 * (i + 1), r.sm.at[i], x * g.bs, g.bs, g.hs,
                       pitch_s, mask_s)
            swap_start(r.sm.at[i], 1 + i)
            weight_landed(1 + i)
            part = dot(r.sm[i, :, pl.ds(mine_lanes, half)],
                       r.w[1 + i, :, pl.ds(mine_lanes, half)], (1, 1))
            swap_landed(r.sm.at[i], 1 + i)
            r.pm[i, own_rows, :] = part + dot(
                r.sm[i, :, pl.ds(their_lanes, half)],
                r.w[1 + i, :, pl.ds(their_lanes, half)], (1, 1))
            if i < 2:
                edges_done = edges(r.pm.at[i], 1 + i)
                sum_start(r.ar2, 1 + i, 2 + i, moments(r.pm.at[i], 1, g.bs, pitch_s))
                weight_prepare(2 + i)
                if i == 0:
                    for k in range(1, n_bands):
                        b = other_band(k)
                        landed(r.cots.at[b], r.cot_rs.at[b])
                    total = r.cots[0].astype(F32)
                    for b in range(1, n_bands):
                        total = total + r.cots[b].astype(F32)
                    r.cot[...] = total
                total = sum_finish(r.ar2, 1 + i, 2 + i)
                store_moments(3 + i, total[0:1], total[1:2])
                edges_done()
            else:
                edges_done = edges(r.pm.at[i], 1 + i)
                rows_back = back_sums = None

        def grad_sums(gref, pref, width, first, rows):
            out = [[], []]
            for t in range(tiles):
                def one(k, carry):
                    at = pl.ds(aligned((first + k) * width, 8), width)
                    v = gref[at, lane(t)]
                    return (carry[0] + fold(v), carry[1] + fold(v * pref[at, lane(t)]))

                zero = jnp.zeros((8, LANE), F32)
                a, b = lax.fori_loop(0, rows, one, (zero, zero))
                out[0].append(rowsum(a))
                out[1].append(rowsum(b))
            return [jnp.concatenate(o, axis=1) for o in out]

        sum_start(r.ar4, 1, 4,
                  moments(r.pm.at[2], 1, g.bs, pitch_s)
                  + grad_sums(r.cot, r.pm.at[2], pitch_s, 1, g.bs))
        total = sum_finish(r.ar4, 1, 4)
        store_moments(5, total[0:1], total[1:2])
        store_back(5, total[2:3], total[3:4])
        edges_done()

        def norm_back(layer, gref, pref, target, rows, width, mask, row0, height):
            for t in range(tiles):
                alpha, kappa, lam = vrow(ALPHA, layer, t), vrow(KAPPA, layer, t), vrow(LAM, layer, t)

                def one(k, _):
                    at = pl.ds(aligned(k * width, 8), width)
                    ok = mask * row_ok(row0 + k, height)
                    target[at, lane(t)] = (
                        gref[at, lane(t)] * alpha + pref[at, lane(t)] * kappa + lam) * ok
                    return 0

                lax.fori_loop(0, rows, one, 0)

        def kernel_grad(aref, gref, base, rows, width):
            for t in range(tiles):
                def one(k, carry):
                    gv = gref[pl.ds(aligned((k + 1) * width, 8), width), lane(t)]
                    turned = [pltpu.roll(gv, width - 1, 0), gv, pltpu.roll(gv, 1, 0)]
                    out = []
                    for u in range(3):
                        av = aref[pl.ds(aligned((k + u) * width, 8), width), lane(t)]
                        for v in range(3):
                            out.append(carry[3 * u + v] + fold(av * turned[v]))
                    return tuple(out)

                zero = jnp.zeros((8, LANE), F32)
                sums = lax.fori_loop(0, rows, one, (zero,) * 9)
                for j in range(9):
                    r.dk[base + j : base + j + 1, lane(t)] = rowsum(sums[j])

        def weight_grad_send(q):
            for k in range(1, n_bands):
                b = other_band(k)
                copy_to(r.dws.at[q, pl.ds(aligned(b * shard, 16), shard)], r.dwr.at[q, x],
                        r.dw_ss.at[q, k], r.dw_rs.at[q, x], s, b, c)

        for i in (2, 1, 0):
            layer = 3 + i
            gref = r.cot if i == 2 else r.gb.at[i + 1]
            norm_back(layer, gref, r.pm.at[i], r.gt.at[i], g.rs, pitch_s, mask_s,
                      x * g.bs - 1, g.hs)
            grad = r.gt[i].astype(BF16)
            r.rsend[i] = dot(grad, r.w[1 + i, :, pl.ds(their_lanes, half)]).astype(BF16)
            copy_to(r.rsend.at[i], r.rrecv.at[i], r.r_ss.at[i], r.r_rs.at[i], s, x, 1 - c)
            part = dot(grad, r.w[1 + i, :, pl.ds(mine_lanes, half)])
            landed(r.rrecv.at[i], r.r_rs.at[i])
            r.gs[...] = part + r.rrecv[i].astype(F32)
            rows = [[] for _ in range(4 if i == 0 else 2)]
            for t in range(tiles):
                taps = flip(taps_of(16 + 9 * (i + 1), t))

                def one(k, carry):
                    block = [
                        r.gs[pl.ds(aligned((k + u) * pitch_s, 8), pitch_s), lane(t)]
                        for u in range(3)
                    ]
                    at = pl.ds(aligned((k + 1) * pitch_s, 8), pitch_s)
                    row = x * g.bs + k
                    h = r.hid[i, at, lane(t)]
                    sig = sigmoid(h)
                    value = conv_row(block, taps) * (sig * (1.0 + h * (1.0 - sig))) * (
                        mask_s * row_ok(row, g.hs))
                    if i == 0:
                        value = value + r.cot[at, lane(t)]
                    r.gb[i, at, lane(t)] = value
                    if i == 0:
                        new = [
                            value, value * r.pside[at, lane(t)],
                            value * window_count(row),
                            value * r.poolraw[at, lane(t)] * (1.0 / 9.0)]
                    else:
                        new = [value, value * r.pm[i - 1, at, lane(t)]]
                    return tuple(a + fold(b) for a, b in zip(carry, new))

                zero = jnp.zeros((8, LANE), F32)
                sums = lax.fori_loop(0, g.bs, one, (zero,) * len(rows))
                for j, v in enumerate(sums):
                    rows[j].append(rowsum(v))
            rows = [jnp.concatenate(o, axis=1) for o in rows]
            edges_done = edges(r.gb.at[i], 4 + i)
            buf, at_e, e = ((r.ar4, 2, 7), (r.ar2, 3, 6), (r.ar2, 4, 5))[i]
            sum_start(buf, at_e, e, rows)
            grad = r.gt[i, own_rows, :].astype(BF16)
            r.dws[1 + i] = dot(grad, r.sm[i], (0, 0)).astype(BF16)
            weight_grad_send(1 + i)
            kernel_grad(r.act.at[i], r.gs, 9 * (i + 1), g.bs, pitch_s)
            if i == 2:
                value = []
                for t in range(tiles):
                    h = (r.pm[2, own_rows, lane(t)] * vrow(ALPHA, 5, t) + vrow(BETA, 5, t)
                         + r.hid[0, own_rows, lane(t)])
                    value.append(h.astype(BF16))
                value = jnp.concatenate(value, axis=1)
                for b in range(n_bands):
                    spot_b = lax.broadcasted_iota(jnp.int32, (half, 2 * LANE), 0) - b * shard
                    pick_b = jnp.where(
                        (spot_b == lax.broadcasted_iota(jnp.int32, (half, 2 * LANE), 1))
                        & (spot_b < g.cc), 1.0, 0.0).astype(BF16)
                    r.outx[b] = dot(value, pick_b).astype(BF16)
                for k in range(1, n_bands):
                    b = other_band(k)
                    copy_to(r.outx.at[b], r.outs.at[x], r.out_ss.at[k], r.out_rs.at[x], s, b, c)
                r.outs[x] = r.outx[x]
            total = sum_finish(buf, at_e, e)
            if i > 0:
                store_back(layer - 1, total[0:1], total[1:2])
            else:
                store_back(2, total[0:1], total[1:2])
                store_back(1, total[2:3], total[3:4])
            edges_done()

        for t in range(tiles):
            alpha, kappa, lam = vrow(ALPHA, 1, t) * (1.0 / 9.0), vrow(KAPPA, 1, t), vrow(LAM, 1, t)

            def spread(v):
                r.tmp[t, pl.ds(0, pitch_s, stride=2), :] = v
                r.tmp[t, pl.ds(1, pitch_s, stride=2), :] = v + pltpu.roll(v, pitch_s - 1, 0)
                return r.tmp[t, 0:pitch, :]

            def one(k, _):
                low = r.gb[0, pl.ds(aligned(k * pitch_s, 8), pitch_s), lane(t)]
                high = r.gb[0, pl.ds(aligned((k + 1) * pitch_s, 8), pitch_s), lane(t)]
                for j, v in enumerate((low + high, high)):
                    row = x * g.bl + 2 * k + j - 1
                    ok = mask_l * row_ok(row, g.hl)
                    p = r.p2[pl.ds(aligned((2 * k + j + 2) * pitch, 8), pitch), lane(t)]
                    r.gt2[pl.ds(aligned((2 * k + j) * pitch, 8), pitch), lane(t)] = (
                        spread(v) * alpha + p * kappa + lam) * ok
                return 0

            lax.fori_loop(0, g.bs + 1, one, 0)
        for k in range(2):
            at = pl.ds(k * (large // 2), large // 2)
            r.rsend2[at, :] = dot(
                r.gt2[at, :].astype(BF16), r.w[0, :, pl.ds(their_lanes, half)]).astype(BF16)
        copy_to(r.rsend2, r.rrecv2, r.r_ss.at[3], r.r_rs.at[3], s, x, 1 - c)
        for k in range(2):
            at = pl.ds(k * (large // 2), large // 2)
            r.gs2[at, :] = dot(r.gt2[at, :].astype(BF16), r.w[0, :, pl.ds(mine_lanes, half)])
        landed(r.rrecv2, r.r_rs.at[3])
        r.gs2[...] = r.gs2[...] + r.rrecv2[...].astype(F32)
        rows = [[], []]
        for t in range(tiles):
            taps = flip(taps_of(16, t))
            alpha, beta = vrow(ALPHA, 0, t), vrow(BETA, 0, t)

            def one(k, carry):
                block = [
                    r.gs2[pl.ds(aligned((k + u) * pitch, 8), pitch), lane(t)] for u in range(3)
                ]
                at = pl.ds(aligned((k + 1) * pitch, 8), pitch)
                p = r.p1[at, lane(t)]
                h = p * alpha + beta
                sig = sigmoid(h)
                value = conv_row(block, taps) * (sig * (1.0 + h * (1.0 - sig))) * (
                    mask_l * row_ok(x * g.bl + k, g.hl))
                r.gb1[at, lane(t)] = value
                return (carry[0] + fold(value), carry[1] + fold(value * p))

            zero = jnp.zeros((8, LANE), F32)
            sums = lax.fori_loop(0, g.bl, one, (zero, zero))
            for j, v in enumerate(sums):
                rows[j].append(rowsum(v))
        rows = [jnp.concatenate(o, axis=1) for o in rows]
        sum_start(r.ar4, 3, 8, rows)

        def own_ok(k, width_rows):
            return jnp.where((k >= 1) & (k <= width_rows), 1.0, 0.0).astype(F32)

        for t in range(tiles):
            alpha, kappa, lam = vrow(ALPHA, 2, t), vrow(KAPPA, 2, t), vrow(LAM, 2, t)

            def one(k, _):
                out = []
                for j in range(2):
                    at = pl.ds(aligned((2 * k + j) * pitch_s, 8), pitch_s)
                    ok = mask_s * (row_ok(x * g.bs + 2 * k + j - 1, g.hs) * own_ok(2 * k + j, g.bs))
                    out.append((r.gb[0, at, lane(t)] * alpha
                                + r.pside[at, lane(t)] * kappa + lam) * ok)
                r.gside[pl.ds(aligned(2 * k * pitch_s, 16), 2 * pitch_s), lane(t)] = (
                    jnp.concatenate(out, axis=0).astype(BF16))
                return 0

            lax.fori_loop(0, g.rs // 2, one, 0)
        own_tiles = pl.ds(aligned(c * n_bands * LANE, LANE), n_bands * LANE)
        their_tiles = pl.ds(aligned((1 - c) * n_bands * LANE, LANE), n_bands * LANE)
        r.sdsend[...] = dot(r.gside[...], r.wp[2, :, their_tiles]).astype(BF16)
        copy_to(r.sdsend, r.sdrecv, r.es_ss.at[1], r.es_rs.at[1], s, x, 1 - c)
        part = dot(r.gside[...], r.wp[2, :, own_tiles])
        landed(r.sdrecv, r.es_rs.at[1])
        part = part + r.sdrecv[...].astype(F32)
        for b in range(n_bands):
            r.sdsum[b] = part[:, b * LANE : (b + 1) * LANE].astype(BF16)
        for k in range(1, n_bands):
            b = other_band(k)
            copy_to(r.sdsum.at[b], r.sdr.at[x], r.esx_ss.at[1, k], r.esx_rs.at[1, x], s, b, c)
        r.sdr[x] = r.sdsum[x]

        lane_at = lax.broadcasted_iota(jnp.int32, (half, g.full), 1)
        low_lanes = lax.rem(lane_at, LANE) < HALF
        both_place = r.place_in[0] + r.place_in[1]

        def entry_weight_grad(e, value):
            r.dwes[e] = dot(value.astype(BF16), both_place, (1, 1)).astype(BF16)
            for k in range(1, n_bands):
                b = other_band(k)
                copy_to(r.dwes.at[e, pl.ds(aligned(b * shard, 16), shard)], r.dwer.at[e, x],
                        r.dw_ss.at[4 + e, k], r.dw_rs.at[4 + e, x], s, b, c)

        entry_weight_grad(1, dot(r.gside[...], r.sidefull[...], (0, 0)))
        r.dws[0] = dot(
            r.gt2[pitch : (g.bl + 1) * pitch, :].astype(BF16), r.s2[...], (0, 0)).astype(BF16)
        weight_grad_send(0)
        kernel_grad(r.a2, r.gs2, 0, g.bl, pitch)
        for k in range(1, n_bands):
            copy_to(r.dk, r.dkx.at[x], r.dk_ss.at[k], r.dk_rs.at[x], s, other_band(k), c)
        r.dkx[x] = r.dk[...]
        total = sum_finish(r.ar4, 3, 8)
        store_back(0, total[0:1], total[1:2])

        for t in range(tiles):
            alpha, kappa, lam = vrow(ALPHA, 0, t), vrow(KAPPA, 0, t), vrow(LAM, 0, t)

            def one(k, _):
                out = []
                for j in range(2):
                    at = pl.ds(aligned((2 * k + j) * pitch, 8), pitch)
                    ok = mask_l * (row_ok(x * g.bl + 2 * k + j - 1, g.hl) * own_ok(2 * k + j, g.bl))
                    out.append((r.gb1[at, lane(t)] * alpha + r.p1[at, lane(t)] * kappa + lam) * ok)
                r.g1[pl.ds(aligned(2 * k * pitch, 16), 2 * pitch), lane(t)] = (
                    jnp.concatenate(out, axis=0).astype(BF16))
                return 0

            lax.fori_loop(0, g.rl // 2, one, 0)

        def entry_part(lanes):
            a = dot(r.g1[0 : g.ka, :], r.wp[0, :, lanes])
            b = dot(r.g1[g.ka : large, :], r.wp[1, :, lanes])
            if g.kb == g.ka:
                return a + b
            return jnp.concatenate([a[0 : g.kb] + b, a[g.kb :]], axis=0)

        r.essend[...] = entry_part(their_tiles).astype(BF16)
        copy_to(r.essend, r.esrecv, r.es_ss.at[0], r.es_rs.at[0], s, x, 1 - c)
        part = entry_part(own_tiles)
        landed(r.esrecv, r.es_rs.at[0])
        part = part + r.esrecv[...].astype(F32)
        for b in range(n_bands):
            r.essum[b] = part[:, b * LANE : (b + 1) * LANE].astype(BF16)
        for k in range(1, n_bands):
            b = other_band(k)
            copy_to(r.essum.at[b], r.esr.at[x], r.esx_ss.at[0, k], r.esx_rs.at[0, x], s, b, c)
        r.esr[x] = r.essum[x]
        grad_a = dot(r.g1[0 : g.ka, :], r.s1full[...], (0, 0))
        grad_b = dot(r.g1[g.ka : large, :], r.s1full[0 : g.kb, :], (0, 0))
        entry_weight_grad(0, jnp.where(low_lanes, grad_a, grad_b))

        spot = lax.broadcasted_iota(jnp.int32, (half, 2 * LANE), 0) - x * shard
        pick_own = jnp.where(
            (spot == lax.broadcasted_iota(jnp.int32, (half, 2 * LANE), 1)) & (spot < g.cc),
            1.0, 0.0).astype(F32)
        final = dot(r.vec[0:24, :], pick_own, precision=lax.Precision.HIGHEST)
        final = final[:, 0 : g.cc]
        at_row = lax.broadcasted_iota(jnp.int32, (6, g.cc), 0)
        count = jnp.where(at_row < 2, g.count_large, g.count_small)
        bessel = count / (count - 1.0)
        r.o_means[...] = (1.0 - MOMENTUM) * r.run_means[...] + MOMENTUM * final[0:6]
        r.o_vars[...] = (1.0 - MOMENTUM) * r.run_vars[...] + MOMENTUM * (final[6:12] * bessel)
        r.o_gains[...] = final[12:18]
        r.o_biases[...] = final[18:24]

        for k in range(1, n_bands):
            b = other_band(k)
            landed(r.outs.at[b], r.out_rs.at[b])
        for b in range(n_bands):
            r.outf[...] = r.outs[b].astype(F32)
            for k in range(g.bs):
                if b * g.bs + k < g.hs:
                    r.o_out[0, b * g.bs + k] = r.outf[k * pitch_s : k * pitch_s + g.ws, 0 : g.cc]

        for k in range(1, n_bands):
            b = other_band(k)
            landed(r.sdr.at[b], r.esx_rs.at[1, b])
        for b in range(n_bands):
            r.sidecp[b * g.bs * pitch_s : (b + 1) * g.bs * pitch_s, :] = (
                r.sdr[b].astype(F32)[pitch_s : (g.bs + 1) * pitch_s])
        for k in range(1, n_bands):
            b = other_band(k)
            landed(r.esr.at[b], r.esx_rs.at[0, b])
        fill(r.gs1, 0, pitch)
        fill(r.gs1, (n_bands * g.bl + 1) * pitch, pitch)
        for b in range(n_bands):
            for k in range(g.na // 2):
                value = r.esr[b, 2 * k * pitch : (2 * k + 2) * pitch, :].astype(F32)
                for j in range(2):
                    i = 2 * k + j
                    if 1 <= i <= g.bl:
                        at = (b * g.bl + i) * pitch
                        r.gs1[at : at + pitch, :] = value[j * pitch : (j + 1) * pitch]
                if 2 * k < g.nb:
                    value = pltpu.roll(value, HALF, 1)
                    for j in range(2):
                        i = g.na + 2 * k + j
                        if 1 <= i <= g.bl:
                            at = (b * g.bl + i) * pitch
                            r.gs1[at : at + pitch, :] = value[j * pitch : (j + 1) * pitch]
        taps = flip(taps_in)

        def in_grad(row):
            block = [r.gs1[pl.ds(aligned((row + u) * pitch, 8), pitch), :] for u in range(3)]
            h = r.x32[pl.ds(aligned((row + 1) * pitch, 8), pitch), :]
            sig = sigmoid(h)
            return conv_row(block, taps) * (sig * (1.0 + h * (1.0 - sig)))

        r.tmp[0] = jnp.zeros((48, LANE), F32)

        def in_rows(k, _):
            r.tmp[0, pl.ds(0, pitch_s, stride=2), :] = r.sidecp[
                pl.ds(aligned(k * pitch_s, 8), pitch_s), :]
            value = in_grad(2 * k) + r.tmp[0, 0:pitch, :]
            r.o_gin[0, 2 * k] = value[0 : g.wl, 0 : g.ci]

            @pl.when(2 * k + 1 < g.hl)
            def _():
                r.o_gin[0, 2 * k + 1] = in_grad(2 * k + 1)[0 : g.wl, 0 : g.ci]

            return 0

        lax.fori_loop(0, g.hs, in_rows, 0)

        def entry_kernel(k, carry):
            gv = r.gs1[pl.ds(aligned((k + 1) * pitch, 8), pitch), :]
            turned = [pltpu.roll(gv, pitch - 1, 0), gv, pltpu.roll(gv, 1, 0)]
            out = []
            for u in range(3):
                av = r.a1[pl.ds(aligned((k + 1 + u) * pitch, 8), pitch), :]
                for v in range(3):
                    out.append(carry[3 * u + v] + fold(av * turned[v]))
            return tuple(out)

        zero = jnp.zeros((8, LANE), F32)
        sums = lax.fori_loop(0, g.hl, entry_kernel, (zero,) * 9)
        for j in range(9):
            r.dke[s, j : j + 1, :] = rowsum(sums[j])

        def send(k, _):
            to = lax.rem(s + k, g.n_sp)
            pltpu.make_async_remote_copy(
                r.dke.at[s], r.dke.at[s], r.dke_ss.at[0], r.dke_rs.at[0],
                device_id=(to, ch), device_id_type=MESH).start()
            return 0

        lax.fori_loop(1, g.n_sp, send, 0, unroll=g.n_sp <= 16)

        for q in (3, 2, 1, 0):
            total = r.dws[q, pl.ds(aligned(x * shard, 16), shard), :].astype(F32)
            for k in range(1, n_bands):
                b = other_band(k)
                landed(r.dwr.at[q, b], r.dw_rs.at[q, b])
                total = total + r.dwr[q, b].astype(F32)
            r.o_dw[q] = total.astype(BF16)
        for e in (1, 0):
            total = r.dwes[e, pl.ds(aligned(x * shard, 16), shard), :].astype(F32)
            for k in range(1, n_bands):
                b = other_band(k)
                landed(r.dwer.at[e, b], r.dw_rs.at[4 + e, b])
                total = total + r.dwer[e, b].astype(F32)
            r.o_dwe[e] = total.astype(BF16)
        for k in range(1, n_bands):
            b = other_band(k)
            landed(r.dkx.at[b], r.dk_rs.at[b])
        total = r.dkx[0]
        for b in range(1, n_bands):
            total = total + r.dkx[b]
        r.o_dk[...] = total

        block = r.dke.at[pl.ds(0, g.n_sp - 1)]
        landed(block, r.dke_rs.at[0])
        sends.append(lambda: landed(block, r.dke_ss.at[0]))
        total = r.dke[0]
        for k in range(1, g.n_sp):
            total = total + r.dke[k]
        r.o_dke[...] = total
        for wait in sends:
            wait()

    return kernel


def body(mesh_shape, *args):
    inputs, cotangent, kernel_entry, kernels, project_entry, projects = args[:6]
    g = geometry(mesh_shape, inputs, cotangent, project_entry, projects)
    table = scratch_table(g)
    names = list(table)
    shapes = [
        (cotangent.shape, F32),
        (inputs.shape, F32),
        ((16, LANE), F32),
        ((4, g.shard, g.wide), BF16),
        ((2, g.shard, g.cin), BF16),
        ((40, g.half), F32),
    ] + [((6, g.cc), F32)] * 4
    vmem = pl.BlockSpec(memory_space=pltpu.VMEM)
    out = pl.pallas_call(
        make_kernel(g, names),
        out_shape=[jax.ShapeDtypeStruct(shape, kind) for shape, kind in shapes],
        in_specs=[vmem] * 10,
        out_specs=[vmem] * 10,
        scratch_shapes=list(table.values()),
        compiler_params=pltpu.CompilerParams(
            collective_id=0, has_side_effects=True, vmem_limit_bytes=60 << 20),
    )(*args)
    x = lax.axis_index("ch") // 2
    dw = lax.psum(out[3], "sp").astype(F32)
    dwe = lax.psum(out[4], "sp").astype(F32)
    dk = lax.psum(out[5], "sp")
    dw = dw[:, : g.cc].reshape(4, g.cc, 2, g.bands, g.shard)[..., : g.cc]
    dw = jnp.swapaxes(dw, 2, 3).reshape(4, g.cc, g.chan)
    dk = lax.dynamic_slice(dk[:36], (0, x * g.shard), (36, g.cc)).reshape(4, 3, 3, g.cc)
    dke = out[2][:9, : g.ci].reshape(3, 3, g.ci)
    return (out[0], out[1], dke, dk, dwe[:, : g.cc], dw, out[6], out[7], out[8], out[9])


def solution(mesh):
    mesh_shape = dict(mesh.shape)
    wide = P("sp", None, None, "ch")
    row = P(None, "ch")
    mid = P(None, "ch", None)
    return jax.shard_map(
        lambda *args: body(mesh_shape, *args),
        mesh=mesh,
        in_specs=(wide, wide, P(None, None, "ch"), P(None, None, None, "ch"), mid, mid,
                  row, row, row, row),
        out_specs=(wide, wide, P(None, None, "ch"), P(None, None, None, "ch"), mid, mid,
                   row, row, row, row),
        check_vma=False,
    )
```

```python
import math
import types

import jax
import jax.numpy as jnp
from jax import lax
from jax.experimental import pallas as pl
from jax.experimental.pallas import tpu as pltpu
from jax.sharding import PartitionSpec as P

MESH = pl.DeviceIdType.MESH
EPSILON = 0.001
MOMENTUM = 0.5
LANE = 128
HALF = 64
F32 = jnp.float32
BF16 = jnp.bfloat16


def round_up(value, step):
    return -(-value // step) * step


def aligned(index, step):
    return pl.multiple_of(index, step)


def sigmoid(values):
    return 0.5 * jnp.tanh(0.5 * values) + 0.5


def dot(left, right, dims=(1, 0), precision=None):
    return lax.dot_general(
        left,
        right,
        (((dims[0],), (dims[1],)), ((), ())),
        precision=precision,
        preferred_element_type=F32,
    )


def fold(value):
    return jnp.sum(value.reshape(value.shape[0] // 8, 8, value.shape[1]), axis=0)


def geometry(mesh_shape, inputs, cotangent, project_entry, projects):
    geo = types.SimpleNamespace()
    geo.n_sp, geo.n_ch = mesh_shape["sp"], mesh_shape["ch"]
    geo.bands = geo.n_ch // 2
    geo.group = geo.n_sp * geo.bands
    _, geo.hl, geo.wl, geo.ci = inputs.shape
    _, geo.hs, geo.ws, geo.cc = cotangent.shape
    geo.cin, geo.chan = project_entry.shape[2], projects.shape[2]
    geo.wide = round_up(geo.chan, 2 * LANE)
    geo.half = geo.wide // 2
    geo.shard = geo.wide // geo.n_ch
    geo.tiles = geo.half // LANE
    geo.pl_, geo.ps = round_up(geo.wl + 1, 8), round_up(geo.ws + 1, 8)
    geo.bs = 2 * math.ceil(geo.hs / (2 * geo.bands))
    geo.bl = 2 * geo.bs
    geo.rs, geo.rl = geo.bs + 2, geo.bl + 2
    geo.na = 2 * math.ceil(geo.rl / 4)
    geo.nb = geo.rl - geo.na
    geo.ka = geo.na * geo.pl_
    geo.kb = geo.nb * geo.pl_
    geo.full = geo.n_ch * LANE
    geo.ny = geo.bands if geo.n_sp % geo.bands == 0 else 1
    geo.nz = geo.n_sp // geo.ny
    geo.tall = geo.shard // 16
    geo.u_mid = geo.tall * (geo.wide // LANE)
    geo.u_dk = round_up(geo.shard, LANE) // LANE
    geo.u_in = geo.tall * (geo.cin // LANE)
    geo.units = [
        round_up(u, geo.n_sp)
        for u in [geo.u_mid + geo.u_dk] * 3 + [geo.u_mid + geo.u_dk + geo.u_in, geo.u_in]
    ]
    geo.count_large = float(geo.n_sp * geo.hl * geo.wl)
    geo.count_small = float(geo.n_sp * geo.hs * geo.ws)
    return geo


IN_NAMES = [
    "inputs",
    "cotangent",
    "kernel_entry",
    "kernels",
    "project_entry",
    "projects",
    "bn_gains",
    "bn_biases",
    "run_means",
    "run_vars",
]
OUT_NAMES = [
    "o_out",
    "o_gin",
    "o_dke",
    "o_dk",
    "o_dwe",
    "o_dw",
    "o_gains",
    "o_biases",
    "o_means",
    "o_vars",
]


def scratch_table(g):
    dma, vm = pltpu.SemaphoreType.DMA, pltpu.VMEM
    small, large = g.rs * g.ps, g.rl * g.pl_
    cp_rows = (g.bands * g.bl + 2) * g.pl_
    x = g.bands
    table = dict(
        x32=vm((cp_rows, LANE), F32),
        a1=vm((cp_rows + 2 * g.pl_, LANE), F32),
        s1=vm((cp_rows, LANE), F32),
        s1pk=vm((x, g.ka, LANE), BF16),
        s1full=vm((g.ka, g.full), BF16),
        sidepk=vm((x, small, LANE), BF16),
        sidefull=vm((small, g.full), BF16),
        sidecp=vm(((x * g.bs + 2) * g.ps, LANE), F32),
        parloc=vm((56, 2 * LANE), F32),
        parx=vm((x, 56, g.half), F32),
        par=vm((56, g.half), F32),
        place=vm((g.wide, g.wide), BF16),
        place_in=vm((2, g.cin, g.full), BF16),
        wpad=vm((g.shard, g.wide), BF16),
        w=vm((4, g.half, g.wide), BF16),
        we=vm((2, g.half, g.cin), BF16),
        wp=vm((3, g.half, g.full), BF16),
        cotpad=vm(((x * g.bs + 2) * g.ps, 2 * LANE), F32),
        cotx=vm(((x * g.bs + 2) * g.ps, g.half), BF16),
        cots=vm((x, small, g.half), BF16),
        cot=vm((small, g.half), F32),
        p1=vm((large, g.half), F32),
        a2=vm((large, g.half), F32),
        s2=vm((g.bl * g.pl_, g.wide), BF16),
        p2=vm((large + 3 * g.pl_, g.half), F32),
        tmp=vm((g.tiles, 48, LANE), F32),
        poolraw=vm((small, g.half), F32),
        pside=vm((small, g.half), F32),
        hid=vm((3, small, g.half), F32),
        act=vm((3, small, g.half), F32),
        sm=vm((3, g.bs * g.ps, g.wide), BF16),
        pm=vm((3, small, g.half), F32),
        gb=vm((3, small, g.half), F32),
        gt=vm((3, small, g.half), F32),
        gs=vm((small, g.half), F32),
        rsend=vm((3, small, g.half), BF16),
        rrecv=vm((3, small, g.half), BF16),
        gside=vm((small, g.half), BF16),
        gt2=vm((large, g.half), F32),
        rsend2=vm((large, g.half), BF16),
        rrecv2=vm((large, g.half), BF16),
        gs2=vm((large, g.half), F32),
        gb1=vm((large, g.half), F32),
        g1=vm((large, g.half), BF16),
        essend=vm((g.ka, x * LANE), BF16),
        esrecv=vm((g.ka, x * LANE), BF16),
        essum=vm((x, g.ka, LANE), BF16),
        esr=vm((x, g.ka, LANE), BF16),
        sdsend=vm((small, x * LANE), BF16),
        sdrecv=vm((small, x * LANE), BF16),
        sdsum=vm((x, small, LANE), BF16),
        sdr=vm((x, small, LANE), BF16),
        gs1=vm((cp_rows, LANE), F32),
        outx=vm((x, g.bs * g.ps, 2 * LANE), BF16),
        outs=vm((x, g.bs * g.ps, 2 * LANE), BF16),
        outf=vm((g.bs * g.ps, 2 * LANE), F32),
        dk=vm((16, g.half), F32),
        pickb=vm((x, g.half, 2 * LANE), BF16),
        dke=vm((g.n_sp, 16, LANE), F32),
        vec=vm((56, g.half), F32),
        ar2=vm((5, g.group, 2, g.half), F32),
        ar4=vm((4, g.group, 4, g.half), F32),
        ar_ss=dma((9,)),
        ar_rs=dma((9,)),
        s1_ss=dma((2 * g.n_ch,)),
        s1_rs=dma((g.n_ch,)),
        sd_ss=dma((2 * g.n_ch,)),
        sd_rs=dma((g.n_ch,)),
        par_ss=dma((x,)),
        par_rs=dma((x,)),
        we_ss=dma((2, x)),
        we_rs=dma((2, x)),
        w_ss=dma((4, x)),
        w_rs=dma((4, x)),
        cot_ss=dma((x,)),
        cot_rs=dma((x,)),
        sm_ss=dma((4,)),
        sm_rs=dma((4,)),
        r_ss=dma((4,)),
        r_rs=dma((4,)),
        halo_ss=dma((7, 2)),
        halo_rs=dma((7, 2)),
        es_ss=dma((2,)),
        es_rs=dma((2,)),
        esx_ss=dma((2, x)),
        esx_rs=dma((2, x)),
        out_ss=dma((x,)),
        out_rs=dma((x,)),
        rx_ss=dma((5, x)),
        rx_rs=dma((5, x)),
        ry_ss=dma((5, g.ny)),
        ry_rs=dma((5, g.ny)),
        rz_ss=dma((5, g.nz)),
        rz_rs=dma((5, g.nz)),
        gz_ss=dma((5, g.nz)),
        gz_rs=dma((5, g.nz)),
        gy_ss=dma((5, g.ny)),
        gy_rs=dma((5, g.ny)),
        dke_ss=dma((1,)),
        dke_rs=dma((1,)),
    )
    for k, u in enumerate(g.units):
        unit = (16, LANE)
        table.update({
            f"rxs{k}": vm((x, u) + unit, BF16),
            f"rxr{k}": vm((x, u) + unit, BF16),
            f"xs{k}": vm((u,) + unit, BF16),
            f"ryr{k}": vm((g.ny, u // g.ny) + unit, BF16),
            f"ys{k}": vm((u // g.ny,) + unit, BF16),
            f"rzr{k}": vm((g.nz, u // g.n_sp) + unit, BF16),
            f"fin{k}": vm((u,) + unit, BF16),
        })
    return table


def make_kernel(g, scratch_names):
    n_bands, half, shard, tiles = g.bands, g.half, g.shard, g.tiles
    pitch, pitch_s = g.pl_, g.ps
    small, large = g.rs * g.ps, g.rl * g.pl_
    AVG, VAR, T1, T0, INV, ALPHA, BETA, KAPPA, LAM = (6 * k for k in range(9))
    counts = (g.count_large, g.count_large) + (g.count_small,) * 4

    def kernel(*refs):
        r = types.SimpleNamespace(**dict(zip(IN_NAMES + OUT_NAMES + scratch_names, refs)))
        s = lax.axis_index("sp")
        ch = lax.axis_index("ch")
        x = ch // 2
        c = lax.rem(ch, 2)
        me = s * n_bands + x
        sends = []

        def copy_to(src, dst, send, recv, s_, x_, c_):
            cp = pltpu.make_async_remote_copy(
                src_ref=src,
                dst_ref=dst,
                send_sem=send,
                recv_sem=recv,
                device_id=(s_, x_ * 2 + c_),
                device_id_type=MESH,
            )
            cp.start()
            sends.append(cp.wait_send)

        def landed(ref, sem):
            pltpu.make_async_copy(ref, ref, sem).wait()

        def other_band(k):
            return lax.rem(x + k, n_bands)

        def edge_copy(src_up, dst_up, src_down, dst_down, e):
            up = pltpu.make_async_remote_copy(
                src_up, dst_up, r.halo_ss.at[e, 0], r.halo_rs.at[e, 0],
                device_id=(s, (x - 1) * 2 + c), device_id_type=MESH)
            down = pltpu.make_async_remote_copy(
                src_down, dst_down, r.halo_ss.at[e, 1], r.halo_rs.at[e, 1],
                device_id=(s, (x + 1) * 2 + c), device_id_type=MESH)

            @pl.when(x > 0)
            def _():
                up.start()

            @pl.when(x < n_bands - 1)
            def _():
                down.start()

            def finish():
                @pl.when(x < n_bands - 1)
                def _():
                    landed(dst_up, r.halo_rs.at[e, 0])

                @pl.when(x > 0)
                def _():
                    landed(dst_down, r.halo_rs.at[e, 1])

            def sent():
                @pl.when(x > 0)
                def _():
                    up.wait_send()

                @pl.when(x < n_bands - 1)
                def _():
                    down.wait_send()

            sends.append(sent)
            return finish

        def edges(ref, e):
            first, last = pl.ds(pitch_s, pitch_s), pl.ds(g.bs * pitch_s, pitch_s)
            return edge_copy(
                ref.at[first], ref.at[pl.ds((g.bs + 1) * pitch_s, pitch_s)],
                ref.at[last], ref.at[pl.ds(0, pitch_s)], e)

        def sum_start(buf, at, e, rows):
            for k, row in enumerate(rows):
                buf[at, me, k : k + 1, :] = row

            def send(k, _):
                to = lax.rem(me + k, g.group)
                pltpu.make_async_remote_copy(
                    buf.at[at, me], buf.at[at, me], r.ar_ss.at[e], r.ar_rs.at[e],
                    device_id=(to // n_bands, lax.rem(to, n_bands) * 2 + c),
                    device_id_type=MESH).start()
                return 0

            lax.fori_loop(1, g.group, send, 0, unroll=g.group <= 16)

        def sum_finish(buf, at, e):
            block = buf.at[at, pl.ds(0, g.group - 1)]
            landed(block, r.ar_rs.at[e])
            sends.append(lambda: landed(block, r.ar_ss.at[e]))
            total = buf[at, 0]
            for k in range(1, g.group):
                total = total + buf[at, k]
            return total

        def fill(ref, start, rows):
            ref[pl.ds(start, rows)] = jnp.zeros((rows,) + ref.shape[1:], ref.dtype)

        def fill_all(ref, step):
            def one(i, _):
                ref[pl.ds(aligned(i * step, 8), step)] = jnp.zeros(
                    (step,) + ref.shape[1:], ref.dtype)
                return 0

            lax.fori_loop(0, ref.shape[0] // step, one, 0)

        def lane(t):
            return pl.ds(t * LANE, LANE)

        def col_mask(width, breadth):
            at = lax.broadcasted_iota(jnp.int32, (width, LANE), 0)
            return jnp.where(at < breadth, 1.0, 0.0).astype(F32)

        def row_ok(row, height):
            return jnp.where((row >= 0) & (row < height), 1.0, 0.0).astype(F32)

        mask_l, mask_s = col_mask(pitch, g.wl), col_mask(pitch_s, g.ws)

        def vrow(kind, layer, t):
            return r.vec[kind + layer : kind + layer + 1, lane(t)]

        def taps_of(base, t):
            return [
                [r.par[base + 3 * u + v : base + 3 * u + v + 1, lane(t)] for v in range(3)]
                for u in range(3)
            ]

        def flip(taps):
            return [[taps[2 - u][2 - v] for v in range(3)] for u in range(3)]

        def conv_row(rows, taps):
            width = rows[0].shape[0]
            side = [
                rows[0] * taps[0][v] + rows[1] * taps[1][v] + rows[2] * taps[2][v]
                for v in range(3)
            ]
            return side[1] + pltpu.roll(side[0], 1, 0) + pltpu.roll(side[2], width - 1, 0)

        def store_moments(layer, total, square):
            n = counts[layer]
            average = total / n
            variance = square / n - average * average
            inverse = lax.rsqrt(variance + EPSILON)
            alpha = inverse * r.par[layer : layer + 1, :]
            r.vec[AVG + layer : AVG + layer + 1, :] = average
            r.vec[VAR + layer : VAR + layer + 1, :] = variance
            r.vec[INV + layer : INV + layer + 1, :] = inverse
            r.vec[ALPHA + layer : ALPHA + layer + 1, :] = alpha
            r.vec[BETA + layer : BETA + layer + 1, :] = (
                r.par[6 + layer : 7 + layer, :] - average * alpha)

        def store_back(layer, total, product):
            n = counts[layer]
            average = r.vec[AVG + layer : AVG + layer + 1, :]
            inverse = r.vec[INV + layer : INV + layer + 1, :]
            alpha = r.vec[ALPHA + layer : ALPHA + layer + 1, :]
            scaled = inverse * (product - average * total)
            r.vec[T0 + layer : T0 + layer + 1, :] = total
            r.vec[T1 + layer : T1 + layer + 1, :] = scaled
            kappa = -alpha * inverse * scaled / n
            r.vec[KAPPA + layer : KAPPA + layer + 1, :] = kappa
            r.vec[LAM + layer : LAM + layer + 1, :] = -alpha * total / n - kappa * average

        def rowsum(value):
            return jnp.sum(value, axis=0, keepdims=True)

        fill_all(r.x32, pitch)
        fill_all(r.a1, pitch)
        fill_all(r.s1, pitch)
        fill_all(r.cotpad, pitch_s)
        fill_all(r.sidecp, pitch_s)
        fill(r.parloc, 0, 56)
        fill_all(r.wpad, 16)
        fill(r.tmp, 0, tiles)
        fill(r.p2, 0, 3 * pitch)
        fill(r.p2, (g.bl + 3) * pitch, 2 * pitch)
        fill(r.gb1, 0, pitch)
        fill(r.gb1, (g.bl + 1) * pitch, pitch)
        fill(r.dk, 0, 16)
        for i in range(3):
            for ref in (r.pm, r.gb):
                ref[i, 0:pitch_s] = jnp.zeros((pitch_s, half), F32)
                ref[i, (g.bs + 1) * pitch_s : small] = jnp.zeros((pitch_s, half), F32)
        for k in range(g.n_sp):
            r.dke[k] = jnp.zeros((16, LANE), F32)

        barrier = pltpu.get_barrier_semaphore()

        def greet(k, _):
            to = lax.rem(me + k, g.group)
            pl.semaphore_signal(
                barrier, inc=1,
                device_id=(to // n_bands, lax.rem(to, n_bands) * 2 + c),
                device_id_type=MESH)
            return 0

        lax.fori_loop(1, g.group, greet, 0)
        pl.semaphore_signal(
            barrier, inc=1, device_id=(s, x * 2 + 1 - c), device_id_type=MESH)

        def entry_silu(row, _):
            value = r.inputs[0, row].astype(F32)
            r.x32[pl.ds(aligned((row + 1) * pitch, 8), g.wl), 0 : g.ci] = value
            r.a1[pl.ds(aligned((row + 2) * pitch, 8), g.wl), 0 : g.ci] = value * sigmoid(value)
            return 0

        lax.fori_loop(0, g.hl, entry_silu, 0)
        r.parloc[0:6, 0 : g.cc] = r.bn_gains[...]
        r.parloc[6:12, 0 : g.cc] = r.bn_biases[...]
        for q in range(4):
            for u in range(3):
                at = 16 + 9 * q + 3 * u
                r.parloc[at : at + 3, 0 : g.cc] = r.kernels[q, u].astype(F32)
        taps_in = [
            [r.kernel_entry[u].astype(F32)[v : v + 1, :] for v in range(3)] for u in range(3)
        ]
        pad_in = jnp.zeros((1, LANE - g.ci), F32)
        taps_in = [[jnp.concatenate([k, pad_in], axis=1) for k in row] for row in taps_in]

        def entry_conv(row, _):
            rows = [
                r.a1[pl.ds(aligned((row + 1 + u) * pitch, 8), pitch), :] for u in range(3)
            ]
            r.s1[pl.ds(aligned((row + 1) * pitch, 8), pitch), :] = (
                conv_row(rows, taps_in) * mask_l)
            return 0

        lax.fori_loop(0, g.hl, entry_conv, 0)
        for b in range(n_bands):
            for k in range(g.na // 2):
                packed = r.s1[(b * g.bl + 2 * k) * pitch : (b * g.bl + 2 * k + 2) * pitch, :]
                if 2 * k < g.nb:
                    at = (b * g.bl + g.na + 2 * k) * pitch
                    packed = packed + pltpu.roll(r.s1[at : at + 2 * pitch, :], HALF, 1)
                r.s1pk[b, 2 * k * pitch : (2 * k + 2) * pitch, :] = packed.astype(BF16)
        for e in range(2):
            r.wpad[0 : g.cc, 0 : g.cin] = r.project_entry[e]
            r.we[e, pl.ds(aligned(x * shard, 16), shard), :] = r.wpad[:, 0 : g.cin]

        pl.semaphore_wait(barrier, g.group)
        tile = c * n_bands + x

        def full_lanes(t):
            return pl.ds(aligned(t * LANE, LANE), LANE)

        for k in range(1, n_bands):
            b = other_band(k)
            copy_to(r.s1pk.at[b], r.s1full.at[:, full_lanes(tile)],
                    r.s1_ss.at[k], r.s1_rs.at[tile], s, b, c)
        copy_to(r.s1pk.at[x], r.s1full.at[:, full_lanes(tile)],
                r.s1_ss.at[0], r.s1_rs.at[tile], s, x, 1 - c)
        r.s1full[:, full_lanes(tile)] = r.s1pk[x]
        for k in range(1, n_bands):
            mine = r.we.at[0, pl.ds(aligned(x * shard, 16), shard)]
            copy_to(mine, mine, r.we_ss.at[0, k], r.we_rs.at[0, x], s, other_band(k), c)

        spot = lax.broadcasted_iota(jnp.int32, (2 * LANE, half), 1) - x * shard
        pick = jnp.where(
            (spot == lax.broadcasted_iota(jnp.int32, (2 * LANE, half), 0)) & (spot < g.cc),
            1.0, 0.0).astype(F32)
        r.parx[x] = dot(r.parloc[...], pick, precision=lax.Precision.HIGHEST)
        for k in range(1, n_bands):
            copy_to(r.parx.at[x], r.parx.at[x], r.par_ss.at[k], r.par_rs.at[x],
                    s, other_band(k), c)

        r.sidecp[...] = jnp.zeros_like(r.sidecp)

        def side_row(row, _):
            at = aligned((2 * row + 1) * pitch, 8)
            r.sidecp[pl.ds(aligned((row + 1) * pitch_s, 8), g.ws), :] = r.x32[
                pl.ds(at, g.ws, stride=2), :]
            return 0

        lax.fori_loop(0, g.hs, side_row, 0)
        for b in range(n_bands):
            r.sidepk[b] = r.sidecp[b * g.bs * pitch_s : b * g.bs * pitch_s + small, :].astype(BF16)
        for k in range(1, n_bands):
            b = other_band(k)
            copy_to(r.sidepk.at[b], r.sidefull.at[:, full_lanes(tile)],
                    r.sd_ss.at[k], r.sd_rs.at[tile], s, b, c)
        copy_to(r.sidepk.at[x], r.sidefull.at[:, full_lanes(tile)],
                r.sd_ss.at[0], r.sd_rs.at[tile], s, x, 1 - c)
        r.sidefull[:, full_lanes(tile)] = r.sidepk[x]
        for k in range(1, n_bands):
            mine = r.we.at[1, pl.ds(aligned(x * shard, 16), shard)]
            copy_to(mine, mine, r.we_ss.at[1, k], r.we_rs.at[1, x], s, other_band(k), c)

        for k in range(1, n_bands):
            t = c * n_bands + other_band(k)
            landed(r.s1full.at[:, full_lanes(t)], r.s1_rs.at[t])
            copy_to(r.s1full.at[:, full_lanes(t)], r.s1full.at[:, full_lanes(t)],
                    r.s1_ss.at[g.n_ch + k], r.s1_rs.at[t], s, x, 1 - c)

        def channel_place(rows, k0, cols, cut, offset):
            k_at = k0 + lax.broadcasted_iota(jnp.int32, (rows, cols), 0)
            p_at = lax.broadcasted_iota(jnp.int32, (rows, cols), 1)
            want = k_at + offset(0)
            for j in range(1, g.n_ch):
                jump = offset(j) - offset(j - 1)
                want = want + jnp.where(k_at >= j * cut, jump, 0)
            return jnp.where(want == p_at, 1.0, 0.0).astype(BF16)

        def offset_wide(j):
            return (j % 2) * half + (j // 2) * shard - j * g.cc

        def offset_in(j):
            return ((j % 2) * n_bands + j // 2) * LANE - j * g.ci

        r.place_in[0] = channel_place(g.cin, 0, g.full, g.ci, offset_in)
        r.place_in[1] = channel_place(
            g.cin, 0, g.full, g.ci, lambda j: offset_in(j) + HALF)
        for k in range(1, n_bands):
            b = other_band(k)
            landed(r.we.at[0, pl.ds(aligned(b * shard, 16), shard)], r.we_rs.at[0, b])
        for a in range(2):
            r.wp[a] = dot(r.we[0], r.place_in[a]).astype(BF16)

        def place_rows(k, _):
            at = aligned(k * 64, 64)
            r.place[pl.ds(at, 64), :] = channel_place(64, at, g.wide, g.cc, offset_wide)
            return 0

        lax.fori_loop(0, g.wide // 64, place_rows, 0)
        fill_all(r.wpad, 16)

        def weight_prepare(q):
            r.wpad[0 : g.cc, 0 : g.chan] = r.projects[q]
            r.w[q, pl.ds(aligned(x * shard, 16), shard), :] = dot(
                r.wpad[...], r.place[...]).astype(BF16)
            for k in range(1, n_bands):
                mine = r.w.at[q, pl.ds(aligned(x * shard, 16), shard)]
                copy_to(mine, mine, r.w_ss.at[q, k], r.w_rs.at[q, x], s, other_band(k), c)

        def weight_landed(q):
            for k in range(1, n_bands):
                b = other_band(k)
                landed(r.w.at[q, pl.ds(aligned(b * shard, 16), shard)], r.w_rs.at[q, b])

        for k in range(n_bands):
            t = (1 - c) * n_bands + k
            landed(r.s1full.at[:, full_lanes(t)], r.s1_rs.at[t])
        r.p1[0 : g.ka, :] = dot(r.s1full[...], r.wp[0], (1, 1))
        r.p1[g.ka : large, :] = dot(r.s1full[0 : g.kb, :], r.wp[1], (1, 1))

        def moments(ref, first, rows, width):
            out = [[], []]
            for t in range(tiles):
                def one(k, carry):
                    v = ref[pl.ds(aligned((first + k) * width, 8), width), lane(t)]
                    return (carry[0] + fold(v), carry[1] + fold(v * v))

                zero = jnp.zeros((8, LANE), F32)
                total, square = lax.fori_loop(0, rows, one, (zero, zero))
                out[0].append(rowsum(total))
                out[1].append(rowsum(square))
            return [jnp.concatenate(o, axis=1) for o in out]

        sum_start(r.ar2, 0, 0, moments(r.p1, 1, g.bl, pitch))
        weight_prepare(0)
        for k in range(1, n_bands):
            b = other_band(k)
            landed(r.parx.at[b], r.par_rs.at[b])
        total = r.parx[0]
        for b in range(1, n_bands):
            total = total + r.parx[b]
        r.par[...] = total
        for k in range(1, n_bands):
            t = c * n_bands + other_band(k)
            landed(r.sidefull.at[:, full_lanes(t)], r.sd_rs.at[t])
            copy_to(r.sidefull.at[:, full_lanes(t)], r.sidefull.at[:, full_lanes(t)],
                    r.sd_ss.at[g.n_ch + k], r.sd_rs.at[t], s, x, 1 - c)
        total = sum_finish(r.ar2, 0, 0)
        store_moments(0, total[0:1], total[1:2])

        for t in range(tiles):
            alpha, beta = vrow(ALPHA, 0, t), vrow(BETA, 0, t)

            def one(k, _):
                at = pl.ds(aligned(k * pitch, 8), pitch)
                h = r.p1[at, lane(t)] * alpha + beta
                ok = mask_l * row_ok(x * g.bl + k - 1, g.hl)
                r.a2[at, lane(t)] = h * sigmoid(h) * ok
                return 0

            lax.fori_loop(0, g.rl, one, 0)
        mine_lanes = aligned(c * half, LANE)
        their_lanes = aligned((1 - c) * half, LANE)

        def own_tile(t):
            return pl.ds(aligned(c * half + t * LANE, LANE), LANE)

        def conv_pairs(source, base, target, row0, rows, height, width, mask):
            for t in range(tiles):
                taps = taps_of(base, t)

                def one(k, _):
                    block = [
                        source[pl.ds(aligned((2 * k + u) * width, 8), width), lane(t)]
                        for u in range(4)
                    ]
                    out = [
                        conv_row(block[j : j + 3], taps) * (mask * row_ok(row0 + 2 * k + j, height))
                        for j in range(2)
                    ]
                    target[pl.ds(aligned(k * 2 * width, 16), 2 * width), own_tile(t)] = (
                        jnp.concatenate(out, axis=0).astype(BF16))
                    return 0

                lax.fori_loop(0, rows // 2, one, 0)

        conv_pairs(r.a2, 16, r.s2, x * g.bl, g.bl, g.hl, pitch, mask_l)

        def swap_start(ref, e):
            mine = ref.at[:, pl.ds(mine_lanes, half)]
            copy_to(mine, mine, r.sm_ss.at[e], r.sm_rs.at[e], s, x, 1 - c)

        def swap_landed(ref, e):
            landed(ref.at[:, pl.ds(their_lanes, half)], r.sm_rs.at[e])

        swap_start(r.s2, 0)
        weight_landed(0)
        rows_all = g.bl * pitch
        step = rows_all // 2
        for k in range(2):
            rows = pl.ds(k * step, step)
            r.p2[3 * pitch + k * step : 3 * pitch + (k + 1) * step, :] = dot(
                r.s2[rows, pl.ds(mine_lanes, half)], r.w[0, :, pl.ds(mine_lanes, half)], (1, 1))
        swap_landed(r.s2, 0)
        for k in range(2):
            rows = pl.ds(k * step, step)
            at = slice(3 * pitch + k * step, 3 * pitch + (k + 1) * step)
            r.p2[at, :] = r.p2[at, :] + dot(
                r.s2[rows, pl.ds(their_lanes, half)], r.w[0, :, pl.ds(their_lanes, half)], (1, 1))
        edges_done = edge_copy(
            r.p2.at[pl.ds(3 * pitch, 2 * pitch)],
            r.p2.at[pl.ds((g.bl + 3) * pitch, 2 * pitch)],
            r.p2.at[pl.ds(g.bl * pitch, 3 * pitch)],
            r.p2.at[pl.ds(0, 3 * pitch)], 0)

        for k in range(1, n_bands):
            b = other_band(k)
            landed(r.we.at[1, pl.ds(aligned(b * shard, 16), shard)], r.we_rs.at[1, b])
        r.wp[2] = dot(r.we[1], r.place_in[0]).astype(BF16)
        for k in range(n_bands):
            t = (1 - c) * n_bands + k
            landed(r.sidefull.at[:, full_lanes(t)], r.sd_rs.at[t])
        r.pside[...] = dot(r.sidefull[...], r.wp[2], (1, 1))
        sum_start(r.ar4, 0, 1,
                  moments(r.p2, 3, g.bl, pitch) + moments(r.pside, 1, g.bs, pitch_s))

        def cot_row(row, _):
            r.cotpad[pl.ds(aligned((row + 1) * pitch_s, 8), g.ws), 0 : g.cc] = (
                r.cotangent[0, row].astype(F32))
            return 0

        lax.fori_loop(0, g.hs, cot_row, 0)
        r.cotx[...] = dot(r.cotpad[...].astype(BF16), pick.astype(BF16)).astype(BF16)
        for k in range(1, n_bands):
            b = other_band(k)
            copy_to(r.cotx.at[pl.ds(aligned(b * g.bs * pitch_s, 16), small)], r.cots.at[x],
                    r.cot_ss.at[k], r.cot_rs.at[x], s, b, c)
        r.cots[x] = r.cotx[pl.ds(aligned(x * g.bs * pitch_s, 16), small), :]
        weight_prepare(1)

        edges_done()
        for t in range(tiles):
            def one(k, _):
                v = (r.p2[pl.ds(aligned(2 * k * pitch, 8), pitch), lane(t)]
                     + r.p2[pl.ds(aligned((2 * k + 1) * pitch, 8), pitch), lane(t)]
                     + r.p2[pl.ds(aligned((2 * k + 2) * pitch, 8), pitch), lane(t)])
                r.tmp[t, 0:pitch, :] = v + pltpu.roll(v, 1, 0) + pltpu.roll(v, pitch - 1, 0)
                r.poolraw[pl.ds(aligned(k * pitch_s, 8), pitch_s), lane(t)] = r.tmp[
                    t, pl.ds(0, pitch_s, stride=2), :]
                return 0

            lax.fori_loop(0, g.rs, one, 0)
        total = sum_finish(r.ar4, 0, 1)
        store_moments(1, total[0:1], total[1:2])
        store_moments(2, total[2:3], total[3:4])

        at_col = lax.broadcasted_iota(jnp.int32, (pitch_s, LANE), 0)
        col_count = mask_s * (
            1.0
            + jnp.where(at_col > 0, 1.0, 0.0)
            + jnp.where(2 * at_col + 1 < g.wl, 1.0, 0.0)) * (1.0 / 9.0)

        def window_count(row):
            inside = jnp.where(row > 0, 1.0, 0.0) + jnp.where(2 * row + 1 < g.hl, 1.0, 0.0) + 1.0
            return col_count * (inside.astype(F32) * row_ok(row, g.hs))

        for t in range(tiles):
            alpha, beta = vrow(ALPHA, 1, t) * (1.0 / 9.0), vrow(BETA, 1, t)
            alpha_2, beta_2 = vrow(ALPHA, 2, t), vrow(BETA, 2, t)

            def one(k, _):
                at = pl.ds(aligned(k * pitch_s, 8), pitch_s)
                row = x * g.bs + k - 1
                ok = mask_s * row_ok(row, g.hs)
                h = (r.poolraw[at, lane(t)] * alpha + window_count(row) * beta
                     + r.pside[at, lane(t)] * alpha_2 + beta_2) * ok
                r.hid[0, at, lane(t)] = h
                r.act[0, at, lane(t)] = h * sigmoid(h)
                return 0

            lax.fori_loop(0, g.rs, one, 0)

        own_rows = slice(pitch_s, (g.bs + 1) * pitch_s)
        for i in range(3):
            if i > 0:
                for t in range(tiles):
                    alpha, beta = vrow(ALPHA, 2 + i, t), vrow(BETA, 2 + i, t)

                    def one(k, _):
                        at = pl.ds(aligned(k * pitch_s, 8), pitch_s)
                        ok = mask_s * row_ok(x * g.bs + k - 1, g.hs)
                        h = (r.pm[i - 1, at, lane(t)] * alpha + beta) * ok
                        r.hid[i, at, lane(t)] = h
                        r.act[i, at, lane(t)] = h * sigmoid(h)
                        return 0

                    lax.fori_loop(0, g.rs, one, 0)
            conv_pairs(r.act.at[i], 16 + 9 * (i + 1), r.sm.at[i], x * g.bs, g.bs, g.hs,
                       pitch_s, mask_s)
            swap_start(r.sm.at[i], 1 + i)
            weight_landed(1 + i)
            part = dot(r.sm[i, :, pl.ds(mine_lanes, half)],
                       r.w[1 + i, :, pl.ds(mine_lanes, half)], (1, 1))
            swap_landed(r.sm.at[i], 1 + i)
            r.pm[i, own_rows, :] = part + dot(
                r.sm[i, :, pl.ds(their_lanes, half)],
                r.w[1 + i, :, pl.ds(their_lanes, half)], (1, 1))
            if i < 2:
                edges_done = edges(r.pm.at[i], 1 + i)
                sum_start(r.ar2, 1 + i, 2 + i, moments(r.pm.at[i], 1, g.bs, pitch_s))
                weight_prepare(2 + i)
                if i == 0:
                    for k in range(1, n_bands):
                        b = other_band(k)
                        landed(r.cots.at[b], r.cot_rs.at[b])
                    total = r.cots[0].astype(F32)
                    for b in range(1, n_bands):
                        total = total + r.cots[b].astype(F32)
                    r.cot[...] = total
                total = sum_finish(r.ar2, 1 + i, 2 + i)
                store_moments(3 + i, total[0:1], total[1:2])
                edges_done()
            else:
                edges_done = edges(r.pm.at[i], 1 + i)
                rows_back = back_sums = None

        def grad_sums(gref, pref, width, first, rows):
            out = [[], []]
            for t in range(tiles):
                def one(k, carry):
                    at = pl.ds(aligned((first + k) * width, 8), width)
                    v = gref[at, lane(t)]
                    return (carry[0] + fold(v), carry[1] + fold(v * pref[at, lane(t)]))

                zero = jnp.zeros((8, LANE), F32)
                a, b = lax.fori_loop(0, rows, one, (zero, zero))
                out[0].append(rowsum(a))
                out[1].append(rowsum(b))
            return [jnp.concatenate(o, axis=1) for o in out]

        sum_start(r.ar4, 1, 4,
                  moments(r.pm.at[2], 1, g.bs, pitch_s)
                  + grad_sums(r.cot, r.pm.at[2], pitch_s, 1, g.bs))
        total = sum_finish(r.ar4, 1, 4)
        store_moments(5, total[0:1], total[1:2])
        store_back(5, total[2:3], total[3:4])
        edges_done()

        def norm_back(layer, gref, pref, target, rows, width, mask, row0, height):
            for t in range(tiles):
                alpha, kappa, lam = vrow(ALPHA, layer, t), vrow(KAPPA, layer, t), vrow(LAM, layer, t)

                def one(k, _):
                    at = pl.ds(aligned(k * width, 8), width)
                    ok = mask * row_ok(row0 + k, height)
                    target[at, lane(t)] = (
                        gref[at, lane(t)] * alpha + pref[at, lane(t)] * kappa + lam) * ok
                    return 0

                lax.fori_loop(0, rows, one, 0)

        def kernel_grad(aref, gref, rows, width):
            for t in range(tiles):
                def one(k, carry):
                    gv = gref[pl.ds(aligned((k + 1) * width, 8), width), lane(t)]
                    turned = [pltpu.roll(gv, width - 1, 0), gv, pltpu.roll(gv, 1, 0)]
                    out = []
                    for u in range(3):
                        av = aref[pl.ds(aligned((k + u) * width, 8), width), lane(t)]
                        for v in range(3):
                            out.append(carry[3 * u + v] + fold(av * turned[v]))
                    return tuple(out)

                zero = jnp.zeros((8, LANE), F32)
                sums = lax.fori_loop(0, rows, one, (zero,) * 9)
                for j in range(9):
                    r.dk[j : j + 1, lane(t)] = rowsum(sums[j])

        yi, zi = lax.rem(s, g.ny), s // g.ny

        def block_of(name, k):
            return getattr(r, f"{name}{k}")

        def put_units(k, first, value, cols):
            value = value.astype(BF16)
            for b in range(n_bands):
                for t in range(cols // LANE):
                    part = value[b * shard : (b + 1) * shard, t * LANE : (t + 1) * LANE]
                    block_of("rxs", k)[b, first + t * g.tall : first + (t + 1) * g.tall] = (
                        part.reshape(g.tall, 16, LANE))

        def put_kernel(k):
            value = r.dk[...].astype(BF16)
            for b in range(n_bands):
                part = dot(value, r.pickb[b]).astype(BF16)
                for t in range(g.u_dk):
                    block_of("rxs", k)[b, g.u_mid + t] = part[:, t * LANE : (t + 1) * LANE]

        def x_send(k):
            for j in range(1, n_bands):
                b = other_band(j)
                copy_to(block_of("rxs", k).at[b], block_of("rxr", k).at[x],
                        r.rx_ss.at[k, j], r.rx_rs.at[k, x], s, b, c)

        def x_sum_y_send(k):
            total = block_of("rxs", k)[x].astype(F32)
            for j in range(1, n_bands):
                b = other_band(j)
                landed(block_of("rxr", k).at[b], r.rx_rs.at[k, b])
                total = total + block_of("rxr", k)[b].astype(F32)
            block_of("xs", k)[...] = total.astype(BF16)
            part = g.units[k] // g.ny
            for j in range(1, g.ny):
                to = lax.rem(yi + j, g.ny)
                copy_to(block_of("xs", k).at[pl.ds(to * part, part)], block_of("ryr", k).at[yi],
                        r.ry_ss.at[k, j], r.ry_rs.at[k, yi], zi * g.ny + to, x, c)

        def y_sum_z_send(k):
            part = g.units[k] // g.ny
            total = block_of("xs", k)[pl.ds(yi * part, part)].astype(F32)
            for j in range(1, g.ny):
                b = lax.rem(yi + j, g.ny)
                landed(block_of("ryr", k).at[b], r.ry_rs.at[k, b])
                total = total + block_of("ryr", k)[b].astype(F32)
            block_of("ys", k)[...] = total.astype(BF16)
            piece = part // g.nz
            for j in range(1, g.nz):
                to = lax.rem(zi + j, g.nz)
                copy_to(block_of("ys", k).at[pl.ds(to * piece, piece)], block_of("rzr", k).at[zi],
                        r.rz_ss.at[k, j], r.rz_rs.at[k, zi], to * g.ny + yi, x, c)

        def z_sum_z_gather(k):
            part = g.units[k] // g.ny
            piece = part // g.nz
            total = block_of("ys", k)[pl.ds(zi * piece, piece)].astype(F32)
            for j in range(1, g.nz):
                b = lax.rem(zi + j, g.nz)
                landed(block_of("rzr", k).at[b], r.rz_rs.at[k, b])
                total = total + block_of("rzr", k)[b].astype(F32)
            at = pl.ds(yi * part + zi * piece, piece)
            block_of("fin", k)[at] = total.astype(BF16)
            for j in range(1, g.nz):
                to = lax.rem(zi + j, g.nz)
                copy_to(block_of("fin", k).at[at], block_of("fin", k).at[at],
                        r.gz_ss.at[k, j], r.gz_rs.at[k, zi], to * g.ny + yi, x, c)

        def y_gather(k):
            part = g.units[k] // g.ny
            piece = part // g.nz
            for j in range(1, g.nz):
                b = lax.rem(zi + j, g.nz)
                landed(block_of("fin", k).at[pl.ds(yi * part + b * piece, piece)],
                       r.gz_rs.at[k, b])
            at = pl.ds(yi * part, part)
            for j in range(1, g.ny):
                to = lax.rem(yi + j, g.ny)
                copy_to(block_of("fin", k).at[at], block_of("fin", k).at[at],
                        r.gy_ss.at[k, j], r.gy_rs.at[k, yi], zi * g.ny + to, x, c)

        def get_units(k, first, cols):
            tiles_in = [
                block_of("fin", k)[first + t * g.tall : first + (t + 1) * g.tall].reshape(
                    shard, LANE)
                for t in range(cols // LANE)
            ]
            return jnp.concatenate(tiles_in, axis=1)

        def finish_block(k):
            part = g.units[k] // g.ny
            for j in range(1, g.ny):
                b = lax.rem(yi + j, g.ny)
                landed(block_of("fin", k).at[pl.ds(b * part, part)], r.gy_rs.at[k, b])
            if k < 4:
                q = 3 - k
                value = dot(get_units(k, 0, g.wide), r.place[...], (1, 1))
                r.o_dw[q] = value[0 : g.cc, 0 : g.chan]
                value = jnp.concatenate(
                    [block_of("fin", k)[g.u_mid + t] for t in range(g.u_dk)], axis=1).astype(F32)
                for u in range(3):
                    r.o_dk[q, u] = value[3 * u : 3 * u + 3, 0 : g.cc]
            if k == 3:
                value = get_units(k, g.u_mid + g.u_dk, g.cin)
                r.o_dwe[1] = value[0 : g.cc].astype(F32)
            if k == 4:
                r.o_dwe[0] = get_units(k, 0, g.cin)[0 : g.cc].astype(F32)

        for b in range(n_bands):
            spot_b = lax.broadcasted_iota(jnp.int32, (half, 2 * LANE), 0) - b * shard
            r.pickb[b] = jnp.where(
                (spot_b == lax.broadcasted_iota(jnp.int32, (half, 2 * LANE), 1))
                & (spot_b < g.cc), 1.0, 0.0).astype(BF16)

        for i in (2, 1, 0):
            layer = 3 + i
            gref = r.cot if i == 2 else r.gb.at[i + 1]
            norm_back(layer, gref, r.pm.at[i], r.gt.at[i], g.rs, pitch_s, mask_s,
                      x * g.bs - 1, g.hs)
            grad = r.gt[i].astype(BF16)
            r.rsend[i] = dot(grad, r.w[1 + i, :, pl.ds(their_lanes, half)]).astype(BF16)
            copy_to(r.rsend.at[i], r.rrecv.at[i], r.r_ss.at[i], r.r_rs.at[i], s, x, 1 - c)
            part = dot(grad, r.w[1 + i, :, pl.ds(mine_lanes, half)])
            landed(r.rrecv.at[i], r.r_rs.at[i])
            r.gs[...] = part + r.rrecv[i].astype(F32)
            rows = [[] for _ in range(4 if i == 0 else 2)]
            for t in range(tiles):
                taps = flip(taps_of(16 + 9 * (i + 1), t))

                def one(k, carry):
                    block = [
                        r.gs[pl.ds(aligned((k + u) * pitch_s, 8), pitch_s), lane(t)]
                        for u in range(3)
                    ]
                    at = pl.ds(aligned((k + 1) * pitch_s, 8), pitch_s)
                    row = x * g.bs + k
                    h = r.hid[i, at, lane(t)]
                    sig = sigmoid(h)
                    value = conv_row(block, taps) * (sig * (1.0 + h * (1.0 - sig))) * (
                        mask_s * row_ok(row, g.hs))
                    if i == 0:
                        value = value + r.cot[at, lane(t)]
                    r.gb[i, at, lane(t)] = value
                    if i == 0:
                        new = [
                            value, value * r.pside[at, lane(t)],
                            value * window_count(row),
                            value * r.poolraw[at, lane(t)] * (1.0 / 9.0)]
                    else:
                        new = [value, value * r.pm[i - 1, at, lane(t)]]
                    return tuple(a + fold(b) for a, b in zip(carry, new))

                zero = jnp.zeros((8, LANE), F32)
                sums = lax.fori_loop(0, g.bs, one, (zero,) * len(rows))
                for j, v in enumerate(sums):
                    rows[j].append(rowsum(v))
            rows = [jnp.concatenate(o, axis=1) for o in rows]
            edges_done = edges(r.gb.at[i], 4 + i)
            buf, at_e, e = ((r.ar4, 2, 7), (r.ar2, 3, 6), (r.ar2, 4, 5))[i]
            sum_start(buf, at_e, e, rows)
            grad = r.gt[i, own_rows, :].astype(BF16)
            if i < 2:
                x_sum_y_send(1 - i)
            if i == 0:
                y_sum_z_send(0)
            put_units(2 - i, 0, dot(grad, r.sm[i], (0, 0)), g.wide)
            kernel_grad(r.act.at[i], r.gs, g.bs, pitch_s)
            put_kernel(2 - i)
            x_send(2 - i)
            if i == 2:
                value = []
                for t in range(tiles):
                    h = (r.pm[2, own_rows, lane(t)] * vrow(ALPHA, 5, t) + vrow(BETA, 5, t)
                         + r.hid[0, own_rows, lane(t)])
                    value.append(h.astype(BF16))
                value = jnp.concatenate(value, axis=1)
                for b in range(n_bands):
                    r.outx[b] = dot(value, r.pickb[b]).astype(BF16)
                for k in range(1, n_bands):
                    b = other_band(k)
                    copy_to(r.outx.at[b], r.outs.at[x], r.out_ss.at[k], r.out_rs.at[x], s, b, c)
                r.outs[x] = r.outx[x]
            total = sum_finish(buf, at_e, e)
            if i > 0:
                store_back(layer - 1, total[0:1], total[1:2])
            else:
                store_back(2, total[0:1], total[1:2])
                store_back(1, total[2:3], total[3:4])
            edges_done()

        for t in range(tiles):
            alpha, kappa, lam = vrow(ALPHA, 1, t) * (1.0 / 9.0), vrow(KAPPA, 1, t), vrow(LAM, 1, t)

            def spread(v):
                r.tmp[t, pl.ds(0, pitch_s, stride=2), :] = v
                r.tmp[t, pl.ds(1, pitch_s, stride=2), :] = v + pltpu.roll(v, pitch_s - 1, 0)
                return r.tmp[t, 0:pitch, :]

            def one(k, _):
                low = r.gb[0, pl.ds(aligned(k * pitch_s, 8), pitch_s), lane(t)]
                high = r.gb[0, pl.ds(aligned((k + 1) * pitch_s, 8), pitch_s), lane(t)]
                for j, v in enumerate((low + high, high)):
                    row = x * g.bl + 2 * k + j - 1
                    ok = mask_l * row_ok(row, g.hl)
                    p = r.p2[pl.ds(aligned((2 * k + j + 2) * pitch, 8), pitch), lane(t)]
                    r.gt2[pl.ds(aligned((2 * k + j) * pitch, 8), pitch), lane(t)] = (
                        spread(v) * alpha + p * kappa + lam) * ok
                return 0

            lax.fori_loop(0, g.bs + 1, one, 0)
        for k in range(2):
            at = pl.ds(k * (large // 2), large // 2)
            r.rsend2[at, :] = dot(
                r.gt2[at, :].astype(BF16), r.w[0, :, pl.ds(their_lanes, half)]).astype(BF16)
        copy_to(r.rsend2, r.rrecv2, r.r_ss.at[3], r.r_rs.at[3], s, x, 1 - c)
        for k in range(2):
            at = pl.ds(k * (large // 2), large // 2)
            r.gs2[at, :] = dot(r.gt2[at, :].astype(BF16), r.w[0, :, pl.ds(mine_lanes, half)])
        z_sum_z_gather(0)
        landed(r.rrecv2, r.r_rs.at[3])
        r.gs2[...] = r.gs2[...] + r.rrecv2[...].astype(F32)
        rows = [[], []]
        for t in range(tiles):
            taps = flip(taps_of(16, t))
            alpha, beta = vrow(ALPHA, 0, t), vrow(BETA, 0, t)

            def one(k, carry):
                block = [
                    r.gs2[pl.ds(aligned((k + u) * pitch, 8), pitch), lane(t)] for u in range(3)
                ]
                at = pl.ds(aligned((k + 1) * pitch, 8), pitch)
                p = r.p1[at, lane(t)]
                h = p * alpha + beta
                sig = sigmoid(h)
                value = conv_row(block, taps) * (sig * (1.0 + h * (1.0 - sig))) * (
                    mask_l * row_ok(x * g.bl + k, g.hl))
                r.gb1[at, lane(t)] = value
                return (carry[0] + fold(value), carry[1] + fold(value * p))

            zero = jnp.zeros((8, LANE), F32)
            sums = lax.fori_loop(0, g.bl, one, (zero, zero))
            for j, v in enumerate(sums):
                rows[j].append(rowsum(v))
        rows = [jnp.concatenate(o, axis=1) for o in rows]
        sum_start(r.ar4, 3, 8, rows)

        def own_ok(k, width_rows):
            return jnp.where((k >= 1) & (k <= width_rows), 1.0, 0.0).astype(F32)

        for t in range(tiles):
            alpha, kappa, lam = vrow(ALPHA, 2, t), vrow(KAPPA, 2, t), vrow(LAM, 2, t)

            def one(k, _):
                out = []
                for j in range(2):
                    at = pl.ds(aligned((2 * k + j) * pitch_s, 8), pitch_s)
                    ok = mask_s * (row_ok(x * g.bs + 2 * k + j - 1, g.hs) * own_ok(2 * k + j, g.bs))
                    out.append((r.gb[0, at, lane(t)] * alpha
                                + r.pside[at, lane(t)] * kappa + lam) * ok)
                r.gside[pl.ds(aligned(2 * k * pitch_s, 16), 2 * pitch_s), lane(t)] = (
                    jnp.concatenate(out, axis=0).astype(BF16))
                return 0

            lax.fori_loop(0, g.rs // 2, one, 0)
        own_tiles = pl.ds(aligned(c * n_bands * LANE, LANE), n_bands * LANE)
        their_tiles = pl.ds(aligned((1 - c) * n_bands * LANE, LANE), n_bands * LANE)
        r.sdsend[...] = dot(r.gside[...], r.wp[2, :, their_tiles]).astype(BF16)
        copy_to(r.sdsend, r.sdrecv, r.es_ss.at[1], r.es_rs.at[1], s, x, 1 - c)
        part = dot(r.gside[...], r.wp[2, :, own_tiles])
        landed(r.sdrecv, r.es_rs.at[1])
        part = part + r.sdrecv[...].astype(F32)
        for b in range(n_bands):
            r.sdsum[b] = part[:, b * LANE : (b + 1) * LANE].astype(BF16)
        for k in range(1, n_bands):
            b = other_band(k)
            copy_to(r.sdsum.at[b], r.sdr.at[x], r.esx_ss.at[1, k], r.esx_rs.at[1, x], s, b, c)
        r.sdr[x] = r.sdsum[x]

        lane_at = lax.broadcasted_iota(jnp.int32, (half, g.full), 1)
        low_lanes = lax.rem(lane_at, LANE) < HALF
        both_place = r.place_in[0] + r.place_in[1]

        x_sum_y_send(2)
        y_sum_z_send(1)
        put_units(3, 0, dot(
            r.gt2[pitch : (g.bl + 1) * pitch, :].astype(BF16), r.s2[...], (0, 0)), g.wide)
        kernel_grad(r.a2, r.gs2, g.bl, pitch)
        put_kernel(3)
        value = dot(r.gside[...], r.sidefull[...], (0, 0)).astype(BF16)
        put_units(3, g.u_mid + g.u_dk, dot(value, both_place, (1, 1)), g.cin)
        x_send(3)
        total = sum_finish(r.ar4, 3, 8)
        store_back(0, total[0:1], total[1:2])

        for t in range(tiles):
            alpha, kappa, lam = vrow(ALPHA, 0, t), vrow(KAPPA, 0, t), vrow(LAM, 0, t)

            def one(k, _):
                out = []
                for j in range(2):
                    at = pl.ds(aligned((2 * k + j) * pitch, 8), pitch)
                    ok = mask_l * (row_ok(x * g.bl + 2 * k + j - 1, g.hl) * own_ok(2 * k + j, g.bl))
                    out.append((r.gb1[at, lane(t)] * alpha + r.p1[at, lane(t)] * kappa + lam) * ok)
                r.g1[pl.ds(aligned(2 * k * pitch, 16), 2 * pitch), lane(t)] = (
                    jnp.concatenate(out, axis=0).astype(BF16))
                return 0

            lax.fori_loop(0, g.rl // 2, one, 0)

        def entry_part(lanes):
            a = dot(r.g1[0 : g.ka, :], r.wp[0, :, lanes])
            b = dot(r.g1[g.ka : large, :], r.wp[1, :, lanes])
            if g.kb == g.ka:
                return a + b
            return jnp.concatenate([a[0 : g.kb] + b, a[g.kb :]], axis=0)

        r.essend[...] = entry_part(their_tiles).astype(BF16)
        copy_to(r.essend, r.esrecv, r.es_ss.at[0], r.es_rs.at[0], s, x, 1 - c)
        part = entry_part(own_tiles)
        landed(r.esrecv, r.es_rs.at[0])
        part = part + r.esrecv[...].astype(F32)
        for b in range(n_bands):
            r.essum[b] = part[:, b * LANE : (b + 1) * LANE].astype(BF16)
        for k in range(1, n_bands):
            b = other_band(k)
            copy_to(r.essum.at[b], r.esr.at[x], r.esx_ss.at[0, k], r.esx_rs.at[0, x], s, b, c)
        r.esr[x] = r.essum[x]
        grad_a = dot(r.g1[0 : g.ka, :], r.s1full[...], (0, 0))
        grad_b = dot(r.g1[g.ka : large, :], r.s1full[0 : g.kb, :], (0, 0))
        value = jnp.where(low_lanes, grad_a, grad_b).astype(BF16)
        put_units(4, 0, dot(value, both_place, (1, 1)), g.cin)
        x_send(4)
        y_gather(0)
        z_sum_z_gather(1)
        y_sum_z_send(2)
        x_sum_y_send(3)

        spot = lax.broadcasted_iota(jnp.int32, (half, 2 * LANE), 0) - x * shard
        pick_own = jnp.where(
            (spot == lax.broadcasted_iota(jnp.int32, (half, 2 * LANE), 1)) & (spot < g.cc),
            1.0, 0.0).astype(F32)
        final = dot(r.vec[0:24, :], pick_own, precision=lax.Precision.HIGHEST)
        final = final[:, 0 : g.cc]
        at_row = lax.broadcasted_iota(jnp.int32, (6, g.cc), 0)
        count = jnp.where(at_row < 2, g.count_large, g.count_small)
        bessel = count / (count - 1.0)
        r.o_means[...] = (1.0 - MOMENTUM) * r.run_means[...] + MOMENTUM * final[0:6]
        r.o_vars[...] = (1.0 - MOMENTUM) * r.run_vars[...] + MOMENTUM * (final[6:12] * bessel)
        r.o_gains[...] = final[12:18]
        r.o_biases[...] = final[18:24]

        for k in range(1, n_bands):
            b = other_band(k)
            landed(r.outs.at[b], r.out_rs.at[b])
        for b in range(n_bands):
            r.outf[...] = r.outs[b].astype(F32)
            for k in range(g.bs):
                if b * g.bs + k < g.hs:
                    r.o_out[0, b * g.bs + k] = r.outf[k * pitch_s : k * pitch_s + g.ws, 0 : g.cc]

        for k in range(1, n_bands):
            b = other_band(k)
            landed(r.sdr.at[b], r.esx_rs.at[1, b])
        for b in range(n_bands):
            r.sidecp[b * g.bs * pitch_s : (b + 1) * g.bs * pitch_s, :] = (
                r.sdr[b].astype(F32)[pitch_s : (g.bs + 1) * pitch_s])
        for k in range(1, n_bands):
            b = other_band(k)
            landed(r.esr.at[b], r.esx_rs.at[0, b])
        fill(r.gs1, 0, pitch)
        fill(r.gs1, (n_bands * g.bl + 1) * pitch, pitch)
        for b in range(n_bands):
            for k in range(g.na // 2):
                value = r.esr[b, 2 * k * pitch : (2 * k + 2) * pitch, :].astype(F32)
                for j in range(2):
                    i = 2 * k + j
                    if 1 <= i <= g.bl:
                        at = (b * g.bl + i) * pitch
                        r.gs1[at : at + pitch, :] = value[j * pitch : (j + 1) * pitch]
                if 2 * k < g.nb:
                    value = pltpu.roll(value, HALF, 1)
                    for j in range(2):
                        i = g.na + 2 * k + j
                        if 1 <= i <= g.bl:
                            at = (b * g.bl + i) * pitch
                            r.gs1[at : at + pitch, :] = value[j * pitch : (j + 1) * pitch]
        taps = flip(taps_in)

        def in_grad(row):
            block = [r.gs1[pl.ds(aligned((row + u) * pitch, 8), pitch), :] for u in range(3)]
            h = r.x32[pl.ds(aligned((row + 1) * pitch, 8), pitch), :]
            sig = sigmoid(h)
            return conv_row(block, taps) * (sig * (1.0 + h * (1.0 - sig)))

        r.tmp[0] = jnp.zeros((48, LANE), F32)

        def in_rows(k, _):
            r.tmp[0, pl.ds(0, pitch_s, stride=2), :] = r.sidecp[
                pl.ds(aligned(k * pitch_s, 8), pitch_s), :]
            value = in_grad(2 * k) + r.tmp[0, 0:pitch, :]
            r.o_gin[0, 2 * k] = value[0 : g.wl, 0 : g.ci]

            @pl.when(2 * k + 1 < g.hl)
            def _():
                r.o_gin[0, 2 * k + 1] = in_grad(2 * k + 1)[0 : g.wl, 0 : g.ci]

            return 0

        lax.fori_loop(0, g.hs, in_rows, 0)

        def entry_kernel(k, carry):
            gv = r.gs1[pl.ds(aligned((k + 1) * pitch, 8), pitch), :]
            turned = [pltpu.roll(gv, pitch - 1, 0), gv, pltpu.roll(gv, 1, 0)]
            out = []
            for u in range(3):
                av = r.a1[pl.ds(aligned((k + 1 + u) * pitch, 8), pitch), :]
                for v in range(3):
                    out.append(carry[3 * u + v] + fold(av * turned[v]))
            return tuple(out)

        zero = jnp.zeros((8, LANE), F32)
        sums = lax.fori_loop(0, g.hl, entry_kernel, (zero,) * 9)
        for j in range(9):
            r.dke[s, j : j + 1, :] = rowsum(sums[j])

        def send(k, _):
            to = lax.rem(s + k, g.n_sp)
            pltpu.make_async_remote_copy(
                r.dke.at[s], r.dke.at[s], r.dke_ss.at[0], r.dke_rs.at[0],
                device_id=(to, ch), device_id_type=MESH).start()
            return 0

        lax.fori_loop(1, g.n_sp, send, 0, unroll=g.n_sp <= 16)

        x_sum_y_send(4)
        y_gather(1)
        z_sum_z_gather(2)
        y_sum_z_send(3)
        finish_block(0)
        y_sum_z_send(4)
        y_gather(2)
        z_sum_z_gather(3)
        finish_block(1)
        z_sum_z_gather(4)
        y_gather(3)
        finish_block(2)
        y_gather(4)
        finish_block(3)
        finish_block(4)
        block = r.dke.at[pl.ds(0, g.n_sp - 1)]
        landed(block, r.dke_rs.at[0])
        sends.append(lambda: landed(block, r.dke_ss.at[0]))
        total = r.dke[0]
        for k in range(1, g.n_sp):
            total = total + r.dke[k]
        for u in range(3):
            r.o_dke[u] = total[3 * u : 3 * u + 3, 0 : g.ci]
        for wait in sends:
            wait()

    return kernel


def body(mesh_shape, *args):
    inputs, cotangent, kernel_entry, kernels, project_entry, projects = args[:6]
    g = geometry(mesh_shape, inputs, cotangent, project_entry, projects)
    table = scratch_table(g)
    names = list(table)
    shapes = [
        (cotangent.shape, F32),
        (inputs.shape, F32),
        (kernel_entry.shape, F32),
        (kernels.shape, F32),
        (project_entry.shape, F32),
        (projects.shape, F32),
    ] + [((6, g.cc), F32)] * 4
    vmem = pl.BlockSpec(memory_space=pltpu.VMEM)
    out = pl.pallas_call(
        make_kernel(g, names),
        out_shape=[jax.ShapeDtypeStruct(shape, kind) for shape, kind in shapes],
        in_specs=[vmem] * 10,
        out_specs=[vmem] * 10,
        scratch_shapes=list(table.values()),
        compiler_params=pltpu.CompilerParams(
            collective_id=0, has_side_effects=True, vmem_limit_bytes=60 << 20),
    )(*args)
    return tuple(out)


def solution(mesh):
    mesh_shape = dict(mesh.shape)
    wide = P("sp", None, None, "ch")
    row = P(None, "ch")
    mid = P(None, "ch", None)
    return jax.shard_map(
        lambda *args: body(mesh_shape, *args),
        mesh=mesh,
        in_specs=(wide, wide, P(None, None, "ch"), P(None, None, None, "ch"), mid, mid,
                  row, row, row, row),
        out_specs=(wide, wide, P(None, None, "ch"), P(None, None, None, "ch"), mid, mid,
                   row, row, row, row),
        check_vma=False,
    )
```

```python
import math
import types

import jax
import jax.numpy as jnp
from jax import lax
from jax.experimental import pallas as pl
from jax.experimental.pallas import tpu as pltpu
from jax.sharding import PartitionSpec as P

MESH = pl.DeviceIdType.MESH
EPSILON = 0.001
MOMENTUM = 0.5
LANE = 128
HALF = 64
F32 = jnp.float32
BF16 = jnp.bfloat16


def round_up(value, step):
    return -(-value // step) * step


def aligned(index, step):
    return pl.multiple_of(index, step)


def sigmoid(values):
    return 0.5 * jnp.tanh(0.5 * values) + 0.5


def dot(left, right, dims=(1, 0), precision=None):
    return lax.dot_general(
        left,
        right,
        (((dims[0],), (dims[1],)), ((), ())),
        precision=precision,
        preferred_element_type=F32,
    )


def fold(value):
    return jnp.sum(value.reshape(value.shape[0] // 8, 8, value.shape[1]), axis=0)


def geometry(mesh_shape, inputs, cotangent, project_entry, projects):
    geo = types.SimpleNamespace()
    geo.n_sp, geo.n_ch = mesh_shape["sp"], mesh_shape["ch"]
    geo.bands = geo.n_ch // 2
    geo.group = geo.n_sp * geo.bands
    _, geo.hl, geo.wl, geo.ci = inputs.shape
    _, geo.hs, geo.ws, geo.cc = cotangent.shape
    geo.cin, geo.chan = project_entry.shape[2], projects.shape[2]
    geo.wide = round_up(geo.chan, 2 * LANE)
    geo.half = geo.wide // 2
    geo.shard = geo.wide // geo.n_ch
    geo.tiles = geo.half // LANE
    geo.pl_, geo.ps = round_up(geo.wl + 1, 8), round_up(geo.ws + 1, 8)
    geo.bs = 2 * math.ceil(geo.hs / (2 * geo.bands))
    geo.bl = 2 * geo.bs
    geo.rs, geo.rl = geo.bs + 2, geo.bl + 2
    geo.na = 2 * math.ceil(geo.rl / 4)
    geo.nb = geo.rl - geo.na
    geo.ka = geo.na * geo.pl_
    geo.kb = geo.nb * geo.pl_
    geo.full = geo.n_ch * LANE
    geo.ny = geo.bands if geo.n_sp % geo.bands == 0 else 1
    geo.nz = geo.n_sp // geo.ny
    geo.tall = geo.shard // 16
    geo.u_mid = geo.tall * (geo.wide // LANE)
    geo.u_dk = round_up(geo.shard, LANE) // LANE
    geo.u_in = geo.tall * (geo.cin // LANE)
    geo.units = [round_up(geo.u_mid, geo.n_sp)] * 4
    geo.flat_units = [round_up(u, geo.n_sp) for u in (geo.u_in, geo.u_in + 4 * geo.u_dk)]
    geo.count_large = float(geo.n_sp * geo.hl * geo.wl)
    geo.count_small = float(geo.n_sp * geo.hs * geo.ws)
    return geo


IN_NAMES = [
    "inputs",
    "cotangent",
    "kernel_entry",
    "kernels",
    "project_entry",
    "projects",
    "bn_gains",
    "bn_biases",
    "run_means",
    "run_vars",
]
OUT_NAMES = [
    "m_out",
    "m_gin",
    "m_dke",
    "m_dk",
    "m_dwe",
    "m_dw",
    "m_vec",
]


def scratch_table(g):
    dma, vm = pltpu.SemaphoreType.DMA, pltpu.VMEM
    small, large = g.rs * g.ps, g.rl * g.pl_
    cp_rows = (g.bands * g.bl + 2) * g.pl_
    x = g.bands
    table = dict(
        x32=vm((cp_rows, LANE), F32),
        a1=vm((cp_rows + 2 * g.pl_, LANE), F32),
        s1=vm((cp_rows, LANE), F32),
        s1pk=vm((x, g.ka, LANE), BF16),
        s1full=vm((g.ka, g.full), BF16),
        sidepk=vm((x, small, LANE), BF16),
        sidefull=vm((small, g.full), BF16),
        sidecp=vm(((x * g.bs + 2) * g.ps, LANE), F32),
        parloc=vm((56, 2 * LANE), F32),
        parx=vm((x, 56, 2 * LANE), F32),
        par=vm((56, g.half), F32),
        place=vm((g.wide, g.wide), BF16),
        place_in=vm((2, g.cin, g.full), BF16),
        wpad=vm((g.shard, g.wide), BF16),
        w=vm((4, g.half, g.wide), BF16),
        we=vm((2, g.half, g.cin), BF16),
        wp=vm((3, g.half, g.full), BF16),
        cotpad=vm(((x * g.bs + 2) * g.ps, 2 * LANE), F32),
        cotx=vm(((x * g.bs + 2) * g.ps, 2 * LANE), BF16),
        cots=vm((x, small, 2 * LANE), BF16),
        picks=vm((x, 2 * LANE, g.half), F32),
        edge_up=vm((2 * g.pl_, g.half), BF16),
        edge_down=vm((4 * g.pl_, g.half), BF16),
        from_below=vm((2 * g.pl_, g.half), BF16),
        from_above=vm((4 * g.pl_, g.half), BF16),
        cot=vm((small, g.half), F32),
        p1=vm((large, g.half), F32),
        a2=vm((large, g.half), F32),
        s2=vm((g.bl * g.pl_, g.wide), BF16),
        p2=vm((large + 3 * g.pl_, g.half), F32),
        tmp=vm((g.tiles, 48, LANE), F32),
        poolraw=vm((small, g.half), F32),
        pside=vm((small, g.half), F32),
        hid=vm((3, small, g.half), F32),
        act=vm((3, small, g.half), F32),
        sm=vm((3, g.bs * g.ps, g.wide), BF16),
        pm=vm((3, small, g.half), F32),
        gb=vm((3, small, g.half), F32),
        gt=vm((3, small, g.half), F32),
        gs=vm((small, g.half), F32),
        rsend=vm((3, small, g.half), BF16),
        rrecv=vm((3, small, g.half), BF16),
        gside=vm((small, g.half), BF16),
        gt2=vm((large, g.half), F32),
        rsend2=vm((large, g.half), BF16),
        rrecv2=vm((large, g.half), BF16),
        gs2=vm((large, g.half), F32),
        gb1=vm((large, g.half), F32),
        g1=vm((large, g.half), BF16),
        essend=vm((g.ka, x * LANE), BF16),
        esrecv=vm((g.ka, x * LANE), BF16),
        essum=vm((x, g.ka, LANE), BF16),
        esr=vm((x, g.ka, LANE), BF16),
        sdsend=vm((small, x * LANE), BF16),
        sdrecv=vm((small, x * LANE), BF16),
        sdsum=vm((x, small, LANE), BF16),
        sdr=vm((x, small, LANE), BF16),
        gs1=vm((cp_rows, LANE), F32),
        outx=vm((x, g.bs * g.ps, 2 * LANE), BF16),
        outs=vm((x, g.bs * g.ps, 2 * LANE), BF16),
        dk=vm((4, 16, g.half), F32),
        pickb=vm((x, g.half, 2 * LANE), BF16),
        dke=vm((g.n_sp, 16, LANE), F32),
        vec=vm((56, g.half), F32),
        ar2=vm((5, g.group, 2, g.half), F32),
        ar4=vm((4, g.group, 4, g.half), F32),
        ar_ss=dma((9,)),
        ar_rs=dma((9,)),
        s1_ss=dma((2 * g.n_ch,)),
        s1_rs=dma((g.n_ch,)),
        sd_ss=dma((2 * g.n_ch,)),
        sd_rs=dma((g.n_ch,)),
        par_ss=dma((x,)),
        par_rs=dma((x,)),
        we_ss=dma((2, x)),
        we_rs=dma((2, x)),
        w_ss=dma((4, 2 * x)),
        w_rs=dma((4, 2 * x)),
        cot_ss=dma((x,)),
        cot_rs=dma((x,)),
        sm_ss=dma((4,)),
        sm_rs=dma((4,)),
        r_ss=dma((4,)),
        r_rs=dma((4,)),
        halo_ss=dma((7, 2)),
        halo_rs=dma((7, 2)),
        es_ss=dma((2,)),
        es_rs=dma((2,)),
        esx_ss=dma((2, x)),
        esx_rs=dma((2, x)),
        out_ss=dma((x,)),
        out_rs=dma((x,)),
        rx_ss=dma((4, x)),
        rx_rs=dma((4, x)),
        ry_ss=dma((4, g.ny)),
        ry_rs=dma((4, g.ny)),
        rz_ss=dma((4, g.nz)),
        rz_rs=dma((4, g.nz)),
        gz_ss=dma((4, g.nz)),
        gz_rs=dma((4, g.nz)),
        gy_ss=dma((4, g.ny)),
        gy_rs=dma((4, g.ny)),
        dke_ss=dma((1,)),
        dke_rs=dma((1,)),
        fl_ss=dma((2, 2)),
        fl_rs=dma((2, 2)),
    )
    for k, u in enumerate(g.units):
        unit = (16, LANE)
        table.update({
            f"rxs{k}": vm((x, u) + unit, BF16),
            f"rxr{k}": vm((x, u) + unit, BF16),
            f"xs{k}": vm((u,) + unit, BF16),
            f"ryr{k}": vm((g.ny, u // g.ny) + unit, BF16),
            f"ys{k}": vm((u // g.ny,) + unit, BF16),
            f"rzr{k}": vm((g.nz, u // g.n_sp) + unit, BF16),
            f"fin{k}": vm((u,) + unit, BF16),
        })
    for k, u in enumerate(g.flat_units):
        table.update({
            f"fls{k}": vm((x, u) + unit, BF16),
            f"flr{k}": vm((g.group, u // g.n_sp) + unit, BF16),
            f"flf{k}": vm((u,) + unit, BF16),
        })
    return table


def make_kernel(g, scratch_names):
    n_bands, half, shard, tiles = g.bands, g.half, g.shard, g.tiles
    pitch, pitch_s = g.pl_, g.ps
    small, large = g.rs * g.ps, g.rl * g.pl_
    AVG, VAR, T1, T0, INV, ALPHA, BETA, KAPPA, LAM = (6 * k for k in range(9))
    counts = (g.count_large, g.count_large) + (g.count_small,) * 4

    def kernel(*refs):
        r = types.SimpleNamespace(**dict(zip(IN_NAMES + OUT_NAMES + scratch_names, refs)))
        s = lax.axis_index("sp")
        ch = lax.axis_index("ch")
        x = ch // 2
        c = lax.rem(ch, 2)
        me = s * n_bands + x
        sends = []

        def copy_to(src, dst, send, recv, s_, x_, c_):
            cp = pltpu.make_async_remote_copy(
                src_ref=src,
                dst_ref=dst,
                send_sem=send,
                recv_sem=recv,
                device_id=(s_, x_ * 2 + c_),
                device_id_type=MESH,
            )
            cp.start()
            sends.append(cp.wait_send)

        def landed(ref, sem):
            pltpu.make_async_copy(ref, ref, sem).wait()

        def other_band(k):
            return lax.rem(x + k, n_bands)

        def edge_copy(src_up, dst_up, src_down, dst_down, e):
            up = pltpu.make_async_remote_copy(
                src_up, dst_up, r.halo_ss.at[e, 0], r.halo_rs.at[e, 0],
                device_id=(s, (x - 1) * 2 + c), device_id_type=MESH)
            down = pltpu.make_async_remote_copy(
                src_down, dst_down, r.halo_ss.at[e, 1], r.halo_rs.at[e, 1],
                device_id=(s, (x + 1) * 2 + c), device_id_type=MESH)

            @pl.when(x > 0)
            def _():
                up.start()

            @pl.when(x < n_bands - 1)
            def _():
                down.start()

            def finish():
                @pl.when(x < n_bands - 1)
                def _():
                    landed(dst_up, r.halo_rs.at[e, 0])

                @pl.when(x > 0)
                def _():
                    landed(dst_down, r.halo_rs.at[e, 1])

            def sent():
                @pl.when(x > 0)
                def _():
                    up.wait_send()

                @pl.when(x < n_bands - 1)
                def _():
                    down.wait_send()

            sends.append(sent)
            return finish

        def edges(ref, e):
            first, last = pl.ds(pitch_s, pitch_s), pl.ds(g.bs * pitch_s, pitch_s)
            return edge_copy(
                ref.at[first], ref.at[pl.ds((g.bs + 1) * pitch_s, pitch_s)],
                ref.at[last], ref.at[pl.ds(0, pitch_s)], e)

        def flipped(value, key):
            out, bit = 0, 1
            while bit <= key:
                here = lax.rem(value // bit, 2)
                out = out + bit * (1 - here if key & bit else here)
                bit *= 2
            return out + (value // bit) * bit

        def hops(key):
            return key // (n_bands * g.ny) + key // n_bands % g.ny + key % n_bands

        few = g.group <= 16
        keys = sorted(range(1, g.group), key=hops, reverse=True) if few else []
        peers = [
            (flipped(s, key // n_bands), flipped(x, key % n_bands)) for key in keys
        ]

        def to_group(src, dst, send, recv, pick=None):
            def one(s_, x_):
                pltpu.make_async_remote_copy(
                    src if pick is None else pick(s_, x_), dst, send, recv,
                    device_id=(s_, x_ * 2 + c), device_id_type=MESH).start()

            for s_, x_ in peers:
                one(s_, x_)

            def loop(k, _):
                to = lax.rem(me + k, g.group)
                one(to // n_bands, lax.rem(to, n_bands))
                return 0

            if not few:
                lax.fori_loop(1, g.group, loop, 0)

        sp_keys = sorted(range(1, g.n_sp), key=lambda k: hops(k * n_bands), reverse=True)
        sp_peers = [flipped(s, key) for key in sp_keys] if few else []

        def to_images(src, dst, send, recv):
            def one(s_):
                pltpu.make_async_remote_copy(
                    src, dst, send, recv, device_id=(s_, ch), device_id_type=MESH).start()

            for s_ in sp_peers:
                one(s_)

            def loop(k, _):
                one(lax.rem(s + k, g.n_sp))
                return 0

            if not few:
                lax.fori_loop(1, g.n_sp, loop, 0)

        def sum_start(buf, at, e, rows):
            for k, row in enumerate(rows):
                buf[at, me, k : k + 1, :] = row

            to_group(buf.at[at, me], buf.at[at, me], r.ar_ss.at[e], r.ar_rs.at[e])

        def sum_finish(buf, at, e):
            block = buf.at[at, pl.ds(0, g.group - 1)]
            landed(block, r.ar_rs.at[e])
            sends.append(lambda: landed(block, r.ar_ss.at[e]))
            total = buf[at, 0]
            for k in range(1, g.group):
                total = total + buf[at, k]
            return total

        def fill(ref, start, rows):
            ref[pl.ds(start, rows)] = jnp.zeros((rows,) + ref.shape[1:], ref.dtype)

        def fill_all(ref, step):
            def one(i, _):
                ref[pl.ds(aligned(i * step, 8), step)] = jnp.zeros(
                    (step,) + ref.shape[1:], ref.dtype)
                return 0

            lax.fori_loop(0, ref.shape[0] // step, one, 0)

        def lane(t):
            return pl.ds(t * LANE, LANE)

        def col_mask(width, breadth):
            at = lax.broadcasted_iota(jnp.int32, (width, LANE), 0)
            return jnp.where(at < breadth, 1.0, 0.0).astype(F32)

        def row_ok(row, height):
            return jnp.where((row >= 0) & (row < height), 1.0, 0.0).astype(F32)

        mask_l, mask_s = col_mask(pitch, g.wl), col_mask(pitch_s, g.ws)

        def vrow(kind, layer, t):
            return r.vec[kind + layer : kind + layer + 1, lane(t)]

        def taps_of(q, t):
            return [
                [r.par[16 + 4 * (3 * u + v) + q : 17 + 4 * (3 * u + v) + q, lane(t)] for v in range(3)]
                for u in range(3)
            ]

        def flip(taps):
            return [[taps[2 - u][2 - v] for v in range(3)] for u in range(3)]

        def conv_row(rows, taps):
            width = rows[0].shape[0]
            side = [
                rows[0] * taps[0][v] + rows[1] * taps[1][v] + rows[2] * taps[2][v]
                for v in range(3)
            ]
            return side[1] + pltpu.roll(side[0], 1, 0) + pltpu.roll(side[2], width - 1, 0)

        def store_moments(layer, total, square):
            n = counts[layer]
            average = total / n
            variance = square / n - average * average
            inverse = lax.rsqrt(variance + EPSILON)
            alpha = inverse * r.par[layer : layer + 1, :]
            r.vec[AVG + layer : AVG + layer + 1, :] = average
            r.vec[VAR + layer : VAR + layer + 1, :] = variance
            r.vec[INV + layer : INV + layer + 1, :] = inverse
            r.vec[ALPHA + layer : ALPHA + layer + 1, :] = alpha
            r.vec[BETA + layer : BETA + layer + 1, :] = (
                r.par[6 + layer : 7 + layer, :] - average * alpha)

        def store_back(layer, total, product):
            n = counts[layer]
            average = r.vec[AVG + layer : AVG + layer + 1, :]
            inverse = r.vec[INV + layer : INV + layer + 1, :]
            alpha = r.vec[ALPHA + layer : ALPHA + layer + 1, :]
            scaled = inverse * (product - average * total)
            r.vec[T0 + layer : T0 + layer + 1, :] = total
            r.vec[T1 + layer : T1 + layer + 1, :] = scaled
            kappa = -alpha * inverse * scaled / n
            r.vec[KAPPA + layer : KAPPA + layer + 1, :] = kappa
            r.vec[LAM + layer : LAM + layer + 1, :] = -alpha * total / n - kappa * average

        def rowsum(value):
            return jnp.sum(value, axis=0, keepdims=True)

        fill_all(r.x32, pitch)
        fill_all(r.a1, pitch)
        fill(r.s1, 0, pitch)
        fill(r.s1, (g.hl + 1) * pitch, (n_bands * g.bl + 1 - g.hl) * pitch)
        fill(r.parloc, 0, 56)
        fill_all(r.wpad, 16)
        fill(r.tmp, 0, tiles)
        fill(r.p2, 0, 3 * pitch)
        fill(r.p2, (g.bl + 3) * pitch, 2 * pitch)
        fill(r.gb1, 0, pitch)
        fill(r.gb1, (g.bl + 1) * pitch, pitch)
        fill(r.dk, 0, 4)
        for i in range(3):
            for ref in (r.pm, r.gb):
                ref[i, 0:pitch_s] = jnp.zeros((pitch_s, half), F32)
                ref[i, (g.bs + 1) * pitch_s : small] = jnp.zeros((pitch_s, half), F32)
        for k in range(g.n_sp):
            r.dke[k] = jnp.zeros((16, LANE), F32)

        barrier = pltpu.get_barrier_semaphore()

        def greet(k, _):
            to = lax.rem(me + k, g.group)
            pl.semaphore_signal(
                barrier, inc=1,
                device_id=(to // n_bands, lax.rem(to, n_bands) * 2 + c),
                device_id_type=MESH)
            return 0

        lax.fori_loop(1, g.group, greet, 0)
        pl.semaphore_signal(
            barrier, inc=1, device_id=(s, x * 2 + 1 - c), device_id_type=MESH)

        def entry_silu(row, _):
            value = r.inputs[0, row].astype(F32)
            r.x32[pl.ds(aligned((row + 1) * pitch, 8), g.wl), 0 : g.ci] = value
            r.a1[pl.ds(aligned((row + 2) * pitch, 8), g.wl), 0 : g.ci] = value * sigmoid(value)
            return 0

        lax.fori_loop(0, g.hl, entry_silu, 0)
        r.parloc[0:6, 0 : g.cc] = r.bn_gains[...]
        r.parloc[6:12, 0 : g.cc] = r.bn_biases[...]
        for j in range(9):
            at = 16 + 4 * j
            r.parloc[at : at + 4, 0 : g.cc] = r.kernels[j // 3, j % 3].astype(F32)
        taps_in = [
            [r.kernel_entry[u].astype(F32)[v : v + 1, :] for v in range(3)] for u in range(3)
        ]
        pad_in = jnp.zeros((1, LANE - g.ci), F32)
        taps_in = [[jnp.concatenate([k, pad_in], axis=1) for k in row] for row in taps_in]

        def entry_conv(row, _):
            rows = [
                r.a1[pl.ds(aligned((row + 1 + u) * pitch, 8), pitch), :] for u in range(3)
            ]
            r.s1[pl.ds(aligned((row + 1) * pitch, 8), pitch), :] = (
                conv_row(rows, taps_in) * mask_l)
            return 0

        lax.fori_loop(0, g.hl, entry_conv, 0)
        for b in range(n_bands):
            for k in range(g.na // 2):
                packed = r.s1[(b * g.bl + 2 * k) * pitch : (b * g.bl + 2 * k + 2) * pitch, :]
                if 2 * k < g.nb:
                    at = (b * g.bl + g.na + 2 * k) * pitch
                    packed = packed + pltpu.roll(r.s1[at : at + 2 * pitch, :], HALF, 1)
                r.s1pk[b, 2 * k * pitch : (2 * k + 2) * pitch, :] = packed.astype(BF16)
        for e in range(2):
            r.wpad[0 : g.cc, 0 : g.cin] = r.project_entry[:, e, :]
            r.we[e, pl.ds(aligned(x * shard, 16), shard), :] = r.wpad[:, 0 : g.cin]

        pl.semaphore_wait(barrier, g.group)
        tile = c * n_bands + x

        def full_lanes(t):
            return pl.ds(aligned(t * LANE, LANE), LANE)

        for k in range(1, n_bands):
            b = other_band(k)
            copy_to(r.s1pk.at[b], r.s1full.at[:, full_lanes(tile)],
                    r.s1_ss.at[k], r.s1_rs.at[tile], s, b, c)
        copy_to(r.s1pk.at[x], r.s1full.at[:, full_lanes(tile)],
                r.s1_ss.at[0], r.s1_rs.at[tile], s, x, 1 - c)
        r.s1full[:, full_lanes(tile)] = r.s1pk[x]
        for k in range(1, n_bands):
            mine = r.we.at[0, pl.ds(aligned(x * shard, 16), shard)]
            copy_to(mine, mine, r.we_ss.at[0, k], r.we_rs.at[0, x], s, other_band(k), c)

        for b in range(n_bands):
            spot = lax.broadcasted_iota(jnp.int32, (2 * LANE, half), 1) - b * shard
            r.picks[b] = jnp.where(
                (spot == lax.broadcasted_iota(jnp.int32, (2 * LANE, half), 0)) & (spot < g.cc),
                1.0, 0.0).astype(F32)
        r.parx[x] = r.parloc[...]

        def send_vectors():
            for k in range(1, n_bands):
                copy_to(r.parx.at[x], r.parx.at[x], r.par_ss.at[k], r.par_rs.at[x],
                        s, other_band(k), c)

        def vectors_landed():
            total = 0.0
            for k in range(1, n_bands):
                b = other_band(k)
                landed(r.parx.at[b], r.par_rs.at[b])
            for b in range(n_bands):
                total = total + dot(r.parx[b], r.picks[b], precision=lax.Precision.HIGHEST)
            r.par[...] = total

        r.sidecp[...] = jnp.zeros_like(r.sidecp)

        def side_row(row, _):
            at = aligned((2 * row + 1) * pitch, 8)
            r.sidecp[pl.ds(aligned((row + 1) * pitch_s, 8), g.ws), :] = r.x32[
                pl.ds(at, g.ws, stride=2), :]
            return 0

        lax.fori_loop(0, g.hs, side_row, 0)
        for b in range(n_bands):
            r.sidepk[b] = r.sidecp[b * g.bs * pitch_s : b * g.bs * pitch_s + small, :].astype(BF16)
        r.sidefull[:, full_lanes(tile)] = r.sidepk[x]

        def send_side():
            for k in range(1, n_bands):
                b = other_band(k)
                copy_to(r.sidepk.at[b], r.sidefull.at[:, full_lanes(tile)],
                        r.sd_ss.at[k], r.sd_rs.at[tile], s, b, c)
            copy_to(r.sidepk.at[x], r.sidefull.at[:, full_lanes(tile)],
                    r.sd_ss.at[0], r.sd_rs.at[tile], s, x, 1 - c)
            for k in range(1, n_bands):
                mine = r.we.at[1, pl.ds(aligned(x * shard, 16), shard)]
                copy_to(mine, mine, r.we_ss.at[1, k], r.we_rs.at[1, x], s, other_band(k), c)

        fill_all(r.cotpad, pitch_s)

        def cot_row(row, _):
            r.cotpad[pl.ds(aligned((row + 1) * pitch_s, 8), g.ws), 0 : g.cc] = (
                r.cotangent[0, row].astype(F32))
            return 0

        lax.fori_loop(0, g.hs, cot_row, 0)
        r.cotx[...] = r.cotpad[...].astype(BF16)
        r.cots[x] = r.cotx[pl.ds(aligned(x * g.bs * pitch_s, 16), small), :]

        def send_cotangent():
            for k in range(1, n_bands):
                b = other_band(k)
                copy_to(r.cotx.at[pl.ds(aligned(b * g.bs * pitch_s, 16), small)], r.cots.at[x],
                        r.cot_ss.at[k], r.cot_rs.at[x], s, b, c)

        def channel_place(rows, k0, cols, cut, offset):
            k_at = k0 + lax.broadcasted_iota(jnp.int32, (rows, cols), 0)
            p_at = lax.broadcasted_iota(jnp.int32, (rows, cols), 1)
            want = k_at + offset(0)
            for j in range(1, g.n_ch):
                jump = offset(j) - offset(j - 1)
                want = want + jnp.where(k_at >= j * cut, jump, 0)
            return jnp.where(want == p_at, 1.0, 0.0).astype(BF16)

        def offset_wide(j):
            return (j % 2) * half + (j // 2) * shard - j * g.cc

        def offset_in(j):
            return ((j % 2) * n_bands + j // 2) * LANE - j * g.ci

        r.place_in[0] = channel_place(g.cin, 0, g.full, g.ci, offset_in)
        r.place_in[1] = channel_place(
            g.cin, 0, g.full, g.ci, lambda j: offset_in(j) + HALF)
        def place_rows(k, _):
            at = aligned(k * 64, 64)
            r.place[pl.ds(at, 64), :] = channel_place(64, at, g.wide, g.cc, offset_wide)
            return 0

        lax.fori_loop(0, g.wide // 64, place_rows, 0)
        fill_all(r.wpad, 16)

        def weight_prepare(q):
            r.wpad[0 : g.cc, 0 : g.chan] = r.projects[:, q, :]
            r.w[q, pl.ds(aligned(x * shard, 16), shard), :] = dot(
                r.wpad[...], r.place[...]).astype(BF16)

        def weight_send(q, part):
            rows = pl.ds(aligned(x * shard + part * (shard // 2), 16), shard // 2)
            for k in range(1, n_bands):
                mine = r.w.at[q, rows]
                copy_to(mine, mine, r.w_ss.at[q, part * n_bands + k],
                        r.w_rs.at[q, part * n_bands + x], s, other_band(k), c)

        def weight_landed(q):
            for k in range(1, n_bands):
                b = other_band(k)
                for part in range(2):
                    rows = pl.ds(aligned(b * shard + part * (shard // 2), 16), shard // 2)
                    landed(r.w.at[q, rows], r.w_rs.at[q, part * n_bands + b])

        weight_prepare(0)
        weight_send(0, 0)

        for k in range(1, n_bands):
            t = c * n_bands + other_band(k)
            landed(r.s1full.at[:, full_lanes(t)], r.s1_rs.at[t])
            copy_to(r.s1full.at[:, full_lanes(t)], r.s1full.at[:, full_lanes(t)],
                    r.s1_ss.at[g.n_ch + k], r.s1_rs.at[t], s, x, 1 - c)

        for k in range(1, n_bands):
            b = other_band(k)
            landed(r.we.at[0, pl.ds(aligned(b * shard, 16), shard)], r.we_rs.at[0, b])
        for a in range(2):
            r.wp[a] = dot(r.we[0], r.place_in[a]).astype(BF16)

        for k in range(n_bands):
            t = (1 - c) * n_bands + k
            landed(r.s1full.at[:, full_lanes(t)], r.s1_rs.at[t])
        r.p1[0 : g.ka, :] = dot(r.s1full[...], r.wp[0], (1, 1))
        r.p1[g.ka : large, :] = dot(r.s1full[0 : g.kb, :], r.wp[1], (1, 1))

        def moments(ref, first, rows, width):
            out = [[], []]
            for t in range(tiles):
                def one(k, carry):
                    v = ref[pl.ds(aligned((first + k) * width, 8), width), lane(t)]
                    return (carry[0] + fold(v), carry[1] + fold(v * v))

                zero = jnp.zeros((8, LANE), F32)
                total, square = lax.fori_loop(0, rows, one, (zero, zero))
                out[0].append(rowsum(total))
                out[1].append(rowsum(square))
            return [jnp.concatenate(o, axis=1) for o in out]

        sum_start(r.ar2, 0, 0, moments(r.p1, 1, g.bl, pitch))
        send_vectors()
        weight_send(0, 1)
        send_side()
        send_cotangent()
        weight_prepare(1)
        vectors_landed()
        total = sum_finish(r.ar2, 0, 0)
        store_moments(0, total[0:1], total[1:2])

        for t in range(tiles):
            alpha, beta = vrow(ALPHA, 0, t), vrow(BETA, 0, t)

            def one(k, _):
                at = pl.ds(aligned(k * pitch, 8), pitch)
                h = r.p1[at, lane(t)] * alpha + beta
                ok = mask_l * row_ok(x * g.bl + k - 1, g.hl)
                r.a2[at, lane(t)] = h * sigmoid(h) * ok
                return 0

            lax.fori_loop(0, g.rl, one, 0)
        mine_lanes = aligned(c * half, LANE)
        their_lanes = aligned((1 - c) * half, LANE)

        def own_tile(t):
            return pl.ds(aligned(c * half + t * LANE, LANE), LANE)

        def conv_pairs(source, q, target, row0, rows, height, width, mask):
            for t in range(tiles):
                taps = taps_of(q, t)

                def one(k, _):
                    block = [
                        source[pl.ds(aligned((2 * k + u) * width, 8), width), lane(t)]
                        for u in range(4)
                    ]
                    out = [
                        conv_row(block[j : j + 3], taps) * (mask * row_ok(row0 + 2 * k + j, height))
                        for j in range(2)
                    ]
                    target[pl.ds(aligned(k * 2 * width, 16), 2 * width), own_tile(t)] = (
                        jnp.concatenate(out, axis=0).astype(BF16))
                    return 0

                lax.fori_loop(0, rows // 2, one, 0)

        conv_pairs(r.a2, 0, r.s2, x * g.bl, g.bl, g.hl, pitch, mask_l)

        def swap_start(ref, e):
            mine = ref.at[:, pl.ds(mine_lanes, half)]
            copy_to(mine, mine, r.sm_ss.at[e], r.sm_rs.at[e], s, x, 1 - c)

        def swap_landed(ref, e):
            landed(ref.at[:, pl.ds(their_lanes, half)], r.sm_rs.at[e])

        swap_start(r.s2, 0)
        for k in range(1, n_bands):
            t = c * n_bands + other_band(k)
            landed(r.sidefull.at[:, full_lanes(t)], r.sd_rs.at[t])
            copy_to(r.sidefull.at[:, full_lanes(t)], r.sidefull.at[:, full_lanes(t)],
                    r.sd_ss.at[g.n_ch + k], r.sd_rs.at[t], s, x, 1 - c)
        weight_landed(0)
        rows_all = g.bl * pitch
        step = rows_all // 2
        for k in range(2):
            rows = pl.ds(k * step, step)
            r.p2[3 * pitch + k * step : 3 * pitch + (k + 1) * step, :] = dot(
                r.s2[rows, pl.ds(mine_lanes, half)], r.w[0, :, pl.ds(mine_lanes, half)], (1, 1))
        swap_landed(r.s2, 0)
        for k in range(2):
            rows = pl.ds(k * step, step)
            at = slice(3 * pitch + k * step, 3 * pitch + (k + 1) * step)
            r.p2[at, :] = r.p2[at, :] + dot(
                r.s2[rows, pl.ds(their_lanes, half)], r.w[0, :, pl.ds(their_lanes, half)], (1, 1))
        for k in range(1, n_bands):
            b = other_band(k)
            landed(r.we.at[1, pl.ds(aligned(b * shard, 16), shard)], r.we_rs.at[1, b])
        r.wp[2] = dot(r.we[1], r.place_in[0]).astype(BF16)
        for k in range(n_bands):
            t = (1 - c) * n_bands + k
            landed(r.sidefull.at[:, full_lanes(t)], r.sd_rs.at[t])
        r.pside[...] = dot(r.sidefull[...], r.wp[2], (1, 1))
        sum_start(r.ar4, 0, 1,
                  moments(r.p2, 3, g.bl, pitch) + moments(r.pside, 1, g.bs, pitch_s))
        r.edge_up[...] = r.p2[3 * pitch : 5 * pitch, :].astype(BF16)
        r.edge_down[...] = r.p2[(g.bl - 1) * pitch : (g.bl + 3) * pitch, :].astype(BF16)
        edges_done = edge_copy(r.edge_up, r.from_below, r.edge_down, r.from_above, 0)
        weight_send(1, 0)
        weight_send(1, 1)
        weight_prepare(2)

        edges_done()

        @pl.when(x > 0)
        def _():
            r.p2[0 : 3 * pitch, :] = r.from_above[...].astype(F32)[pitch : 4 * pitch]

        @pl.when(x < n_bands - 1)
        def _():
            r.p2[(g.bl + 3) * pitch : (g.bl + 5) * pitch, :] = r.from_below[...].astype(F32)

        for t in range(tiles):
            def one(k, _):
                v = (r.p2[pl.ds(aligned(2 * k * pitch, 8), pitch), lane(t)]
                     + r.p2[pl.ds(aligned((2 * k + 1) * pitch, 8), pitch), lane(t)]
                     + r.p2[pl.ds(aligned((2 * k + 2) * pitch, 8), pitch), lane(t)])
                r.tmp[t, 0:pitch, :] = v + pltpu.roll(v, 1, 0) + pltpu.roll(v, pitch - 1, 0)
                r.poolraw[pl.ds(aligned(k * pitch_s, 8), pitch_s), lane(t)] = r.tmp[
                    t, pl.ds(0, pitch_s, stride=2), :]
                return 0

            lax.fori_loop(0, g.rs, one, 0)
        total = sum_finish(r.ar4, 0, 1)
        store_moments(1, total[0:1], total[1:2])
        store_moments(2, total[2:3], total[3:4])

        at_col = lax.broadcasted_iota(jnp.int32, (pitch_s, LANE), 0)
        col_count = mask_s * (
            1.0
            + jnp.where(at_col > 0, 1.0, 0.0)
            + jnp.where(2 * at_col + 1 < g.wl, 1.0, 0.0)) * (1.0 / 9.0)

        def window_count(row):
            inside = jnp.where(row > 0, 1.0, 0.0) + jnp.where(2 * row + 1 < g.hl, 1.0, 0.0) + 1.0
            return col_count * (inside.astype(F32) * row_ok(row, g.hs))

        for t in range(tiles):
            alpha, beta = vrow(ALPHA, 1, t) * (1.0 / 9.0), vrow(BETA, 1, t)
            alpha_2, beta_2 = vrow(ALPHA, 2, t), vrow(BETA, 2, t)

            def one(k, _):
                at = pl.ds(aligned(k * pitch_s, 8), pitch_s)
                row = x * g.bs + k - 1
                ok = mask_s * row_ok(row, g.hs)
                h = (r.poolraw[at, lane(t)] * alpha + window_count(row) * beta
                     + r.pside[at, lane(t)] * alpha_2 + beta_2) * ok
                r.hid[0, at, lane(t)] = h
                r.act[0, at, lane(t)] = h * sigmoid(h)
                return 0

            lax.fori_loop(0, g.rs, one, 0)

        def make_picks():
            for b in range(n_bands):
                spot_b = lax.broadcasted_iota(jnp.int32, (half, 2 * LANE), 0) - b * shard
                r.pickb[b] = jnp.where(
                    (spot_b == lax.broadcasted_iota(jnp.int32, (half, 2 * LANE), 1))
                    & (spot_b < g.cc), 1.0, 0.0).astype(BF16)

        own_rows = slice(pitch_s, (g.bs + 1) * pitch_s)
        for i in range(3):
            if i > 0:
                for t in range(tiles):
                    alpha, beta = vrow(ALPHA, 2 + i, t), vrow(BETA, 2 + i, t)

                    def one(k, _):
                        at = pl.ds(aligned(k * pitch_s, 8), pitch_s)
                        ok = mask_s * row_ok(x * g.bs + k - 1, g.hs)
                        h = (r.pm[i - 1, at, lane(t)] * alpha + beta) * ok
                        r.hid[i, at, lane(t)] = h
                        r.act[i, at, lane(t)] = h * sigmoid(h)
                        return 0

                    lax.fori_loop(0, g.rs, one, 0)
            conv_pairs(r.act.at[i], i + 1, r.sm.at[i], x * g.bs, g.bs, g.hs,
                       pitch_s, mask_s)
            swap_start(r.sm.at[i], 1 + i)
            weight_landed(1 + i)
            part = dot(r.sm[i, :, pl.ds(mine_lanes, half)],
                       r.w[1 + i, :, pl.ds(mine_lanes, half)], (1, 1))
            swap_landed(r.sm.at[i], 1 + i)
            r.pm[i, own_rows, :] = part + dot(
                r.sm[i, :, pl.ds(their_lanes, half)],
                r.w[1 + i, :, pl.ds(their_lanes, half)], (1, 1))
            if i < 2:
                sum_start(r.ar2, 1 + i, 2 + i, moments(r.pm.at[i], 1, g.bs, pitch_s))
                edges_done = edges(r.pm.at[i], 1 + i)
                weight_send(2 + i, 0)
                weight_send(2 + i, 1)
                if i == 0:
                    weight_prepare(3)
                    for k in range(1, n_bands):
                        b = other_band(k)
                        landed(r.cots.at[b], r.cot_rs.at[b])
                    total = 0.0
                    for b in range(n_bands):
                        total = total + dot(r.cots[b], r.picks[b].astype(BF16))
                    r.cot[...] = total
                total = sum_finish(r.ar2, 1 + i, 2 + i)
                store_moments(3 + i, total[0:1], total[1:2])
                edges_done()

        def grad_sums(gref, pref, width, first, rows):
            out = [[], []]
            for t in range(tiles):
                def one(k, carry):
                    at = pl.ds(aligned((first + k) * width, 8), width)
                    v = gref[at, lane(t)]
                    return (carry[0] + fold(v), carry[1] + fold(v * pref[at, lane(t)]))

                zero = jnp.zeros((8, LANE), F32)
                a, b = lax.fori_loop(0, rows, one, (zero, zero))
                out[0].append(rowsum(a))
                out[1].append(rowsum(b))
            return [jnp.concatenate(o, axis=1) for o in out]

        sum_start(r.ar4, 1, 4,
                  moments(r.pm.at[2], 1, g.bs, pitch_s)
                  + grad_sums(r.cot, r.pm.at[2], pitch_s, 1, g.bs))
        edges_done = edges(r.pm.at[2], 3)
        make_picks()
        total = sum_finish(r.ar4, 1, 4)
        store_moments(5, total[0:1], total[1:2])
        store_back(5, total[2:3], total[3:4])
        edges_done()

        def norm_back(layer, gref, pref, target, rows, width, mask, row0, height):
            for t in range(tiles):
                alpha, kappa, lam = vrow(ALPHA, layer, t), vrow(KAPPA, layer, t), vrow(LAM, layer, t)

                def one(k, _):
                    at = pl.ds(aligned(k * width, 8), width)
                    ok = mask * row_ok(row0 + k, height)
                    target[at, lane(t)] = (
                        gref[at, lane(t)] * alpha + pref[at, lane(t)] * kappa + lam) * ok
                    return 0

                lax.fori_loop(0, rows, one, 0)

        def kernel_grad(aref, gref, q, rows, width):
            for t in range(tiles):
                def one(k, carry):
                    gv = gref[pl.ds(aligned((k + 1) * width, 8), width), lane(t)]
                    turned = [pltpu.roll(gv, width - 1, 0), gv, pltpu.roll(gv, 1, 0)]
                    out = []
                    for u in range(3):
                        av = aref[pl.ds(aligned((k + u) * width, 8), width), lane(t)]
                        for v in range(3):
                            out.append(carry[3 * u + v] + fold(av * turned[v]))
                    return tuple(out)

                zero = jnp.zeros((8, LANE), F32)
                sums = lax.fori_loop(0, rows, one, (zero,) * 9)
                for j in range(9):
                    r.dk[q, j : j + 1, lane(t)] = rowsum(sums[j])

        yi, zi = lax.rem(s, g.ny), s // g.ny

        def block_of(name, k):
            return getattr(r, f"{name}{k}")

        def put_units(name, k, value, cols):
            value = value.astype(BF16)
            for b in range(n_bands):
                for t in range(cols // LANE):
                    part = value[b * shard : (b + 1) * shard, t * LANE : (t + 1) * LANE]
                    block_of(name, k)[b, t * g.tall : (t + 1) * g.tall] = (
                        part.reshape(g.tall, 16, LANE))

        def put_kernels():
            for q in range(4):
                value = r.dk[q].astype(BF16)
                for b in range(n_bands):
                    part = dot(value, r.pickb[b]).astype(BF16)
                    for t in range(g.u_dk):
                        at = g.u_in + q * g.u_dk + t
                        r.fls1[b, at] = part[:, t * LANE : (t + 1) * LANE]

        def x_send(k):
            for j in range(1, n_bands):
                b = other_band(j)
                copy_to(block_of("rxs", k).at[b], block_of("rxr", k).at[x],
                        r.rx_ss.at[k, j], r.rx_rs.at[k, x], s, b, c)

        def x_sum_y_send(k):
            total = block_of("rxs", k)[x].astype(F32)
            for j in range(1, n_bands):
                b = other_band(j)
                landed(block_of("rxr", k).at[b], r.rx_rs.at[k, b])
                total = total + block_of("rxr", k)[b].astype(F32)
            block_of("xs", k)[...] = total.astype(BF16)
            part = g.units[k] // g.ny
            for j in range(1, g.ny):
                to = lax.rem(yi + j, g.ny)
                copy_to(block_of("xs", k).at[pl.ds(to * part, part)], block_of("ryr", k).at[yi],
                        r.ry_ss.at[k, j], r.ry_rs.at[k, yi], zi * g.ny + to, x, c)

        def y_sum_z_send(k):
            part = g.units[k] // g.ny
            total = block_of("xs", k)[pl.ds(yi * part, part)].astype(F32)
            for j in range(1, g.ny):
                b = lax.rem(yi + j, g.ny)
                landed(block_of("ryr", k).at[b], r.ry_rs.at[k, b])
                total = total + block_of("ryr", k)[b].astype(F32)
            block_of("ys", k)[...] = total.astype(BF16)
            piece = part // g.nz
            for j in range(1, g.nz):
                to = lax.rem(zi + j, g.nz)
                copy_to(block_of("ys", k).at[pl.ds(to * piece, piece)], block_of("rzr", k).at[zi],
                        r.rz_ss.at[k, j], r.rz_rs.at[k, zi], to * g.ny + yi, x, c)

        def z_sum_z_gather(k):
            part = g.units[k] // g.ny
            piece = part // g.nz
            total = block_of("ys", k)[pl.ds(zi * piece, piece)].astype(F32)
            for j in range(1, g.nz):
                b = lax.rem(zi + j, g.nz)
                landed(block_of("rzr", k).at[b], r.rz_rs.at[k, b])
                total = total + block_of("rzr", k)[b].astype(F32)
            at = pl.ds(yi * part + zi * piece, piece)
            block_of("fin", k)[at] = total.astype(BF16)
            for j in range(1, g.nz):
                to = lax.rem(zi + j, g.nz)
                copy_to(block_of("fin", k).at[at], block_of("fin", k).at[at],
                        r.gz_ss.at[k, j], r.gz_rs.at[k, zi], to * g.ny + yi, x, c)

        def y_gather(k):
            part = g.units[k] // g.ny
            piece = part // g.nz
            for j in range(1, g.nz):
                b = lax.rem(zi + j, g.nz)
                landed(block_of("fin", k).at[pl.ds(yi * part + b * piece, piece)],
                       r.gz_rs.at[k, b])
            at = pl.ds(yi * part, part)
            for j in range(1, g.ny):
                to = lax.rem(yi + j, g.ny)
                copy_to(block_of("fin", k).at[at], block_of("fin", k).at[at],
                        r.gy_ss.at[k, j], r.gy_rs.at[k, yi], zi * g.ny + to, x, c)

        def get_units(name, k, cols):
            tiles_in = [
                block_of(name, k)[t * g.tall : (t + 1) * g.tall].reshape(shard, LANE)
                for t in range(cols // LANE)
            ]
            return jnp.concatenate(tiles_in, axis=1)

        def finish_block(k):
            part = g.units[k] // g.ny
            for j in range(1, g.ny):
                b = lax.rem(yi + j, g.ny)
                landed(block_of("fin", k).at[pl.ds(b * part, part)], r.gy_rs.at[k, b])
            r.m_dw[3 - k] = dot(get_units("fin", k, g.wide), r.place[...], (1, 1)).astype(BF16)

        def flat_send(k):
            piece = g.flat_units[k] // g.n_sp
            to_group(None, block_of("flr", k).at[me], r.fl_ss.at[k, 0], r.fl_rs.at[k, 0],
                     lambda s_, x_: block_of("fls", k).at[x_, pl.ds(s_ * piece, piece)])
            block_of("flr", k)[me] = block_of("fls", k)[x, pl.ds(s * piece, piece)]

        def flat_sum(k):
            piece = g.flat_units[k] // g.n_sp
            others = block_of("flr", k).at[pl.ds(0, g.group - 1)]
            landed(others, r.fl_rs.at[k, 0])
            sends.append(lambda: landed(others, r.fl_ss.at[k, 0]))
            total = block_of("flr", k)[0].astype(F32)
            for j in range(1, g.group):
                total = total + block_of("flr", k)[j].astype(F32)
            at = pl.ds(s * piece, piece)
            mine = block_of("flf", k).at[at]
            mine[...] = total.astype(BF16)
            to_images(mine, mine, r.fl_ss.at[k, 1], r.fl_rs.at[k, 1])

        def flat_finish(k):
            piece = g.flat_units[k] // g.n_sp
            others = block_of("flf", k).at[pl.ds(0, (g.n_sp - 1) * piece)]
            landed(others, r.fl_rs.at[k, 1])
            sends.append(lambda: landed(others, r.fl_ss.at[k, 1]))
            r.m_dwe[1 - k] = get_units("flf", k, g.cin)
            if k == 1:
                for q in range(4):
                    for t in range(g.u_dk):
                        r.m_dk[q, :, lane(t)] = r.flf1[g.u_in + q * g.u_dk + t].astype(F32)

        for i in (2, 1, 0):
            layer = 3 + i
            gref = r.cot if i == 2 else r.gb.at[i + 1]
            norm_back(layer, gref, r.pm.at[i], r.gt.at[i], g.rs, pitch_s, mask_s,
                      x * g.bs - 1, g.hs)
            grad = r.gt[i].astype(BF16)
            r.rsend[i] = dot(grad, r.w[1 + i, :, pl.ds(their_lanes, half)]).astype(BF16)
            copy_to(r.rsend.at[i], r.rrecv.at[i], r.r_ss.at[i], r.r_rs.at[i], s, x, 1 - c)
            part = dot(grad, r.w[1 + i, :, pl.ds(mine_lanes, half)])
            grad = r.gt[i, own_rows, :].astype(BF16)
            put_units("rxs", 2 - i, dot(grad, r.sm[i], (0, 0)), g.wide)
            landed(r.rrecv.at[i], r.r_rs.at[i])
            r.gs[...] = part + r.rrecv[i].astype(F32)
            rows = [[] for _ in range(4 if i == 0 else 2)]
            for t in range(tiles):
                taps = flip(taps_of(i + 1, t))

                def one(k, carry):
                    block = [
                        r.gs[pl.ds(aligned((k + u) * pitch_s, 8), pitch_s), lane(t)]
                        for u in range(3)
                    ]
                    at = pl.ds(aligned((k + 1) * pitch_s, 8), pitch_s)
                    row = x * g.bs + k
                    h = r.hid[i, at, lane(t)]
                    sig = sigmoid(h)
                    value = conv_row(block, taps) * (sig * (1.0 + h * (1.0 - sig))) * (
                        mask_s * row_ok(row, g.hs))
                    if i == 0:
                        value = value + r.cot[at, lane(t)]
                    r.gb[i, at, lane(t)] = value
                    if i == 0:
                        new = [
                            value, value * r.pside[at, lane(t)],
                            value * window_count(row),
                            value * r.poolraw[at, lane(t)] * (1.0 / 9.0)]
                    else:
                        new = [value, value * r.pm[i - 1, at, lane(t)]]
                    return tuple(a + fold(b) for a, b in zip(carry, new))

                zero = jnp.zeros((8, LANE), F32)
                sums = lax.fori_loop(0, g.bs, one, (zero,) * len(rows))
                for j, v in enumerate(sums):
                    rows[j].append(rowsum(v))
            rows = [jnp.concatenate(o, axis=1) for o in rows]
            buf, at_e, e = ((r.ar4, 2, 7), (r.ar2, 3, 6), (r.ar2, 4, 5))[i]
            sum_start(buf, at_e, e, rows)
            edges_done = edges(r.gb.at[i], 4 + i)
            x_send(2 - i)
            if i < 2:
                x_sum_y_send(1 - i)
            if i == 0:
                y_sum_z_send(0)
            kernel_grad(r.act.at[i], r.gs, i + 1, g.bs, pitch_s)
            if i == 2:
                value = []
                for t in range(tiles):
                    h = (r.pm[2, own_rows, lane(t)] * vrow(ALPHA, 5, t) + vrow(BETA, 5, t)
                         + r.hid[0, own_rows, lane(t)])
                    value.append(h.astype(BF16))
                value = jnp.concatenate(value, axis=1)
                for b in range(n_bands):
                    r.outx[b] = dot(value, r.pickb[b]).astype(BF16)
                for k in range(1, n_bands):
                    b = other_band(k)
                    copy_to(r.outx.at[b], r.outs.at[x], r.out_ss.at[k], r.out_rs.at[x], s, b, c)
                r.outs[x] = r.outx[x]
            total = sum_finish(buf, at_e, e)
            if i > 0:
                store_back(layer - 1, total[0:1], total[1:2])
            else:
                store_back(2, total[0:1], total[1:2])
                store_back(1, total[2:3], total[3:4])
            edges_done()

        for t in range(tiles):
            alpha, kappa, lam = vrow(ALPHA, 1, t) * (1.0 / 9.0), vrow(KAPPA, 1, t), vrow(LAM, 1, t)

            def spread(v):
                r.tmp[t, pl.ds(0, pitch_s, stride=2), :] = v
                r.tmp[t, pl.ds(1, pitch_s, stride=2), :] = v + pltpu.roll(v, pitch_s - 1, 0)
                return r.tmp[t, 0:pitch, :]

            def one(k, _):
                low = r.gb[0, pl.ds(aligned(k * pitch_s, 8), pitch_s), lane(t)]
                high = r.gb[0, pl.ds(aligned((k + 1) * pitch_s, 8), pitch_s), lane(t)]
                for j, v in enumerate((low + high, high)):
                    row = x * g.bl + 2 * k + j - 1
                    ok = mask_l * row_ok(row, g.hl)
                    p = r.p2[pl.ds(aligned((2 * k + j + 2) * pitch, 8), pitch), lane(t)]
                    r.gt2[pl.ds(aligned((2 * k + j) * pitch, 8), pitch), lane(t)] = (
                        spread(v) * alpha + p * kappa + lam) * ok
                return 0

            lax.fori_loop(0, g.bs + 1, one, 0)
        for k in range(2):
            at = pl.ds(k * (large // 2), large // 2)
            r.rsend2[at, :] = dot(
                r.gt2[at, :].astype(BF16), r.w[0, :, pl.ds(their_lanes, half)]).astype(BF16)
        copy_to(r.rsend2, r.rrecv2, r.r_ss.at[3], r.r_rs.at[3], s, x, 1 - c)
        for k in range(2):
            at = pl.ds(k * (large // 2), large // 2)
            r.gs2[at, :] = dot(r.gt2[at, :].astype(BF16), r.w[0, :, pl.ds(mine_lanes, half)])
        put_units("rxs", 3, dot(
            r.gt2[pitch : (g.bl + 1) * pitch, :].astype(BF16), r.s2[...], (0, 0)), g.wide)
        x_send(3)
        z_sum_z_gather(0)
        landed(r.rrecv2, r.r_rs.at[3])
        r.gs2[...] = r.gs2[...] + r.rrecv2[...].astype(F32)
        rows = [[], []]
        for t in range(tiles):
            taps = flip(taps_of(0, t))
            alpha, beta = vrow(ALPHA, 0, t), vrow(BETA, 0, t)

            def one(k, carry):
                block = [
                    r.gs2[pl.ds(aligned((k + u) * pitch, 8), pitch), lane(t)] for u in range(3)
                ]
                at = pl.ds(aligned((k + 1) * pitch, 8), pitch)
                p = r.p1[at, lane(t)]
                h = p * alpha + beta
                sig = sigmoid(h)
                value = conv_row(block, taps) * (sig * (1.0 + h * (1.0 - sig))) * (
                    mask_l * row_ok(x * g.bl + k, g.hl))
                r.gb1[at, lane(t)] = value
                return (carry[0] + fold(value), carry[1] + fold(value * p))

            zero = jnp.zeros((8, LANE), F32)
            sums = lax.fori_loop(0, g.bl, one, (zero, zero))
            for j, v in enumerate(sums):
                rows[j].append(rowsum(v))
        rows = [jnp.concatenate(o, axis=1) for o in rows]
        sum_start(r.ar4, 3, 8, rows)

        def own_ok(k, width_rows):
            return jnp.where((k >= 1) & (k <= width_rows), 1.0, 0.0).astype(F32)

        for t in range(tiles):
            alpha, kappa, lam = vrow(ALPHA, 2, t), vrow(KAPPA, 2, t), vrow(LAM, 2, t)

            def one(k, _):
                out = []
                for j in range(2):
                    at = pl.ds(aligned((2 * k + j) * pitch_s, 8), pitch_s)
                    ok = mask_s * (row_ok(x * g.bs + 2 * k + j - 1, g.hs) * own_ok(2 * k + j, g.bs))
                    out.append((r.gb[0, at, lane(t)] * alpha
                                + r.pside[at, lane(t)] * kappa + lam) * ok)
                r.gside[pl.ds(aligned(2 * k * pitch_s, 16), 2 * pitch_s), lane(t)] = (
                    jnp.concatenate(out, axis=0).astype(BF16))
                return 0

            lax.fori_loop(0, g.rs // 2, one, 0)
        own_tiles = pl.ds(aligned(c * n_bands * LANE, LANE), n_bands * LANE)
        their_tiles = pl.ds(aligned((1 - c) * n_bands * LANE, LANE), n_bands * LANE)
        r.sdsend[...] = dot(r.gside[...], r.wp[2, :, their_tiles]).astype(BF16)
        copy_to(r.sdsend, r.sdrecv, r.es_ss.at[1], r.es_rs.at[1], s, x, 1 - c)
        part = dot(r.gside[...], r.wp[2, :, own_tiles])
        landed(r.sdrecv, r.es_rs.at[1])
        part = part + r.sdrecv[...].astype(F32)
        for b in range(n_bands):
            r.sdsum[b] = part[:, b * LANE : (b + 1) * LANE].astype(BF16)
        for k in range(1, n_bands):
            b = other_band(k)
            copy_to(r.sdsum.at[b], r.sdr.at[x], r.esx_ss.at[1, k], r.esx_rs.at[1, x], s, b, c)
        r.sdr[x] = r.sdsum[x]

        lane_at = lax.broadcasted_iota(jnp.int32, (half, g.full), 1)
        low_lanes = lax.rem(lane_at, LANE) < HALF
        both_place = r.place_in[0] + r.place_in[1]

        value = dot(r.gside[...], r.sidefull[...], (0, 0)).astype(BF16)
        put_units("fls", 0, dot(value, both_place, (1, 1)), g.cin)
        flat_send(0)
        x_sum_y_send(2)
        y_sum_z_send(1)
        y_gather(0)
        kernel_grad(r.a2, r.gs2, 0, g.bl, pitch)
        put_kernels()
        x_sum_y_send(3)
        total = sum_finish(r.ar4, 3, 8)
        store_back(0, total[0:1], total[1:2])

        for t in range(tiles):
            alpha, kappa, lam = vrow(ALPHA, 0, t), vrow(KAPPA, 0, t), vrow(LAM, 0, t)

            def one(k, _):
                out = []
                for j in range(2):
                    at = pl.ds(aligned((2 * k + j) * pitch, 8), pitch)
                    ok = mask_l * (row_ok(x * g.bl + 2 * k + j - 1, g.hl) * own_ok(2 * k + j, g.bl))
                    out.append((r.gb1[at, lane(t)] * alpha + r.p1[at, lane(t)] * kappa + lam) * ok)
                r.g1[pl.ds(aligned(2 * k * pitch, 16), 2 * pitch), lane(t)] = (
                    jnp.concatenate(out, axis=0).astype(BF16))
                return 0

            lax.fori_loop(0, g.rl // 2, one, 0)

        def entry_part(lanes):
            a = dot(r.g1[0 : g.ka, :], r.wp[0, :, lanes])
            b = dot(r.g1[g.ka : large, :], r.wp[1, :, lanes])
            if g.kb == g.ka:
                return a + b
            return jnp.concatenate([a[0 : g.kb] + b, a[g.kb :]], axis=0)

        r.essend[...] = entry_part(their_tiles).astype(BF16)
        copy_to(r.essend, r.esrecv, r.es_ss.at[0], r.es_rs.at[0], s, x, 1 - c)
        part = entry_part(own_tiles)
        landed(r.esrecv, r.es_rs.at[0])
        part = part + r.esrecv[...].astype(F32)
        for b in range(n_bands):
            r.essum[b] = part[:, b * LANE : (b + 1) * LANE].astype(BF16)
        for k in range(1, n_bands):
            b = other_band(k)
            copy_to(r.essum.at[b], r.esr.at[x], r.esx_ss.at[0, k], r.esx_rs.at[0, x], s, b, c)
        r.esr[x] = r.essum[x]
        grad_a = dot(r.g1[0 : g.ka, :], r.s1full[...], (0, 0))
        grad_b = dot(r.g1[g.ka : large, :], r.s1full[0 : g.kb, :], (0, 0))
        value = jnp.where(low_lanes, grad_a, grad_b).astype(BF16)
        put_units("fls", 1, dot(value, both_place, (1, 1)), g.cin)
        flat_send(1)
        y_sum_z_send(2)
        z_sum_z_gather(1)
        flat_sum(0)
        finish_block(0)
        y_sum_z_send(3)

        spot = lax.broadcasted_iota(jnp.int32, (half, 2 * LANE), 0) - x * shard
        pick_own = jnp.where(
            (spot == lax.broadcasted_iota(jnp.int32, (half, 2 * LANE), 1)) & (spot < g.cc),
            1.0, 0.0).astype(F32)
        final = dot(r.vec[0:24, :], pick_own, precision=lax.Precision.HIGHEST)
        final = final[:, 0 : g.cc]
        at_row = lax.broadcasted_iota(jnp.int32, (6, g.cc), 0)
        count = jnp.where(at_row < 2, g.count_large, g.count_small)
        bessel = count / (count - 1.0)
        final = jnp.concatenate([
            (1.0 - MOMENTUM) * r.run_means[...] + MOMENTUM * final[0:6],
            (1.0 - MOMENTUM) * r.run_vars[...] + MOMENTUM * (final[6:12] * bessel),
            final[12:24]], axis=0)
        r.m_vec[:, 0 : g.cc] = final

        for k in range(1, n_bands):
            b = other_band(k)
            landed(r.outs.at[b], r.out_rs.at[b])
        for b in range(n_bands):
            r.m_out[b * g.bs * pitch_s : (b + 1) * g.bs * pitch_s, :] = r.outs[b].astype(F32)

        for k in range(1, n_bands):
            b = other_band(k)
            landed(r.sdr.at[b], r.esx_rs.at[1, b])
        for b in range(n_bands):
            r.sidecp[b * g.bs * pitch_s : (b + 1) * g.bs * pitch_s, :] = (
                r.sdr[b].astype(F32)[pitch_s : (g.bs + 1) * pitch_s])
        for k in range(1, n_bands):
            b = other_band(k)
            landed(r.esr.at[b], r.esx_rs.at[0, b])
        fill(r.gs1, 0, pitch)
        fill(r.gs1, (n_bands * g.bl + 1) * pitch, pitch)
        for b in range(n_bands):
            for k in range(g.na // 2):
                value = r.esr[b, 2 * k * pitch : (2 * k + 2) * pitch, :].astype(F32)
                for j in range(2):
                    i = 2 * k + j
                    if 1 <= i <= g.bl:
                        at = (b * g.bl + i) * pitch
                        r.gs1[at : at + pitch, :] = value[j * pitch : (j + 1) * pitch]
                if 2 * k < g.nb:
                    value = pltpu.roll(value, HALF, 1)
                    for j in range(2):
                        i = g.na + 2 * k + j
                        if 1 <= i <= g.bl:
                            at = (b * g.bl + i) * pitch
                            r.gs1[at : at + pitch, :] = value[j * pitch : (j + 1) * pitch]
        taps = flip(taps_in)

        def in_grad(row):
            block = [r.gs1[pl.ds(aligned((row + u) * pitch, 8), pitch), :] for u in range(3)]
            h = r.x32[pl.ds(aligned((row + 1) * pitch, 8), pitch), :]
            sig = sigmoid(h)
            return conv_row(block, taps) * (sig * (1.0 + h * (1.0 - sig)))

        r.tmp[0] = jnp.zeros((48, LANE), F32)

        def in_rows(k, _):
            r.tmp[0, pl.ds(0, pitch_s, stride=2), :] = r.sidecp[
                pl.ds(aligned(k * pitch_s, 8), pitch_s), :]
            value = in_grad(2 * k) + r.tmp[0, 0:pitch, :]
            r.m_gin[pl.ds(aligned(2 * k * pitch, 8), pitch), :] = value

            r.m_gin[pl.ds(aligned((2 * k + 1) * pitch, 8), pitch), :] = in_grad(2 * k + 1)
            return 0

        lax.fori_loop(0, g.hs, in_rows, 0)

        def entry_kernel(k, carry):
            gv = r.gs1[pl.ds(aligned((k + 1) * pitch, 8), pitch), :]
            turned = [pltpu.roll(gv, pitch - 1, 0), gv, pltpu.roll(gv, 1, 0)]
            out = []
            for u in range(3):
                av = r.a1[pl.ds(aligned((k + 1 + u) * pitch, 8), pitch), :]
                for v in range(3):
                    out.append(carry[3 * u + v] + fold(av * turned[v]))
            return tuple(out)

        zero = jnp.zeros((8, LANE), F32)
        sums = lax.fori_loop(0, g.hl, entry_kernel, (zero,) * 9)
        for j in range(9):
            r.dke[s, j : j + 1, :] = rowsum(sums[j])

        to_images(r.dke.at[s], r.dke.at[s], r.dke_ss.at[0], r.dke_rs.at[0])

        z_sum_z_gather(2)
        y_gather(1)
        z_sum_z_gather(3)
        flat_sum(1)
        y_gather(2)
        finish_block(1)
        flat_finish(0)
        y_gather(3)
        finish_block(2)
        flat_finish(1)
        finish_block(3)

        block = r.dke.at[pl.ds(0, g.n_sp - 1)]
        landed(block, r.dke_rs.at[0])
        sends.append(lambda: landed(block, r.dke_ss.at[0]))
        total = r.dke[0]
        for k in range(1, g.n_sp):
            total = total + r.dke[k]
        r.m_dke[...] = total
        for wait in sends:
            wait()

    return kernel


def body(mesh_shape, *args):
    inputs, cotangent, kernel_entry, kernels, project_entry, projects = args[:6]
    g = geometry(mesh_shape, inputs, cotangent, project_entry, projects)
    operands = list(args)
    operands[3] = jnp.transpose(kernels, (1, 2, 0, 3))
    operands[4] = jnp.transpose(project_entry, (1, 0, 2))
    operands[5] = jnp.transpose(projects, (1, 0, 2))
    table = scratch_table(g)
    names = list(table)
    shapes = [
        ((g.bands * g.bs * g.ps, 2 * LANE), F32),
        ((2 * g.hs * g.pl_, LANE), F32),
        ((16, LANE), F32),
        ((4, 16, 2 * LANE), F32),
        ((2, g.shard, g.cin), BF16),
        ((4, g.shard, g.wide), BF16),
        ((24, 2 * LANE), F32),
    ]
    vmem = pl.BlockSpec(memory_space=pltpu.VMEM)
    parts = pl.pallas_call(
        make_kernel(g, names),
        out_shape=[jax.ShapeDtypeStruct(shape, kind) for shape, kind in shapes],
        in_specs=[vmem] * 10,
        out_specs=[vmem] * len(shapes),
        scratch_shapes=list(table.values()),
        compiler_params=pltpu.CompilerParams(
            collective_id=0, has_side_effects=True, vmem_limit_bytes=60 << 20),
    )(*operands)

    def write(m_out, m_gin, m_dke, m_dk, m_dwe, m_dw, m_vec, *outs):
        o_out, o_gin, o_dke, o_dk, o_dwe, o_dw, o_gains, o_biases, o_means, o_vars = outs
        for q in range(4):
            o_dw[:, q, :] = m_dw[q].astype(F32)[0 : g.cc, 0 : g.chan]
        for e in range(2):
            o_dwe[:, e, :] = m_dwe[e].astype(F32)[0 : g.cc]
        for row in range(g.hs):
            o_out[row, :, 0, :] = m_out[row * g.ps : row * g.ps + g.ws, 0 : g.cc]

        def one(row, _):
            o_gin[row, :, 0, :] = m_gin[pl.ds(aligned(row * g.pl_, 8), g.wl), 0 : g.ci]
            return 0

        lax.fori_loop(0, g.hl, one, 0)
        for j in range(9):
            for q in range(4):
                o_dk[j // 3, j % 3, q : q + 1, :] = m_dk[q, j : j + 1, 0 : g.cc]
        for u in range(3):
            o_dke[u] = m_dke[3 * u : 3 * u + 3, 0 : g.ci]
        for k, ref in enumerate((o_means, o_vars, o_gains, o_biases)):
            ref[...] = m_vec[6 * k : 6 * k + 6, 0 : g.cc]

    results = [
        (g.hs, g.ws, 1, g.cc),
        (g.hl, g.wl, 1, g.ci),
        kernel_entry.shape,
        operands[3].shape,
        operands[4].shape,
        operands[5].shape,
    ] + [(6, g.cc)] * 4
    out = pl.pallas_call(
        write,
        out_shape=[jax.ShapeDtypeStruct(shape, F32) for shape in results],
        in_specs=[vmem] * len(shapes),
        out_specs=[vmem] * 10,
        compiler_params=pltpu.CompilerParams(vmem_limit_bytes=62 << 20),
    )(*parts)
    out = list(out)
    out[0] = jnp.transpose(out[0], (2, 0, 1, 3))
    out[1] = jnp.transpose(out[1], (2, 0, 1, 3))
    out[3] = jnp.transpose(out[3], (2, 0, 1, 3))
    out[4] = jnp.transpose(out[4], (1, 0, 2))
    out[5] = jnp.transpose(out[5], (1, 0, 2))
    return tuple(out)


def solution(mesh):
    mesh_shape = dict(mesh.shape)
    wide = P("sp", None, None, "ch")
    row = P(None, "ch")
    mid = P(None, "ch", None)
    return jax.shard_map(
        lambda *args: body(mesh_shape, *args),
        mesh=mesh,
        in_specs=(wide, wide, P(None, None, "ch"), P(None, None, None, "ch"), mid, mid,
                  row, row, row, row),
        out_specs=(wide, wide, P(None, None, "ch"), P(None, None, None, "ch"), mid, mid,
                   row, row, row, row),
        check_vma=False,
    )
```

```python
import math
import types

import jax
import jax.numpy as jnp
from jax import lax
from jax.experimental import pallas as pl
from jax.experimental.pallas import tpu as pltpu
from jax.sharding import PartitionSpec as P

MESH = pl.DeviceIdType.MESH
EPSILON = 0.001
MOMENTUM = 0.5
LANE = 128
HALF = 64
F32 = jnp.float32
BF16 = jnp.bfloat16


def round_up(value, step):
    return -(-value // step) * step


UN_S, UN_L, UN_ES, UN_EC, UN_SR, UN_IR, UN_EK, UN_W = 12, 10, 4, 4, 4, 4, 4, 4


def aligned(index, step):
    return index if isinstance(index, int) else pl.multiple_of(index, step)


def repeat(count, one, carry, unroll=4):
    def some(k, carry):
        for j in range(unroll):
            carry = one(k * unroll + j, carry)
        return carry

    whole = count // unroll if count > unroll else 0
    if whole:
        carry = lax.fori_loop(0, whole, some, carry)
    for k in range(whole * unroll, count):
        carry = one(k, carry)
    return carry


def sigmoid(values):
    return 0.5 * jnp.tanh(0.5 * values) + 0.5


def dot(left, right, dims=(1, 0), precision=None):
    return lax.dot_general(
        left,
        right,
        (((dims[0],), (dims[1],)), ((), ())),
        precision=precision,
        preferred_element_type=F32,
    )


def fold(value):
    return jnp.sum(value.reshape(value.shape[0] // 8, 8, value.shape[1]), axis=0)


def geometry(mesh_shape, inputs, cotangent, project_entry, projects):
    geo = types.SimpleNamespace()
    geo.n_sp, geo.n_ch = mesh_shape["sp"], mesh_shape["ch"]
    geo.bands = geo.n_ch // 2
    geo.group = geo.n_sp * geo.bands
    _, geo.hl, geo.wl, geo.ci = inputs.shape
    _, geo.hs, geo.ws, geo.cc = cotangent.shape
    geo.cin, geo.chan = project_entry.shape[2], projects.shape[2]
    geo.wide = round_up(geo.chan, 2 * LANE)
    geo.half = geo.wide // 2
    geo.shard = geo.wide // geo.n_ch
    geo.tiles = geo.half // LANE
    geo.pl_, geo.ps = round_up(geo.wl + 1, 8), round_up(geo.ws + 1, 8)
    geo.bs = 2 * math.ceil(geo.hs / (2 * geo.bands))
    geo.bl = 2 * geo.bs
    geo.rs, geo.rl = geo.bs + 2, geo.bl + 2
    geo.na = 2 * math.ceil(geo.rl / 4)
    geo.nb = geo.rl - geo.na
    geo.ka = geo.na * geo.pl_
    geo.kb = geo.nb * geo.pl_
    geo.full = geo.n_ch * LANE
    geo.ny = geo.bands if geo.n_sp % geo.bands == 0 else 1
    geo.nz = geo.n_sp // geo.ny
    geo.tall = geo.shard // 16
    geo.u_mid = geo.tall * (geo.wide // LANE)
    geo.u_dk = round_up(geo.shard, LANE) // LANE
    geo.u_in = geo.tall * (geo.cin // LANE)
    geo.units = [
        round_up(u, geo.n_sp)
        for u in [geo.u_mid] * 4 + [geo.u_in, geo.u_in + 4 * geo.u_dk]
    ]
    geo.plane = geo.bands * geo.ny
    geo.count_large = float(geo.n_sp * geo.hl * geo.wl)
    geo.count_small = float(geo.n_sp * geo.hs * geo.ws)
    return geo


IN_NAMES = [
    "inputs",
    "cotangent",
    "kernel_entry",
    "kernels",
    "project_entry",
    "projects",
    "bn_gains",
    "bn_biases",
    "run_means",
    "run_vars",
]
OUT_NAMES = [
    "m_out",
    "m_gin",
    "m_dke",
    "m_dk",
    "m_dwe",
    "m_dw",
    "m_vec",
]


def scratch_table(g):
    dma, vm = pltpu.SemaphoreType.DMA, pltpu.VMEM
    small, large = g.rs * g.ps, g.rl * g.pl_
    cp_rows = (g.bands * g.bl + 2) * g.pl_
    x = g.bands
    table = dict(
        x32=vm((cp_rows, LANE), F32),
        a1=vm((cp_rows + 2 * g.pl_, LANE), F32),
        s1=vm((cp_rows, LANE), F32),
        s1pk=vm((x, g.ka, LANE), BF16),
        s1full=vm((g.ka, g.full), BF16),
        sidepk=vm((x, small, LANE), BF16),
        sidefull=vm((small, g.full), BF16),
        sidecp=vm(((x * g.bs + 2) * g.ps, LANE), F32),
        parloc=vm((56, 2 * LANE), F32),
        parx=vm((x, 56, 2 * LANE), F32),
        par=vm((56, g.half), F32),
        place=vm((g.wide, g.wide), BF16),
        place_in=vm((2, g.cin, g.full), BF16),
        wpad=vm((g.shard, g.wide), BF16),
        w=vm((4, g.half, g.wide), BF16),
        we=vm((2, g.half, g.cin), BF16),
        wp=vm((3, g.half, g.full), BF16),
        cotpad=vm(((x * g.bs + 2) * g.ps, 2 * LANE), F32),
        cotx=vm(((x * g.bs + 2) * g.ps, 2 * LANE), BF16),
        cots=vm((x, small, 2 * LANE), BF16),
        picks=vm((x, 2 * LANE, g.half), F32),
        edge_up=vm((2 * g.pl_, g.half), BF16),
        edge_down=vm((4 * g.pl_, g.half), BF16),
        from_below=vm((2 * g.pl_, g.half), BF16),
        from_above=vm((4 * g.pl_, g.half), BF16),
        cot=vm((small, g.half), F32),
        p1=vm((large, g.half), F32),
        a2=vm((large, g.half), F32),
        s2=vm((g.bl * g.pl_, g.wide), BF16),
        p2=vm((large + 3 * g.pl_, g.half), F32),
        tmp=vm((g.tiles, 48, LANE), F32),
        poolraw=vm((small, g.half), F32),
        pside=vm((small, g.half), F32),
        hid=vm((3, small, g.half), F32),
        act=vm((3, small, g.half), F32),
        sm=vm((3, g.bs * g.ps, g.wide), BF16),
        pm=vm((3, small, g.half), F32),
        gb=vm((3, small, g.half), F32),
        gt=vm((3, small, g.half), F32),
        gs=vm((small, g.half), F32),
        rsend=vm((3, small, g.half), BF16),
        rrecv=vm((3, small, g.half), BF16),
        gside=vm((small, g.half), BF16),
        gt2=vm((large, g.half), F32),
        rsend2=vm((large, g.half), BF16),
        rrecv2=vm((large, g.half), BF16),
        gs2=vm((large, g.half), F32),
        gb1=vm((large, g.half), F32),
        g1=vm((large, g.half), BF16),
        essend=vm((g.ka, x * LANE), BF16),
        esrecv=vm((g.ka, x * LANE), BF16),
        essum=vm((x, g.ka, LANE), BF16),
        esr=vm((x, g.ka, LANE), BF16),
        sdsend=vm((small, x * LANE), BF16),
        sdrecv=vm((small, x * LANE), BF16),
        sdsum=vm((x, small, LANE), BF16),
        sdr=vm((x, small, LANE), BF16),
        gs1=vm((cp_rows, LANE), F32),
        outx=vm((x, g.bs * g.ps, 2 * LANE), BF16),
        outs=vm((x, g.bs * g.ps, 2 * LANE), BF16),
        dk=vm((4, 16, g.half), F32),
        pickb=vm((x, g.half, 2 * LANE), BF16),
        dke=vm((g.n_sp, 16, LANE), F32),
        vec=vm((56, g.half), F32),
        ar2=vm((5, g.group, 2, g.half), F32),
        ar4=vm((4, g.group, 4, g.half), F32),
        ar_ss=dma((9,)),
        ar_rs=dma((9,)),
        s1_ss=dma((2 * g.n_ch,)),
        s1_rs=dma((g.n_ch,)),
        sd_ss=dma((2 * g.n_ch,)),
        sd_rs=dma((g.n_ch,)),
        par_ss=dma((x,)),
        par_rs=dma((x,)),
        we_ss=dma((2, x)),
        we_rs=dma((2, x)),
        w_ss=dma((4, 2 * x)),
        w_rs=dma((4, 2 * x)),
        cot_ss=dma((x,)),
        cot_rs=dma((x,)),
        sm_ss=dma((4,)),
        sm_rs=dma((4,)),
        r_ss=dma((4,)),
        r_rs=dma((4,)),
        halo_ss=dma((7, 2)),
        halo_rs=dma((7, 2)),
        es_ss=dma((2,)),
        es_rs=dma((2,)),
        esx_ss=dma((2, x)),
        esx_rs=dma((2, x)),
        out_ss=dma((x,)),
        out_rs=dma((x,)),
        ra_ss=dma((6, g.plane)),
        ra_rs=dma((6, g.plane)),
        rz_ss=dma((6, g.nz)),
        rz_rs=dma((6, g.nz)),
        gz_ss=dma((4, g.nz)),
        gz_rs=dma((4, g.nz)),
        gy_ss=dma((4, g.ny)),
        gy_rs=dma((4, g.ny)),
        ga_ss=dma((2,)),
        ga_rs=dma((2,)),
        dke_ss=dma((1,)),
        dke_rs=dma((1,)),
    )
    for k, u in enumerate(g.units):
        unit = (16, LANE)
        table.update({
            f"part{k}": vm((x, u) + unit, BF16),
            f"plane{k}": vm((g.plane, u // g.ny) + unit, BF16),
            f"ys{k}": vm((u // g.ny,) + unit, BF16),
            f"rzr{k}": vm((g.nz, u // g.n_sp) + unit, BF16),
            f"fin{k}": vm((u,) + unit, BF16),
        })
    return table


def make_kernel(g, scratch_names):
    n_bands, half, shard, tiles = g.bands, g.half, g.shard, g.tiles
    pitch, pitch_s = g.pl_, g.ps
    small, large = g.rs * g.ps, g.rl * g.pl_
    AVG, VAR, T1, T0, INV, ALPHA, BETA, KAPPA, LAM = (6 * k for k in range(9))
    counts = (g.count_large, g.count_large) + (g.count_small,) * 4

    def kernel(*refs):
        r = types.SimpleNamespace(**dict(zip(IN_NAMES + OUT_NAMES + scratch_names, refs)))
        s = lax.axis_index("sp")
        ch = lax.axis_index("ch")
        x = ch // 2
        c = lax.rem(ch, 2)
        me = s * n_bands + x
        sends = []

        def copy_to(src, dst, send, recv, s_, x_, c_):
            cp = pltpu.make_async_remote_copy(
                src_ref=src,
                dst_ref=dst,
                send_sem=send,
                recv_sem=recv,
                device_id=(s_, x_ * 2 + c_),
                device_id_type=MESH,
            )
            cp.start()
            sends.append(cp.wait_send)

        def landed(ref, sem):
            pltpu.make_async_copy(ref, ref, sem).wait()

        def other_band(k):
            return lax.rem(x + k, n_bands)

        def edge_copy(src_up, dst_up, src_down, dst_down, e):
            up = pltpu.make_async_remote_copy(
                src_up, dst_up, r.halo_ss.at[e, 0], r.halo_rs.at[e, 0],
                device_id=(s, (x - 1) * 2 + c), device_id_type=MESH)
            down = pltpu.make_async_remote_copy(
                src_down, dst_down, r.halo_ss.at[e, 1], r.halo_rs.at[e, 1],
                device_id=(s, (x + 1) * 2 + c), device_id_type=MESH)

            @pl.when(x > 0)
            def _():
                up.start()

            @pl.when(x < n_bands - 1)
            def _():
                down.start()

            def finish():
                @pl.when(x < n_bands - 1)
                def _():
                    landed(dst_up, r.halo_rs.at[e, 0])

                @pl.when(x > 0)
                def _():
                    landed(dst_down, r.halo_rs.at[e, 1])

            def sent():
                @pl.when(x > 0)
                def _():
                    up.wait_send()

                @pl.when(x < n_bands - 1)
                def _():
                    down.wait_send()

            sends.append(sent)
            return finish

        def edges(ref, e):
            first, last = pl.ds(pitch_s, pitch_s), pl.ds(g.bs * pitch_s, pitch_s)
            return edge_copy(
                ref.at[first], ref.at[pl.ds((g.bs + 1) * pitch_s, pitch_s)],
                ref.at[last], ref.at[pl.ds(0, pitch_s)], e)

        def flipped(value, key):
            out, bit = 0, 1
            while bit <= key:
                here = lax.rem(value // bit, 2)
                out = out + bit * (1 - here if key & bit else here)
                bit *= 2
            return out + (value // bit) * bit

        def hops(key):
            return key // (n_bands * g.ny) + key // n_bands % g.ny + key % n_bands

        few = g.group <= 16
        keys = sorted(range(1, g.group), key=hops, reverse=True) if few else []
        peers = [
            (flipped(s, key // n_bands), flipped(x, key % n_bands)) for key in keys
        ]

        def to_group(src, dst, send, recv, pick=None):
            def one(s_, x_):
                pltpu.make_async_remote_copy(
                    src if pick is None else pick(s_, x_), dst, send, recv,
                    device_id=(s_, x_ * 2 + c), device_id_type=MESH).start()

            for s_, x_ in peers:
                one(s_, x_)

            def loop(k, _):
                to = lax.rem(me + k, g.group)
                one(to // n_bands, lax.rem(to, n_bands))
                return 0

            if not few:
                lax.fori_loop(1, g.group, loop, 0)

        sp_keys = sorted(range(1, g.n_sp), key=lambda k: hops(k * n_bands), reverse=True)
        sp_peers = [flipped(s, key) for key in sp_keys] if few else []

        def to_images(src, dst, send, recv):
            def one(s_):
                pltpu.make_async_remote_copy(
                    src, dst, send, recv, device_id=(s_, ch), device_id_type=MESH).start()

            for s_ in sp_peers:
                one(s_)

            def loop(k, _):
                one(lax.rem(s + k, g.n_sp))
                return 0

            if not few:
                lax.fori_loop(1, g.n_sp, loop, 0)

        def sum_start(buf, at, e, rows):
            for k, row in enumerate(rows):
                buf[at, me, k : k + 1, :] = row

            to_group(buf.at[at, me], buf.at[at, me], r.ar_ss.at[e], r.ar_rs.at[e])

        def sum_finish(buf, at, e):
            block = buf.at[at, pl.ds(0, g.group - 1)]
            landed(block, r.ar_rs.at[e])
            sends.append(lambda: landed(block, r.ar_ss.at[e]))
            total = buf[at, 0]
            for k in range(1, g.group):
                total = total + buf[at, k]
            return total

        def fill(ref, start, rows):
            ref[pl.ds(start, rows)] = jnp.zeros((rows,) + ref.shape[1:], ref.dtype)

        def fill_all(ref, step):
            def one(i, _):
                ref[pl.ds(aligned(i * step, 8), step)] = jnp.zeros(
                    (step,) + ref.shape[1:], ref.dtype)
                return 0

            repeat(ref.shape[0] // step, one, 0, 1)

        def lane(t):
            return pl.ds(t * LANE, LANE)

        def col_mask(width, breadth):
            at = lax.broadcasted_iota(jnp.int32, (width, LANE), 0)
            return jnp.where(at < breadth, 1.0, 0.0).astype(F32)

        def row_ok(row, height):
            return jnp.where((row >= 0) & (row < height), 1.0, 0.0).astype(F32)

        mask_l, mask_s = col_mask(pitch, g.wl), col_mask(pitch_s, g.ws)

        def vrow(kind, layer, t):
            return r.vec[kind + layer : kind + layer + 1, lane(t)]

        def taps_of(q, t):
            return [
                [r.par[16 + 4 * (3 * u + v) + q : 17 + 4 * (3 * u + v) + q, lane(t)] for v in range(3)]
                for u in range(3)
            ]

        def flip(taps):
            return [[taps[2 - u][2 - v] for v in range(3)] for u in range(3)]

        def conv_row(rows, taps):
            width = rows[0].shape[0]
            side = [
                rows[0] * taps[0][v] + rows[1] * taps[1][v] + rows[2] * taps[2][v]
                for v in range(3)
            ]
            return side[1] + pltpu.roll(side[0], 1, 0) + pltpu.roll(side[2], width - 1, 0)

        def store_moments(layer, total, square):
            n = counts[layer]
            average = total / n
            variance = square / n - average * average
            inverse = lax.rsqrt(variance + EPSILON)
            alpha = inverse * r.par[layer : layer + 1, :]
            r.vec[AVG + layer : AVG + layer + 1, :] = average
            r.vec[VAR + layer : VAR + layer + 1, :] = variance
            r.vec[INV + layer : INV + layer + 1, :] = inverse
            r.vec[ALPHA + layer : ALPHA + layer + 1, :] = alpha
            r.vec[BETA + layer : BETA + layer + 1, :] = (
                r.par[6 + layer : 7 + layer, :] - average * alpha)

        def store_back(layer, total, product):
            n = counts[layer]
            average = r.vec[AVG + layer : AVG + layer + 1, :]
            inverse = r.vec[INV + layer : INV + layer + 1, :]
            alpha = r.vec[ALPHA + layer : ALPHA + layer + 1, :]
            scaled = inverse * (product - average * total)
            r.vec[T0 + layer : T0 + layer + 1, :] = total
            r.vec[T1 + layer : T1 + layer + 1, :] = scaled
            kappa = -alpha * inverse * scaled / n
            r.vec[KAPPA + layer : KAPPA + layer + 1, :] = kappa
            r.vec[LAM + layer : LAM + layer + 1, :] = -alpha * total / n - kappa * average

        def rowsum(value):
            return jnp.sum(value, axis=0, keepdims=True)

        fill_all(r.x32, pitch)
        fill_all(r.a1, pitch)
        fill(r.s1, 0, pitch)
        fill(r.s1, (g.hl + 1) * pitch, (n_bands * g.bl + 1 - g.hl) * pitch)
        fill(r.parloc, 0, 56)
        fill_all(r.wpad, 16)
        fill(r.tmp, 0, tiles)
        fill(r.p2, 0, 3 * pitch)
        fill(r.p2, (g.bl + 3) * pitch, 2 * pitch)
        fill(r.gb1, 0, pitch)
        fill(r.gb1, (g.bl + 1) * pitch, pitch)
        fill(r.dk, 0, 4)
        for i in range(3):
            for ref in (r.pm, r.gb):
                ref[i, 0:pitch_s] = jnp.zeros((pitch_s, half), F32)
                ref[i, (g.bs + 1) * pitch_s : small] = jnp.zeros((pitch_s, half), F32)
        for k in range(g.n_sp):
            r.dke[k] = jnp.zeros((16, LANE), F32)

        barrier = pltpu.get_barrier_semaphore()

        def greet(k, _):
            to = lax.rem(me + k, g.group)
            pl.semaphore_signal(
                barrier, inc=1,
                device_id=(to // n_bands, lax.rem(to, n_bands) * 2 + c),
                device_id_type=MESH)
            return 0

        lax.fori_loop(1, g.group, greet, 0)
        pl.semaphore_signal(
            barrier, inc=1, device_id=(s, x * 2 + 1 - c), device_id_type=MESH)

        def entry_silu(row, _):
            value = r.inputs[0, row].astype(F32)
            r.x32[pl.ds(aligned((row + 1) * pitch, 8), g.wl), 0 : g.ci] = value
            r.a1[pl.ds(aligned((row + 2) * pitch, 8), g.wl), 0 : g.ci] = value * sigmoid(value)
            return 0

        repeat(g.hl, entry_silu, 0, UN_ES)
        r.parloc[0:6, 0 : g.cc] = r.bn_gains[...]
        r.parloc[6:12, 0 : g.cc] = r.bn_biases[...]
        for j in range(9):
            at = 16 + 4 * j
            r.parloc[at : at + 4, 0 : g.cc] = r.kernels[j // 3, j % 3].astype(F32)
        taps_in = [
            [r.kernel_entry[u].astype(F32)[v : v + 1, :] for v in range(3)] for u in range(3)
        ]
        pad_in = jnp.zeros((1, LANE - g.ci), F32)
        taps_in = [[jnp.concatenate([k, pad_in], axis=1) for k in row] for row in taps_in]

        def entry_conv(row, _):
            rows = [
                r.a1[pl.ds(aligned((row + 1 + u) * pitch, 8), pitch), :] for u in range(3)
            ]
            r.s1[pl.ds(aligned((row + 1) * pitch, 8), pitch), :] = (
                conv_row(rows, taps_in) * mask_l)
            return 0

        repeat(g.hl, entry_conv, 0, UN_EC)
        for b in range(n_bands):
            for k in range(g.na // 2):
                packed = r.s1[(b * g.bl + 2 * k) * pitch : (b * g.bl + 2 * k + 2) * pitch, :]
                if 2 * k < g.nb:
                    at = (b * g.bl + g.na + 2 * k) * pitch
                    packed = packed + pltpu.roll(r.s1[at : at + 2 * pitch, :], HALF, 1)
                r.s1pk[b, 2 * k * pitch : (2 * k + 2) * pitch, :] = packed.astype(BF16)
        for e in range(2):
            r.wpad[0 : g.cc, 0 : g.cin] = r.project_entry[:, e, :]
            r.we[e, pl.ds(aligned(x * shard, 16), shard), :] = r.wpad[:, 0 : g.cin]

        pl.semaphore_wait(barrier, g.group)
        tile = c * n_bands + x

        def full_lanes(t):
            return pl.ds(aligned(t * LANE, LANE), LANE)

        for k in range(1, n_bands):
            b = other_band(k)
            copy_to(r.s1pk.at[b], r.s1full.at[:, full_lanes(tile)],
                    r.s1_ss.at[k], r.s1_rs.at[tile], s, b, c)
        copy_to(r.s1pk.at[x], r.s1full.at[:, full_lanes(tile)],
                r.s1_ss.at[0], r.s1_rs.at[tile], s, x, 1 - c)
        r.s1full[:, full_lanes(tile)] = r.s1pk[x]
        for k in range(1, n_bands):
            mine = r.we.at[0, pl.ds(aligned(x * shard, 16), shard)]
            copy_to(mine, mine, r.we_ss.at[0, k], r.we_rs.at[0, x], s, other_band(k), c)

        for b in range(n_bands):
            spot = lax.broadcasted_iota(jnp.int32, (2 * LANE, half), 1) - b * shard
            r.picks[b] = jnp.where(
                (spot == lax.broadcasted_iota(jnp.int32, (2 * LANE, half), 0)) & (spot < g.cc),
                1.0, 0.0).astype(F32)
        r.parx[x] = r.parloc[...]

        def send_vectors():
            for k in range(1, n_bands):
                copy_to(r.parx.at[x], r.parx.at[x], r.par_ss.at[k], r.par_rs.at[x],
                        s, other_band(k), c)

        def vectors_landed():
            total = 0.0
            for k in range(1, n_bands):
                b = other_band(k)
                landed(r.parx.at[b], r.par_rs.at[b])
            for b in range(n_bands):
                total = total + dot(r.parx[b], r.picks[b], precision=lax.Precision.HIGHEST)
            r.par[...] = total

        r.sidecp[...] = jnp.zeros_like(r.sidecp)

        def side_row(row, _):
            at = aligned((2 * row + 1) * pitch, 8)
            r.sidecp[pl.ds(aligned((row + 1) * pitch_s, 8), g.ws), :] = r.x32[
                pl.ds(at, g.ws, stride=2), :]
            return 0

        repeat(g.hs, side_row, 0, UN_SR)
        for b in range(n_bands):
            r.sidepk[b] = r.sidecp[b * g.bs * pitch_s : b * g.bs * pitch_s + small, :].astype(BF16)
        r.sidefull[:, full_lanes(tile)] = r.sidepk[x]

        def send_side():
            for k in range(1, n_bands):
                b = other_band(k)
                copy_to(r.sidepk.at[b], r.sidefull.at[:, full_lanes(tile)],
                        r.sd_ss.at[k], r.sd_rs.at[tile], s, b, c)
            copy_to(r.sidepk.at[x], r.sidefull.at[:, full_lanes(tile)],
                    r.sd_ss.at[0], r.sd_rs.at[tile], s, x, 1 - c)
            for k in range(1, n_bands):
                mine = r.we.at[1, pl.ds(aligned(x * shard, 16), shard)]
                copy_to(mine, mine, r.we_ss.at[1, k], r.we_rs.at[1, x], s, other_band(k), c)

        fill_all(r.cotpad, pitch_s)

        def cot_row(row, _):
            r.cotpad[pl.ds(aligned((row + 1) * pitch_s, 8), g.ws), 0 : g.cc] = (
                r.cotangent[0, row].astype(F32))
            return 0

        repeat(g.hs, cot_row, 0, UN_SR)
        r.cotx[...] = r.cotpad[...].astype(BF16)
        r.cots[x] = r.cotx[pl.ds(aligned(x * g.bs * pitch_s, 16), small), :]

        def send_cotangent():
            for k in range(1, n_bands):
                b = other_band(k)
                copy_to(r.cotx.at[pl.ds(aligned(b * g.bs * pitch_s, 16), small)], r.cots.at[x],
                        r.cot_ss.at[k], r.cot_rs.at[x], s, b, c)

        def channel_place(rows, k0, cols, cut, offset):
            k_at = k0 + lax.broadcasted_iota(jnp.int32, (rows, cols), 0)
            p_at = lax.broadcasted_iota(jnp.int32, (rows, cols), 1)
            want = k_at + offset(0)
            for j in range(1, g.n_ch):
                jump = offset(j) - offset(j - 1)
                want = want + jnp.where(k_at >= j * cut, jump, 0)
            return jnp.where(want == p_at, 1.0, 0.0).astype(BF16)

        def offset_wide(j):
            return (j % 2) * half + (j // 2) * shard - j * g.cc

        def offset_in(j):
            return ((j % 2) * n_bands + j // 2) * LANE - j * g.ci

        r.place_in[0] = channel_place(g.cin, 0, g.full, g.ci, offset_in)
        r.place_in[1] = channel_place(
            g.cin, 0, g.full, g.ci, lambda j: offset_in(j) + HALF)
        def place_rows(k, _):
            at = aligned(k * 64, 64)
            r.place[pl.ds(at, 64), :] = channel_place(64, at, g.wide, g.cc, offset_wide)
            return 0

        repeat(g.wide // 64, place_rows, 0, 2)
        fill_all(r.wpad, 16)

        def weight_prepare(q):
            r.wpad[0 : g.cc, 0 : g.chan] = r.projects[:, q, :]
            r.w[q, pl.ds(aligned(x * shard, 16), shard), :] = dot(
                r.wpad[...], r.place[...]).astype(BF16)

        def weight_send(q, part):
            rows = pl.ds(aligned(x * shard + part * (shard // 2), 16), shard // 2)
            for k in range(1, n_bands):
                mine = r.w.at[q, rows]
                copy_to(mine, mine, r.w_ss.at[q, part * n_bands + k],
                        r.w_rs.at[q, part * n_bands + x], s, other_band(k), c)

        def weight_landed(q):
            for k in range(1, n_bands):
                b = other_band(k)
                for part in range(2):
                    rows = pl.ds(aligned(b * shard + part * (shard // 2), 16), shard // 2)
                    landed(r.w.at[q, rows], r.w_rs.at[q, part * n_bands + b])

        weight_prepare(0)
        weight_send(0, 0)
        weight_prepare(1)

        for k in range(1, n_bands):
            t = c * n_bands + other_band(k)
            landed(r.s1full.at[:, full_lanes(t)], r.s1_rs.at[t])
            copy_to(r.s1full.at[:, full_lanes(t)], r.s1full.at[:, full_lanes(t)],
                    r.s1_ss.at[g.n_ch + k], r.s1_rs.at[t], s, x, 1 - c)

        for k in range(1, n_bands):
            b = other_band(k)
            landed(r.we.at[0, pl.ds(aligned(b * shard, 16), shard)], r.we_rs.at[0, b])
        for a in range(2):
            r.wp[a] = dot(r.we[0], r.place_in[a]).astype(BF16)

        for k in range(n_bands):
            t = (1 - c) * n_bands + k
            landed(r.s1full.at[:, full_lanes(t)], r.s1_rs.at[t])
        r.p1[0 : g.ka, :] = dot(r.s1full[...], r.wp[0], (1, 1))
        r.p1[g.ka : large, :] = dot(r.s1full[0 : g.kb, :], r.wp[1], (1, 1))

        def moments(ref, first, rows, width):
            out = [[], []]
            for t in range(tiles):
                def one(k, carry):
                    v = ref[pl.ds(aligned((first + k) * width, 8), width), lane(t)]
                    return (carry[0] + fold(v), carry[1] + fold(v * v))

                zero = jnp.zeros((8, LANE), F32)
                total, square = repeat(rows, one, (zero, zero), UN_S if width == pitch_s else UN_L)
                out[0].append(rowsum(total))
                out[1].append(rowsum(square))
            return [jnp.concatenate(o, axis=1) for o in out]

        sum_start(r.ar2, 0, 0, moments(r.p1, 1, g.bl, pitch))
        send_vectors()
        weight_send(0, 1)
        send_side()
        weight_send(1, 0)
        weight_send(1, 1)
        weight_prepare(2)
        vectors_landed()
        total = sum_finish(r.ar2, 0, 0)
        store_moments(0, total[0:1], total[1:2])

        for t in range(tiles):
            alpha, beta = vrow(ALPHA, 0, t), vrow(BETA, 0, t)

            def one(k, _):
                at = pl.ds(aligned(k * pitch, 8), pitch)
                h = r.p1[at, lane(t)] * alpha + beta
                ok = mask_l * row_ok(x * g.bl + k - 1, g.hl)
                r.a2[at, lane(t)] = h * sigmoid(h) * ok
                return 0

            repeat(g.rl, one, 0, UN_L)
        mine_lanes = aligned(c * half, LANE)
        their_lanes = aligned((1 - c) * half, LANE)

        def own_tile(t):
            return pl.ds(aligned(c * half + t * LANE, LANE), LANE)

        def conv_pairs(source, q, target, row0, rows, height, width, mask):
            for t in range(tiles):
                taps = taps_of(q, t)

                def one(k, _):
                    block = [
                        source[pl.ds(aligned((2 * k + u) * width, 8), width), lane(t)]
                        for u in range(4)
                    ]
                    out = [
                        conv_row(block[j : j + 3], taps) * (mask * row_ok(row0 + 2 * k + j, height))
                        for j in range(2)
                    ]
                    target[pl.ds(aligned(k * 2 * width, 16), 2 * width), own_tile(t)] = (
                        jnp.concatenate(out, axis=0).astype(BF16))
                    return 0

                repeat(rows // 2, one, 0, UN_S if width == pitch_s else UN_L)

        conv_pairs(r.a2, 0, r.s2, x * g.bl, g.bl, g.hl, pitch, mask_l)

        def swap_start(ref, e):
            mine = ref.at[:, pl.ds(mine_lanes, half)]
            copy_to(mine, mine, r.sm_ss.at[e], r.sm_rs.at[e], s, x, 1 - c)

        def swap_landed(ref, e):
            landed(ref.at[:, pl.ds(their_lanes, half)], r.sm_rs.at[e])

        swap_start(r.s2, 0)
        for k in range(1, n_bands):
            t = c * n_bands + other_band(k)
            landed(r.sidefull.at[:, full_lanes(t)], r.sd_rs.at[t])
            copy_to(r.sidefull.at[:, full_lanes(t)], r.sidefull.at[:, full_lanes(t)],
                    r.sd_ss.at[g.n_ch + k], r.sd_rs.at[t], s, x, 1 - c)
        weight_landed(0)
        rows_all = g.bl * pitch
        step = rows_all // 2
        for k in range(2):
            rows = pl.ds(k * step, step)
            r.p2[3 * pitch + k * step : 3 * pitch + (k + 1) * step, :] = dot(
                r.s2[rows, pl.ds(mine_lanes, half)], r.w[0, :, pl.ds(mine_lanes, half)], (1, 1))
        swap_landed(r.s2, 0)
        for k in range(2):
            rows = pl.ds(k * step, step)
            at = slice(3 * pitch + k * step, 3 * pitch + (k + 1) * step)
            r.p2[at, :] = r.p2[at, :] + dot(
                r.s2[rows, pl.ds(their_lanes, half)], r.w[0, :, pl.ds(their_lanes, half)], (1, 1))
        for k in range(1, n_bands):
            b = other_band(k)
            landed(r.we.at[1, pl.ds(aligned(b * shard, 16), shard)], r.we_rs.at[1, b])
        r.wp[2] = dot(r.we[1], r.place_in[0]).astype(BF16)
        for k in range(n_bands):
            t = (1 - c) * n_bands + k
            landed(r.sidefull.at[:, full_lanes(t)], r.sd_rs.at[t])
        r.pside[...] = dot(r.sidefull[...], r.wp[2], (1, 1))
        sum_start(r.ar4, 0, 1,
                  moments(r.p2, 3, g.bl, pitch) + moments(r.pside, 1, g.bs, pitch_s))
        r.edge_up[...] = r.p2[3 * pitch : 5 * pitch, :].astype(BF16)
        r.edge_down[...] = r.p2[(g.bl - 1) * pitch : (g.bl + 3) * pitch, :].astype(BF16)
        edges_done = edge_copy(r.edge_up, r.from_below, r.edge_down, r.from_above, 0)
        weight_send(2, 0)
        weight_send(2, 1)
        weight_prepare(3)

        edges_done()

        @pl.when(x > 0)
        def _():
            r.p2[0 : 3 * pitch, :] = r.from_above[...].astype(F32)[pitch : 4 * pitch]

        @pl.when(x < n_bands - 1)
        def _():
            r.p2[(g.bl + 3) * pitch : (g.bl + 5) * pitch, :] = r.from_below[...].astype(F32)

        for t in range(tiles):
            def one(k, _):
                v = (r.p2[pl.ds(aligned(2 * k * pitch, 8), pitch), lane(t)]
                     + r.p2[pl.ds(aligned((2 * k + 1) * pitch, 8), pitch), lane(t)]
                     + r.p2[pl.ds(aligned((2 * k + 2) * pitch, 8), pitch), lane(t)])
                r.tmp[t, 0:pitch, :] = v + pltpu.roll(v, 1, 0) + pltpu.roll(v, pitch - 1, 0)
                r.poolraw[pl.ds(aligned(k * pitch_s, 8), pitch_s), lane(t)] = r.tmp[
                    t, pl.ds(0, pitch_s, stride=2), :]
                return 0

            repeat(g.rs, one, 0, UN_S)
        total = sum_finish(r.ar4, 0, 1)
        store_moments(1, total[0:1], total[1:2])
        store_moments(2, total[2:3], total[3:4])

        at_col = lax.broadcasted_iota(jnp.int32, (pitch_s, LANE), 0)
        col_count = mask_s * (
            1.0
            + jnp.where(at_col > 0, 1.0, 0.0)
            + jnp.where(2 * at_col + 1 < g.wl, 1.0, 0.0)) * (1.0 / 9.0)

        def window_count(row):
            inside = jnp.where(row > 0, 1.0, 0.0) + jnp.where(2 * row + 1 < g.hl, 1.0, 0.0) + 1.0
            return col_count * (inside.astype(F32) * row_ok(row, g.hs))

        for t in range(tiles):
            alpha, beta = vrow(ALPHA, 1, t) * (1.0 / 9.0), vrow(BETA, 1, t)
            alpha_2, beta_2 = vrow(ALPHA, 2, t), vrow(BETA, 2, t)

            def one(k, _):
                at = pl.ds(aligned(k * pitch_s, 8), pitch_s)
                row = x * g.bs + k - 1
                ok = mask_s * row_ok(row, g.hs)
                h = (r.poolraw[at, lane(t)] * alpha + window_count(row) * beta
                     + r.pside[at, lane(t)] * alpha_2 + beta_2) * ok
                r.hid[0, at, lane(t)] = h
                r.act[0, at, lane(t)] = h * sigmoid(h)
                return 0

            repeat(g.rs, one, 0, UN_S)

        def make_picks():
            for b in range(n_bands):
                spot_b = lax.broadcasted_iota(jnp.int32, (half, 2 * LANE), 0) - b * shard
                r.pickb[b] = jnp.where(
                    (spot_b == lax.broadcasted_iota(jnp.int32, (half, 2 * LANE), 1))
                    & (spot_b < g.cc), 1.0, 0.0).astype(BF16)

        own_rows = slice(pitch_s, (g.bs + 1) * pitch_s)
        for i in range(3):
            if i > 0:
                for t in range(tiles):
                    alpha, beta = vrow(ALPHA, 2 + i, t), vrow(BETA, 2 + i, t)

                    def one(k, _):
                        at = pl.ds(aligned(k * pitch_s, 8), pitch_s)
                        ok = mask_s * row_ok(x * g.bs + k - 1, g.hs)
                        h = (r.pm[i - 1, at, lane(t)] * alpha + beta) * ok
                        r.hid[i, at, lane(t)] = h
                        r.act[i, at, lane(t)] = h * sigmoid(h)
                        return 0

                    repeat(g.rs, one, 0, UN_S)
            conv_pairs(r.act.at[i], i + 1, r.sm.at[i], x * g.bs, g.bs, g.hs,
                       pitch_s, mask_s)
            swap_start(r.sm.at[i], 1 + i)
            weight_landed(1 + i)
            part = dot(r.sm[i, :, pl.ds(mine_lanes, half)],
                       r.w[1 + i, :, pl.ds(mine_lanes, half)], (1, 1))
            swap_landed(r.sm.at[i], 1 + i)
            r.pm[i, own_rows, :] = part + dot(
                r.sm[i, :, pl.ds(their_lanes, half)],
                r.w[1 + i, :, pl.ds(their_lanes, half)], (1, 1))
            if i < 2:
                sum_start(r.ar2, 1 + i, 2 + i, moments(r.pm.at[i], 1, g.bs, pitch_s))
                edges_done = edges(r.pm.at[i], 1 + i)
                if i == 0:
                    weight_send(3, 0)
                    weight_send(3, 1)
                else:
                    send_cotangent()
                total = sum_finish(r.ar2, 1 + i, 2 + i)
                store_moments(3 + i, total[0:1], total[1:2])
                edges_done()

        def grad_sums(gref, pref, width, first, rows):
            out = [[], []]
            for t in range(tiles):
                def one(k, carry):
                    at = pl.ds(aligned((first + k) * width, 8), width)
                    v = gref[at, lane(t)]
                    return (carry[0] + fold(v), carry[1] + fold(v * pref[at, lane(t)]))

                zero = jnp.zeros((8, LANE), F32)
                a, b = repeat(rows, one, (zero, zero), UN_S if width == pitch_s else UN_L)
                out[0].append(rowsum(a))
                out[1].append(rowsum(b))
            return [jnp.concatenate(o, axis=1) for o in out]

        for k in range(1, n_bands):
            b = other_band(k)
            landed(r.cots.at[b], r.cot_rs.at[b])
        total = 0.0
        for b in range(n_bands):
            total = total + dot(r.cots[b], r.picks[b].astype(BF16))
        r.cot[...] = total
        sum_start(r.ar4, 1, 4,
                  moments(r.pm.at[2], 1, g.bs, pitch_s)
                  + grad_sums(r.cot, r.pm.at[2], pitch_s, 1, g.bs))
        edges_done = edges(r.pm.at[2], 3)
        make_picks()
        total = sum_finish(r.ar4, 1, 4)
        store_moments(5, total[0:1], total[1:2])
        store_back(5, total[2:3], total[3:4])
        edges_done()

        def norm_back(layer, gref, pref, target, rows, width, mask, row0, height):
            for t in range(tiles):
                alpha, kappa, lam = vrow(ALPHA, layer, t), vrow(KAPPA, layer, t), vrow(LAM, layer, t)

                def one(k, _):
                    at = pl.ds(aligned(k * width, 8), width)
                    ok = mask * row_ok(row0 + k, height)
                    target[at, lane(t)] = (
                        gref[at, lane(t)] * alpha + pref[at, lane(t)] * kappa + lam) * ok
                    return 0

                repeat(rows, one, 0, UN_S if width == pitch_s else UN_L)

        def kernel_grad(aref, gref, q, rows, width):
            for t in range(tiles):
                def one(k, carry):
                    gv = gref[pl.ds(aligned((k + 1) * width, 8), width), lane(t)]
                    turned = [pltpu.roll(gv, width - 1, 0), gv, pltpu.roll(gv, 1, 0)]
                    out = []
                    for u in range(3):
                        av = aref[pl.ds(aligned((k + u) * width, 8), width), lane(t)]
                        for v in range(3):
                            out.append(carry[3 * u + v] + fold(av * turned[v]))
                    return tuple(out)

                zero = jnp.zeros((8, LANE), F32)
                sums = repeat(rows, one, (zero,) * 9, UN_S if width == pitch_s else UN_L)
                for j in range(9):
                    r.dk[q, j : j + 1, lane(t)] = rowsum(sums[j])

        yi, zi = lax.rem(s, g.ny), s // g.ny

        def block_of(name, k):
            return getattr(r, f"{name}{k}")

        def put_units(k, value, cols):
            value = value.astype(BF16)
            for b in range(n_bands):
                for t in range(cols // LANE):
                    part = value[b * shard : (b + 1) * shard, t * LANE : (t + 1) * LANE]
                    block_of("part", k)[b, t * g.tall : (t + 1) * g.tall] = (
                        part.reshape(g.tall, 16, LANE))

        def put_kernels():
            for q in range(4):
                value = r.dk[q].astype(BF16)
                for b in range(n_bands):
                    part = dot(value, r.pickb[b]).astype(BF16)
                    for t in range(g.u_dk):
                        at = g.u_in + q * g.u_dk + t
                        r.part5[b, at] = part[:, t * LANE : (t + 1) * LANE]

        def plane_send(k):
            part = g.units[k] // g.ny
            me_plane = x * g.ny + yi
            for key in range(1, g.plane):
                to = lax.rem(me_plane + key, g.plane)
                x_, y_ = to // g.ny, lax.rem(to, g.ny)
                copy_to(block_of("part", k).at[x_, pl.ds(y_ * part, part)],
                        block_of("plane", k).at[me_plane],
                        r.ra_ss.at[k, key], r.ra_rs.at[k, me_plane], zi * g.ny + y_, x_, c)

        def plane_sum_z_send(k):
            part = g.units[k] // g.ny
            me_plane = x * g.ny + yi
            total = block_of("part", k)[x, pl.ds(yi * part, part)].astype(F32)
            for key in range(1, g.plane):
                b = lax.rem(me_plane + key, g.plane)
                landed(block_of("plane", k).at[b], r.ra_rs.at[k, b])
                total = total + block_of("plane", k)[b].astype(F32)
            block_of("ys", k)[...] = total.astype(BF16)
            piece = part // g.nz
            for j in range(1, g.nz):
                to = lax.rem(zi + j, g.nz)
                copy_to(block_of("ys", k).at[pl.ds(to * piece, piece)], block_of("rzr", k).at[zi],
                        r.rz_ss.at[k, j], r.rz_rs.at[k, zi], to * g.ny + yi, x, c)

        def z_sum(k):
            part = g.units[k] // g.ny
            piece = part // g.nz
            total = block_of("ys", k)[pl.ds(zi * piece, piece)].astype(F32)
            for j in range(1, g.nz):
                b = lax.rem(zi + j, g.nz)
                landed(block_of("rzr", k).at[b], r.rz_rs.at[k, b])
                total = total + block_of("rzr", k)[b].astype(F32)
            at = pl.ds(yi * part + zi * piece, piece)
            block_of("fin", k)[at] = total.astype(BF16)
            return at

        def z_gather(k):
            at = z_sum(k)
            for j in range(1, g.nz):
                to = lax.rem(zi + j, g.nz)
                copy_to(block_of("fin", k).at[at], block_of("fin", k).at[at],
                        r.gz_ss.at[k, j], r.gz_rs.at[k, zi], to * g.ny + yi, x, c)

        def all_gather(k):
            mine = block_of("fin", k).at[z_sum(k)]
            to_images(mine, mine, r.ga_ss.at[k - 4], r.ga_rs.at[k - 4])

        def y_gather(k):
            part = g.units[k] // g.ny
            piece = part // g.nz
            for j in range(1, g.nz):
                b = lax.rem(zi + j, g.nz)
                landed(block_of("fin", k).at[pl.ds(yi * part + b * piece, piece)],
                       r.gz_rs.at[k, b])
            at = pl.ds(yi * part, part)
            for j in range(1, g.ny):
                to = lax.rem(yi + j, g.ny)
                copy_to(block_of("fin", k).at[at], block_of("fin", k).at[at],
                        r.gy_ss.at[k, j], r.gy_rs.at[k, yi], zi * g.ny + to, x, c)

        def get_units(k, cols):
            tiles_in = [
                block_of("fin", k)[t * g.tall : (t + 1) * g.tall].reshape(shard, LANE)
                for t in range(cols // LANE)
            ]
            return jnp.concatenate(tiles_in, axis=1)

        def finish_block(k):
            part = g.units[k] // g.ny
            for j in range(1, g.ny):
                b = lax.rem(yi + j, g.ny)
                landed(block_of("fin", k).at[pl.ds(b * part, part)], r.gy_rs.at[k, b])
            r.m_dw[3 - k] = dot(get_units(k, g.wide), r.place[...], (1, 1)).astype(BF16)

        def finish_entry(k):
            piece = g.units[k] // g.n_sp
            others = block_of("fin", k).at[pl.ds(0, (g.n_sp - 1) * piece)]
            landed(others, r.ga_rs.at[k - 4])
            sends.append(lambda: landed(others, r.ga_ss.at[k - 4]))
            r.m_dwe[5 - k] = get_units(k, g.cin)
            if k == 5:
                for q in range(4):
                    for t in range(g.u_dk):
                        r.m_dk[q, :, lane(t)] = r.fin5[g.u_in + q * g.u_dk + t].astype(F32)

        for i in (2, 1, 0):
            layer = 3 + i
            gref = r.cot if i == 2 else r.gb.at[i + 1]
            norm_back(layer, gref, r.pm.at[i], r.gt.at[i], g.rs, pitch_s, mask_s,
                      x * g.bs - 1, g.hs)
            grad = r.gt[i].astype(BF16)
            r.rsend[i] = dot(grad, r.w[1 + i, :, pl.ds(their_lanes, half)]).astype(BF16)
            copy_to(r.rsend.at[i], r.rrecv.at[i], r.r_ss.at[i], r.r_rs.at[i], s, x, 1 - c)
            part = dot(grad, r.w[1 + i, :, pl.ds(mine_lanes, half)])
            grad = r.gt[i, own_rows, :].astype(BF16)
            put_units(2 - i, dot(grad, r.sm[i], (0, 0)), g.wide)
            landed(r.rrecv.at[i], r.r_rs.at[i])
            r.gs[...] = part + r.rrecv[i].astype(F32)
            rows = [[] for _ in range(4 if i == 0 else 2)]
            for t in range(tiles):
                taps = flip(taps_of(i + 1, t))

                def one(k, carry):
                    block = [
                        r.gs[pl.ds(aligned((k + u) * pitch_s, 8), pitch_s), lane(t)]
                        for u in range(3)
                    ]
                    at = pl.ds(aligned((k + 1) * pitch_s, 8), pitch_s)
                    row = x * g.bs + k
                    h = r.hid[i, at, lane(t)]
                    sig = sigmoid(h)
                    value = conv_row(block, taps) * (sig * (1.0 + h * (1.0 - sig))) * (
                        mask_s * row_ok(row, g.hs))
                    if i == 0:
                        value = value + r.cot[at, lane(t)]
                    r.gb[i, at, lane(t)] = value
                    if i == 0:
                        new = [
                            value, value * r.pside[at, lane(t)],
                            value * window_count(row),
                            value * r.poolraw[at, lane(t)] * (1.0 / 9.0)]
                    else:
                        new = [value, value * r.pm[i - 1, at, lane(t)]]
                    return tuple(a + fold(b) for a, b in zip(carry, new))

                zero = jnp.zeros((8, LANE), F32)
                sums = repeat(g.bs, one, (zero,) * len(rows), UN_S)
                for j, v in enumerate(sums):
                    rows[j].append(rowsum(v))
            rows = [jnp.concatenate(o, axis=1) for o in rows]
            buf, at_e, e = ((r.ar4, 2, 7), (r.ar2, 3, 6), (r.ar2, 4, 5))[i]
            sum_start(buf, at_e, e, rows)
            edges_done = edges(r.gb.at[i], 4 + i)
            plane_send(2 - i)
            if i < 2:
                plane_sum_z_send(1 - i)
            if i == 0:
                z_gather(0)
            kernel_grad(r.act.at[i], r.gs, i + 1, g.bs, pitch_s)
            if i == 2:
                value = []
                for t in range(tiles):
                    h = (r.pm[2, own_rows, lane(t)] * vrow(ALPHA, 5, t) + vrow(BETA, 5, t)
                         + r.hid[0, own_rows, lane(t)])
                    value.append(h.astype(BF16))
                value = jnp.concatenate(value, axis=1)
                for b in range(n_bands):
                    r.outx[b] = dot(value, r.pickb[b]).astype(BF16)
                for k in range(1, n_bands):
                    b = other_band(k)
                    copy_to(r.outx.at[b], r.outs.at[x], r.out_ss.at[k], r.out_rs.at[x], s, b, c)
                r.outs[x] = r.outx[x]
            total = sum_finish(buf, at_e, e)
            if i > 0:
                store_back(layer - 1, total[0:1], total[1:2])
            else:
                store_back(2, total[0:1], total[1:2])
                store_back(1, total[2:3], total[3:4])
            edges_done()

        for t in range(tiles):
            alpha, kappa, lam = vrow(ALPHA, 1, t) * (1.0 / 9.0), vrow(KAPPA, 1, t), vrow(LAM, 1, t)

            def spread(v):
                r.tmp[t, pl.ds(0, pitch_s, stride=2), :] = v
                r.tmp[t, pl.ds(1, pitch_s, stride=2), :] = v + pltpu.roll(v, pitch_s - 1, 0)
                return r.tmp[t, 0:pitch, :]

            def one(k, _):
                low = r.gb[0, pl.ds(aligned(k * pitch_s, 8), pitch_s), lane(t)]
                high = r.gb[0, pl.ds(aligned((k + 1) * pitch_s, 8), pitch_s), lane(t)]
                for j, v in enumerate((low + high, high)):
                    row = x * g.bl + 2 * k + j - 1
                    ok = mask_l * row_ok(row, g.hl)
                    p = r.p2[pl.ds(aligned((2 * k + j + 2) * pitch, 8), pitch), lane(t)]
                    r.gt2[pl.ds(aligned((2 * k + j) * pitch, 8), pitch), lane(t)] = (
                        spread(v) * alpha + p * kappa + lam) * ok
                return 0

            repeat(g.bs + 1, one, 0, UN_S)
        for k in range(2):
            at = pl.ds(k * (large // 2), large // 2)
            r.rsend2[at, :] = dot(
                r.gt2[at, :].astype(BF16), r.w[0, :, pl.ds(their_lanes, half)]).astype(BF16)
        copy_to(r.rsend2, r.rrecv2, r.r_ss.at[3], r.r_rs.at[3], s, x, 1 - c)
        for k in range(2):
            at = pl.ds(k * (large // 2), large // 2)
            r.gs2[at, :] = dot(r.gt2[at, :].astype(BF16), r.w[0, :, pl.ds(mine_lanes, half)])
        put_units(3, dot(
            r.gt2[pitch : (g.bl + 1) * pitch, :].astype(BF16), r.s2[...], (0, 0)), g.wide)
        plane_send(3)
        z_gather(1)
        y_gather(0)
        landed(r.rrecv2, r.r_rs.at[3])
        r.gs2[...] = r.gs2[...] + r.rrecv2[...].astype(F32)
        rows = [[], []]
        for t in range(tiles):
            taps = flip(taps_of(0, t))
            alpha, beta = vrow(ALPHA, 0, t), vrow(BETA, 0, t)

            def one(k, carry):
                block = [
                    r.gs2[pl.ds(aligned((k + u) * pitch, 8), pitch), lane(t)] for u in range(3)
                ]
                at = pl.ds(aligned((k + 1) * pitch, 8), pitch)
                p = r.p1[at, lane(t)]
                h = p * alpha + beta
                sig = sigmoid(h)
                value = conv_row(block, taps) * (sig * (1.0 + h * (1.0 - sig))) * (
                    mask_l * row_ok(x * g.bl + k, g.hl))
                r.gb1[at, lane(t)] = value
                return (carry[0] + fold(value), carry[1] + fold(value * p))

            zero = jnp.zeros((8, LANE), F32)
            sums = repeat(g.bl, one, (zero, zero), UN_L)
            for j, v in enumerate(sums):
                rows[j].append(rowsum(v))
        rows = [jnp.concatenate(o, axis=1) for o in rows]
        sum_start(r.ar4, 3, 8, rows)

        def own_ok(k, width_rows):
            return jnp.where((k >= 1) & (k <= width_rows), 1.0, 0.0).astype(F32)

        for t in range(tiles):
            alpha, kappa, lam = vrow(ALPHA, 2, t), vrow(KAPPA, 2, t), vrow(LAM, 2, t)

            def one(k, _):
                out = []
                for j in range(2):
                    at = pl.ds(aligned((2 * k + j) * pitch_s, 8), pitch_s)
                    ok = mask_s * (row_ok(x * g.bs + 2 * k + j - 1, g.hs) * own_ok(2 * k + j, g.bs))
                    out.append((r.gb[0, at, lane(t)] * alpha
                                + r.pside[at, lane(t)] * kappa + lam) * ok)
                r.gside[pl.ds(aligned(2 * k * pitch_s, 16), 2 * pitch_s), lane(t)] = (
                    jnp.concatenate(out, axis=0).astype(BF16))
                return 0

            repeat(g.rs // 2, one, 0, UN_S)
        own_tiles = pl.ds(aligned(c * n_bands * LANE, LANE), n_bands * LANE)
        their_tiles = pl.ds(aligned((1 - c) * n_bands * LANE, LANE), n_bands * LANE)
        r.sdsend[...] = dot(r.gside[...], r.wp[2, :, their_tiles]).astype(BF16)
        copy_to(r.sdsend, r.sdrecv, r.es_ss.at[1], r.es_rs.at[1], s, x, 1 - c)
        part = dot(r.gside[...], r.wp[2, :, own_tiles])
        landed(r.sdrecv, r.es_rs.at[1])
        part = part + r.sdrecv[...].astype(F32)
        for b in range(n_bands):
            r.sdsum[b] = part[:, b * LANE : (b + 1) * LANE].astype(BF16)
        for k in range(1, n_bands):
            b = other_band(k)
            copy_to(r.sdsum.at[b], r.sdr.at[x], r.esx_ss.at[1, k], r.esx_rs.at[1, x], s, b, c)
        r.sdr[x] = r.sdsum[x]

        lane_at = lax.broadcasted_iota(jnp.int32, (half, g.full), 1)
        low_lanes = lax.rem(lane_at, LANE) < HALF
        both_place = r.place_in[0] + r.place_in[1]

        value = dot(r.gside[...], r.sidefull[...], (0, 0)).astype(BF16)
        put_units(4, dot(value, both_place, (1, 1)), g.cin)
        plane_send(4)
        plane_sum_z_send(2)
        y_gather(1)
        kernel_grad(r.a2, r.gs2, 0, g.bl, pitch)
        put_kernels()
        plane_sum_z_send(3)
        total = sum_finish(r.ar4, 3, 8)
        store_back(0, total[0:1], total[1:2])

        for t in range(tiles):
            alpha, kappa, lam = vrow(ALPHA, 0, t), vrow(KAPPA, 0, t), vrow(LAM, 0, t)

            def one(k, _):
                out = []
                for j in range(2):
                    at = pl.ds(aligned((2 * k + j) * pitch, 8), pitch)
                    ok = mask_l * (row_ok(x * g.bl + 2 * k + j - 1, g.hl) * own_ok(2 * k + j, g.bl))
                    out.append((r.gb1[at, lane(t)] * alpha + r.p1[at, lane(t)] * kappa + lam) * ok)
                r.g1[pl.ds(aligned(2 * k * pitch, 16), 2 * pitch), lane(t)] = (
                    jnp.concatenate(out, axis=0).astype(BF16))
                return 0

            repeat(g.rl // 2, one, 0, UN_L)

        def entry_part(lanes):
            a = dot(r.g1[0 : g.ka, :], r.wp[0, :, lanes])
            b = dot(r.g1[g.ka : large, :], r.wp[1, :, lanes])
            if g.kb == g.ka:
                return a + b
            return jnp.concatenate([a[0 : g.kb] + b, a[g.kb :]], axis=0)

        r.essend[...] = entry_part(their_tiles).astype(BF16)
        copy_to(r.essend, r.esrecv, r.es_ss.at[0], r.es_rs.at[0], s, x, 1 - c)
        part = entry_part(own_tiles)
        landed(r.esrecv, r.es_rs.at[0])
        part = part + r.esrecv[...].astype(F32)
        for b in range(n_bands):
            r.essum[b] = part[:, b * LANE : (b + 1) * LANE].astype(BF16)
        for k in range(1, n_bands):
            b = other_band(k)
            copy_to(r.essum.at[b], r.esr.at[x], r.esx_ss.at[0, k], r.esx_rs.at[0, x], s, b, c)
        r.esr[x] = r.essum[x]
        grad_a = dot(r.g1[0 : g.ka, :], r.s1full[...], (0, 0))
        grad_b = dot(r.g1[g.ka : large, :], r.s1full[0 : g.kb, :], (0, 0))
        value = jnp.where(low_lanes, grad_a, grad_b).astype(BF16)
        put_units(5, dot(value, both_place, (1, 1)), g.cin)
        plane_send(5)
        z_gather(2)
        plane_sum_z_send(4)
        finish_block(0)
        finish_block(1)

        spot = lax.broadcasted_iota(jnp.int32, (half, 2 * LANE), 0) - x * shard
        pick_own = jnp.where(
            (spot == lax.broadcasted_iota(jnp.int32, (half, 2 * LANE), 1)) & (spot < g.cc),
            1.0, 0.0).astype(F32)
        final = dot(r.vec[0:24, :], pick_own, precision=lax.Precision.HIGHEST)
        final = final[:, 0 : g.cc]
        at_row = lax.broadcasted_iota(jnp.int32, (6, g.cc), 0)
        count = jnp.where(at_row < 2, g.count_large, g.count_small)
        bessel = count / (count - 1.0)
        final = jnp.concatenate([
            (1.0 - MOMENTUM) * r.run_means[...] + MOMENTUM * final[0:6],
            (1.0 - MOMENTUM) * r.run_vars[...] + MOMENTUM * (final[6:12] * bessel),
            final[12:24]], axis=0)
        r.m_vec[:, 0 : g.cc] = final

        for k in range(1, n_bands):
            b = other_band(k)
            landed(r.outs.at[b], r.out_rs.at[b])
        for b in range(n_bands):
            r.m_out[b * g.bs * pitch_s : (b + 1) * g.bs * pitch_s, :] = r.outs[b].astype(F32)

        for k in range(1, n_bands):
            b = other_band(k)
            landed(r.sdr.at[b], r.esx_rs.at[1, b])
        for b in range(n_bands):
            r.sidecp[b * g.bs * pitch_s : (b + 1) * g.bs * pitch_s, :] = (
                r.sdr[b].astype(F32)[pitch_s : (g.bs + 1) * pitch_s])
        for k in range(1, n_bands):
            b = other_band(k)
            landed(r.esr.at[b], r.esx_rs.at[0, b])
        fill(r.gs1, 0, pitch)
        fill(r.gs1, (n_bands * g.bl + 1) * pitch, pitch)
        for b in range(n_bands):
            for k in range(g.na // 2):
                value = r.esr[b, 2 * k * pitch : (2 * k + 2) * pitch, :].astype(F32)
                for j in range(2):
                    i = 2 * k + j
                    if 1 <= i <= g.bl:
                        at = (b * g.bl + i) * pitch
                        r.gs1[at : at + pitch, :] = value[j * pitch : (j + 1) * pitch]
                if 2 * k < g.nb:
                    value = pltpu.roll(value, HALF, 1)
                    for j in range(2):
                        i = g.na + 2 * k + j
                        if 1 <= i <= g.bl:
                            at = (b * g.bl + i) * pitch
                            r.gs1[at : at + pitch, :] = value[j * pitch : (j + 1) * pitch]
        taps = flip(taps_in)

        def in_grad(row):
            block = [r.gs1[pl.ds(aligned((row + u) * pitch, 8), pitch), :] for u in range(3)]
            h = r.x32[pl.ds(aligned((row + 1) * pitch, 8), pitch), :]
            sig = sigmoid(h)
            return conv_row(block, taps) * (sig * (1.0 + h * (1.0 - sig)))

        r.tmp[0] = jnp.zeros((48, LANE), F32)

        def in_rows(k, _):
            r.tmp[0, pl.ds(0, pitch_s, stride=2), :] = r.sidecp[
                pl.ds(aligned(k * pitch_s, 8), pitch_s), :]
            value = in_grad(2 * k) + r.tmp[0, 0:pitch, :]
            r.m_gin[pl.ds(aligned(2 * k * pitch, 8), pitch), :] = value

            r.m_gin[pl.ds(aligned((2 * k + 1) * pitch, 8), pitch), :] = in_grad(2 * k + 1)
            return 0

        repeat(g.hs, in_rows, 0, UN_IR)

        def entry_kernel(k, carry):
            gv = r.gs1[pl.ds(aligned((k + 1) * pitch, 8), pitch), :]
            turned = [pltpu.roll(gv, pitch - 1, 0), gv, pltpu.roll(gv, 1, 0)]
            out = []
            for u in range(3):
                av = r.a1[pl.ds(aligned((k + 1 + u) * pitch, 8), pitch), :]
                for v in range(3):
                    out.append(carry[3 * u + v] + fold(av * turned[v]))
            return tuple(out)

        zero = jnp.zeros((8, LANE), F32)
        sums = repeat(g.hl, entry_kernel, (zero,) * 9, UN_EK)
        for j in range(9):
            r.dke[s, j : j + 1, :] = rowsum(sums[j])

        to_images(r.dke.at[s], r.dke.at[s], r.dke_ss.at[0], r.dke_rs.at[0])

        z_gather(3)
        plane_sum_z_send(5)
        y_gather(2)
        all_gather(4)
        all_gather(5)
        y_gather(3)
        finish_block(2)
        finish_entry(4)
        finish_block(3)
        finish_entry(5)

        block = r.dke.at[pl.ds(0, g.n_sp - 1)]
        landed(block, r.dke_rs.at[0])
        sends.append(lambda: landed(block, r.dke_ss.at[0]))
        total = r.dke[0]
        for k in range(1, g.n_sp):
            total = total + r.dke[k]
        r.m_dke[...] = total
        for wait in sends:
            wait()

    return kernel


def body(mesh_shape, *args):
    inputs, cotangent, kernel_entry, kernels, project_entry, projects = args[:6]
    g = geometry(mesh_shape, inputs, cotangent, project_entry, projects)
    operands = list(args)
    operands[3] = jnp.transpose(kernels, (1, 2, 0, 3))
    operands[4] = jnp.transpose(project_entry, (1, 0, 2))
    operands[5] = jnp.transpose(projects, (1, 0, 2))
    table = scratch_table(g)
    names = list(table)
    shapes = [
        ((g.bands * g.bs * g.ps, 2 * LANE), F32),
        ((2 * g.hs * g.pl_, LANE), F32),
        ((16, LANE), F32),
        ((4, 16, 2 * LANE), F32),
        ((2, g.shard, g.cin), BF16),
        ((4, g.shard, g.wide), BF16),
        ((24, 2 * LANE), F32),
    ]
    vmem = pl.BlockSpec(memory_space=pltpu.VMEM)
    parts = pl.pallas_call(
        make_kernel(g, names),
        out_shape=[jax.ShapeDtypeStruct(shape, kind) for shape, kind in shapes],
        in_specs=[vmem] * 10,
        out_specs=[vmem] * len(shapes),
        scratch_shapes=list(table.values()),
        compiler_params=pltpu.CompilerParams(
            collective_id=0, has_side_effects=True, vmem_limit_bytes=60 << 20),
    )(*operands)

    def write(m_out, m_gin, m_dke, m_dk, m_dwe, m_dw, m_vec, *outs):
        o_out, o_gin, o_dke, o_dk, o_dwe, o_dw, o_gains, o_biases, o_means, o_vars = outs
        for q in range(4):
            o_dw[:, q, :] = m_dw[q].astype(F32)[0 : g.cc, 0 : g.chan]
        for e in range(2):
            o_dwe[:, e, :] = m_dwe[e].astype(F32)[0 : g.cc]
        for row in range(g.hs):
            o_out[row, :, 0, :] = m_out[row * g.ps : row * g.ps + g.ws, 0 : g.cc]

        def one(row, _):
            o_gin[row, :, 0, :] = m_gin[pl.ds(aligned(row * g.pl_, 8), g.wl), 0 : g.ci]
            return 0

        repeat(g.hl, one, 0, UN_W)
        for j in range(9):
            for q in range(4):
                o_dk[j // 3, j % 3, q : q + 1, :] = m_dk[q, j : j + 1, 0 : g.cc]
        for u in range(3):
            o_dke[u] = m_dke[3 * u : 3 * u + 3, 0 : g.ci]
        for k, ref in enumerate((o_means, o_vars, o_gains, o_biases)):
            ref[...] = m_vec[6 * k : 6 * k + 6, 0 : g.cc]

    results = [
        (g.hs, g.ws, 1, g.cc),
        (g.hl, g.wl, 1, g.ci),
        kernel_entry.shape,
        operands[3].shape,
        operands[4].shape,
        operands[5].shape,
    ] + [(6, g.cc)] * 4
    out = pl.pallas_call(
        write,
        out_shape=[jax.ShapeDtypeStruct(shape, F32) for shape in results],
        in_specs=[vmem] * len(shapes),
        out_specs=[vmem] * 10,
        compiler_params=pltpu.CompilerParams(vmem_limit_bytes=62 << 20),
    )(*parts)
    out = list(out)
    out[0] = jnp.transpose(out[0], (2, 0, 1, 3))
    out[1] = jnp.transpose(out[1], (2, 0, 1, 3))
    out[3] = jnp.transpose(out[3], (2, 0, 1, 3))
    out[4] = jnp.transpose(out[4], (1, 0, 2))
    out[5] = jnp.transpose(out[5], (1, 0, 2))
    return tuple(out)


def solution(mesh):
    mesh_shape = dict(mesh.shape)
    wide = P("sp", None, None, "ch")
    row = P(None, "ch")
    mid = P(None, "ch", None)
    return jax.shard_map(
        lambda *args: body(mesh_shape, *args),
        mesh=mesh,
        in_specs=(wide, wide, P(None, None, "ch"), P(None, None, None, "ch"), mid, mid,
                  row, row, row, row),
        out_specs=(wide, wide, P(None, None, "ch"), P(None, None, None, "ch"), mid, mid,
                   row, row, row, row),
        check_vma=False,
    )
```

```python
import math
import types

import jax
import jax.numpy as jnp
from jax import lax
from jax.experimental import pallas as pl
from jax.experimental.pallas import tpu as pltpu
from jax.sharding import PartitionSpec as P

MESH = pl.DeviceIdType.MESH
EPSILON = 0.001
MOMENTUM = 0.5
LANE = 128
HALF = 64
F32 = jnp.float32
BF16 = jnp.bfloat16


def round_up(value, step):
    return -(-value // step) * step


UN_S, UN_L, UN_ES, UN_EC, UN_SR, UN_IR, UN_EK, UN_W = 12, 10, 4, 4, 4, 4, 4, 4


def aligned(index, step):
    return index if isinstance(index, int) else pl.multiple_of(index, step)


def repeat(count, one, carry, unroll=4):
    def some(k, carry):
        for j in range(unroll):
            carry = one(k * unroll + j, carry)
        return carry

    whole = count // unroll if count > unroll else 0
    if whole:
        carry = lax.fori_loop(0, whole, some, carry)
    for k in range(whole * unroll, count):
        carry = one(k, carry)
    return carry


def sigmoid(values):
    return 0.5 * jnp.tanh(0.5 * values) + 0.5


def dot(left, right, dims=(1, 0), precision=None):
    return lax.dot_general(
        left,
        right,
        (((dims[0],), (dims[1],)), ((), ())),
        precision=precision,
        preferred_element_type=F32,
    )


def fold(value):
    return jnp.sum(value.reshape(value.shape[0] // 8, 8, value.shape[1]), axis=0)


def geometry(mesh_shape, inputs, cotangent, project_entry, projects):
    geo = types.SimpleNamespace()
    geo.n_sp, geo.n_ch = mesh_shape["sp"], mesh_shape["ch"]
    geo.bands = geo.n_ch // 2
    geo.group = geo.n_sp * geo.bands
    _, geo.hl, geo.wl, geo.ci = inputs.shape
    _, geo.hs, geo.ws, geo.cc = cotangent.shape
    geo.cin, geo.chan = project_entry.shape[2], projects.shape[2]
    geo.wide = round_up(geo.chan, 2 * LANE)
    geo.half = geo.wide // 2
    geo.shard = geo.wide // geo.n_ch
    geo.tiles = geo.half // LANE
    geo.pl_, geo.ps = round_up(geo.wl + 1, 8), round_up(geo.ws + 1, 8)
    geo.bs = 2 * math.ceil(geo.hs / (2 * geo.bands))
    geo.bl = 2 * geo.bs
    geo.rs, geo.rl = geo.bs + 2, geo.bl + 2
    geo.na = 2 * math.ceil(geo.rl / 4)
    geo.nb = geo.rl - geo.na
    geo.ka = geo.na * geo.pl_
    geo.kb = geo.nb * geo.pl_
    geo.full = geo.n_ch * LANE
    geo.ny = geo.bands if geo.n_sp % geo.bands == 0 else 1
    geo.nz = geo.n_sp // geo.ny
    geo.tall = geo.shard // 16
    geo.u_mid = geo.tall * (geo.wide // LANE)
    geo.u_dk = round_up(geo.shard, LANE) // LANE
    geo.u_in = geo.tall * (geo.cin // LANE)
    geo.units = [
        round_up(u, geo.n_sp)
        for u in [geo.u_mid] * 3 + [geo.u_mid // 2] * 2 + [geo.u_in + 4 * geo.u_dk, geo.u_in]
    ]
    geo.plane = geo.bands * geo.ny
    geo.count_large = float(geo.n_sp * geo.hl * geo.wl)
    geo.count_small = float(geo.n_sp * geo.hs * geo.ws)
    return geo


IN_NAMES = [
    "inputs",
    "cotangent",
    "kernel_entry",
    "kernels",
    "project_entry",
    "projects",
    "bn_gains",
    "bn_biases",
    "run_means",
    "run_vars",
]
OUT_NAMES = [
    "m_out",
    "m_gin",
    "m_dke",
    "m_dk",
    "m_dwe",
    "m_dw",
    "m_vec",
]


def scratch_table(g):
    dma, vm = pltpu.SemaphoreType.DMA, pltpu.VMEM
    small, large = g.rs * g.ps, g.rl * g.pl_
    cp_rows = (g.bands * g.bl + 2) * g.pl_
    x = g.bands
    table = dict(
        x32=vm((cp_rows, LANE), F32),
        a1=vm((cp_rows + 2 * g.pl_, LANE), F32),
        s1=vm((cp_rows, LANE), F32),
        s1pk=vm((x, g.ka, LANE), BF16),
        s1full=vm((g.ka, g.full), BF16),
        sidepk=vm((x, small, LANE), BF16),
        sidefull=vm((small, g.full), BF16),
        sidecp=vm(((x * g.bs + 2) * g.ps, LANE), F32),
        parloc=vm((56, 2 * LANE), F32),
        parx=vm((x, 56, 2 * LANE), F32),
        par=vm((56, g.half), F32),
        place=vm((g.wide, g.wide), BF16),
        place_in=vm((2, g.cin, g.full), BF16),
        wpad=vm((g.shard, g.wide), BF16),
        w=vm((4, g.half, g.wide), BF16),
        we=vm((2, g.half, g.cin), BF16),
        wp=vm((3, g.half, g.full), BF16),
        cotpad=vm(((x * g.bs + 2) * g.ps, 2 * LANE), F32),
        cotx=vm(((x * g.bs + 2) * g.ps, 2 * LANE), BF16),
        cots=vm((x, small, 2 * LANE), BF16),
        picks=vm((x, 2 * LANE, g.half), F32),
        edge_up=vm((2 * g.pl_, g.half), BF16),
        edge_down=vm((4 * g.pl_, g.half), BF16),
        from_below=vm((2 * g.pl_, g.half), BF16),
        from_above=vm((4 * g.pl_, g.half), BF16),
        cot=vm((small, g.half), F32),
        p1=vm((large, g.half), F32),
        a2=vm((large, g.half), F32),
        s2=vm((g.bl * g.pl_, g.wide), BF16),
        p2=vm((large + 3 * g.pl_, g.half), F32),
        tmp=vm((g.tiles, 48, LANE), F32),
        poolraw=vm((small, g.half), F32),
        pside=vm((small, g.half), F32),
        hid=vm((3, small, g.half), F32),
        act=vm((3, small, g.half), F32),
        sm=vm((3, g.bs * g.ps, g.wide), BF16),
        pm=vm((3, small, g.half), F32),
        gb=vm((3, small, g.half), F32),
        gt=vm((3, small, g.half), F32),
        gs=vm((small, g.half), F32),
        rsend=vm((3, small, g.half), BF16),
        rrecv=vm((3, small, g.half), BF16),
        gside=vm((small, g.half), BF16),
        gt2=vm((large, g.half), F32),
        rsend2=vm((large, g.half), BF16),
        rrecv2=vm((large, g.half), BF16),
        gs2=vm((large, g.half), F32),
        gb1=vm((large, g.half), F32),
        g1=vm((large, g.half), BF16),
        essend=vm((g.ka, x * LANE), BF16),
        esrecv=vm((g.ka, x * LANE), BF16),
        essum=vm((x, g.ka, LANE), BF16),
        esr=vm((x, g.ka, LANE), BF16),
        sdsend=vm((small, x * LANE), BF16),
        sdrecv=vm((small, x * LANE), BF16),
        sdsum=vm((x, small, LANE), BF16),
        sdr=vm((x, small, LANE), BF16),
        gs1=vm((cp_rows, LANE), F32),
        outx=vm((x, g.bs * g.ps, 2 * LANE), BF16),
        outs=vm((x, g.bs * g.ps, 2 * LANE), BF16),
        dk=vm((4, 16, g.half), F32),
        pickb=vm((x, g.half, 2 * LANE), BF16),
        dke=vm((g.n_sp, 16, LANE), F32),
        vec=vm((56, g.half), F32),
        ar2=vm((5, g.group, 2, g.half), F32),
        ar4=vm((4, g.group, 4, g.half), F32),
        ar_ss=dma((9,)),
        ar_rs=dma((9,)),
        s1_ss=dma((2 * g.n_ch,)),
        s1_rs=dma((g.n_ch,)),
        sd_ss=dma((2 * g.n_ch,)),
        sd_rs=dma((g.n_ch,)),
        par_ss=dma((x,)),
        par_rs=dma((x,)),
        we_ss=dma((2, x)),
        we_rs=dma((2, x)),
        w_ss=dma((4, 2 * x)),
        w_rs=dma((4, 2 * x)),
        cot_ss=dma((x,)),
        cot_rs=dma((x,)),
        sm_ss=dma((4,)),
        sm_rs=dma((4,)),
        r_ss=dma((4,)),
        r_rs=dma((4,)),
        halo_ss=dma((7, 2)),
        halo_rs=dma((7, 2)),
        es_ss=dma((2,)),
        es_rs=dma((2,)),
        esx_ss=dma((2, x)),
        esx_rs=dma((2, x)),
        out_ss=dma((x,)),
        out_rs=dma((x,)),
        ra_ss=dma((7, g.plane)),
        ra_rs=dma((7, g.plane)),
        rz_ss=dma((7, g.nz)),
        rz_rs=dma((7, g.nz)),
        gz_ss=dma((5, g.nz)),
        gz_rs=dma((5, g.nz)),
        gy_ss=dma((5, g.ny)),
        gy_rs=dma((5, g.ny)),
        ga_ss=dma((2,)),
        ga_rs=dma((2,)),
        dke_ss=dma((1,)),
        dke_rs=dma((1,)),
    )
    for k, u in enumerate(g.units):
        unit = (16, LANE)
        table.update({
            f"part{k}": vm((x, u) + unit, BF16),
            f"plane{k}": vm((g.plane, u // g.ny) + unit, BF16),
            f"ys{k}": vm((u // g.ny,) + unit, BF16),
            f"rzr{k}": vm((g.nz, u // g.n_sp) + unit, BF16),
            f"fin{k}": vm((u,) + unit, BF16),
        })
    return table


def make_kernel(g, scratch_names):
    n_bands, half, shard, tiles = g.bands, g.half, g.shard, g.tiles
    pitch, pitch_s = g.pl_, g.ps
    small, large = g.rs * g.ps, g.rl * g.pl_
    AVG, VAR, T1, T0, INV, ALPHA, BETA, KAPPA, LAM = (6 * k for k in range(9))
    counts = (g.count_large, g.count_large) + (g.count_small,) * 4

    def kernel(*refs):
        r = types.SimpleNamespace(**dict(zip(IN_NAMES + OUT_NAMES + scratch_names, refs)))
        s = lax.axis_index("sp")
        ch = lax.axis_index("ch")
        x = ch // 2
        c = lax.rem(ch, 2)
        me = s * n_bands + x
        yi, zi = lax.rem(s, g.ny), s // g.ny
        sends = []

        def copy_to(src, dst, send, recv, s_, x_, c_):
            cp = pltpu.make_async_remote_copy(
                src_ref=src,
                dst_ref=dst,
                send_sem=send,
                recv_sem=recv,
                device_id=(s_, x_ * 2 + c_),
                device_id_type=MESH,
            )
            cp.start()
            sends.append(cp.wait_send)

        def landed(ref, sem):
            pltpu.make_async_copy(ref, ref, sem).wait()

        def other_band(k):
            return lax.rem(x + k, n_bands)

        def edge_copy(src_up, dst_up, src_down, dst_down, e):
            up = pltpu.make_async_remote_copy(
                src_up, dst_up, r.halo_ss.at[e, 0], r.halo_rs.at[e, 0],
                device_id=(s, (x - 1) * 2 + c), device_id_type=MESH)
            down = pltpu.make_async_remote_copy(
                src_down, dst_down, r.halo_ss.at[e, 1], r.halo_rs.at[e, 1],
                device_id=(s, (x + 1) * 2 + c), device_id_type=MESH)

            @pl.when(x > 0)
            def _():
                up.start()

            @pl.when(x < n_bands - 1)
            def _():
                down.start()

            def finish():
                @pl.when(x < n_bands - 1)
                def _():
                    landed(dst_up, r.halo_rs.at[e, 0])

                @pl.when(x > 0)
                def _():
                    landed(dst_down, r.halo_rs.at[e, 1])

            def sent():
                @pl.when(x > 0)
                def _():
                    up.wait_send()

                @pl.when(x < n_bands - 1)
                def _():
                    down.wait_send()

            sends.append(sent)
            return finish

        def edges(ref, e):
            first, last = pl.ds(pitch_s, pitch_s), pl.ds(g.bs * pitch_s, pitch_s)
            return edge_copy(
                ref.at[first], ref.at[pl.ds((g.bs + 1) * pitch_s, pitch_s)],
                ref.at[last], ref.at[pl.ds(0, pitch_s)], e)

        def flipped(value, key):
            out, bit = 0, 1
            while bit <= key:
                here = lax.rem(value // bit, 2)
                out = out + bit * (1 - here if key & bit else here)
                bit *= 2
            return out + (value // bit) * bit

        def hops(key):
            return key // (n_bands * g.ny) + key // n_bands % g.ny + key % n_bands

        few = g.group <= 16
        keys = sorted(range(1, g.group), key=hops, reverse=True) if few else []
        peers = [
            (flipped(s, key // n_bands), flipped(x, key % n_bands)) for key in keys
        ]

        def to_group(src, dst, send, recv, pick=None):
            def one(s_, x_):
                pltpu.make_async_remote_copy(
                    src if pick is None else pick(s_, x_), dst, send, recv,
                    device_id=(s_, x_ * 2 + c), device_id_type=MESH).start()

            for s_, x_ in peers:
                one(s_, x_)

            def loop(k, _):
                to = lax.rem(me + k, g.group)
                one(to // n_bands, lax.rem(to, n_bands))
                return 0

            if not few:
                lax.fori_loop(1, g.group, loop, 0)

        sp_keys = sorted(range(1, g.n_sp), key=lambda k: hops(k * n_bands), reverse=True)
        sp_peers = [flipped(s, key) for key in sp_keys] if few else []

        def to_images(src, dst, send, recv):
            def one(s_):
                pltpu.make_async_remote_copy(
                    src, dst, send, recv, device_id=(s_, ch), device_id_type=MESH).start()

            for s_ in sp_peers:
                one(s_)

            def loop(k, _):
                one(lax.rem(s + k, g.n_sp))
                return 0

            if not few:
                lax.fori_loop(1, g.n_sp, loop, 0)

        def sum_start(buf, at, e, rows):
            for k, row in enumerate(rows):
                buf[at, me, k : k + 1, :] = row

            to_group(buf.at[at, me], buf.at[at, me], r.ar_ss.at[e], r.ar_rs.at[e])

        def sum_finish(buf, at, e):
            block = buf.at[at, pl.ds(0, g.group - 1)]
            landed(block, r.ar_rs.at[e])
            sends.append(lambda: landed(block, r.ar_ss.at[e]))
            total = buf[at, 0]
            for k in range(1, g.group):
                total = total + buf[at, k]
            return total

        def fill(ref, start, rows):
            ref[pl.ds(start, rows)] = jnp.zeros((rows,) + ref.shape[1:], ref.dtype)

        def fill_all(ref, step):
            def one(i, _):
                ref[pl.ds(aligned(i * step, 8), step)] = jnp.zeros(
                    (step,) + ref.shape[1:], ref.dtype)
                return 0

            repeat(ref.shape[0] // step, one, 0, 1)

        def lane(t):
            return pl.ds(t * LANE, LANE)

        def col_mask(width, breadth):
            at = lax.broadcasted_iota(jnp.int32, (width, LANE), 0)
            return jnp.where(at < breadth, 1.0, 0.0).astype(F32)

        def row_ok(row, height):
            return jnp.where((row >= 0) & (row < height), 1.0, 0.0).astype(F32)

        mask_l, mask_s = col_mask(pitch, g.wl), col_mask(pitch_s, g.ws)

        def vrow(kind, layer, t):
            return r.vec[kind + layer : kind + layer + 1, lane(t)]

        def taps_of(q, t):
            return [
                [r.par[16 + 4 * (3 * u + v) + q : 17 + 4 * (3 * u + v) + q, lane(t)] for v in range(3)]
                for u in range(3)
            ]

        def flip(taps):
            return [[taps[2 - u][2 - v] for v in range(3)] for u in range(3)]

        def conv_row(rows, taps):
            width = rows[0].shape[0]
            side = [
                rows[0] * taps[0][v] + rows[1] * taps[1][v] + rows[2] * taps[2][v]
                for v in range(3)
            ]
            return side[1] + pltpu.roll(side[0], 1, 0) + pltpu.roll(side[2], width - 1, 0)

        def store_moments(layer, total, square):
            n = counts[layer]
            average = total / n
            variance = square / n - average * average
            inverse = lax.rsqrt(variance + EPSILON)
            alpha = inverse * r.par[layer : layer + 1, :]
            r.vec[AVG + layer : AVG + layer + 1, :] = average
            r.vec[VAR + layer : VAR + layer + 1, :] = variance
            r.vec[INV + layer : INV + layer + 1, :] = inverse
            r.vec[ALPHA + layer : ALPHA + layer + 1, :] = alpha
            r.vec[BETA + layer : BETA + layer + 1, :] = (
                r.par[6 + layer : 7 + layer, :] - average * alpha)

        def store_back(layer, total, product):
            n = counts[layer]
            average = r.vec[AVG + layer : AVG + layer + 1, :]
            inverse = r.vec[INV + layer : INV + layer + 1, :]
            alpha = r.vec[ALPHA + layer : ALPHA + layer + 1, :]
            scaled = inverse * (product - average * total)
            r.vec[T0 + layer : T0 + layer + 1, :] = total
            r.vec[T1 + layer : T1 + layer + 1, :] = scaled
            kappa = -alpha * inverse * scaled / n
            r.vec[KAPPA + layer : KAPPA + layer + 1, :] = kappa
            r.vec[LAM + layer : LAM + layer + 1, :] = -alpha * total / n - kappa * average

        def rowsum(value):
            return jnp.sum(value, axis=0, keepdims=True)

        fill_all(r.x32, pitch)
        fill_all(r.a1, pitch)
        fill(r.s1, 0, pitch)
        fill(r.s1, (g.hl + 1) * pitch, (n_bands * g.bl + 1 - g.hl) * pitch)
        fill(r.parloc, 0, 56)
        fill_all(r.wpad, 16)
        fill(r.tmp, 0, tiles)
        fill(r.p2, 0, 3 * pitch)
        fill(r.p2, (g.bl + 3) * pitch, 2 * pitch)
        fill(r.gb1, 0, pitch)
        fill(r.gb1, (g.bl + 1) * pitch, pitch)
        fill(r.dk, 0, 4)
        for i in range(3):
            for ref in (r.pm, r.gb):
                ref[i, 0:pitch_s] = jnp.zeros((pitch_s, half), F32)
                ref[i, (g.bs + 1) * pitch_s : small] = jnp.zeros((pitch_s, half), F32)
        for k in range(g.n_sp):
            r.dke[k] = jnp.zeros((16, LANE), F32)

        barrier = pltpu.get_barrier_semaphore()

        def greet(k, _):
            to = lax.rem(me + k, g.group)
            pl.semaphore_signal(
                barrier, inc=1,
                device_id=(to // n_bands, lax.rem(to, n_bands) * 2 + c),
                device_id_type=MESH)
            return 0

        lax.fori_loop(1, g.group, greet, 0)
        pl.semaphore_signal(
            barrier, inc=1, device_id=(s, x * 2 + 1 - c), device_id_type=MESH)

        def entry_silu(row, _):
            value = r.inputs[0, row].astype(F32)
            r.x32[pl.ds(aligned((row + 1) * pitch, 8), g.wl), 0 : g.ci] = value
            r.a1[pl.ds(aligned((row + 2) * pitch, 8), g.wl), 0 : g.ci] = value * sigmoid(value)
            return 0

        repeat(g.hl, entry_silu, 0, UN_ES)
        r.parloc[0:6, 0 : g.cc] = r.bn_gains[...]
        r.parloc[6:12, 0 : g.cc] = r.bn_biases[...]
        for j in range(9):
            at = 16 + 4 * j
            r.parloc[at : at + 4, 0 : g.cc] = r.kernels[j // 3, j % 3].astype(F32)
        taps_in = [
            [r.kernel_entry[u].astype(F32)[v : v + 1, :] for v in range(3)] for u in range(3)
        ]
        pad_in = jnp.zeros((1, LANE - g.ci), F32)
        taps_in = [[jnp.concatenate([k, pad_in], axis=1) for k in row] for row in taps_in]

        def entry_conv(row, _):
            rows = [
                r.a1[pl.ds(aligned((row + 1 + u) * pitch, 8), pitch), :] for u in range(3)
            ]
            r.s1[pl.ds(aligned((row + 1) * pitch, 8), pitch), :] = (
                conv_row(rows, taps_in) * mask_l)
            return 0

        repeat(g.hl, entry_conv, 0, UN_EC)
        for b in range(n_bands):
            for k in range(g.na // 2):
                packed = r.s1[(b * g.bl + 2 * k) * pitch : (b * g.bl + 2 * k + 2) * pitch, :]
                if 2 * k < g.nb:
                    at = (b * g.bl + g.na + 2 * k) * pitch
                    packed = packed + pltpu.roll(r.s1[at : at + 2 * pitch, :], HALF, 1)
                r.s1pk[b, 2 * k * pitch : (2 * k + 2) * pitch, :] = packed.astype(BF16)
        for e in range(2):
            r.wpad[0 : g.cc, 0 : g.cin] = r.project_entry[:, e, :]
            r.we[e, pl.ds(aligned(x * shard, 16), shard), :] = r.wpad[:, 0 : g.cin]

        pl.semaphore_wait(barrier, g.group)
        tile = c * n_bands + x

        def full_lanes(t):
            return pl.ds(aligned(t * LANE, LANE), LANE)

        for k in range(1, n_bands):
            b = other_band(k)
            copy_to(r.s1pk.at[b], r.s1full.at[:, full_lanes(tile)],
                    r.s1_ss.at[k], r.s1_rs.at[tile], s, b, c)
        copy_to(r.s1pk.at[x], r.s1full.at[:, full_lanes(tile)],
                r.s1_ss.at[0], r.s1_rs.at[tile], s, x, 1 - c)
        r.s1full[:, full_lanes(tile)] = r.s1pk[x]
        for k in range(1, n_bands):
            mine = r.we.at[0, pl.ds(aligned(x * shard, 16), shard)]
            copy_to(mine, mine, r.we_ss.at[0, k], r.we_rs.at[0, x], s, other_band(k), c)

        for b in range(n_bands):
            spot = lax.broadcasted_iota(jnp.int32, (2 * LANE, half), 1) - b * shard
            r.picks[b] = jnp.where(
                (spot == lax.broadcasted_iota(jnp.int32, (2 * LANE, half), 0)) & (spot < g.cc),
                1.0, 0.0).astype(F32)
        r.parx[x] = r.parloc[...]

        def send_vectors():
            for k in range(1, n_bands):
                copy_to(r.parx.at[x], r.parx.at[x], r.par_ss.at[k], r.par_rs.at[x],
                        s, other_band(k), c)

        def vectors_landed():
            total = 0.0
            for k in range(1, n_bands):
                b = other_band(k)
                landed(r.parx.at[b], r.par_rs.at[b])
            for b in range(n_bands):
                total = total + dot(r.parx[b], r.picks[b], precision=lax.Precision.HIGHEST)
            r.par[...] = total

        r.sidecp[...] = jnp.zeros_like(r.sidecp)

        def side_row(row, _):
            at = aligned((2 * row + 1) * pitch, 8)
            r.sidecp[pl.ds(aligned((row + 1) * pitch_s, 8), g.ws), :] = r.x32[
                pl.ds(at, g.ws, stride=2), :]
            return 0

        repeat(g.hs, side_row, 0, UN_SR)
        for b in range(n_bands):
            r.sidepk[b] = r.sidecp[b * g.bs * pitch_s : b * g.bs * pitch_s + small, :].astype(BF16)
        r.sidefull[:, full_lanes(tile)] = r.sidepk[x]

        def send_side():
            for k in range(1, n_bands):
                b = other_band(k)
                copy_to(r.sidepk.at[b], r.sidefull.at[:, full_lanes(tile)],
                        r.sd_ss.at[k], r.sd_rs.at[tile], s, b, c)
            copy_to(r.sidepk.at[x], r.sidefull.at[:, full_lanes(tile)],
                    r.sd_ss.at[0], r.sd_rs.at[tile], s, x, 1 - c)
            for k in range(1, n_bands):
                mine = r.we.at[1, pl.ds(aligned(x * shard, 16), shard)]
                copy_to(mine, mine, r.we_ss.at[1, k], r.we_rs.at[1, x], s, other_band(k), c)

        fill_all(r.cotpad, pitch_s)

        def cot_row(row, _):
            r.cotpad[pl.ds(aligned((row + 1) * pitch_s, 8), g.ws), 0 : g.cc] = (
                r.cotangent[0, row].astype(F32))
            return 0

        repeat(g.hs, cot_row, 0, UN_SR)
        r.cotx[...] = r.cotpad[...].astype(BF16)
        r.cots[x] = r.cotx[pl.ds(aligned(x * g.bs * pitch_s, 16), small), :]

        def send_cotangent():
            for k in range(1, n_bands):
                b = other_band(k)
                copy_to(r.cotx.at[pl.ds(aligned(b * g.bs * pitch_s, 16), small)], r.cots.at[x],
                        r.cot_ss.at[k], r.cot_rs.at[x], s, b, c)

        def channel_place(rows, k0, cols, cut, offset):
            k_at = k0 + lax.broadcasted_iota(jnp.int32, (rows, cols), 0)
            p_at = lax.broadcasted_iota(jnp.int32, (rows, cols), 1)
            want = k_at + offset(0)
            for j in range(1, g.n_ch):
                jump = offset(j) - offset(j - 1)
                want = want + jnp.where(k_at >= j * cut, jump, 0)
            return jnp.where(want == p_at, 1.0, 0.0).astype(BF16)

        def offset_wide(j):
            return (j % 2) * half + (j // 2) * shard - j * g.cc

        def offset_in(j):
            return ((j % 2) * n_bands + j // 2) * LANE - j * g.ci

        r.place_in[0] = channel_place(g.cin, 0, g.full, g.ci, offset_in)
        r.place_in[1] = channel_place(
            g.cin, 0, g.full, g.ci, lambda j: offset_in(j) + HALF)
        def place_rows(k, _):
            at = aligned(k * 64, 64)
            r.place[pl.ds(at, 64), :] = channel_place(64, at, g.wide, g.cc, offset_wide)
            return 0

        repeat(g.wide // 64, place_rows, 0, 2)
        fill_all(r.wpad, 16)

        def weight_prepare(q):
            r.wpad[0 : g.cc, 0 : g.chan] = r.projects[:, q, :]
            r.w[q, pl.ds(aligned(x * shard, 16), shard), :] = dot(
                r.wpad[...], r.place[...]).astype(BF16)

        odd = lax.rem(yi, 2) if g.ny > 1 else 0
        pair = zi * g.ny + yi + 1 - 2 * odd
        halves = 2 if g.ny > 1 else 1

        def shard_part(q, b, part):
            size = shard // halves
            return r.w.at[q, pl.ds(aligned(b * shard + part * size, 16), size)]

        def weight_send(q):
            mine = shard_part(q, x, odd)
            for k in range(1, n_bands):
                copy_to(mine, mine, r.w_ss.at[q, k], r.w_rs.at[q, x], s, other_band(k), c)

        def weight_forward(q):
            for k in range(1, n_bands):
                b = other_band(k)
                got = shard_part(q, b, odd)
                landed(got, r.w_rs.at[q, b])
                if halves > 1:
                    copy_to(got, got, r.w_ss.at[q, n_bands + k], r.w_rs.at[q, n_bands + b],
                            pair, x, c)

        def weight_landed(q):
            for k in range(1, n_bands):
                b = other_band(k)
                if halves > 1:
                    landed(shard_part(q, b, 1 - odd), r.w_rs.at[q, n_bands + b])

        weight_prepare(0)
        weight_send(0)
        weight_prepare(1)
        weight_prepare(2)

        for k in range(1, n_bands):
            t = c * n_bands + other_band(k)
            landed(r.s1full.at[:, full_lanes(t)], r.s1_rs.at[t])
            copy_to(r.s1full.at[:, full_lanes(t)], r.s1full.at[:, full_lanes(t)],
                    r.s1_ss.at[g.n_ch + k], r.s1_rs.at[t], s, x, 1 - c)

        for k in range(1, n_bands):
            b = other_band(k)
            landed(r.we.at[0, pl.ds(aligned(b * shard, 16), shard)], r.we_rs.at[0, b])
        for a in range(2):
            r.wp[a] = dot(r.we[0], r.place_in[a]).astype(BF16)

        for k in range(n_bands):
            t = (1 - c) * n_bands + k
            landed(r.s1full.at[:, full_lanes(t)], r.s1_rs.at[t])
        r.p1[0 : g.ka, :] = dot(r.s1full[...], r.wp[0], (1, 1))
        r.p1[g.ka : large, :] = dot(r.s1full[0 : g.kb, :], r.wp[1], (1, 1))

        def moments(ref, first, rows, width):
            out = [[], []]
            for t in range(tiles):
                def one(k, carry):
                    v = ref[pl.ds(aligned((first + k) * width, 8), width), lane(t)]
                    return (carry[0] + fold(v), carry[1] + fold(v * v))

                zero = jnp.zeros((8, LANE), F32)
                total, square = repeat(rows, one, (zero, zero), UN_S if width == pitch_s else UN_L)
                out[0].append(rowsum(total))
                out[1].append(rowsum(square))
            return [jnp.concatenate(o, axis=1) for o in out]

        sum_start(r.ar2, 0, 0, moments(r.p1, 1, g.bl, pitch))
        send_vectors()
        send_side()
        weight_send(1)
        weight_send(2)
        weight_prepare(3)
        weight_forward(0)
        vectors_landed()
        total = sum_finish(r.ar2, 0, 0)
        store_moments(0, total[0:1], total[1:2])

        for t in range(tiles):
            alpha, beta = vrow(ALPHA, 0, t), vrow(BETA, 0, t)

            def one(k, _):
                at = pl.ds(aligned(k * pitch, 8), pitch)
                h = r.p1[at, lane(t)] * alpha + beta
                ok = mask_l * row_ok(x * g.bl + k - 1, g.hl)
                r.a2[at, lane(t)] = h * sigmoid(h) * ok
                return 0

            repeat(g.rl, one, 0, UN_L)
        mine_lanes = aligned(c * half, LANE)
        their_lanes = aligned((1 - c) * half, LANE)

        def own_tile(t):
            return pl.ds(aligned(c * half + t * LANE, LANE), LANE)

        def conv_pairs(source, q, target, row0, rows, height, width, mask):
            for t in range(tiles):
                taps = taps_of(q, t)

                def one(k, _):
                    block = [
                        source[pl.ds(aligned((2 * k + u) * width, 8), width), lane(t)]
                        for u in range(4)
                    ]
                    out = [
                        conv_row(block[j : j + 3], taps) * (mask * row_ok(row0 + 2 * k + j, height))
                        for j in range(2)
                    ]
                    target[pl.ds(aligned(k * 2 * width, 16), 2 * width), own_tile(t)] = (
                        jnp.concatenate(out, axis=0).astype(BF16))
                    return 0

                repeat(rows // 2, one, 0, UN_S if width == pitch_s else UN_L)

        conv_pairs(r.a2, 0, r.s2, x * g.bl, g.bl, g.hl, pitch, mask_l)

        def swap_start(ref, e):
            mine = ref.at[:, pl.ds(mine_lanes, half)]
            copy_to(mine, mine, r.sm_ss.at[e], r.sm_rs.at[e], s, x, 1 - c)

        def swap_landed(ref, e):
            landed(ref.at[:, pl.ds(their_lanes, half)], r.sm_rs.at[e])

        swap_start(r.s2, 0)
        weight_landed(0)
        rows_all = g.bl * pitch
        step = rows_all // 2
        for k in range(2):
            rows = pl.ds(k * step, step)
            r.p2[3 * pitch + k * step : 3 * pitch + (k + 1) * step, :] = dot(
                r.s2[rows, pl.ds(mine_lanes, half)], r.w[0, :, pl.ds(mine_lanes, half)], (1, 1))
        for k in range(1, n_bands):
            t = c * n_bands + other_band(k)
            landed(r.sidefull.at[:, full_lanes(t)], r.sd_rs.at[t])
            copy_to(r.sidefull.at[:, full_lanes(t)], r.sidefull.at[:, full_lanes(t)],
                    r.sd_ss.at[g.n_ch + k], r.sd_rs.at[t], s, x, 1 - c)
        swap_landed(r.s2, 0)
        for k in range(2):
            rows = pl.ds(k * step, step)
            at = slice(3 * pitch + k * step, 3 * pitch + (k + 1) * step)
            r.p2[at, :] = r.p2[at, :] + dot(
                r.s2[rows, pl.ds(their_lanes, half)], r.w[0, :, pl.ds(their_lanes, half)], (1, 1))
        for k in range(1, n_bands):
            b = other_band(k)
            landed(r.we.at[1, pl.ds(aligned(b * shard, 16), shard)], r.we_rs.at[1, b])
        r.wp[2] = dot(r.we[1], r.place_in[0]).astype(BF16)
        for k in range(n_bands):
            t = (1 - c) * n_bands + k
            landed(r.sidefull.at[:, full_lanes(t)], r.sd_rs.at[t])
        r.pside[...] = dot(r.sidefull[...], r.wp[2], (1, 1))
        sum_start(r.ar4, 0, 1,
                  moments(r.p2, 3, g.bl, pitch) + moments(r.pside, 1, g.bs, pitch_s))
        r.edge_up[...] = r.p2[3 * pitch : 5 * pitch, :].astype(BF16)
        r.edge_down[...] = r.p2[(g.bl - 1) * pitch : (g.bl + 3) * pitch, :].astype(BF16)
        edges_done = edge_copy(r.edge_up, r.from_below, r.edge_down, r.from_above, 0)
        weight_send(3)
        weight_forward(1)

        edges_done()

        @pl.when(x > 0)
        def _():
            r.p2[0 : 3 * pitch, :] = r.from_above[...].astype(F32)[pitch : 4 * pitch]

        @pl.when(x < n_bands - 1)
        def _():
            r.p2[(g.bl + 3) * pitch : (g.bl + 5) * pitch, :] = r.from_below[...].astype(F32)

        for t in range(tiles):
            def one(k, _):
                v = (r.p2[pl.ds(aligned(2 * k * pitch, 8), pitch), lane(t)]
                     + r.p2[pl.ds(aligned((2 * k + 1) * pitch, 8), pitch), lane(t)]
                     + r.p2[pl.ds(aligned((2 * k + 2) * pitch, 8), pitch), lane(t)])
                r.tmp[t, 0:pitch, :] = v + pltpu.roll(v, 1, 0) + pltpu.roll(v, pitch - 1, 0)
                r.poolraw[pl.ds(aligned(k * pitch_s, 8), pitch_s), lane(t)] = r.tmp[
                    t, pl.ds(0, pitch_s, stride=2), :]
                return 0

            repeat(g.rs, one, 0, UN_S)
        weight_forward(2)
        total = sum_finish(r.ar4, 0, 1)
        store_moments(1, total[0:1], total[1:2])
        store_moments(2, total[2:3], total[3:4])

        at_col = lax.broadcasted_iota(jnp.int32, (pitch_s, LANE), 0)
        col_count = mask_s * (
            1.0
            + jnp.where(at_col > 0, 1.0, 0.0)
            + jnp.where(2 * at_col + 1 < g.wl, 1.0, 0.0)) * (1.0 / 9.0)

        def window_count(row):
            inside = jnp.where(row > 0, 1.0, 0.0) + jnp.where(2 * row + 1 < g.hl, 1.0, 0.0) + 1.0
            return col_count * (inside.astype(F32) * row_ok(row, g.hs))

        for t in range(tiles):
            alpha, beta = vrow(ALPHA, 1, t) * (1.0 / 9.0), vrow(BETA, 1, t)
            alpha_2, beta_2 = vrow(ALPHA, 2, t), vrow(BETA, 2, t)

            def one(k, _):
                at = pl.ds(aligned(k * pitch_s, 8), pitch_s)
                row = x * g.bs + k - 1
                ok = mask_s * row_ok(row, g.hs)
                h = (r.poolraw[at, lane(t)] * alpha + window_count(row) * beta
                     + r.pside[at, lane(t)] * alpha_2 + beta_2) * ok
                r.hid[0, at, lane(t)] = h
                r.act[0, at, lane(t)] = h * sigmoid(h)
                return 0

            repeat(g.rs, one, 0, UN_S)

        def make_picks():
            for b in range(n_bands):
                spot_b = lax.broadcasted_iota(jnp.int32, (half, 2 * LANE), 0) - b * shard
                r.pickb[b] = jnp.where(
                    (spot_b == lax.broadcasted_iota(jnp.int32, (half, 2 * LANE), 1))
                    & (spot_b < g.cc), 1.0, 0.0).astype(BF16)

        own_rows = slice(pitch_s, (g.bs + 1) * pitch_s)
        for i in range(3):
            if i > 0:
                for t in range(tiles):
                    alpha, beta = vrow(ALPHA, 2 + i, t), vrow(BETA, 2 + i, t)

                    def one(k, _):
                        at = pl.ds(aligned(k * pitch_s, 8), pitch_s)
                        ok = mask_s * row_ok(x * g.bs + k - 1, g.hs)
                        h = (r.pm[i - 1, at, lane(t)] * alpha + beta) * ok
                        r.hid[i, at, lane(t)] = h
                        r.act[i, at, lane(t)] = h * sigmoid(h)
                        return 0

                    repeat(g.rs, one, 0, UN_S)
            conv_pairs(r.act.at[i], i + 1, r.sm.at[i], x * g.bs, g.bs, g.hs,
                       pitch_s, mask_s)
            swap_start(r.sm.at[i], 1 + i)
            weight_landed(1 + i)
            part = dot(r.sm[i, :, pl.ds(mine_lanes, half)],
                       r.w[1 + i, :, pl.ds(mine_lanes, half)], (1, 1))
            swap_landed(r.sm.at[i], 1 + i)
            r.pm[i, own_rows, :] = part + dot(
                r.sm[i, :, pl.ds(their_lanes, half)],
                r.w[1 + i, :, pl.ds(their_lanes, half)], (1, 1))
            if i < 2:
                sum_start(r.ar2, 1 + i, 2 + i, moments(r.pm.at[i], 1, g.bs, pitch_s))
                edges_done = edges(r.pm.at[i], 1 + i)
                if i == 0:
                    send_cotangent()
                    weight_forward(3)
                total = sum_finish(r.ar2, 1 + i, 2 + i)
                store_moments(3 + i, total[0:1], total[1:2])
                edges_done()

        def grad_sums(gref, pref, width, first, rows):
            out = [[], []]
            for t in range(tiles):
                def one(k, carry):
                    at = pl.ds(aligned((first + k) * width, 8), width)
                    v = gref[at, lane(t)]
                    return (carry[0] + fold(v), carry[1] + fold(v * pref[at, lane(t)]))

                zero = jnp.zeros((8, LANE), F32)
                a, b = repeat(rows, one, (zero, zero), UN_S if width == pitch_s else UN_L)
                out[0].append(rowsum(a))
                out[1].append(rowsum(b))
            return [jnp.concatenate(o, axis=1) for o in out]

        for k in range(1, n_bands):
            b = other_band(k)
            landed(r.cots.at[b], r.cot_rs.at[b])
        total = 0.0
        for b in range(n_bands):
            total = total + dot(r.cots[b], r.picks[b].astype(BF16))
        r.cot[...] = total
        sum_start(r.ar4, 1, 4,
                  moments(r.pm.at[2], 1, g.bs, pitch_s)
                  + grad_sums(r.cot, r.pm.at[2], pitch_s, 1, g.bs))
        edges_done = edges(r.pm.at[2], 3)
        make_picks()
        total = sum_finish(r.ar4, 1, 4)
        store_moments(5, total[0:1], total[1:2])
        store_back(5, total[2:3], total[3:4])
        edges_done()

        def norm_back(layer, gref, pref, target, rows, width, mask, row0, height):
            for t in range(tiles):
                alpha, kappa, lam = vrow(ALPHA, layer, t), vrow(KAPPA, layer, t), vrow(LAM, layer, t)

                def one(k, _):
                    at = pl.ds(aligned(k * width, 8), width)
                    ok = mask * row_ok(row0 + k, height)
                    target[at, lane(t)] = (
                        gref[at, lane(t)] * alpha + pref[at, lane(t)] * kappa + lam) * ok
                    return 0

                repeat(rows, one, 0, UN_S if width == pitch_s else UN_L)

        def kernel_grad(aref, gref, q, rows, width):
            for t in range(tiles):
                def one(k, carry):
                    gv = gref[pl.ds(aligned((k + 1) * width, 8), width), lane(t)]
                    turned = [pltpu.roll(gv, width - 1, 0), gv, pltpu.roll(gv, 1, 0)]
                    out = []
                    for u in range(3):
                        av = aref[pl.ds(aligned((k + u) * width, 8), width), lane(t)]
                        for v in range(3):
                            out.append(carry[3 * u + v] + fold(av * turned[v]))
                    return tuple(out)

                zero = jnp.zeros((8, LANE), F32)
                sums = repeat(rows, one, (zero,) * 9, UN_S if width == pitch_s else UN_L)
                for j in range(9):
                    r.dk[q, j : j + 1, lane(t)] = rowsum(sums[j])


        def block_of(name, k):
            return getattr(r, f"{name}{k}")

        def put_units(k, value, first, cols):
            value = value[:, first : first + cols].astype(BF16)
            for b in range(n_bands):
                for t in range(cols // LANE):
                    part = value[b * shard : (b + 1) * shard, t * LANE : (t + 1) * LANE]
                    block_of("part", k)[b, t * g.tall : (t + 1) * g.tall] = (
                        part.reshape(g.tall, 16, LANE))

        def put_kernels():
            for q in range(4):
                value = r.dk[q].astype(BF16)
                for b in range(n_bands):
                    part = dot(value, r.pickb[b]).astype(BF16)
                    for t in range(g.u_dk):
                        at = g.u_in + q * g.u_dk + t
                        r.part5[b, at] = part[:, t * LANE : (t + 1) * LANE]

        def plane_send(k):
            part = g.units[k] // g.ny
            me_plane = x * g.ny + yi
            for key in range(1, g.plane):
                to = lax.rem(me_plane + key, g.plane)
                x_, y_ = to // g.ny, lax.rem(to, g.ny)
                copy_to(block_of("part", k).at[x_, pl.ds(y_ * part, part)],
                        block_of("plane", k).at[me_plane],
                        r.ra_ss.at[k, key], r.ra_rs.at[k, me_plane], zi * g.ny + y_, x_, c)

        def plane_sum_z_send(k):
            part = g.units[k] // g.ny
            me_plane = x * g.ny + yi
            total = block_of("part", k)[x, pl.ds(yi * part, part)].astype(F32)
            for key in range(1, g.plane):
                b = lax.rem(me_plane + key, g.plane)
                landed(block_of("plane", k).at[b], r.ra_rs.at[k, b])
                total = total + block_of("plane", k)[b].astype(F32)
            block_of("ys", k)[...] = total.astype(BF16)
            piece = part // g.nz
            for j in range(1, g.nz):
                to = lax.rem(zi + j, g.nz)
                copy_to(block_of("ys", k).at[pl.ds(to * piece, piece)], block_of("rzr", k).at[zi],
                        r.rz_ss.at[k, j], r.rz_rs.at[k, zi], to * g.ny + yi, x, c)

        def z_sum(k):
            part = g.units[k] // g.ny
            piece = part // g.nz
            total = block_of("ys", k)[pl.ds(zi * piece, piece)].astype(F32)
            for j in range(1, g.nz):
                b = lax.rem(zi + j, g.nz)
                landed(block_of("rzr", k).at[b], r.rz_rs.at[k, b])
                total = total + block_of("rzr", k)[b].astype(F32)
            at = pl.ds(yi * part + zi * piece, piece)
            block_of("fin", k)[at] = total.astype(BF16)
            return at

        def z_gather(k):
            at = z_sum(k)
            for j in range(1, g.nz):
                to = lax.rem(zi + j, g.nz)
                copy_to(block_of("fin", k).at[at], block_of("fin", k).at[at],
                        r.gz_ss.at[k, j], r.gz_rs.at[k, zi], to * g.ny + yi, x, c)

        def all_gather(k):
            mine = block_of("fin", k).at[z_sum(k)]
            to_images(mine, mine, r.ga_ss.at[k - 5], r.ga_rs.at[k - 5])

        def y_gather(k):
            part = g.units[k] // g.ny
            piece = part // g.nz
            for j in range(1, g.nz):
                b = lax.rem(zi + j, g.nz)
                landed(block_of("fin", k).at[pl.ds(yi * part + b * piece, piece)],
                       r.gz_rs.at[k, b])
            at = pl.ds(yi * part, part)
            for j in range(1, g.ny):
                to = lax.rem(yi + j, g.ny)
                copy_to(block_of("fin", k).at[at], block_of("fin", k).at[at],
                        r.gy_ss.at[k, j], r.gy_rs.at[k, yi], zi * g.ny + to, x, c)

        def get_units(k, cols):
            tiles_in = [
                block_of("fin", k)[t * g.tall : (t + 1) * g.tall].reshape(shard, LANE)
                for t in range(cols // LANE)
            ]
            return jnp.concatenate(tiles_in, axis=1)

        def y_landed(k):
            part = g.units[k] // g.ny
            for j in range(1, g.ny):
                b = lax.rem(yi + j, g.ny)
                landed(block_of("fin", k).at[pl.ds(b * part, part)], r.gy_rs.at[k, b])

        def finish_block(k):
            y_landed(k)
            r.m_dw[3 - k] = dot(get_units(k, g.wide), r.place[...], (1, 1)).astype(BF16)

        def finish_halves():
            y_landed(3)
            y_landed(4)
            value = jnp.concatenate(
                [get_units(3, g.wide // 2), get_units(4, g.wide // 2)], axis=1)
            r.m_dw[0] = dot(value, r.place[...], (1, 1)).astype(BF16)

        def finish_entry(k):
            piece = g.units[k] // g.n_sp
            others = block_of("fin", k).at[pl.ds(0, (g.n_sp - 1) * piece)]
            landed(others, r.ga_rs.at[k - 5])
            sends.append(lambda: landed(others, r.ga_ss.at[k - 5]))
            r.m_dwe[6 - k] = get_units(k, g.cin)
            if k == 5:
                for q in range(4):
                    for t in range(g.u_dk):
                        r.m_dk[q, :, lane(t)] = r.fin5[g.u_in + q * g.u_dk + t].astype(F32)

        def output_landed():
            for k in range(1, n_bands):
                b = other_band(k)
                landed(r.outs.at[b], r.out_rs.at[b])
            for b in range(n_bands):
                r.m_out[b * g.bs * pitch_s : (b + 1) * g.bs * pitch_s, :] = r.outs[b].astype(F32)

        def send_output():
            for k in range(1, n_bands):
                b = other_band(k)
                copy_to(r.outx.at[b], r.outs.at[x], r.out_ss.at[k], r.out_rs.at[x], s, b, c)

        for i in (2, 1, 0):
            layer = 3 + i
            gref = r.cot if i == 2 else r.gb.at[i + 1]
            norm_back(layer, gref, r.pm.at[i], r.gt.at[i], g.rs, pitch_s, mask_s,
                      x * g.bs - 1, g.hs)
            grad = r.gt[i].astype(BF16)
            r.rsend[i] = dot(grad, r.w[1 + i, :, pl.ds(their_lanes, half)]).astype(BF16)
            copy_to(r.rsend.at[i], r.rrecv.at[i], r.r_ss.at[i], r.r_rs.at[i], s, x, 1 - c)
            part = dot(grad, r.w[1 + i, :, pl.ds(mine_lanes, half)])
            grad = r.gt[i, own_rows, :].astype(BF16)
            put_units(2 - i, dot(grad, r.sm[i], (0, 0)), 0, g.wide)
            landed(r.rrecv.at[i], r.r_rs.at[i])
            r.gs[...] = part + r.rrecv[i].astype(F32)
            rows = [[] for _ in range(4 if i == 0 else 2)]
            for t in range(tiles):
                taps = flip(taps_of(i + 1, t))

                def one(k, carry):
                    block = [
                        r.gs[pl.ds(aligned((k + u) * pitch_s, 8), pitch_s), lane(t)]
                        for u in range(3)
                    ]
                    at = pl.ds(aligned((k + 1) * pitch_s, 8), pitch_s)
                    row = x * g.bs + k
                    h = r.hid[i, at, lane(t)]
                    sig = sigmoid(h)
                    value = conv_row(block, taps) * (sig * (1.0 + h * (1.0 - sig))) * (
                        mask_s * row_ok(row, g.hs))
                    if i == 0:
                        value = value + r.cot[at, lane(t)]
                    r.gb[i, at, lane(t)] = value
                    if i == 0:
                        new = [
                            value, value * r.pside[at, lane(t)],
                            value * window_count(row),
                            value * r.poolraw[at, lane(t)] * (1.0 / 9.0)]
                    else:
                        new = [value, value * r.pm[i - 1, at, lane(t)]]
                    return tuple(a + fold(b) for a, b in zip(carry, new))

                zero = jnp.zeros((8, LANE), F32)
                sums = repeat(g.bs, one, (zero,) * len(rows), UN_S)
                for j, v in enumerate(sums):
                    rows[j].append(rowsum(v))
            rows = [jnp.concatenate(o, axis=1) for o in rows]
            buf, at_e, e = ((r.ar4, 2, 7), (r.ar2, 3, 6), (r.ar2, 4, 5))[i]
            sum_start(buf, at_e, e, rows)
            edges_done = edges(r.gb.at[i], 4 + i)
            plane_send(2 - i)
            if i < 2:
                plane_sum_z_send(1 - i)
            if i == 0:
                z_gather(0)
            kernel_grad(r.act.at[i], r.gs, i + 1, g.bs, pitch_s)
            if i == 2:
                value = []
                for t in range(tiles):
                    h = (r.pm[2, own_rows, lane(t)] * vrow(ALPHA, 5, t) + vrow(BETA, 5, t)
                         + r.hid[0, own_rows, lane(t)])
                    value.append(h.astype(BF16))
                value = jnp.concatenate(value, axis=1)
                for b in range(n_bands):
                    r.outx[b] = dot(value, r.pickb[b]).astype(BF16)
                r.outs[x] = r.outx[x]
            total = sum_finish(buf, at_e, e)
            if i > 0:
                store_back(layer - 1, total[0:1], total[1:2])
            else:
                store_back(2, total[0:1], total[1:2])
                store_back(1, total[2:3], total[3:4])
            edges_done()

        for t in range(tiles):
            alpha, kappa, lam = vrow(ALPHA, 1, t) * (1.0 / 9.0), vrow(KAPPA, 1, t), vrow(LAM, 1, t)

            def spread(v):
                r.tmp[t, pl.ds(0, pitch_s, stride=2), :] = v
                r.tmp[t, pl.ds(1, pitch_s, stride=2), :] = v + pltpu.roll(v, pitch_s - 1, 0)
                return r.tmp[t, 0:pitch, :]

            def one(k, _):
                low = r.gb[0, pl.ds(aligned(k * pitch_s, 8), pitch_s), lane(t)]
                high = r.gb[0, pl.ds(aligned((k + 1) * pitch_s, 8), pitch_s), lane(t)]
                for j, v in enumerate((low + high, high)):
                    row = x * g.bl + 2 * k + j - 1
                    ok = mask_l * row_ok(row, g.hl)
                    p = r.p2[pl.ds(aligned((2 * k + j + 2) * pitch, 8), pitch), lane(t)]
                    r.gt2[pl.ds(aligned((2 * k + j) * pitch, 8), pitch), lane(t)] = (
                        spread(v) * alpha + p * kappa + lam) * ok
                return 0

            repeat(g.bs + 1, one, 0, UN_S)
        for k in range(2):
            at = pl.ds(k * (large // 2), large // 2)
            r.rsend2[at, :] = dot(
                r.gt2[at, :].astype(BF16), r.w[0, :, pl.ds(their_lanes, half)]).astype(BF16)
        copy_to(r.rsend2, r.rrecv2, r.r_ss.at[3], r.r_rs.at[3], s, x, 1 - c)
        for k in range(2):
            at = pl.ds(k * (large // 2), large // 2)
            r.gs2[at, :] = dot(r.gt2[at, :].astype(BF16), r.w[0, :, pl.ds(mine_lanes, half)])
        grad = r.gt2[pitch : (g.bl + 1) * pitch, :].astype(BF16)
        hw = g.wide // 2
        put_units(3, dot(grad, r.s2[:, 0:hw], (0, 0)), 0, hw)
        plane_send(3)
        put_units(4, dot(grad, r.s2[:, hw:], (0, 0)), 0, hw)
        z_gather(1)
        y_gather(0)
        landed(r.rrecv2, r.r_rs.at[3])
        r.gs2[...] = r.gs2[...] + r.rrecv2[...].astype(F32)
        rows = [[], []]
        for t in range(tiles):
            taps = flip(taps_of(0, t))
            alpha, beta = vrow(ALPHA, 0, t), vrow(BETA, 0, t)

            def one(k, carry):
                block = [
                    r.gs2[pl.ds(aligned((k + u) * pitch, 8), pitch), lane(t)] for u in range(3)
                ]
                at = pl.ds(aligned((k + 1) * pitch, 8), pitch)
                p = r.p1[at, lane(t)]
                h = p * alpha + beta
                sig = sigmoid(h)
                value = conv_row(block, taps) * (sig * (1.0 + h * (1.0 - sig))) * (
                    mask_l * row_ok(x * g.bl + k, g.hl))
                r.gb1[at, lane(t)] = value
                return (carry[0] + fold(value), carry[1] + fold(value * p))

            zero = jnp.zeros((8, LANE), F32)
            sums = repeat(g.bl, one, (zero, zero), UN_L)
            for j, v in enumerate(sums):
                rows[j].append(rowsum(v))
        rows = [jnp.concatenate(o, axis=1) for o in rows]
        sum_start(r.ar4, 3, 8, rows)
        plane_send(4)
        plane_sum_z_send(2)

        def own_ok(k, width_rows):
            return jnp.where((k >= 1) & (k <= width_rows), 1.0, 0.0).astype(F32)

        for t in range(tiles):
            alpha, kappa, lam = vrow(ALPHA, 2, t), vrow(KAPPA, 2, t), vrow(LAM, 2, t)

            def one(k, _):
                out = []
                for j in range(2):
                    at = pl.ds(aligned((2 * k + j) * pitch_s, 8), pitch_s)
                    ok = mask_s * (row_ok(x * g.bs + 2 * k + j - 1, g.hs) * own_ok(2 * k + j, g.bs))
                    out.append((r.gb[0, at, lane(t)] * alpha
                                + r.pside[at, lane(t)] * kappa + lam) * ok)
                r.gside[pl.ds(aligned(2 * k * pitch_s, 16), 2 * pitch_s), lane(t)] = (
                    jnp.concatenate(out, axis=0).astype(BF16))
                return 0

            repeat(g.rs // 2, one, 0, UN_S)
        own_tiles = pl.ds(aligned(c * n_bands * LANE, LANE), n_bands * LANE)
        their_tiles = pl.ds(aligned((1 - c) * n_bands * LANE, LANE), n_bands * LANE)
        r.sdsend[...] = dot(r.gside[...], r.wp[2, :, their_tiles]).astype(BF16)
        copy_to(r.sdsend, r.sdrecv, r.es_ss.at[1], r.es_rs.at[1], s, x, 1 - c)
        part = dot(r.gside[...], r.wp[2, :, own_tiles])
        landed(r.sdrecv, r.es_rs.at[1])
        part = part + r.sdrecv[...].astype(F32)
        for b in range(n_bands):
            r.sdsum[b] = part[:, b * LANE : (b + 1) * LANE].astype(BF16)
        for k in range(1, n_bands):
            b = other_band(k)
            copy_to(r.sdsum.at[b], r.sdr.at[x], r.esx_ss.at[1, k], r.esx_rs.at[1, x], s, b, c)
        r.sdr[x] = r.sdsum[x]

        lane_at = lax.broadcasted_iota(jnp.int32, (half, g.full), 1)
        low_lanes = lax.rem(lane_at, LANE) < HALF
        both_place = r.place_in[0] + r.place_in[1]

        value = dot(r.gside[...], r.sidefull[...], (0, 0)).astype(BF16)
        put_units(5, dot(value, both_place, (1, 1)), 0, g.cin)
        kernel_grad(r.a2, r.gs2, 0, g.bl, pitch)
        put_kernels()
        plane_send(5)
        y_gather(1)
        plane_sum_z_send(3)
        total = sum_finish(r.ar4, 3, 8)
        store_back(0, total[0:1], total[1:2])

        for t in range(tiles):
            alpha, kappa, lam = vrow(ALPHA, 0, t), vrow(KAPPA, 0, t), vrow(LAM, 0, t)

            def one(k, _):
                out = []
                for j in range(2):
                    at = pl.ds(aligned((2 * k + j) * pitch, 8), pitch)
                    ok = mask_l * (row_ok(x * g.bl + 2 * k + j - 1, g.hl) * own_ok(2 * k + j, g.bl))
                    out.append((r.gb1[at, lane(t)] * alpha + r.p1[at, lane(t)] * kappa + lam) * ok)
                r.g1[pl.ds(aligned(2 * k * pitch, 16), 2 * pitch), lane(t)] = (
                    jnp.concatenate(out, axis=0).astype(BF16))
                return 0

            repeat(g.rl // 2, one, 0, UN_L)

        def entry_part(lanes):
            a = dot(r.g1[0 : g.ka, :], r.wp[0, :, lanes])
            b = dot(r.g1[g.ka : large, :], r.wp[1, :, lanes])
            if g.kb == g.ka:
                return a + b
            return jnp.concatenate([a[0 : g.kb] + b, a[g.kb :]], axis=0)

        r.essend[...] = entry_part(their_tiles).astype(BF16)
        copy_to(r.essend, r.esrecv, r.es_ss.at[0], r.es_rs.at[0], s, x, 1 - c)
        part = entry_part(own_tiles)
        grad_a = dot(r.g1[0 : g.ka, :], r.s1full[...], (0, 0))
        grad_b = dot(r.g1[g.ka : large, :], r.s1full[0 : g.kb, :], (0, 0))
        value = jnp.where(low_lanes, grad_a, grad_b).astype(BF16)
        put_units(6, dot(value, both_place, (1, 1)), 0, g.cin)
        landed(r.esrecv, r.es_rs.at[0])
        part = part + r.esrecv[...].astype(F32)
        for b in range(n_bands):
            r.essum[b] = part[:, b * LANE : (b + 1) * LANE].astype(BF16)
        for k in range(1, n_bands):
            b = other_band(k)
            copy_to(r.essum.at[b], r.esr.at[x], r.esx_ss.at[0, k], r.esx_rs.at[0, x], s, b, c)
        r.esr[x] = r.essum[x]
        plane_send(6)
        z_gather(2)
        plane_sum_z_send(4)
        z_gather(3)
        plane_sum_z_send(5)
        send_output()
        finish_block(0)
        finish_block(1)

        spot = lax.broadcasted_iota(jnp.int32, (half, 2 * LANE), 0) - x * shard
        pick_own = jnp.where(
            (spot == lax.broadcasted_iota(jnp.int32, (half, 2 * LANE), 1)) & (spot < g.cc),
            1.0, 0.0).astype(F32)
        final = dot(r.vec[0:24, :], pick_own, precision=lax.Precision.HIGHEST)
        final = final[:, 0 : g.cc]
        at_row = lax.broadcasted_iota(jnp.int32, (6, g.cc), 0)
        count = jnp.where(at_row < 2, g.count_large, g.count_small)
        bessel = count / (count - 1.0)
        final = jnp.concatenate([
            (1.0 - MOMENTUM) * r.run_means[...] + MOMENTUM * final[0:6],
            (1.0 - MOMENTUM) * r.run_vars[...] + MOMENTUM * (final[6:12] * bessel),
            final[12:24]], axis=0)
        r.m_vec[:, 0 : g.cc] = final

        for k in range(1, n_bands):
            b = other_band(k)
            landed(r.sdr.at[b], r.esx_rs.at[1, b])
        for b in range(n_bands):
            r.sidecp[b * g.bs * pitch_s : (b + 1) * g.bs * pitch_s, :] = (
                r.sdr[b].astype(F32)[pitch_s : (g.bs + 1) * pitch_s])
        for k in range(1, n_bands):
            b = other_band(k)
            landed(r.esr.at[b], r.esx_rs.at[0, b])
        fill(r.gs1, 0, pitch)
        fill(r.gs1, (n_bands * g.bl + 1) * pitch, pitch)
        for b in range(n_bands):
            for k in range(g.na // 2):
                value = r.esr[b, 2 * k * pitch : (2 * k + 2) * pitch, :].astype(F32)
                for j in range(2):
                    i = 2 * k + j
                    if 1 <= i <= g.bl:
                        at = (b * g.bl + i) * pitch
                        r.gs1[at : at + pitch, :] = value[j * pitch : (j + 1) * pitch]
                if 2 * k < g.nb:
                    value = pltpu.roll(value, HALF, 1)
                    for j in range(2):
                        i = g.na + 2 * k + j
                        if 1 <= i <= g.bl:
                            at = (b * g.bl + i) * pitch
                            r.gs1[at : at + pitch, :] = value[j * pitch : (j + 1) * pitch]
        taps = flip(taps_in)

        def in_grad(row):
            block = [r.gs1[pl.ds(aligned((row + u) * pitch, 8), pitch), :] for u in range(3)]
            h = r.x32[pl.ds(aligned((row + 1) * pitch, 8), pitch), :]
            sig = sigmoid(h)
            return conv_row(block, taps) * (sig * (1.0 + h * (1.0 - sig)))

        r.tmp[0] = jnp.zeros((48, LANE), F32)

        def in_rows(k, _):
            r.tmp[0, pl.ds(0, pitch_s, stride=2), :] = r.sidecp[
                pl.ds(aligned(k * pitch_s, 8), pitch_s), :]
            value = in_grad(2 * k) + r.tmp[0, 0:pitch, :]
            r.m_gin[pl.ds(aligned(2 * k * pitch, 8), pitch), :] = value

            r.m_gin[pl.ds(aligned((2 * k + 1) * pitch, 8), pitch), :] = in_grad(2 * k + 1)
            return 0

        repeat(g.hs, in_rows, 0, UN_IR)

        def entry_kernel(k, carry):
            gv = r.gs1[pl.ds(aligned((k + 1) * pitch, 8), pitch), :]
            turned = [pltpu.roll(gv, pitch - 1, 0), gv, pltpu.roll(gv, 1, 0)]
            out = []
            for u in range(3):
                av = r.a1[pl.ds(aligned((k + 1 + u) * pitch, 8), pitch), :]
                for v in range(3):
                    out.append(carry[3 * u + v] + fold(av * turned[v]))
            return tuple(out)

        zero = jnp.zeros((8, LANE), F32)
        sums = repeat(g.hl, entry_kernel, (zero,) * 9, UN_EK)
        for j in range(9):
            r.dke[s, j : j + 1, :] = rowsum(sums[j])

        to_images(r.dke.at[s], r.dke.at[s], r.dke_ss.at[0], r.dke_rs.at[0])

        y_gather(2)
        plane_sum_z_send(6)
        z_gather(4)
        y_gather(3)
        all_gather(5)
        finish_block(2)
        all_gather(6)
        y_gather(4)
        output_landed()
        finish_entry(5)
        finish_halves()
        finish_entry(6)

        block = r.dke.at[pl.ds(0, g.n_sp - 1)]
        landed(block, r.dke_rs.at[0])
        sends.append(lambda: landed(block, r.dke_ss.at[0]))
        total = r.dke[0]
        for k in range(1, g.n_sp):
            total = total + r.dke[k]
        r.m_dke[...] = total
        for wait in sends:
            wait()

    return kernel


def body(mesh_shape, *args):
    inputs, cotangent, kernel_entry, kernels, project_entry, projects = args[:6]
    g = geometry(mesh_shape, inputs, cotangent, project_entry, projects)
    operands = list(args)
    operands[3] = jnp.transpose(kernels, (1, 2, 0, 3))
    operands[4] = jnp.transpose(project_entry, (1, 0, 2))
    operands[5] = jnp.transpose(projects, (1, 0, 2))
    table = scratch_table(g)
    names = list(table)
    shapes = [
        ((g.bands * g.bs * g.ps, 2 * LANE), F32),
        ((2 * g.hs * g.pl_, LANE), F32),
        ((16, LANE), F32),
        ((4, 16, 2 * LANE), F32),
        ((2, g.shard, g.cin), BF16),
        ((4, g.shard, g.wide), BF16),
        ((24, 2 * LANE), F32),
    ]
    vmem = pl.BlockSpec(memory_space=pltpu.VMEM)
    parts = pl.pallas_call(
        make_kernel(g, names),
        out_shape=[jax.ShapeDtypeStruct(shape, kind) for shape, kind in shapes],
        in_specs=[vmem] * 10,
        out_specs=[vmem] * len(shapes),
        scratch_shapes=list(table.values()),
        compiler_params=pltpu.CompilerParams(
            collective_id=0, has_side_effects=True, vmem_limit_bytes=60 << 20),
    )(*operands)

    def write(m_out, m_gin, m_dke, m_dk, m_dwe, m_dw, m_vec, *outs):
        o_out, o_gin, o_dke, o_dk, o_dwe, o_dw, o_gains, o_biases, o_means, o_vars = outs
        for q in range(4):
            o_dw[:, q, :] = m_dw[q].astype(F32)[0 : g.cc, 0 : g.chan]
        for e in range(2):
            o_dwe[:, e, :] = m_dwe[e].astype(F32)[0 : g.cc]
        for row in range(g.hs):
            o_out[row, :, 0, :] = m_out[row * g.ps : row * g.ps + g.ws, 0 : g.cc]

        def one(row, _):
            o_gin[row, :, 0, :] = m_gin[pl.ds(aligned(row * g.pl_, 8), g.wl), 0 : g.ci]
            return 0

        repeat(g.hl, one, 0, UN_W)
        for j in range(9):
            for q in range(4):
                o_dk[j // 3, j % 3, q : q + 1, :] = m_dk[q, j : j + 1, 0 : g.cc]
        for u in range(3):
            o_dke[u] = m_dke[3 * u : 3 * u + 3, 0 : g.ci]
        for k, ref in enumerate((o_means, o_vars, o_gains, o_biases)):
            ref[...] = m_vec[6 * k : 6 * k + 6, 0 : g.cc]

    results = [
        (g.hs, g.ws, 1, g.cc),
        (g.hl, g.wl, 1, g.ci),
        kernel_entry.shape,
        operands[3].shape,
        operands[4].shape,
        operands[5].shape,
    ] + [(6, g.cc)] * 4
    out = pl.pallas_call(
        write,
        out_shape=[jax.ShapeDtypeStruct(shape, F32) for shape in results],
        in_specs=[vmem] * len(shapes),
        out_specs=[vmem] * 10,
        compiler_params=pltpu.CompilerParams(vmem_limit_bytes=62 << 20),
    )(*parts)
    out = list(out)
    out[0] = jnp.transpose(out[0], (2, 0, 1, 3))
    out[1] = jnp.transpose(out[1], (2, 0, 1, 3))
    out[3] = jnp.transpose(out[3], (2, 0, 1, 3))
    out[4] = jnp.transpose(out[4], (1, 0, 2))
    out[5] = jnp.transpose(out[5], (1, 0, 2))
    return tuple(out)


def solution(mesh):
    mesh_shape = dict(mesh.shape)
    wide = P("sp", None, None, "ch")
    row = P(None, "ch")
    mid = P(None, "ch", None)
    return jax.shard_map(
        lambda *args: body(mesh_shape, *args),
        mesh=mesh,
        in_specs=(wide, wide, P(None, None, "ch"), P(None, None, None, "ch"), mid, mid,
                  row, row, row, row),
        out_specs=(wide, wide, P(None, None, "ch"), P(None, None, None, "ch"), mid, mid,
                   row, row, row, row),
        check_vma=False,
    )
```

```python
import math
import types

import jax
import jax.numpy as jnp
from jax import lax
from jax.experimental import pallas as pl
from jax.experimental.pallas import tpu as pltpu
from jax.sharding import PartitionSpec as P

MESH = pl.DeviceIdType.MESH
EPSILON = 0.001
MOMENTUM = 0.5
LANE = 128
HALF = 64
F32 = jnp.float32
BF16 = jnp.bfloat16


def round_up(value, step):
    return -(-value // step) * step


UN_S, UN_L, UN_ES, UN_EC, UN_SR, UN_IR, UN_EK, UN_W = 12, 10, 4, 4, 4, 4, 4, 4


def aligned(index, step):
    return index if isinstance(index, int) else pl.multiple_of(index, step)


def repeat(count, one, carry, unroll=4):
    def some(k, carry):
        for j in range(unroll):
            carry = one(k * unroll + j, carry)
        return carry

    whole = count // unroll if count > unroll else 0
    if whole:
        carry = lax.fori_loop(0, whole, some, carry)
    for k in range(whole * unroll, count):
        carry = one(k, carry)
    return carry


def sigmoid(values):
    return 0.5 * jnp.tanh(0.5 * values) + 0.5


def dot(left, right, dims=(1, 0), precision=None):
    return lax.dot_general(
        left,
        right,
        (((dims[0],), (dims[1],)), ((), ())),
        precision=precision,
        preferred_element_type=F32,
    )


def fold(value):
    return jnp.sum(value.reshape(value.shape[0] // 8, 8, value.shape[1]), axis=0)


def geometry(mesh_shape, inputs, cotangent, project_entry, projects):
    geo = types.SimpleNamespace()
    geo.n_sp, geo.n_ch = mesh_shape["sp"], mesh_shape["ch"]
    geo.bands = geo.n_ch // 2
    geo.group = geo.n_sp * geo.bands
    _, geo.hl, geo.wl, geo.ci = inputs.shape
    _, geo.hs, geo.ws, geo.cc = cotangent.shape
    geo.cin, geo.chan = project_entry.shape[2], projects.shape[2]
    geo.wide = round_up(geo.chan, 2 * LANE)
    geo.half = geo.wide // 2
    geo.shard = geo.wide // geo.n_ch
    geo.tiles = geo.half // LANE
    geo.pl_, geo.ps = round_up(geo.wl + 1, 8), round_up(geo.ws + 1, 8)
    geo.bs = 2 * math.ceil(geo.hs / (2 * geo.bands))
    geo.bl = 2 * geo.bs
    geo.rs, geo.rl = geo.bs + 2, geo.bl + 2
    geo.na = 2 * math.ceil(geo.rl / 4)
    geo.nb = geo.rl - geo.na
    geo.ka = geo.na * geo.pl_
    geo.kb = geo.nb * geo.pl_
    geo.full = geo.n_ch * LANE
    geo.ny = geo.bands if geo.n_sp % geo.bands == 0 else 1
    geo.nz = geo.n_sp // geo.ny
    geo.tall = geo.shard // 16
    geo.u_mid = geo.tall * (geo.wide // LANE)
    geo.u_dk = round_up(geo.shard, LANE) // LANE
    geo.u_in = geo.tall * (geo.cin // LANE)
    geo.units = [
        round_up(u, geo.n_sp)
        for u in [geo.u_mid] * 3 + [geo.u_mid // 2] * 2 + [geo.u_in + 4 * geo.u_dk, geo.u_in]
    ]
    geo.plane = geo.bands * geo.ny
    geo.count_large = float(geo.n_sp * geo.hl * geo.wl)
    geo.count_small = float(geo.n_sp * geo.hs * geo.ws)
    return geo


IN_NAMES = [
    "inputs",
    "cotangent",
    "kernel_entry",
    "kernels",
    "project_entry",
    "projects",
    "bn_gains",
    "bn_biases",
    "run_means",
    "run_vars",
]
OUT_NAMES = [
    "m_out",
    "m_gin",
    "m_dke",
    "m_dk",
    "m_dwe",
    "m_dw",
    "m_gains",
    "m_biases",
    "m_means",
    "m_vars",
]


def scratch_table(g):
    dma, vm = pltpu.SemaphoreType.DMA, pltpu.VMEM
    small, large = g.rs * g.ps, g.rl * g.pl_
    cp_rows = (g.bands * g.bl + 2) * g.pl_
    x = g.bands
    table = dict(
        x32=vm((cp_rows, LANE), F32),
        a1=vm((cp_rows + 2 * g.pl_, LANE), F32),
        s1=vm((cp_rows, LANE), F32),
        s1pk=vm((x, g.ka, LANE), BF16),
        s1full=vm((g.ka, g.full), BF16),
        sidepk=vm((x, small, LANE), BF16),
        sidefull=vm((small, g.full), BF16),
        sidecp=vm(((x * g.bs + 2) * g.ps, LANE), F32),
        parloc=vm((56, 2 * LANE), F32),
        parx=vm((x, 56, 2 * LANE), F32),
        par=vm((56, g.half), F32),
        place=vm((g.wide, g.wide), BF16),
        place_in=vm((2, g.cin, g.full), BF16),
        wpad=vm((g.shard, g.wide), BF16),
        w=vm((4, g.half, g.wide), BF16),
        we=vm((2, g.half, g.cin), BF16),
        wp=vm((3, g.half, g.full), BF16),
        cotpad=vm(((x * g.bs + 2) * g.ps, 2 * LANE), F32),
        cotx=vm(((x * g.bs + 2) * g.ps, 2 * LANE), BF16),
        cots=vm((x, small, 2 * LANE), BF16),
        picks=vm((x, 2 * LANE, g.half), F32),
        edge_up=vm((2 * g.pl_, g.half), BF16),
        edge_down=vm((4 * g.pl_, g.half), BF16),
        from_below=vm((2 * g.pl_, g.half), BF16),
        from_above=vm((4 * g.pl_, g.half), BF16),
        cot=vm((small, g.half), F32),
        p1=vm((large, g.half), F32),
        a2=vm((large, g.half), F32),
        s2=vm((g.bl * g.pl_, g.wide), BF16),
        p2=vm((large + 3 * g.pl_, g.half), F32),
        tmp=vm((g.tiles, 48, LANE), F32),
        poolraw=vm((small, g.half), F32),
        pside=vm((small, g.half), F32),
        hid=vm((3, small, g.half), F32),
        act=vm((3, small, g.half), F32),
        sm=vm((3, g.bs * g.ps, g.wide), BF16),
        pm=vm((3, small, g.half), F32),
        gb=vm((3, small, g.half), F32),
        gt=vm((3, small, g.half), F32),
        gs=vm((small, g.half), F32),
        rsend=vm((3, small, g.half), BF16),
        rrecv=vm((3, small, g.half), BF16),
        gside=vm((small, g.half), BF16),
        gt2=vm((large, g.half), F32),
        rsend2=vm((large, g.half), BF16),
        rrecv2=vm((large, g.half), BF16),
        gs2=vm((large, g.half), F32),
        gb1=vm((large, g.half), F32),
        g1=vm((large, g.half), BF16),
        essend=vm((g.ka, x * LANE), BF16),
        esrecv=vm((g.ka, x * LANE), BF16),
        essum=vm((x, g.ka, LANE), BF16),
        esr=vm((x, g.ka, LANE), BF16),
        sdsend=vm((small, x * LANE), BF16),
        sdrecv=vm((small, x * LANE), BF16),
        sdsum=vm((x, small, LANE), BF16),
        sdr=vm((x, small, LANE), BF16),
        gs1=vm((cp_rows, LANE), F32),
        outx=vm((x, g.bs * g.ps, 2 * LANE), BF16),
        outs=vm((x, g.bs * g.ps, 2 * LANE), BF16),
        dk=vm((4, 16, g.half), F32),
        pickb=vm((x, g.half, 2 * LANE), BF16),
        dke=vm((g.n_sp, 16, LANE), F32),
        vec=vm((56, g.half), F32),
        ar2=vm((5, g.group, 2, g.half), F32),
        ar4=vm((4, g.group, 4, g.half), F32),
        ar_ss=dma((9,)),
        ar_rs=dma((9,)),
        s1_ss=dma((2 * g.n_ch,)),
        s1_rs=dma((g.n_ch,)),
        sd_ss=dma((2 * g.n_ch,)),
        sd_rs=dma((g.n_ch,)),
        par_ss=dma((x,)),
        par_rs=dma((x,)),
        we_ss=dma((2, x)),
        we_rs=dma((2, x)),
        w_ss=dma((4, 2 * x)),
        w_rs=dma((4, 2 * x)),
        cot_ss=dma((x,)),
        cot_rs=dma((x,)),
        sm_ss=dma((4,)),
        sm_rs=dma((4,)),
        r_ss=dma((4,)),
        r_rs=dma((4,)),
        halo_ss=dma((7, 2)),
        halo_rs=dma((7, 2)),
        es_ss=dma((2,)),
        es_rs=dma((2,)),
        esx_ss=dma((2, x)),
        esx_rs=dma((2, x)),
        out_ss=dma((x,)),
        out_rs=dma((x,)),
        ra_ss=dma((7, g.plane)),
        ra_rs=dma((7, g.plane)),
        rz_ss=dma((7, g.nz)),
        rz_rs=dma((7, g.nz)),
        gz_ss=dma((5, g.nz)),
        gz_rs=dma((5, g.nz)),
        gy_ss=dma((5, g.ny)),
        gy_rs=dma((5, g.ny)),
        ga_ss=dma((2,)),
        ga_rs=dma((2,)),
        dke_ss=dma((1,)),
        dke_rs=dma((1,)),
    )
    for k, u in enumerate(g.units):
        unit = (16, LANE)
        table.update({
            f"part{k}": vm((x, u) + unit, BF16),
            f"plane{k}": vm((g.plane, u // g.ny) + unit, BF16),
            f"ys{k}": vm((u // g.ny,) + unit, BF16),
            f"rzr{k}": vm((g.nz, u // g.n_sp) + unit, BF16),
            f"fin{k}": vm((u,) + unit, BF16),
        })
    return table


def make_kernel(g, scratch_names):
    n_bands, half, shard, tiles = g.bands, g.half, g.shard, g.tiles
    pitch, pitch_s = g.pl_, g.ps
    small, large = g.rs * g.ps, g.rl * g.pl_
    AVG, VAR, T1, T0, INV, ALPHA, BETA, KAPPA, LAM = (6 * k for k in range(9))
    counts = (g.count_large, g.count_large) + (g.count_small,) * 4

    def kernel(*refs):
        r = types.SimpleNamespace(**dict(zip(IN_NAMES + OUT_NAMES + scratch_names, refs)))
        s = lax.axis_index("sp")
        ch = lax.axis_index("ch")
        x = ch // 2
        c = lax.rem(ch, 2)
        me = s * n_bands + x
        yi, zi = lax.rem(s, g.ny), s // g.ny
        sends = []

        def copy_to(src, dst, send, recv, s_, x_, c_):
            cp = pltpu.make_async_remote_copy(
                src_ref=src,
                dst_ref=dst,
                send_sem=send,
                recv_sem=recv,
                device_id=(s_, x_ * 2 + c_),
                device_id_type=MESH,
            )
            cp.start()
            sends.append(cp.wait_send)

        def landed(ref, sem):
            pltpu.make_async_copy(ref, ref, sem).wait()

        def other_band(k):
            return lax.rem(x + k, n_bands)

        def edge_copy(src_up, dst_up, src_down, dst_down, e):
            up = pltpu.make_async_remote_copy(
                src_up, dst_up, r.halo_ss.at[e, 0], r.halo_rs.at[e, 0],
                device_id=(s, (x - 1) * 2 + c), device_id_type=MESH)
            down = pltpu.make_async_remote_copy(
                src_down, dst_down, r.halo_ss.at[e, 1], r.halo_rs.at[e, 1],
                device_id=(s, (x + 1) * 2 + c), device_id_type=MESH)

            @pl.when(x > 0)
            def _():
                up.start()

            @pl.when(x < n_bands - 1)
            def _():
                down.start()

            def finish():
                @pl.when(x < n_bands - 1)
                def _():
                    landed(dst_up, r.halo_rs.at[e, 0])

                @pl.when(x > 0)
                def _():
                    landed(dst_down, r.halo_rs.at[e, 1])

            def sent():
                @pl.when(x > 0)
                def _():
                    up.wait_send()

                @pl.when(x < n_bands - 1)
                def _():
                    down.wait_send()

            sends.append(sent)
            return finish

        def edges(ref, e):
            first, last = pl.ds(pitch_s, pitch_s), pl.ds(g.bs * pitch_s, pitch_s)
            return edge_copy(
                ref.at[first], ref.at[pl.ds((g.bs + 1) * pitch_s, pitch_s)],
                ref.at[last], ref.at[pl.ds(0, pitch_s)], e)

        def flipped(value, key):
            out, bit = 0, 1
            while bit <= key:
                here = lax.rem(value // bit, 2)
                out = out + bit * (1 - here if key & bit else here)
                bit *= 2
            return out + (value // bit) * bit

        def hops(key):
            return key // (n_bands * g.ny) + key // n_bands % g.ny + key % n_bands

        few = g.group <= 16
        keys = sorted(range(1, g.group), key=hops, reverse=True) if few else []
        peers = [
            (flipped(s, key // n_bands), flipped(x, key % n_bands)) for key in keys
        ]

        def to_group(src, dst, send, recv, pick=None):
            def one(s_, x_):
                pltpu.make_async_remote_copy(
                    src if pick is None else pick(s_, x_), dst, send, recv,
                    device_id=(s_, x_ * 2 + c), device_id_type=MESH).start()

            for s_, x_ in peers:
                one(s_, x_)

            def loop(k, _):
                to = lax.rem(me + k, g.group)
                one(to // n_bands, lax.rem(to, n_bands))
                return 0

            if not few:
                lax.fori_loop(1, g.group, loop, 0)

        sp_keys = sorted(range(1, g.n_sp), key=lambda k: hops(k * n_bands), reverse=True)
        sp_peers = [flipped(s, key) for key in sp_keys] if few else []

        def to_images(src, dst, send, recv):
            def one(s_):
                pltpu.make_async_remote_copy(
                    src, dst, send, recv, device_id=(s_, ch), device_id_type=MESH).start()

            for s_ in sp_peers:
                one(s_)

            def loop(k, _):
                one(lax.rem(s + k, g.n_sp))
                return 0

            if not few:
                lax.fori_loop(1, g.n_sp, loop, 0)

        def sum_start(buf, at, e, rows):
            for k, row in enumerate(rows):
                buf[at, me, k : k + 1, :] = row

            to_group(buf.at[at, me], buf.at[at, me], r.ar_ss.at[e], r.ar_rs.at[e])

        def sum_finish(buf, at, e):
            block = buf.at[at, pl.ds(0, g.group - 1)]
            landed(block, r.ar_rs.at[e])
            sends.append(lambda: landed(block, r.ar_ss.at[e]))
            total = buf[at, 0]
            for k in range(1, g.group):
                total = total + buf[at, k]
            return total

        def fill(ref, start, rows):
            ref[pl.ds(start, rows)] = jnp.zeros((rows,) + ref.shape[1:], ref.dtype)

        def fill_all(ref, step):
            def one(i, _):
                ref[pl.ds(aligned(i * step, 8), step)] = jnp.zeros(
                    (step,) + ref.shape[1:], ref.dtype)
                return 0

            repeat(ref.shape[0] // step, one, 0, 1)

        def lane(t):
            return pl.ds(t * LANE, LANE)

        def col_mask(width, breadth):
            at = lax.broadcasted_iota(jnp.int32, (width, LANE), 0)
            return jnp.where(at < breadth, 1.0, 0.0).astype(F32)

        def row_ok(row, height):
            return jnp.where((row >= 0) & (row < height), 1.0, 0.0).astype(F32)

        mask_l, mask_s = col_mask(pitch, g.wl), col_mask(pitch_s, g.ws)

        def vrow(kind, layer, t):
            return r.vec[kind + layer : kind + layer + 1, lane(t)]

        def taps_of(q, t):
            return [
                [r.par[16 + 4 * (3 * u + v) + q : 17 + 4 * (3 * u + v) + q, lane(t)] for v in range(3)]
                for u in range(3)
            ]

        def flip(taps):
            return [[taps[2 - u][2 - v] for v in range(3)] for u in range(3)]

        def conv_row(rows, taps):
            width = rows[0].shape[0]
            side = [
                rows[0] * taps[0][v] + rows[1] * taps[1][v] + rows[2] * taps[2][v]
                for v in range(3)
            ]
            return side[1] + pltpu.roll(side[0], 1, 0) + pltpu.roll(side[2], width - 1, 0)

        def store_moments(layer, total, square):
            n = counts[layer]
            average = total / n
            variance = square / n - average * average
            inverse = lax.rsqrt(variance + EPSILON)
            alpha = inverse * r.par[layer : layer + 1, :]
            r.vec[AVG + layer : AVG + layer + 1, :] = average
            r.vec[VAR + layer : VAR + layer + 1, :] = variance
            r.vec[INV + layer : INV + layer + 1, :] = inverse
            r.vec[ALPHA + layer : ALPHA + layer + 1, :] = alpha
            r.vec[BETA + layer : BETA + layer + 1, :] = (
                r.par[6 + layer : 7 + layer, :] - average * alpha)

        def store_back(layer, total, product):
            n = counts[layer]
            average = r.vec[AVG + layer : AVG + layer + 1, :]
            inverse = r.vec[INV + layer : INV + layer + 1, :]
            alpha = r.vec[ALPHA + layer : ALPHA + layer + 1, :]
            scaled = inverse * (product - average * total)
            r.vec[T0 + layer : T0 + layer + 1, :] = total
            r.vec[T1 + layer : T1 + layer + 1, :] = scaled
            kappa = -alpha * inverse * scaled / n
            r.vec[KAPPA + layer : KAPPA + layer + 1, :] = kappa
            r.vec[LAM + layer : LAM + layer + 1, :] = -alpha * total / n - kappa * average

        def rowsum(value):
            return jnp.sum(value, axis=0, keepdims=True)

        barrier = pltpu.get_barrier_semaphore()

        def greet(s_, x_):
            pl.semaphore_signal(
                barrier, inc=1, device_id=(s_, x_ * 2 + c), device_id_type=MESH)

        def greet_some(k, _):
            to = lax.rem(me + k, g.group)
            greet(to // n_bands, lax.rem(to, n_bands))
            return 0

        for s_, x_ in peers:
            greet(s_, x_)
        if not few:
            lax.fori_loop(1, g.group, greet_some, 0)
        pl.semaphore_signal(
            barrier, inc=1, device_id=(s, x * 2 + 1 - c), device_id_type=MESH)

        fill_all(r.x32, pitch)
        fill_all(r.a1, pitch)
        fill(r.s1, 0, pitch)
        fill(r.s1, (g.hl + 1) * pitch, (n_bands * g.bl + 1 - g.hl) * pitch)
        fill(r.parloc, 0, 56)
        fill_all(r.wpad, 16)
        fill(r.tmp, 0, tiles)
        fill(r.p2, 0, 3 * pitch)
        fill(r.p2, (g.bl + 3) * pitch, 2 * pitch)
        fill(r.gb1, 0, pitch)
        fill(r.gb1, (g.bl + 1) * pitch, pitch)
        fill(r.dk, 0, 4)
        r.dke[s] = jnp.zeros((16, LANE), F32)
        for first, edge in ((0, x == 0), ((g.bs + 1) * pitch_s, x == n_bands - 1)):
            @pl.when(edge)
            def _():
                for i in range(3):
                    for ref in (r.pm, r.gb):
                        ref[i, first : first + pitch_s] = jnp.zeros((pitch_s, half), F32)

        def entry_silu(row, _):
            value = r.inputs[0, row].astype(F32)
            r.x32[pl.ds(aligned((row + 1) * pitch, 8), g.wl), 0 : g.ci] = value
            r.a1[pl.ds(aligned((row + 2) * pitch, 8), g.wl), 0 : g.ci] = value * sigmoid(value)
            return 0

        repeat(g.hl, entry_silu, 0, UN_ES)
        r.parloc[0:6, 0 : g.cc] = r.bn_gains[...]
        r.parloc[6:12, 0 : g.cc] = r.bn_biases[...]
        for j in range(9):
            at = 16 + 4 * j
            r.parloc[at : at + 4, 0 : g.cc] = r.kernels[j // 3, j % 3].astype(F32)
        taps_in = [
            [r.kernel_entry[u].astype(F32)[v : v + 1, :] for v in range(3)] for u in range(3)
        ]
        pad_in = jnp.zeros((1, LANE - g.ci), F32)
        taps_in = [[jnp.concatenate([k, pad_in], axis=1) for k in row] for row in taps_in]

        def entry_conv(row, _):
            rows = [
                r.a1[pl.ds(aligned((row + 1 + u) * pitch, 8), pitch), :] for u in range(3)
            ]
            r.s1[pl.ds(aligned((row + 1) * pitch, 8), pitch), :] = (
                conv_row(rows, taps_in) * mask_l)
            return 0

        repeat(g.hl, entry_conv, 0, UN_EC)
        for b in range(n_bands):
            for k in range(g.na // 2):
                packed = r.s1[(b * g.bl + 2 * k) * pitch : (b * g.bl + 2 * k + 2) * pitch, :]
                if 2 * k < g.nb:
                    at = (b * g.bl + g.na + 2 * k) * pitch
                    packed = packed + pltpu.roll(r.s1[at : at + 2 * pitch, :], HALF, 1)
                r.s1pk[b, 2 * k * pitch : (2 * k + 2) * pitch, :] = packed.astype(BF16)
        for e in range(2):
            r.wpad[0 : g.cc, 0 : g.cin] = r.project_entry[:, e, :]
            r.we[e, pl.ds(aligned(x * shard, 16), shard), :] = r.wpad[:, 0 : g.cin]

        pl.semaphore_wait(barrier, g.group)
        tile = c * n_bands + x

        def full_lanes(t):
            return pl.ds(aligned(t * LANE, LANE), LANE)

        for k in range(1, n_bands):
            b = other_band(k)
            copy_to(r.s1pk.at[b], r.s1full.at[:, full_lanes(tile)],
                    r.s1_ss.at[k], r.s1_rs.at[tile], s, b, c)
        copy_to(r.s1pk.at[x], r.s1full.at[:, full_lanes(tile)],
                r.s1_ss.at[0], r.s1_rs.at[tile], s, x, 1 - c)
        r.s1full[:, full_lanes(tile)] = r.s1pk[x]
        for k in range(1, n_bands):
            mine = r.we.at[0, pl.ds(aligned(x * shard, 16), shard)]
            copy_to(mine, mine, r.we_ss.at[0, k], r.we_rs.at[0, x], s, other_band(k), c)

        for b in range(n_bands):
            spot = lax.broadcasted_iota(jnp.int32, (2 * LANE, half), 1) - b * shard
            r.picks[b] = jnp.where(
                (spot == lax.broadcasted_iota(jnp.int32, (2 * LANE, half), 0)) & (spot < g.cc),
                1.0, 0.0).astype(F32)
        r.parx[x] = r.parloc[...]

        def send_vectors():
            for k in range(1, n_bands):
                copy_to(r.parx.at[x], r.parx.at[x], r.par_ss.at[k], r.par_rs.at[x],
                        s, other_band(k), c)

        def vectors_landed():
            total = 0.0
            for k in range(1, n_bands):
                b = other_band(k)
                landed(r.parx.at[b], r.par_rs.at[b])
            for b in range(n_bands):
                total = total + dot(r.parx[b], r.picks[b], precision=lax.Precision.HIGHEST)
            r.par[...] = total

        r.sidecp[...] = jnp.zeros_like(r.sidecp)

        def side_row(row, _):
            at = aligned((2 * row + 1) * pitch, 8)
            r.sidecp[pl.ds(aligned((row + 1) * pitch_s, 8), g.ws), :] = r.x32[
                pl.ds(at, g.ws, stride=2), :]
            return 0

        repeat(g.hs, side_row, 0, UN_SR)
        for b in range(n_bands):
            r.sidepk[b] = r.sidecp[b * g.bs * pitch_s : b * g.bs * pitch_s + small, :].astype(BF16)
        r.sidefull[:, full_lanes(tile)] = r.sidepk[x]

        def send_side():
            for k in range(1, n_bands):
                b = other_band(k)
                copy_to(r.sidepk.at[b], r.sidefull.at[:, full_lanes(tile)],
                        r.sd_ss.at[k], r.sd_rs.at[tile], s, b, c)
            copy_to(r.sidepk.at[x], r.sidefull.at[:, full_lanes(tile)],
                    r.sd_ss.at[0], r.sd_rs.at[tile], s, x, 1 - c)
            for k in range(1, n_bands):
                mine = r.we.at[1, pl.ds(aligned(x * shard, 16), shard)]
                copy_to(mine, mine, r.we_ss.at[1, k], r.we_rs.at[1, x], s, other_band(k), c)

        fill_all(r.cotpad, pitch_s)

        def cot_row(row, _):
            r.cotpad[pl.ds(aligned((row + 1) * pitch_s, 8), g.ws), 0 : g.cc] = (
                r.cotangent[0, row].astype(F32))
            return 0

        repeat(g.hs, cot_row, 0, UN_SR)
        r.cotx[...] = r.cotpad[...].astype(BF16)
        r.cots[x] = r.cotx[pl.ds(aligned(x * g.bs * pitch_s, 16), small), :]

        def send_cotangent():
            for k in range(1, n_bands):
                b = other_band(k)
                copy_to(r.cotx.at[pl.ds(aligned(b * g.bs * pitch_s, 16), small)], r.cots.at[x],
                        r.cot_ss.at[k], r.cot_rs.at[x], s, b, c)

        def channel_place(rows, k0, cols, cut, offset):
            k_at = k0 + lax.broadcasted_iota(jnp.int32, (rows, cols), 0)
            p_at = lax.broadcasted_iota(jnp.int32, (rows, cols), 1)
            want = k_at + offset(0)
            for j in range(1, g.n_ch):
                jump = offset(j) - offset(j - 1)
                want = want + jnp.where(k_at >= j * cut, jump, 0)
            return jnp.where(want == p_at, 1.0, 0.0).astype(BF16)

        def offset_wide(j):
            return (j % 2) * half + (j // 2) * shard - j * g.cc

        def offset_in(j):
            return ((j % 2) * n_bands + j // 2) * LANE - j * g.ci

        r.place_in[0] = channel_place(g.cin, 0, g.full, g.ci, offset_in)
        r.place_in[1] = channel_place(
            g.cin, 0, g.full, g.ci, lambda j: offset_in(j) + HALF)
        def place_rows(k, _):
            at = aligned(k * 64, 64)
            r.place[pl.ds(at, 64), :] = channel_place(64, at, g.wide, g.cc, offset_wide)
            return 0

        repeat(g.wide // 64, place_rows, 0, 2)
        fill_all(r.wpad, 16)

        def weight_prepare(q):
            r.wpad[0 : g.cc, 0 : g.chan] = r.projects[:, q, :]
            r.w[q, pl.ds(aligned(x * shard, 16), shard), :] = dot(
                r.wpad[...], r.place[...]).astype(BF16)

        odd = lax.rem(yi, 2) if g.ny > 1 else 0
        pair = zi * g.ny + yi + 1 - 2 * odd
        halves = 2 if g.ny > 1 else 1

        def shard_part(q, b, part):
            size = shard // halves
            return r.w.at[q, pl.ds(aligned(b * shard + part * size, 16), size)]

        def weight_send(q):
            mine = shard_part(q, x, odd)
            for k in range(1, n_bands):
                copy_to(mine, mine, r.w_ss.at[q, k], r.w_rs.at[q, x], s, other_band(k), c)

        def weight_forward(q):
            for k in range(1, n_bands):
                b = other_band(k)
                got = shard_part(q, b, odd)
                landed(got, r.w_rs.at[q, b])
                if halves > 1:
                    copy_to(got, got, r.w_ss.at[q, n_bands + k], r.w_rs.at[q, n_bands + b],
                            pair, x, c)

        def weight_landed(q):
            for k in range(1, n_bands):
                b = other_band(k)
                if halves > 1:
                    landed(shard_part(q, b, 1 - odd), r.w_rs.at[q, n_bands + b])

        weight_prepare(0)
        weight_send(0)
        weight_prepare(1)
        weight_prepare(2)

        for k in range(1, n_bands):
            t = c * n_bands + other_band(k)
            landed(r.s1full.at[:, full_lanes(t)], r.s1_rs.at[t])
            copy_to(r.s1full.at[:, full_lanes(t)], r.s1full.at[:, full_lanes(t)],
                    r.s1_ss.at[g.n_ch + k], r.s1_rs.at[t], s, x, 1 - c)

        for k in range(1, n_bands):
            b = other_band(k)
            landed(r.we.at[0, pl.ds(aligned(b * shard, 16), shard)], r.we_rs.at[0, b])
        for a in range(2):
            r.wp[a] = dot(r.we[0], r.place_in[a]).astype(BF16)

        for k in range(n_bands):
            t = (1 - c) * n_bands + k
            landed(r.s1full.at[:, full_lanes(t)], r.s1_rs.at[t])
        r.p1[0 : g.ka, :] = dot(r.s1full[...], r.wp[0], (1, 1))
        r.p1[g.ka : large, :] = dot(r.s1full[0 : g.kb, :], r.wp[1], (1, 1))

        def moments(ref, first, rows, width):
            out = [[], []]
            for t in range(tiles):
                def one(k, carry):
                    v = ref[pl.ds(aligned((first + k) * width, 8), width), lane(t)]
                    return (carry[0] + fold(v), carry[1] + fold(v * v))

                zero = jnp.zeros((8, LANE), F32)
                total, square = repeat(rows, one, (zero, zero), UN_S if width == pitch_s else UN_L)
                out[0].append(rowsum(total))
                out[1].append(rowsum(square))
            return [jnp.concatenate(o, axis=1) for o in out]

        sum_start(r.ar2, 0, 0, moments(r.p1, 1, g.bl, pitch))
        send_vectors()
        send_side()
        weight_send(1)
        weight_send(2)
        weight_prepare(3)
        weight_forward(0)
        vectors_landed()
        total = sum_finish(r.ar2, 0, 0)
        store_moments(0, total[0:1], total[1:2])

        for t in range(tiles):
            alpha, beta = vrow(ALPHA, 0, t), vrow(BETA, 0, t)

            def one(k, _):
                at = pl.ds(aligned(k * pitch, 8), pitch)
                h = r.p1[at, lane(t)] * alpha + beta
                ok = mask_l * row_ok(x * g.bl + k - 1, g.hl)
                r.a2[at, lane(t)] = h * sigmoid(h) * ok
                return 0

            repeat(g.rl, one, 0, UN_L)
        mine_lanes = aligned(c * half, LANE)
        their_lanes = aligned((1 - c) * half, LANE)

        def own_tile(t):
            return pl.ds(aligned(c * half + t * LANE, LANE), LANE)

        def conv_pairs(source, q, target, row0, rows, height, width, mask):
            for t in range(tiles):
                taps = taps_of(q, t)

                def one(k, _):
                    block = [
                        source[pl.ds(aligned((2 * k + u) * width, 8), width), lane(t)]
                        for u in range(4)
                    ]
                    out = [
                        conv_row(block[j : j + 3], taps) * (mask * row_ok(row0 + 2 * k + j, height))
                        for j in range(2)
                    ]
                    target[pl.ds(aligned(k * 2 * width, 16), 2 * width), own_tile(t)] = (
                        jnp.concatenate(out, axis=0).astype(BF16))
                    return 0

                repeat(rows // 2, one, 0, UN_S if width == pitch_s else UN_L)

        conv_pairs(r.a2, 0, r.s2, x * g.bl, g.bl, g.hl, pitch, mask_l)

        def swap_start(ref, e):
            mine = ref.at[:, pl.ds(mine_lanes, half)]
            copy_to(mine, mine, r.sm_ss.at[e], r.sm_rs.at[e], s, x, 1 - c)

        def swap_landed(ref, e):
            landed(ref.at[:, pl.ds(their_lanes, half)], r.sm_rs.at[e])

        swap_start(r.s2, 0)
        weight_landed(0)
        rows_all = g.bl * pitch
        step = rows_all // 2
        for k in range(2):
            rows = pl.ds(k * step, step)
            r.p2[3 * pitch + k * step : 3 * pitch + (k + 1) * step, :] = dot(
                r.s2[rows, pl.ds(mine_lanes, half)], r.w[0, :, pl.ds(mine_lanes, half)], (1, 1))
        for k in range(1, n_bands):
            t = c * n_bands + other_band(k)
            landed(r.sidefull.at[:, full_lanes(t)], r.sd_rs.at[t])
            copy_to(r.sidefull.at[:, full_lanes(t)], r.sidefull.at[:, full_lanes(t)],
                    r.sd_ss.at[g.n_ch + k], r.sd_rs.at[t], s, x, 1 - c)
        swap_landed(r.s2, 0)
        for k in range(2):
            rows = pl.ds(k * step, step)
            at = slice(3 * pitch + k * step, 3 * pitch + (k + 1) * step)
            r.p2[at, :] = r.p2[at, :] + dot(
                r.s2[rows, pl.ds(their_lanes, half)], r.w[0, :, pl.ds(their_lanes, half)], (1, 1))
        for k in range(1, n_bands):
            b = other_band(k)
            landed(r.we.at[1, pl.ds(aligned(b * shard, 16), shard)], r.we_rs.at[1, b])
        r.wp[2] = dot(r.we[1], r.place_in[0]).astype(BF16)
        for k in range(n_bands):
            t = (1 - c) * n_bands + k
            landed(r.sidefull.at[:, full_lanes(t)], r.sd_rs.at[t])
        r.pside[...] = dot(r.sidefull[...], r.wp[2], (1, 1))
        sum_start(r.ar4, 0, 1,
                  moments(r.p2, 3, g.bl, pitch) + moments(r.pside, 1, g.bs, pitch_s))
        r.edge_up[...] = r.p2[3 * pitch : 5 * pitch, :].astype(BF16)
        r.edge_down[...] = r.p2[(g.bl - 1) * pitch : (g.bl + 3) * pitch, :].astype(BF16)
        edges_done = edge_copy(r.edge_up, r.from_below, r.edge_down, r.from_above, 0)
        weight_send(3)
        weight_forward(1)

        edges_done()

        @pl.when(x > 0)
        def _():
            r.p2[0 : 3 * pitch, :] = r.from_above[...].astype(F32)[pitch : 4 * pitch]

        @pl.when(x < n_bands - 1)
        def _():
            r.p2[(g.bl + 3) * pitch : (g.bl + 5) * pitch, :] = r.from_below[...].astype(F32)

        for t in range(tiles):
            def one(k, _):
                v = (r.p2[pl.ds(aligned(2 * k * pitch, 8), pitch), lane(t)]
                     + r.p2[pl.ds(aligned((2 * k + 1) * pitch, 8), pitch), lane(t)]
                     + r.p2[pl.ds(aligned((2 * k + 2) * pitch, 8), pitch), lane(t)])
                r.tmp[t, 0:pitch, :] = v + pltpu.roll(v, 1, 0) + pltpu.roll(v, pitch - 1, 0)
                r.poolraw[pl.ds(aligned(k * pitch_s, 8), pitch_s), lane(t)] = r.tmp[
                    t, pl.ds(0, pitch_s, stride=2), :]
                return 0

            repeat(g.rs, one, 0, UN_S)
        weight_forward(2)
        total = sum_finish(r.ar4, 0, 1)
        store_moments(1, total[0:1], total[1:2])
        store_moments(2, total[2:3], total[3:4])

        at_col = lax.broadcasted_iota(jnp.int32, (pitch_s, LANE), 0)
        col_count = mask_s * (
            1.0
            + jnp.where(at_col > 0, 1.0, 0.0)
            + jnp.where(2 * at_col + 1 < g.wl, 1.0, 0.0)) * (1.0 / 9.0)

        def window_count(row):
            inside = jnp.where(row > 0, 1.0, 0.0) + jnp.where(2 * row + 1 < g.hl, 1.0, 0.0) + 1.0
            return col_count * (inside.astype(F32) * row_ok(row, g.hs))

        for t in range(tiles):
            alpha, beta = vrow(ALPHA, 1, t) * (1.0 / 9.0), vrow(BETA, 1, t)
            alpha_2, beta_2 = vrow(ALPHA, 2, t), vrow(BETA, 2, t)

            def one(k, _):
                at = pl.ds(aligned(k * pitch_s, 8), pitch_s)
                row = x * g.bs + k - 1
                ok = mask_s * row_ok(row, g.hs)
                h = (r.poolraw[at, lane(t)] * alpha + window_count(row) * beta
                     + r.pside[at, lane(t)] * alpha_2 + beta_2) * ok
                r.hid[0, at, lane(t)] = h
                r.act[0, at, lane(t)] = h * sigmoid(h)
                return 0

            repeat(g.rs, one, 0, UN_S)

        def make_picks():
            for b in range(n_bands):
                spot_b = lax.broadcasted_iota(jnp.int32, (half, 2 * LANE), 0) - b * shard
                r.pickb[b] = jnp.where(
                    (spot_b == lax.broadcasted_iota(jnp.int32, (half, 2 * LANE), 1))
                    & (spot_b < g.cc), 1.0, 0.0).astype(BF16)

        own_rows = slice(pitch_s, (g.bs + 1) * pitch_s)
        for i in range(3):
            if i > 0:
                for t in range(tiles):
                    alpha, beta = vrow(ALPHA, 2 + i, t), vrow(BETA, 2 + i, t)

                    def one(k, _):
                        at = pl.ds(aligned(k * pitch_s, 8), pitch_s)
                        ok = mask_s * row_ok(x * g.bs + k - 1, g.hs)
                        h = (r.pm[i - 1, at, lane(t)] * alpha + beta) * ok
                        r.hid[i, at, lane(t)] = h
                        r.act[i, at, lane(t)] = h * sigmoid(h)
                        return 0

                    repeat(g.rs, one, 0, UN_S)
            conv_pairs(r.act.at[i], i + 1, r.sm.at[i], x * g.bs, g.bs, g.hs,
                       pitch_s, mask_s)
            swap_start(r.sm.at[i], 1 + i)
            weight_landed(1 + i)
            part = dot(r.sm[i, :, pl.ds(mine_lanes, half)],
                       r.w[1 + i, :, pl.ds(mine_lanes, half)], (1, 1))
            swap_landed(r.sm.at[i], 1 + i)
            r.pm[i, own_rows, :] = part + dot(
                r.sm[i, :, pl.ds(their_lanes, half)],
                r.w[1 + i, :, pl.ds(their_lanes, half)], (1, 1))
            if i < 2:
                sum_start(r.ar2, 1 + i, 2 + i, moments(r.pm.at[i], 1, g.bs, pitch_s))
                edges_done = edges(r.pm.at[i], 1 + i)
                if i == 0:
                    send_cotangent()
                    weight_forward(3)
                total = sum_finish(r.ar2, 1 + i, 2 + i)
                store_moments(3 + i, total[0:1], total[1:2])
                edges_done()

        def grad_sums(gref, pref, width, first, rows):
            out = [[], []]
            for t in range(tiles):
                def one(k, carry):
                    at = pl.ds(aligned((first + k) * width, 8), width)
                    v = gref[at, lane(t)]
                    return (carry[0] + fold(v), carry[1] + fold(v * pref[at, lane(t)]))

                zero = jnp.zeros((8, LANE), F32)
                a, b = repeat(rows, one, (zero, zero), UN_S if width == pitch_s else UN_L)
                out[0].append(rowsum(a))
                out[1].append(rowsum(b))
            return [jnp.concatenate(o, axis=1) for o in out]

        for k in range(1, n_bands):
            b = other_band(k)
            landed(r.cots.at[b], r.cot_rs.at[b])
        total = 0.0
        for b in range(n_bands):
            total = total + dot(r.cots[b], r.picks[b].astype(BF16))
        r.cot[...] = total
        sum_start(r.ar4, 1, 4,
                  moments(r.pm.at[2], 1, g.bs, pitch_s)
                  + grad_sums(r.cot, r.pm.at[2], pitch_s, 1, g.bs))
        edges_done = edges(r.pm.at[2], 3)
        make_picks()
        total = sum_finish(r.ar4, 1, 4)
        store_moments(5, total[0:1], total[1:2])
        store_back(5, total[2:3], total[3:4])
        edges_done()

        def norm_back(layer, gref, pref, target, rows, width, mask, row0, height):
            for t in range(tiles):
                alpha, kappa, lam = vrow(ALPHA, layer, t), vrow(KAPPA, layer, t), vrow(LAM, layer, t)

                def one(k, _):
                    at = pl.ds(aligned(k * width, 8), width)
                    ok = mask * row_ok(row0 + k, height)
                    target[at, lane(t)] = (
                        gref[at, lane(t)] * alpha + pref[at, lane(t)] * kappa + lam) * ok
                    return 0

                repeat(rows, one, 0, UN_S if width == pitch_s else UN_L)

        def kernel_grad(aref, gref, q, rows, width):
            for t in range(tiles):
                def one(k, carry):
                    gv = gref[pl.ds(aligned((k + 1) * width, 8), width), lane(t)]
                    turned = [pltpu.roll(gv, width - 1, 0), gv, pltpu.roll(gv, 1, 0)]
                    out = []
                    for u in range(3):
                        av = aref[pl.ds(aligned((k + u) * width, 8), width), lane(t)]
                        for v in range(3):
                            out.append(carry[3 * u + v] + fold(av * turned[v]))
                    return tuple(out)

                zero = jnp.zeros((8, LANE), F32)
                sums = repeat(rows, one, (zero,) * 9, UN_S if width == pitch_s else UN_L)
                for j in range(9):
                    r.dk[q, j : j + 1, lane(t)] = rowsum(sums[j])


        def block_of(name, k):
            return getattr(r, f"{name}{k}")

        def put_units(k, value, first, cols):
            value = value[:, first : first + cols].astype(BF16)
            for b in range(n_bands):
                for t in range(cols // LANE):
                    part = value[b * shard : (b + 1) * shard, t * LANE : (t + 1) * LANE]
                    block_of("part", k)[b, t * g.tall : (t + 1) * g.tall] = (
                        part.reshape(g.tall, 16, LANE))

        def put_kernels():
            for q in range(4):
                value = r.dk[q].astype(BF16)
                for b in range(n_bands):
                    part = dot(value, r.pickb[b]).astype(BF16)
                    for t in range(g.u_dk):
                        at = g.u_in + q * g.u_dk + t
                        r.part5[b, at] = part[:, t * LANE : (t + 1) * LANE]

        def plane_send(k):
            part = g.units[k] // g.ny
            me_plane = x * g.ny + yi
            for key in range(1, g.plane):
                to = lax.rem(me_plane + key, g.plane)
                x_, y_ = to // g.ny, lax.rem(to, g.ny)
                copy_to(block_of("part", k).at[x_, pl.ds(y_ * part, part)],
                        block_of("plane", k).at[me_plane],
                        r.ra_ss.at[k, key], r.ra_rs.at[k, me_plane], zi * g.ny + y_, x_, c)

        def plane_sum_z_send(k):
            part = g.units[k] // g.ny
            me_plane = x * g.ny + yi
            total = block_of("part", k)[x, pl.ds(yi * part, part)].astype(F32)
            for key in range(1, g.plane):
                b = lax.rem(me_plane + key, g.plane)
                landed(block_of("plane", k).at[b], r.ra_rs.at[k, b])
                total = total + block_of("plane", k)[b].astype(F32)
            block_of("ys", k)[...] = total.astype(BF16)
            piece = part // g.nz
            for j in range(1, g.nz):
                to = lax.rem(zi + j, g.nz)
                copy_to(block_of("ys", k).at[pl.ds(to * piece, piece)], block_of("rzr", k).at[zi],
                        r.rz_ss.at[k, j], r.rz_rs.at[k, zi], to * g.ny + yi, x, c)

        def z_sum(k):
            part = g.units[k] // g.ny
            piece = part // g.nz
            total = block_of("ys", k)[pl.ds(zi * piece, piece)].astype(F32)
            for j in range(1, g.nz):
                b = lax.rem(zi + j, g.nz)
                landed(block_of("rzr", k).at[b], r.rz_rs.at[k, b])
                total = total + block_of("rzr", k)[b].astype(F32)
            at = pl.ds(yi * part + zi * piece, piece)
            block_of("fin", k)[at] = total.astype(BF16)
            return at

        def z_gather(k):
            at = z_sum(k)
            for j in range(1, g.nz):
                to = lax.rem(zi + j, g.nz)
                copy_to(block_of("fin", k).at[at], block_of("fin", k).at[at],
                        r.gz_ss.at[k, j], r.gz_rs.at[k, zi], to * g.ny + yi, x, c)

        def all_gather(k):
            mine = block_of("fin", k).at[z_sum(k)]
            to_images(mine, mine, r.ga_ss.at[k - 5], r.ga_rs.at[k - 5])

        def y_gather(k):
            part = g.units[k] // g.ny
            piece = part // g.nz
            for j in range(1, g.nz):
                b = lax.rem(zi + j, g.nz)
                landed(block_of("fin", k).at[pl.ds(yi * part + b * piece, piece)],
                       r.gz_rs.at[k, b])
            at = pl.ds(yi * part, part)
            for j in range(1, g.ny):
                to = lax.rem(yi + j, g.ny)
                copy_to(block_of("fin", k).at[at], block_of("fin", k).at[at],
                        r.gy_ss.at[k, j], r.gy_rs.at[k, yi], zi * g.ny + to, x, c)

        def get_units(k, cols):
            tiles_in = [
                block_of("fin", k)[t * g.tall : (t + 1) * g.tall].reshape(shard, LANE)
                for t in range(cols // LANE)
            ]
            return jnp.concatenate(tiles_in, axis=1)

        def y_landed(k):
            part = g.units[k] // g.ny
            for j in range(1, g.ny):
                b = lax.rem(yi + j, g.ny)
                landed(block_of("fin", k).at[pl.ds(b * part, part)], r.gy_rs.at[k, b])

        def finish_block(k):
            y_landed(k)
            value = dot(get_units(k, g.wide), r.place[...], (1, 1))
            r.m_dw[:, 3 - k, :] = value[0 : g.cc, 0 : g.chan]

        def finish_halves():
            y_landed(3)
            y_landed(4)
            value = jnp.concatenate(
                [get_units(3, g.wide // 2), get_units(4, g.wide // 2)], axis=1)
            value = dot(value, r.place[...], (1, 1))
            r.m_dw[:, 0, :] = value[0 : g.cc, 0 : g.chan]

        def finish_entry(k):
            piece = g.units[k] // g.n_sp
            others = block_of("fin", k).at[pl.ds(0, (g.n_sp - 1) * piece)]
            landed(others, r.ga_rs.at[k - 5])
            sends.append(lambda: landed(others, r.ga_ss.at[k - 5]))
            r.m_dwe[:, 6 - k, :] = get_units(k, g.cin).astype(F32)[0 : g.cc]
            if k == 5:
                for q in range(4):
                    at = g.u_in + q * g.u_dk
                    value = jnp.concatenate(
                        [r.fin5[at + t] for t in range(g.u_dk)], axis=1).astype(F32)
                    for j in range(9):
                        r.m_dk[j // 3, j % 3, q : q + 1, :] = value[j : j + 1, 0 : g.cc]

        def output_landed():
            for k in range(1, n_bands):
                b = other_band(k)
                landed(r.outs.at[b], r.out_rs.at[b])
            for b in range(n_bands):
                value = r.outs[b].astype(F32)
                for k in range(g.bs):
                    if b * g.bs + k < g.hs:
                        r.m_out[b * g.bs + k, :, 0, :] = value[
                            k * pitch_s : k * pitch_s + g.ws, 0 : g.cc]

        def send_output():
            for k in range(1, n_bands):
                b = other_band(k)
                copy_to(r.outx.at[b], r.outs.at[x], r.out_ss.at[k], r.out_rs.at[x], s, b, c)

        for i in (2, 1, 0):
            layer = 3 + i
            gref = r.cot if i == 2 else r.gb.at[i + 1]
            norm_back(layer, gref, r.pm.at[i], r.gt.at[i], g.rs, pitch_s, mask_s,
                      x * g.bs - 1, g.hs)
            grad = r.gt[i].astype(BF16)
            r.rsend[i] = dot(grad, r.w[1 + i, :, pl.ds(their_lanes, half)]).astype(BF16)
            copy_to(r.rsend.at[i], r.rrecv.at[i], r.r_ss.at[i], r.r_rs.at[i], s, x, 1 - c)
            part = dot(grad, r.w[1 + i, :, pl.ds(mine_lanes, half)])
            grad = r.gt[i, own_rows, :].astype(BF16)
            put_units(2 - i, dot(grad, r.sm[i], (0, 0)), 0, g.wide)
            landed(r.rrecv.at[i], r.r_rs.at[i])
            r.gs[...] = part + r.rrecv[i].astype(F32)
            rows = [[] for _ in range(4 if i == 0 else 2)]
            for t in range(tiles):
                taps = flip(taps_of(i + 1, t))

                def one(k, carry):
                    block = [
                        r.gs[pl.ds(aligned((k + u) * pitch_s, 8), pitch_s), lane(t)]
                        for u in range(3)
                    ]
                    at = pl.ds(aligned((k + 1) * pitch_s, 8), pitch_s)
                    row = x * g.bs + k
                    h = r.hid[i, at, lane(t)]
                    sig = sigmoid(h)
                    value = conv_row(block, taps) * (sig * (1.0 + h * (1.0 - sig))) * (
                        mask_s * row_ok(row, g.hs))
                    if i == 0:
                        value = value + r.cot[at, lane(t)]
                    r.gb[i, at, lane(t)] = value
                    if i == 0:
                        new = [
                            value, value * r.pside[at, lane(t)],
                            value * window_count(row),
                            value * r.poolraw[at, lane(t)] * (1.0 / 9.0)]
                    else:
                        new = [value, value * r.pm[i - 1, at, lane(t)]]
                    return tuple(a + fold(b) for a, b in zip(carry, new))

                zero = jnp.zeros((8, LANE), F32)
                sums = repeat(g.bs, one, (zero,) * len(rows), UN_S)
                for j, v in enumerate(sums):
                    rows[j].append(rowsum(v))
            rows = [jnp.concatenate(o, axis=1) for o in rows]
            buf, at_e, e = ((r.ar4, 2, 7), (r.ar2, 3, 6), (r.ar2, 4, 5))[i]
            sum_start(buf, at_e, e, rows)
            edges_done = edges(r.gb.at[i], 4 + i)
            plane_send(2 - i)
            if i < 2:
                plane_sum_z_send(1 - i)
            if i == 0:
                z_gather(0)
            kernel_grad(r.act.at[i], r.gs, i + 1, g.bs, pitch_s)
            if i == 2:
                value = []
                for t in range(tiles):
                    h = (r.pm[2, own_rows, lane(t)] * vrow(ALPHA, 5, t) + vrow(BETA, 5, t)
                         + r.hid[0, own_rows, lane(t)])
                    value.append(h.astype(BF16))
                value = jnp.concatenate(value, axis=1)
                for b in range(n_bands):
                    r.outx[b] = dot(value, r.pickb[b]).astype(BF16)
                r.outs[x] = r.outx[x]
            total = sum_finish(buf, at_e, e)
            if i > 0:
                store_back(layer - 1, total[0:1], total[1:2])
            else:
                store_back(2, total[0:1], total[1:2])
                store_back(1, total[2:3], total[3:4])
            edges_done()

        for t in range(tiles):
            alpha, kappa, lam = vrow(ALPHA, 1, t) * (1.0 / 9.0), vrow(KAPPA, 1, t), vrow(LAM, 1, t)

            def spread(v):
                r.tmp[t, pl.ds(0, pitch_s, stride=2), :] = v
                r.tmp[t, pl.ds(1, pitch_s, stride=2), :] = v + pltpu.roll(v, pitch_s - 1, 0)
                return r.tmp[t, 0:pitch, :]

            def one(k, _):
                low = r.gb[0, pl.ds(aligned(k * pitch_s, 8), pitch_s), lane(t)]
                high = r.gb[0, pl.ds(aligned((k + 1) * pitch_s, 8), pitch_s), lane(t)]
                for j, v in enumerate((low + high, high)):
                    row = x * g.bl + 2 * k + j - 1
                    ok = mask_l * row_ok(row, g.hl)
                    p = r.p2[pl.ds(aligned((2 * k + j + 2) * pitch, 8), pitch), lane(t)]
                    r.gt2[pl.ds(aligned((2 * k + j) * pitch, 8), pitch), lane(t)] = (
                        spread(v) * alpha + p * kappa + lam) * ok
                return 0

            repeat(g.bs + 1, one, 0, UN_S)
        for k in range(2):
            at = pl.ds(k * (large // 2), large // 2)
            r.rsend2[at, :] = dot(
                r.gt2[at, :].astype(BF16), r.w[0, :, pl.ds(their_lanes, half)]).astype(BF16)
        copy_to(r.rsend2, r.rrecv2, r.r_ss.at[3], r.r_rs.at[3], s, x, 1 - c)
        for k in range(2):
            at = pl.ds(k * (large // 2), large // 2)
            r.gs2[at, :] = dot(r.gt2[at, :].astype(BF16), r.w[0, :, pl.ds(mine_lanes, half)])
        grad = r.gt2[pitch : (g.bl + 1) * pitch, :].astype(BF16)
        hw = g.wide // 2
        put_units(3, dot(grad, r.s2[:, 0:hw], (0, 0)), 0, hw)
        plane_send(3)
        put_units(4, dot(grad, r.s2[:, hw:], (0, 0)), 0, hw)
        z_gather(1)
        y_gather(0)
        landed(r.rrecv2, r.r_rs.at[3])
        r.gs2[...] = r.gs2[...] + r.rrecv2[...].astype(F32)
        rows = [[], []]
        for t in range(tiles):
            taps = flip(taps_of(0, t))
            alpha, beta = vrow(ALPHA, 0, t), vrow(BETA, 0, t)

            def one(k, carry):
                block = [
                    r.gs2[pl.ds(aligned((k + u) * pitch, 8), pitch), lane(t)] for u in range(3)
                ]
                at = pl.ds(aligned((k + 1) * pitch, 8), pitch)
                p = r.p1[at, lane(t)]
                h = p * alpha + beta
                sig = sigmoid(h)
                value = conv_row(block, taps) * (sig * (1.0 + h * (1.0 - sig))) * (
                    mask_l * row_ok(x * g.bl + k, g.hl))
                r.gb1[at, lane(t)] = value
                return (carry[0] + fold(value), carry[1] + fold(value * p))

            zero = jnp.zeros((8, LANE), F32)
            sums = repeat(g.bl, one, (zero, zero), UN_L)
            for j, v in enumerate(sums):
                rows[j].append(rowsum(v))
        rows = [jnp.concatenate(o, axis=1) for o in rows]
        sum_start(r.ar4, 3, 8, rows)
        plane_send(4)
        plane_sum_z_send(2)

        def own_ok(k, width_rows):
            return jnp.where((k >= 1) & (k <= width_rows), 1.0, 0.0).astype(F32)

        for t in range(tiles):
            alpha, kappa, lam = vrow(ALPHA, 2, t), vrow(KAPPA, 2, t), vrow(LAM, 2, t)

            def one(k, _):
                out = []
                for j in range(2):
                    at = pl.ds(aligned((2 * k + j) * pitch_s, 8), pitch_s)
                    ok = mask_s * (row_ok(x * g.bs + 2 * k + j - 1, g.hs) * own_ok(2 * k + j, g.bs))
                    out.append((r.gb[0, at, lane(t)] * alpha
                                + r.pside[at, lane(t)] * kappa + lam) * ok)
                r.gside[pl.ds(aligned(2 * k * pitch_s, 16), 2 * pitch_s), lane(t)] = (
                    jnp.concatenate(out, axis=0).astype(BF16))
                return 0

            repeat(g.rs // 2, one, 0, UN_S)
        own_tiles = pl.ds(aligned(c * n_bands * LANE, LANE), n_bands * LANE)
        their_tiles = pl.ds(aligned((1 - c) * n_bands * LANE, LANE), n_bands * LANE)
        r.sdsend[...] = dot(r.gside[...], r.wp[2, :, their_tiles]).astype(BF16)
        copy_to(r.sdsend, r.sdrecv, r.es_ss.at[1], r.es_rs.at[1], s, x, 1 - c)
        part = dot(r.gside[...], r.wp[2, :, own_tiles])
        landed(r.sdrecv, r.es_rs.at[1])
        part = part + r.sdrecv[...].astype(F32)
        for b in range(n_bands):
            r.sdsum[b] = part[:, b * LANE : (b + 1) * LANE].astype(BF16)
        for k in range(1, n_bands):
            b = other_band(k)
            copy_to(r.sdsum.at[b], r.sdr.at[x], r.esx_ss.at[1, k], r.esx_rs.at[1, x], s, b, c)
        r.sdr[x] = r.sdsum[x]

        lane_at = lax.broadcasted_iota(jnp.int32, (half, g.full), 1)
        low_lanes = lax.rem(lane_at, LANE) < HALF
        both_place = r.place_in[0] + r.place_in[1]

        value = dot(r.gside[...], r.sidefull[...], (0, 0)).astype(BF16)
        put_units(5, dot(value, both_place, (1, 1)), 0, g.cin)
        kernel_grad(r.a2, r.gs2, 0, g.bl, pitch)
        put_kernels()
        plane_send(5)
        y_gather(1)
        plane_sum_z_send(3)
        total = sum_finish(r.ar4, 3, 8)
        store_back(0, total[0:1], total[1:2])

        for t in range(tiles):
            alpha, kappa, lam = vrow(ALPHA, 0, t), vrow(KAPPA, 0, t), vrow(LAM, 0, t)

            def one(k, _):
                out = []
                for j in range(2):
                    at = pl.ds(aligned((2 * k + j) * pitch, 8), pitch)
                    ok = mask_l * (row_ok(x * g.bl + 2 * k + j - 1, g.hl) * own_ok(2 * k + j, g.bl))
                    out.append((r.gb1[at, lane(t)] * alpha + r.p1[at, lane(t)] * kappa + lam) * ok)
                r.g1[pl.ds(aligned(2 * k * pitch, 16), 2 * pitch), lane(t)] = (
                    jnp.concatenate(out, axis=0).astype(BF16))
                return 0

            repeat(g.rl // 2, one, 0, UN_L)

        def entry_part(lanes):
            a = dot(r.g1[0 : g.ka, :], r.wp[0, :, lanes])
            b = dot(r.g1[g.ka : large, :], r.wp[1, :, lanes])
            if g.kb == g.ka:
                return a + b
            return jnp.concatenate([a[0 : g.kb] + b, a[g.kb :]], axis=0)

        r.essend[...] = entry_part(their_tiles).astype(BF16)
        copy_to(r.essend, r.esrecv, r.es_ss.at[0], r.es_rs.at[0], s, x, 1 - c)
        part = entry_part(own_tiles)
        grad_a = dot(r.g1[0 : g.ka, :], r.s1full[...], (0, 0))
        grad_b = dot(r.g1[g.ka : large, :], r.s1full[0 : g.kb, :], (0, 0))
        value = jnp.where(low_lanes, grad_a, grad_b).astype(BF16)
        put_units(6, dot(value, both_place, (1, 1)), 0, g.cin)
        landed(r.esrecv, r.es_rs.at[0])
        part = part + r.esrecv[...].astype(F32)
        for b in range(n_bands):
            r.essum[b] = part[:, b * LANE : (b + 1) * LANE].astype(BF16)
        for k in range(1, n_bands):
            b = other_band(k)
            copy_to(r.essum.at[b], r.esr.at[x], r.esx_ss.at[0, k], r.esx_rs.at[0, x], s, b, c)
        r.esr[x] = r.essum[x]
        plane_send(6)
        z_gather(2)
        plane_sum_z_send(4)
        z_gather(3)
        plane_sum_z_send(5)
        send_output()
        finish_block(0)
        finish_block(1)

        spot = lax.broadcasted_iota(jnp.int32, (half, 2 * LANE), 0) - x * shard
        pick_own = jnp.where(
            (spot == lax.broadcasted_iota(jnp.int32, (half, 2 * LANE), 1)) & (spot < g.cc),
            1.0, 0.0).astype(F32)
        final = dot(r.vec[0:24, :], pick_own, precision=lax.Precision.HIGHEST)
        final = final[:, 0 : g.cc]
        at_row = lax.broadcasted_iota(jnp.int32, (6, g.cc), 0)
        count = jnp.where(at_row < 2, g.count_large, g.count_small)
        bessel = count / (count - 1.0)
        r.m_means[...] = (1.0 - MOMENTUM) * r.run_means[...] + MOMENTUM * final[0:6]
        r.m_vars[...] = (1.0 - MOMENTUM) * r.run_vars[...] + MOMENTUM * (final[6:12] * bessel)
        r.m_gains[...] = final[12:18]
        r.m_biases[...] = final[18:24]

        for k in range(1, n_bands):
            b = other_band(k)
            landed(r.sdr.at[b], r.esx_rs.at[1, b])
        for b in range(n_bands):
            r.sidecp[b * g.bs * pitch_s : (b + 1) * g.bs * pitch_s, :] = (
                r.sdr[b].astype(F32)[pitch_s : (g.bs + 1) * pitch_s])
        for k in range(1, n_bands):
            b = other_band(k)
            landed(r.esr.at[b], r.esx_rs.at[0, b])
        fill(r.gs1, 0, pitch)
        fill(r.gs1, (n_bands * g.bl + 1) * pitch, pitch)
        for b in range(n_bands):
            for k in range(g.na // 2):
                value = r.esr[b, 2 * k * pitch : (2 * k + 2) * pitch, :].astype(F32)
                for j in range(2):
                    i = 2 * k + j
                    if 1 <= i <= g.bl:
                        at = (b * g.bl + i) * pitch
                        r.gs1[at : at + pitch, :] = value[j * pitch : (j + 1) * pitch]
                if 2 * k < g.nb:
                    value = pltpu.roll(value, HALF, 1)
                    for j in range(2):
                        i = g.na + 2 * k + j
                        if 1 <= i <= g.bl:
                            at = (b * g.bl + i) * pitch
                            r.gs1[at : at + pitch, :] = value[j * pitch : (j + 1) * pitch]
        def entry_kernel(k, carry):
            gv = r.gs1[pl.ds(aligned((k + 1) * pitch, 8), pitch), :]
            turned = [pltpu.roll(gv, pitch - 1, 0), gv, pltpu.roll(gv, 1, 0)]
            out = []
            for u in range(3):
                av = r.a1[pl.ds(aligned((k + 1 + u) * pitch, 8), pitch), :]
                for v in range(3):
                    out.append(carry[3 * u + v] + fold(av * turned[v]))
            return tuple(out)

        zero = jnp.zeros((8, LANE), F32)
        sums = repeat(g.hl, entry_kernel, (zero,) * 9, UN_EK)
        for j in range(9):
            r.dke[s, j : j + 1, :] = rowsum(sums[j])

        to_images(r.dke.at[s], r.dke.at[s], r.dke_ss.at[0], r.dke_rs.at[0])

        taps = flip(taps_in)

        def in_grad(row):
            block = [r.gs1[pl.ds(aligned((row + u) * pitch, 8), pitch), :] for u in range(3)]
            h = r.x32[pl.ds(aligned((row + 1) * pitch, 8), pitch), :]
            sig = sigmoid(h)
            return conv_row(block, taps) * (sig * (1.0 + h * (1.0 - sig)))

        r.tmp[0] = jnp.zeros((48, LANE), F32)

        def in_rows(k, _):
            r.tmp[0, pl.ds(0, pitch_s, stride=2), :] = r.sidecp[
                pl.ds(aligned(k * pitch_s, 8), pitch_s), :]
            value = in_grad(2 * k) + r.tmp[0, 0:pitch, :]
            r.m_gin[2 * k, :, 0, :] = value[0 : g.wl, 0 : g.ci]
            return 0

        def in_odd_rows(k, _):
            r.m_gin[2 * k + 1, :, 0, :] = in_grad(2 * k + 1)[0 : g.wl, 0 : g.ci]
            return 0

        repeat(g.hs, in_rows, 0, UN_IR)
        repeat(g.hl // 2, in_odd_rows, 0, UN_IR)

        y_gather(2)
        plane_sum_z_send(6)
        z_gather(4)
        y_gather(3)
        all_gather(5)
        finish_block(2)
        all_gather(6)
        y_gather(4)
        output_landed()
        finish_entry(5)
        finish_halves()
        finish_entry(6)

        block = r.dke.at[pl.ds(0, g.n_sp - 1)]
        landed(block, r.dke_rs.at[0])
        sends.append(lambda: landed(block, r.dke_ss.at[0]))
        total = r.dke[0]
        for k in range(1, g.n_sp):
            total = total + r.dke[k]
        for u in range(3):
            r.m_dke[u] = total[3 * u : 3 * u + 3, 0 : g.ci]
        for wait in sends:
            wait()

    return kernel


def body(mesh_shape, *args):
    inputs, cotangent, kernel_entry, kernels, project_entry, projects = args[:6]
    g = geometry(mesh_shape, inputs, cotangent, project_entry, projects)
    operands = list(args)
    operands[3] = jnp.transpose(kernels, (1, 2, 0, 3))
    operands[4] = jnp.transpose(project_entry, (1, 0, 2))
    operands[5] = jnp.transpose(projects, (1, 0, 2))
    operands = [pltpu.with_memory_space_constraint(o, pltpu.HBM) for o in operands]
    table = scratch_table(g)
    names = list(table)
    results = [
        (g.hs, g.ws, 1, g.cc),
        (g.hl, g.wl, 1, g.ci),
        kernel_entry.shape,
        operands[3].shape,
        operands[4].shape,
        operands[5].shape,
    ] + [(6, g.cc)] * 4
    results = [jax.ShapeDtypeStruct(shape, F32) for shape in results]
    vmem = pl.BlockSpec(memory_space=pltpu.VMEM)
    parts = pl.pallas_call(
        make_kernel(g, names),
        out_shape=[pltpu.VMEM(o.shape, o.dtype) for o in results],
        in_specs=[vmem] * 10,
        out_specs=[vmem] * 10,
        scratch_shapes=list(table.values()),
        compiler_params=pltpu.CompilerParams(
            collective_id=0, has_side_effects=True, vmem_limit_bytes=54 << 20),
    )(*operands)

    def write(*refs):
        copies = [
            pltpu.make_async_copy(refs[k], refs[10 + k], refs[20].at[k]) for k in range(10)
        ]
        for copy in copies:
            copy.start()
        for copy in copies:
            copy.wait()

    out = pl.pallas_call(
        write,
        out_shape=results,
        in_specs=[vmem] * 10,
        out_specs=[pl.BlockSpec(memory_space=pl.ANY)] * 10,
        scratch_shapes=[pltpu.SemaphoreType.DMA((10,))],
        compiler_params=pltpu.CompilerParams(vmem_limit_bytes=16 << 20),
    )(*parts)
    out = list(out)
    out[0] = jnp.transpose(out[0], (2, 0, 1, 3))
    out[1] = jnp.transpose(out[1], (2, 0, 1, 3))
    out[3] = jnp.transpose(out[3], (2, 0, 1, 3))
    out[4] = jnp.transpose(out[4], (1, 0, 2))
    out[5] = jnp.transpose(out[5], (1, 0, 2))
    return tuple(out)


def solution(mesh):
    mesh_shape = dict(mesh.shape)
    wide = P("sp", None, None, "ch")
    row = P(None, "ch")
    mid = P(None, "ch", None)
    return jax.shard_map(
        lambda *args: body(mesh_shape, *args),
        mesh=mesh,
        in_specs=(wide, wide, P(None, None, "ch"), P(None, None, None, "ch"), mid, mid,
                  row, row, row, row),
        out_specs=(wide, wide, P(None, None, "ch"), P(None, None, None, "ch"), mid, mid,
                   row, row, row, row),
        check_vma=False,
    )
```

```python
import math
import types

import jax
import jax.numpy as jnp
from jax import lax
from jax.experimental import pallas as pl
from jax.experimental.pallas import tpu as pltpu
from jax.sharding import PartitionSpec as P

MESH = pl.DeviceIdType.MESH
EPSILON = 0.001
MOMENTUM = 0.5
LANE = 128
HALF = 64
F32 = jnp.float32
BF16 = jnp.bfloat16


def round_up(value, step):
    return -(-value // step) * step


UN_S, UN_L, UN_ES, UN_EC, UN_SR, UN_IR, UN_EK, UN_W = 12, 10, 4, 4, 4, 4, 4, 4


def aligned(index, step):
    return index if isinstance(index, int) else pl.multiple_of(index, step)


def repeat(count, one, carry, unroll=4):
    def some(k, carry):
        for j in range(unroll):
            carry = one(k * unroll + j, carry)
        return carry

    whole = count // unroll if count > unroll else 0
    if whole:
        carry = lax.fori_loop(0, whole, some, carry)
    for k in range(whole * unroll, count):
        carry = one(k, carry)
    return carry


def sigmoid(values):
    return 0.5 * jnp.tanh(0.5 * values) + 0.5


def dot(left, right, dims=(1, 0), precision=None):
    return lax.dot_general(
        left,
        right,
        (((dims[0],), (dims[1],)), ((), ())),
        precision=precision,
        preferred_element_type=F32,
    )


def fold(value):
    return jnp.sum(value.reshape(value.shape[0] // 8, 8, value.shape[1]), axis=0)


def geometry(mesh_shape, inputs, cotangent, project_entry, projects):
    geo = types.SimpleNamespace()
    geo.n_sp, geo.n_ch = mesh_shape["sp"], mesh_shape["ch"]
    geo.bands = geo.n_ch // 2
    geo.group = geo.n_sp * geo.bands
    _, geo.hl, geo.wl, geo.ci = inputs.shape
    _, geo.hs, geo.ws, geo.cc = cotangent.shape
    geo.cin, geo.chan = project_entry.shape[2], projects.shape[2]
    geo.wide = round_up(geo.chan, 2 * LANE)
    geo.half = geo.wide // 2
    geo.shard = geo.wide // geo.n_ch
    geo.tiles = geo.half // LANE
    geo.pl_, geo.ps = round_up(geo.wl + 1, 8), round_up(geo.ws + 1, 8)
    geo.bs = 2 * math.ceil(geo.hs / (2 * geo.bands))
    geo.bl = 2 * geo.bs
    geo.rs, geo.rl = geo.bs + 2, geo.bl + 2
    geo.na = 2 * math.ceil(geo.rl / 4)
    geo.nb = geo.rl - geo.na
    geo.ka = geo.na * geo.pl_
    geo.kb = geo.nb * geo.pl_
    geo.full = geo.n_ch * LANE
    geo.ny = geo.bands if geo.n_sp % geo.bands == 0 else 1
    geo.nz = geo.n_sp // geo.ny
    geo.tall = geo.shard // 16
    geo.u_mid = geo.tall * (geo.wide // LANE)
    geo.u_dk = round_up(geo.shard, LANE) // LANE
    geo.u_in = geo.tall * (geo.cin // LANE)
    geo.units = [
        round_up(u, geo.n_sp)
        for u in [geo.u_mid] * 3 + [geo.u_mid // 2] * 2 + [geo.u_in + 4 * geo.u_dk, geo.u_in]
    ]
    geo.plane = geo.bands * geo.ny
    geo.count_large = float(geo.n_sp * geo.hl * geo.wl)
    geo.count_small = float(geo.n_sp * geo.hs * geo.ws)
    return geo


IN_NAMES = [
    "inputs",
    "cotangent",
    "kernel_entry",
    "kernels",
    "project_entry",
    "projects",
    "bn_gains",
    "bn_biases",
    "run_means",
    "run_vars",
]
OUT_NAMES = [
    "m_out",
    "m_gin",
    "m_dke",
    "m_dk",
    "m_dwe",
    "m_dw",
    "m_gains",
    "m_biases",
    "m_means",
    "m_vars",
]


def scratch_table(g):
    dma, vm = pltpu.SemaphoreType.DMA, pltpu.VMEM
    small, large = g.rs * g.ps, g.rl * g.pl_
    cp_rows = (g.bands * g.bl + 2) * g.pl_
    x = g.bands
    table = dict(
        x32=vm((cp_rows, LANE), F32),
        a1=vm((cp_rows + 2 * g.pl_, LANE), F32),
        s1=vm((cp_rows, LANE), F32),
        s1pk=vm((x, g.ka, LANE), BF16),
        s1full=vm((g.ka, g.full), BF16),
        sidepk=vm((x, small, LANE), BF16),
        sidefull=vm((small, g.full), BF16),
        sidecp=vm(((x * g.bs + 2) * g.ps, LANE), F32),
        parloc=vm((56, 2 * LANE), F32),
        parx=vm((x, 56, 2 * LANE), F32),
        par=vm((56, g.half), F32),
        place=vm((g.wide, g.wide), BF16),
        place_in=vm((2, g.cin, g.full), BF16),
        wpad=vm((g.shard, g.wide), BF16),
        w=vm((4, g.half, g.wide), BF16),
        we=vm((2, g.half, g.cin), BF16),
        wp=vm((3, g.half, g.full), BF16),
        cotpad=vm(((x * g.bs + 2) * g.ps, 2 * LANE), F32),
        cotx=vm(((x * g.bs + 2) * g.ps, 2 * LANE), BF16),
        cots=vm((x, small, 2 * LANE), BF16),
        picks=vm((x, 2 * LANE, g.half), F32),
        edge_up=vm((2 * g.pl_, g.half), BF16),
        edge_down=vm((4 * g.pl_, g.half), BF16),
        from_below=vm((2 * g.pl_, g.half), BF16),
        from_above=vm((4 * g.pl_, g.half), BF16),
        cot=vm((small, g.half), F32),
        p1=vm((large, g.half), F32),
        a2=vm((large, g.half), F32),
        s2=vm((g.bl * g.pl_, g.wide), BF16),
        p2=vm((large + 3 * g.pl_, g.half), F32),
        tmp=vm((g.tiles, 48, LANE), F32),
        poolraw=vm((small, g.half), F32),
        pside=vm((small, g.half), F32),
        hid=vm((3, small, g.half), F32),
        act=vm((3, small, g.half), F32),
        sm=vm((3, g.bs * g.ps, g.wide), BF16),
        pm=vm((3, small, g.half), F32),
        gb=vm((3, small, g.half), F32),
        gt=vm((3, small, g.half), F32),
        gs=vm((small, g.half), F32),
        rsend=vm((3, small, g.half), BF16),
        rrecv=vm((3, small, g.half), BF16),
        gside=vm((small, g.half), BF16),
        gt2=vm((large, g.half), F32),
        rsend2=vm((large, g.half), BF16),
        rrecv2=vm((large, g.half), BF16),
        gs2=vm((large, g.half), F32),
        gb1=vm((large, g.half), F32),
        g1=vm((large, g.half), BF16),
        essend=vm((g.ka, x * LANE), BF16),
        esrecv=vm((g.ka, x * LANE), BF16),
        essum=vm((x, g.ka, LANE), BF16),
        esr=vm((x, g.ka, LANE), BF16),
        sdsend=vm((small, x * LANE), BF16),
        sdrecv=vm((small, x * LANE), BF16),
        sdsum=vm((x, small, LANE), BF16),
        sdr=vm((x, small, LANE), BF16),
        gs1=vm((cp_rows, LANE), F32),
        outx=vm((x, g.bs * g.ps, 2 * LANE), BF16),
        outs=vm((x, g.bs * g.ps, 2 * LANE), BF16),
        dk=vm((4, 16, g.half), F32),
        pickb=vm((x, g.half, 2 * LANE), BF16),
        dke=vm((g.n_sp, 16, LANE), F32),
        vec=vm((56, g.half), F32),
        ar2=vm((6, g.group, 2, g.half), F32),
        ar4=vm((3, g.group, 4, g.half), F32),
        ar_ss=dma((9,)),
        ar_rs=dma((9,)),
        s1_ss=dma((2 * g.n_ch,)),
        s1_rs=dma((g.n_ch,)),
        sd_ss=dma((2 * g.n_ch,)),
        sd_rs=dma((g.n_ch,)),
        par_ss=dma((x,)),
        par_rs=dma((x,)),
        we_ss=dma((2, x)),
        we_rs=dma((2, x)),
        w_ss=dma((4, 2 * x)),
        w_rs=dma((4, 2 * x)),
        cot_ss=dma((x,)),
        cot_rs=dma((x,)),
        sm_ss=dma((4,)),
        sm_rs=dma((4,)),
        r_ss=dma((4,)),
        r_rs=dma((4,)),
        halo_ss=dma((7, 2)),
        halo_rs=dma((7, 2)),
        es_ss=dma((2,)),
        es_rs=dma((2,)),
        esx_ss=dma((2, x)),
        esx_rs=dma((2, x)),
        out_ss=dma((x,)),
        out_rs=dma((x,)),
        ra_ss=dma((7, g.plane)),
        ra_rs=dma((7, g.plane)),
        rz_ss=dma((7, g.nz)),
        rz_rs=dma((7, g.nz)),
        gz_ss=dma((5, g.nz)),
        gz_rs=dma((5, g.nz)),
        gy_ss=dma((5, g.ny)),
        gy_rs=dma((5, g.ny)),
        ga_ss=dma((2,)),
        ga_rs=dma((2,)),
        dke_ss=dma((1,)),
        dke_rs=dma((1,)),
    )
    for k, u in enumerate(g.units):
        unit = (16, LANE)
        table.update({
            f"part{k}": vm((x, u) + unit, BF16),
            f"plane{k}": vm((g.plane, u // g.ny) + unit, BF16),
            f"ys{k}": vm((u // g.ny,) + unit, BF16),
            f"rzr{k}": vm((g.nz, u // g.n_sp) + unit, BF16),
            f"fin{k}": vm((u,) + unit, BF16),
        })
    return table


def make_kernel(g, scratch_names):
    n_bands, half, shard, tiles = g.bands, g.half, g.shard, g.tiles
    pitch, pitch_s = g.pl_, g.ps
    small, large = g.rs * g.ps, g.rl * g.pl_
    AVG, VAR, T1, T0, INV, ALPHA, BETA, KAPPA, LAM = (6 * k for k in range(9))
    counts = (g.count_large, g.count_large) + (g.count_small,) * 4

    def kernel(*refs):
        r = types.SimpleNamespace(**dict(zip(IN_NAMES + OUT_NAMES + scratch_names, refs)))
        s = lax.axis_index("sp")
        ch = lax.axis_index("ch")
        x = ch // 2
        c = lax.rem(ch, 2)
        me = s * n_bands + x
        yi, zi = lax.rem(s, g.ny), s // g.ny
        sends = []
        older = [0]

        def drain():
            for wait in sends[: older[0]]:
                wait()
            del sends[: older[0]]
            older[0] = 0


        def copy_to(src, dst, send, recv, s_, x_, c_):
            cp = pltpu.make_async_remote_copy(
                src_ref=src,
                dst_ref=dst,
                send_sem=send,
                recv_sem=recv,
                device_id=(s_, x_ * 2 + c_),
                device_id_type=MESH,
            )
            cp.start()
            sends.append(cp.wait_send)

        def landed(ref, sem):
            pltpu.make_async_copy(ref, ref, sem).wait()

        def other_band(k):
            return lax.rem(x + k, n_bands)

        def edge_copy(src_up, dst_up, src_down, dst_down, e):
            up = pltpu.make_async_remote_copy(
                src_up, dst_up, r.halo_ss.at[e, 0], r.halo_rs.at[e, 0],
                device_id=(s, (x - 1) * 2 + c), device_id_type=MESH)
            down = pltpu.make_async_remote_copy(
                src_down, dst_down, r.halo_ss.at[e, 1], r.halo_rs.at[e, 1],
                device_id=(s, (x + 1) * 2 + c), device_id_type=MESH)

            @pl.when(x > 0)
            def _():
                up.start()

            @pl.when(x < n_bands - 1)
            def _():
                down.start()

            def finish():
                @pl.when(x < n_bands - 1)
                def _():
                    landed(dst_up, r.halo_rs.at[e, 0])

                @pl.when(x > 0)
                def _():
                    landed(dst_down, r.halo_rs.at[e, 1])

            def sent():
                @pl.when(x > 0)
                def _():
                    up.wait_send()

                @pl.when(x < n_bands - 1)
                def _():
                    down.wait_send()

            sends.append(sent)
            return finish

        def edges(ref, e):
            first, last = pl.ds(pitch_s, pitch_s), pl.ds(g.bs * pitch_s, pitch_s)
            return edge_copy(
                ref.at[first], ref.at[pl.ds((g.bs + 1) * pitch_s, pitch_s)],
                ref.at[last], ref.at[pl.ds(0, pitch_s)], e)

        def flipped(value, key):
            out, bit = 0, 1
            while bit <= key:
                here = lax.rem(value // bit, 2)
                out = out + bit * (1 - here if key & bit else here)
                bit *= 2
            return out + (value // bit) * bit

        def hops(key):
            return key // (n_bands * g.ny) + key // n_bands % g.ny + key % n_bands

        few = g.group <= 16
        keys = sorted(range(1, g.group), key=hops, reverse=True) if few else []
        peers = [
            (flipped(s, key // n_bands), flipped(x, key % n_bands)) for key in keys
        ]

        def to_group(src, dst, send, recv, pick=None):
            def one(s_, x_):
                pltpu.make_async_remote_copy(
                    src if pick is None else pick(s_, x_), dst, send, recv,
                    device_id=(s_, x_ * 2 + c), device_id_type=MESH).start()

            for s_, x_ in peers:
                one(s_, x_)

            def loop(k, _):
                to = lax.rem(me + k, g.group)
                one(to // n_bands, lax.rem(to, n_bands))
                return 0

            if not few:
                lax.fori_loop(1, g.group, loop, 0)

        sp_keys = sorted(range(1, g.n_sp), key=lambda k: hops(k * n_bands), reverse=True)
        sp_peers = [flipped(s, key) for key in sp_keys] if few else []

        def to_images(src, dst, send, recv):
            def one(s_):
                pltpu.make_async_remote_copy(
                    src, dst, send, recv, device_id=(s_, ch), device_id_type=MESH).start()

            for s_ in sp_peers:
                one(s_)

            def loop(k, _):
                one(lax.rem(s + k, g.n_sp))
                return 0

            if not few:
                lax.fori_loop(1, g.n_sp, loop, 0)

        def sum_start(buf, at, e, rows):
            older[0] = len(sends)
            for k, row in enumerate(rows):
                buf[at, me, k : k + 1, :] = row

            to_group(buf.at[at, me], buf.at[at, me], r.ar_ss.at[e], r.ar_rs.at[e])

        def sum_finish(buf, at, e):
            drain()
            block = buf.at[at, pl.ds(0, g.group - 1)]
            landed(block, r.ar_rs.at[e])
            sends.append(lambda: landed(block, r.ar_ss.at[e]))
            total = buf[at, 0]
            for k in range(1, g.group):
                total = total + buf[at, k]
            return total

        def fill(ref, start, rows):
            ref[pl.ds(start, rows)] = jnp.zeros((rows,) + ref.shape[1:], ref.dtype)

        def fill_all(ref, step):
            def one(i, _):
                ref[pl.ds(aligned(i * step, 8), step)] = jnp.zeros(
                    (step,) + ref.shape[1:], ref.dtype)
                return 0

            repeat(ref.shape[0] // step, one, 0, 1)

        def lane(t):
            return pl.ds(t * LANE, LANE)

        def col_mask(width, breadth):
            at = lax.broadcasted_iota(jnp.int32, (width, LANE), 0)
            return jnp.where(at < breadth, 1.0, 0.0).astype(F32)

        def row_ok(row, height):
            return jnp.where((row >= 0) & (row < height), 1.0, 0.0).astype(F32)

        mask_l, mask_s = col_mask(pitch, g.wl), col_mask(pitch_s, g.ws)

        def vrow(kind, layer, t):
            return r.vec[kind + layer : kind + layer + 1, lane(t)]

        def taps_of(q, t):
            return [
                [r.par[16 + 4 * (3 * u + v) + q : 17 + 4 * (3 * u + v) + q, lane(t)] for v in range(3)]
                for u in range(3)
            ]

        def flip(taps):
            return [[taps[2 - u][2 - v] for v in range(3)] for u in range(3)]

        def conv_row(rows, taps):
            width = rows[0].shape[0]
            side = [
                rows[0] * taps[0][v] + rows[1] * taps[1][v] + rows[2] * taps[2][v]
                for v in range(3)
            ]
            return side[1] + pltpu.roll(side[0], 1, 0) + pltpu.roll(side[2], width - 1, 0)

        def store_moments(layer, total, square):
            n = counts[layer]
            average = total / n
            variance = square / n - average * average
            inverse = lax.rsqrt(variance + EPSILON)
            alpha = inverse * r.par[layer : layer + 1, :]
            r.vec[AVG + layer : AVG + layer + 1, :] = average
            r.vec[VAR + layer : VAR + layer + 1, :] = variance
            r.vec[INV + layer : INV + layer + 1, :] = inverse
            r.vec[ALPHA + layer : ALPHA + layer + 1, :] = alpha
            r.vec[BETA + layer : BETA + layer + 1, :] = (
                r.par[6 + layer : 7 + layer, :] - average * alpha)

        def store_back(layer, total, product):
            n = counts[layer]
            average = r.vec[AVG + layer : AVG + layer + 1, :]
            inverse = r.vec[INV + layer : INV + layer + 1, :]
            alpha = r.vec[ALPHA + layer : ALPHA + layer + 1, :]
            scaled = inverse * (product - average * total)
            r.vec[T0 + layer : T0 + layer + 1, :] = total
            r.vec[T1 + layer : T1 + layer + 1, :] = scaled
            kappa = -alpha * inverse * scaled / n
            r.vec[KAPPA + layer : KAPPA + layer + 1, :] = kappa
            r.vec[LAM + layer : LAM + layer + 1, :] = -alpha * total / n - kappa * average

        def rowsum(value):
            return jnp.sum(value, axis=0, keepdims=True)

        barrier = pltpu.get_barrier_semaphore()

        def greet(s_, x_):
            pl.semaphore_signal(
                barrier, inc=1, device_id=(s_, x_ * 2 + c), device_id_type=MESH)

        def greet_some(k, _):
            to = lax.rem(me + k, g.group)
            greet(to // n_bands, lax.rem(to, n_bands))
            return 0

        for s_, x_ in peers:
            greet(s_, x_)
        if not few:
            lax.fori_loop(1, g.group, greet_some, 0)
        pl.semaphore_signal(
            barrier, inc=1, device_id=(s, x * 2 + 1 - c), device_id_type=MESH)

        fill_all(r.x32, pitch)
        fill_all(r.a1, pitch)
        fill(r.s1, 0, pitch)
        fill(r.s1, (g.hl + 1) * pitch, (n_bands * g.bl + 1 - g.hl) * pitch)
        fill(r.parloc, 0, 56)
        fill_all(r.wpad, 16)
        fill(r.tmp, 0, tiles)
        fill(r.p2, 0, 3 * pitch)
        fill(r.p2, (g.bl + 3) * pitch, 2 * pitch)
        fill(r.gb1, 0, pitch)
        fill(r.gb1, (g.bl + 1) * pitch, pitch)
        fill(r.dk, 0, 4)
        r.dke[s] = jnp.zeros((16, LANE), F32)
        for first, edge in ((0, x == 0), ((g.bs + 1) * pitch_s, x == n_bands - 1)):
            @pl.when(edge)
            def _():
                for i in range(3):
                    for ref in (r.pm, r.gb):
                        ref[i, first : first + pitch_s] = jnp.zeros((pitch_s, half), F32)

        def entry_silu(row, _):
            value = r.inputs[0, row].astype(F32)
            r.x32[pl.ds(aligned((row + 1) * pitch, 8), g.wl), 0 : g.ci] = value
            r.a1[pl.ds(aligned((row + 2) * pitch, 8), g.wl), 0 : g.ci] = value * sigmoid(value)
            return 0

        repeat(g.hl, entry_silu, 0, UN_ES)
        r.parloc[0:6, 0 : g.cc] = r.bn_gains[...]
        r.parloc[6:12, 0 : g.cc] = r.bn_biases[...]
        for j in range(9):
            at = 16 + 4 * j
            r.parloc[at : at + 4, 0 : g.cc] = r.kernels[j // 3, j % 3].astype(F32)
        taps_in = [
            [r.kernel_entry[u].astype(F32)[v : v + 1, :] for v in range(3)] for u in range(3)
        ]
        pad_in = jnp.zeros((1, LANE - g.ci), F32)
        taps_in = [[jnp.concatenate([k, pad_in], axis=1) for k in row] for row in taps_in]

        def entry_conv(row, _):
            rows = [
                r.a1[pl.ds(aligned((row + 1 + u) * pitch, 8), pitch), :] for u in range(3)
            ]
            r.s1[pl.ds(aligned((row + 1) * pitch, 8), pitch), :] = (
                conv_row(rows, taps_in) * mask_l)
            return 0

        repeat(g.hl, entry_conv, 0, UN_EC)
        for b in range(n_bands):
            for k in range(g.na // 2):
                packed = r.s1[(b * g.bl + 2 * k) * pitch : (b * g.bl + 2 * k + 2) * pitch, :]
                if 2 * k < g.nb:
                    at = (b * g.bl + g.na + 2 * k) * pitch
                    packed = packed + pltpu.roll(r.s1[at : at + 2 * pitch, :], HALF, 1)
                r.s1pk[b, 2 * k * pitch : (2 * k + 2) * pitch, :] = packed.astype(BF16)
        for e in range(2):
            r.wpad[0 : g.cc, 0 : g.cin] = r.project_entry[:, e, :]
            r.we[e, pl.ds(aligned(x * shard, 16), shard), :] = r.wpad[:, 0 : g.cin]

        pl.semaphore_wait(barrier, g.group)
        tile = c * n_bands + x

        def full_lanes(t):
            return pl.ds(aligned(t * LANE, LANE), LANE)

        for k in range(1, n_bands):
            b = other_band(k)
            copy_to(r.s1pk.at[b], r.s1full.at[:, full_lanes(tile)],
                    r.s1_ss.at[k], r.s1_rs.at[tile], s, b, c)
        copy_to(r.s1pk.at[x], r.s1full.at[:, full_lanes(tile)],
                r.s1_ss.at[0], r.s1_rs.at[tile], s, x, 1 - c)
        r.s1full[:, full_lanes(tile)] = r.s1pk[x]
        for k in range(1, n_bands):
            mine = r.we.at[0, pl.ds(aligned(x * shard, 16), shard)]
            copy_to(mine, mine, r.we_ss.at[0, k], r.we_rs.at[0, x], s, other_band(k), c)

        for b in range(n_bands):
            spot = lax.broadcasted_iota(jnp.int32, (2 * LANE, half), 1) - b * shard
            r.picks[b] = jnp.where(
                (spot == lax.broadcasted_iota(jnp.int32, (2 * LANE, half), 0)) & (spot < g.cc),
                1.0, 0.0).astype(F32)
        r.parx[x] = r.parloc[...]

        def send_vectors():
            for k in range(1, n_bands):
                copy_to(r.parx.at[x], r.parx.at[x], r.par_ss.at[k], r.par_rs.at[x],
                        s, other_band(k), c)

        def vectors_landed():
            total = 0.0
            for k in range(1, n_bands):
                b = other_band(k)
                landed(r.parx.at[b], r.par_rs.at[b])
            for b in range(n_bands):
                total = total + dot(r.parx[b], r.picks[b], precision=lax.Precision.HIGHEST)
            r.par[...] = total

        r.sidecp[...] = jnp.zeros_like(r.sidecp)

        def side_row(row, _):
            at = aligned((2 * row + 1) * pitch, 8)
            r.sidecp[pl.ds(aligned((row + 1) * pitch_s, 8), g.ws), :] = r.x32[
                pl.ds(at, g.ws, stride=2), :]
            return 0

        repeat(g.hs, side_row, 0, UN_SR)
        for b in range(n_bands):
            r.sidepk[b] = r.sidecp[b * g.bs * pitch_s : b * g.bs * pitch_s + small, :].astype(BF16)
        r.sidefull[:, full_lanes(tile)] = r.sidepk[x]

        def send_side():
            for k in range(1, n_bands):
                b = other_band(k)
                copy_to(r.sidepk.at[b], r.sidefull.at[:, full_lanes(tile)],
                        r.sd_ss.at[k], r.sd_rs.at[tile], s, b, c)
            copy_to(r.sidepk.at[x], r.sidefull.at[:, full_lanes(tile)],
                    r.sd_ss.at[0], r.sd_rs.at[tile], s, x, 1 - c)
            for k in range(1, n_bands):
                mine = r.we.at[1, pl.ds(aligned(x * shard, 16), shard)]
                copy_to(mine, mine, r.we_ss.at[1, k], r.we_rs.at[1, x], s, other_band(k), c)

        fill_all(r.cotpad, pitch_s)

        def cot_row(row, _):
            r.cotpad[pl.ds(aligned((row + 1) * pitch_s, 8), g.ws), 0 : g.cc] = (
                r.cotangent[0, row].astype(F32))
            return 0

        repeat(g.hs, cot_row, 0, UN_SR)
        r.cotx[...] = r.cotpad[...].astype(BF16)
        r.cots[x] = r.cotx[pl.ds(aligned(x * g.bs * pitch_s, 16), small), :]

        def send_cotangent():
            for k in range(1, n_bands):
                b = other_band(k)
                copy_to(r.cotx.at[pl.ds(aligned(b * g.bs * pitch_s, 16), small)], r.cots.at[x],
                        r.cot_ss.at[k], r.cot_rs.at[x], s, b, c)

        def channel_place(rows, k0, cols, cut, offset):
            k_at = k0 + lax.broadcasted_iota(jnp.int32, (rows, cols), 0)
            p_at = lax.broadcasted_iota(jnp.int32, (rows, cols), 1)
            want = k_at + offset(0)
            for j in range(1, g.n_ch):
                jump = offset(j) - offset(j - 1)
                want = want + jnp.where(k_at >= j * cut, jump, 0)
            return jnp.where(want == p_at, 1.0, 0.0).astype(BF16)

        def offset_wide(j):
            return (j % 2) * half + (j // 2) * shard - j * g.cc

        def offset_in(j):
            return ((j % 2) * n_bands + j // 2) * LANE - j * g.ci

        r.place_in[0] = channel_place(g.cin, 0, g.full, g.ci, offset_in)
        r.place_in[1] = channel_place(
            g.cin, 0, g.full, g.ci, lambda j: offset_in(j) + HALF)
        def place_rows(k, _):
            at = aligned(k * 64, 64)
            r.place[pl.ds(at, 64), :] = channel_place(64, at, g.wide, g.cc, offset_wide)
            return 0

        repeat(g.wide // 64, place_rows, 0, 2)
        fill_all(r.wpad, 16)

        def weight_prepare(q):
            r.wpad[0 : g.cc, 0 : g.chan] = r.projects[:, q, :]
            r.w[q, pl.ds(aligned(x * shard, 16), shard), :] = dot(
                r.wpad[...], r.place[...]).astype(BF16)

        odd = lax.rem(yi, 2) if g.ny > 1 else 0
        pair = zi * g.ny + yi + 1 - 2 * odd
        halves = 2 if g.ny > 1 else 1

        def shard_part(q, b, part):
            size = shard // halves
            return r.w.at[q, pl.ds(aligned(b * shard + part * size, 16), size)]

        def weight_send(q):
            mine = shard_part(q, x, odd)
            for k in range(1, n_bands):
                copy_to(mine, mine, r.w_ss.at[q, k], r.w_rs.at[q, x], s, other_band(k), c)

        def weight_forward(q):
            for k in range(1, n_bands):
                b = other_band(k)
                got = shard_part(q, b, odd)
                landed(got, r.w_rs.at[q, b])
                if halves > 1:
                    copy_to(got, got, r.w_ss.at[q, n_bands + k], r.w_rs.at[q, n_bands + b],
                            pair, x, c)

        def weight_landed(q):
            for k in range(1, n_bands):
                b = other_band(k)
                if halves > 1:
                    landed(shard_part(q, b, 1 - odd), r.w_rs.at[q, n_bands + b])

        weight_prepare(0)
        weight_send(0)
        weight_prepare(1)
        weight_prepare(2)

        for k in range(1, n_bands):
            t = c * n_bands + other_band(k)
            landed(r.s1full.at[:, full_lanes(t)], r.s1_rs.at[t])
            copy_to(r.s1full.at[:, full_lanes(t)], r.s1full.at[:, full_lanes(t)],
                    r.s1_ss.at[g.n_ch + k], r.s1_rs.at[t], s, x, 1 - c)

        for k in range(1, n_bands):
            b = other_band(k)
            landed(r.we.at[0, pl.ds(aligned(b * shard, 16), shard)], r.we_rs.at[0, b])
        for a in range(2):
            r.wp[a] = dot(r.we[0], r.place_in[a]).astype(BF16)

        for k in range(n_bands):
            t = (1 - c) * n_bands + k
            landed(r.s1full.at[:, full_lanes(t)], r.s1_rs.at[t])
        r.p1[0 : g.ka, :] = dot(r.s1full[...], r.wp[0], (1, 1))
        r.p1[g.ka : large, :] = dot(r.s1full[0 : g.kb, :], r.wp[1], (1, 1))

        def moments(ref, first, rows, width):
            out = [[], []]
            for t in range(tiles):
                def one(k, carry):
                    v = ref[pl.ds(aligned((first + k) * width, 8), width), lane(t)]
                    return (carry[0] + fold(v), carry[1] + fold(v * v))

                zero = jnp.zeros((8, LANE), F32)
                total, square = repeat(rows, one, (zero, zero), UN_S if width == pitch_s else UN_L)
                out[0].append(rowsum(total))
                out[1].append(rowsum(square))
            return [jnp.concatenate(o, axis=1) for o in out]

        sum_start(r.ar2, 0, 0, moments(r.p1, 1, g.bl, pitch))
        send_vectors()
        send_side()
        weight_send(1)
        weight_send(2)
        weight_forward(0)
        weight_prepare(3)
        vectors_landed()
        total = sum_finish(r.ar2, 0, 0)
        store_moments(0, total[0:1], total[1:2])

        for t in range(tiles):
            alpha, beta = vrow(ALPHA, 0, t), vrow(BETA, 0, t)

            def one(k, _):
                at = pl.ds(aligned(k * pitch, 8), pitch)
                h = r.p1[at, lane(t)] * alpha + beta
                ok = mask_l * row_ok(x * g.bl + k - 1, g.hl)
                r.a2[at, lane(t)] = h * sigmoid(h) * ok
                return 0

            repeat(g.rl, one, 0, UN_L)
        mine_lanes = aligned(c * half, LANE)
        their_lanes = aligned((1 - c) * half, LANE)

        def own_tile(t):
            return pl.ds(aligned(c * half + t * LANE, LANE), LANE)

        def conv_pairs(source, q, target, row0, rows, height, width, mask):
            for t in range(tiles):
                taps = taps_of(q, t)

                def one(k, _):
                    block = [
                        source[pl.ds(aligned((2 * k + u) * width, 8), width), lane(t)]
                        for u in range(4)
                    ]
                    out = [
                        conv_row(block[j : j + 3], taps) * (mask * row_ok(row0 + 2 * k + j, height))
                        for j in range(2)
                    ]
                    target[pl.ds(aligned(k * 2 * width, 16), 2 * width), own_tile(t)] = (
                        jnp.concatenate(out, axis=0).astype(BF16))
                    return 0

                repeat(rows // 2, one, 0, UN_S if width == pitch_s else UN_L)

        conv_pairs(r.a2, 0, r.s2, x * g.bl, g.bl, g.hl, pitch, mask_l)

        def swap_start(ref, e):
            mine = ref.at[:, pl.ds(mine_lanes, half)]
            copy_to(mine, mine, r.sm_ss.at[e], r.sm_rs.at[e], s, x, 1 - c)

        def swap_landed(ref, e):
            landed(ref.at[:, pl.ds(their_lanes, half)], r.sm_rs.at[e])

        swap_start(r.s2, 0)
        weight_landed(0)
        rows_all = g.bl * pitch
        step = rows_all // 2
        for k in range(2):
            rows = pl.ds(k * step, step)
            r.p2[3 * pitch + k * step : 3 * pitch + (k + 1) * step, :] = dot(
                r.s2[rows, pl.ds(mine_lanes, half)], r.w[0, :, pl.ds(mine_lanes, half)], (1, 1))
        for k in range(1, n_bands):
            t = c * n_bands + other_band(k)
            landed(r.sidefull.at[:, full_lanes(t)], r.sd_rs.at[t])
            copy_to(r.sidefull.at[:, full_lanes(t)], r.sidefull.at[:, full_lanes(t)],
                    r.sd_ss.at[g.n_ch + k], r.sd_rs.at[t], s, x, 1 - c)
        swap_landed(r.s2, 0)
        for k in range(2):
            rows = pl.ds(k * step, step)
            at = slice(3 * pitch + k * step, 3 * pitch + (k + 1) * step)
            r.p2[at, :] = r.p2[at, :] + dot(
                r.s2[rows, pl.ds(their_lanes, half)], r.w[0, :, pl.ds(their_lanes, half)], (1, 1))
        for k in range(1, n_bands):
            b = other_band(k)
            landed(r.we.at[1, pl.ds(aligned(b * shard, 16), shard)], r.we_rs.at[1, b])
        r.wp[2] = dot(r.we[1], r.place_in[0]).astype(BF16)
        for k in range(n_bands):
            t = (1 - c) * n_bands + k
            landed(r.sidefull.at[:, full_lanes(t)], r.sd_rs.at[t])
        r.pside[...] = dot(r.sidefull[...], r.wp[2], (1, 1))
        sum_start(r.ar4, 0, 1,
                  moments(r.p2, 3, g.bl, pitch) + moments(r.pside, 1, g.bs, pitch_s))
        r.edge_up[...] = r.p2[3 * pitch : 5 * pitch, :].astype(BF16)
        r.edge_down[...] = r.p2[(g.bl - 1) * pitch : (g.bl + 3) * pitch, :].astype(BF16)
        edges_done = edge_copy(r.edge_up, r.from_below, r.edge_down, r.from_above, 0)
        weight_send(3)
        weight_forward(1)

        edges_done()

        @pl.when(x > 0)
        def _():
            r.p2[0 : 3 * pitch, :] = r.from_above[...].astype(F32)[pitch : 4 * pitch]

        @pl.when(x < n_bands - 1)
        def _():
            r.p2[(g.bl + 3) * pitch : (g.bl + 5) * pitch, :] = r.from_below[...].astype(F32)

        for t in range(tiles):
            def one(k, _):
                v = (r.p2[pl.ds(aligned(2 * k * pitch, 8), pitch), lane(t)]
                     + r.p2[pl.ds(aligned((2 * k + 1) * pitch, 8), pitch), lane(t)]
                     + r.p2[pl.ds(aligned((2 * k + 2) * pitch, 8), pitch), lane(t)])
                r.tmp[t, 0:pitch, :] = v + pltpu.roll(v, 1, 0) + pltpu.roll(v, pitch - 1, 0)
                r.poolraw[pl.ds(aligned(k * pitch_s, 8), pitch_s), lane(t)] = r.tmp[
                    t, pl.ds(0, pitch_s, stride=2), :]
                return 0

            repeat(g.rs, one, 0, UN_S)
        weight_forward(2)
        total = sum_finish(r.ar4, 0, 1)
        store_moments(1, total[0:1], total[1:2])
        store_moments(2, total[2:3], total[3:4])

        at_col = lax.broadcasted_iota(jnp.int32, (pitch_s, LANE), 0)
        col_count = mask_s * (
            1.0
            + jnp.where(at_col > 0, 1.0, 0.0)
            + jnp.where(2 * at_col + 1 < g.wl, 1.0, 0.0)) * (1.0 / 9.0)

        def window_count(row):
            inside = jnp.where(row > 0, 1.0, 0.0) + jnp.where(2 * row + 1 < g.hl, 1.0, 0.0) + 1.0
            return col_count * (inside.astype(F32) * row_ok(row, g.hs))

        for t in range(tiles):
            alpha, beta = vrow(ALPHA, 1, t) * (1.0 / 9.0), vrow(BETA, 1, t)
            alpha_2, beta_2 = vrow(ALPHA, 2, t), vrow(BETA, 2, t)

            def one(k, _):
                at = pl.ds(aligned(k * pitch_s, 8), pitch_s)
                row = x * g.bs + k - 1
                ok = mask_s * row_ok(row, g.hs)
                h = (r.poolraw[at, lane(t)] * alpha + window_count(row) * beta
                     + r.pside[at, lane(t)] * alpha_2 + beta_2) * ok
                r.hid[0, at, lane(t)] = h
                r.act[0, at, lane(t)] = h * sigmoid(h)
                return 0

            repeat(g.rs, one, 0, UN_S)

        def make_picks():
            for b in range(n_bands):
                spot_b = lax.broadcasted_iota(jnp.int32, (half, 2 * LANE), 0) - b * shard
                r.pickb[b] = jnp.where(
                    (spot_b == lax.broadcasted_iota(jnp.int32, (half, 2 * LANE), 1))
                    & (spot_b < g.cc), 1.0, 0.0).astype(BF16)

        own_rows = slice(pitch_s, (g.bs + 1) * pitch_s)
        for i in range(3):
            if i > 0:
                for t in range(tiles):
                    alpha, beta = vrow(ALPHA, 2 + i, t), vrow(BETA, 2 + i, t)

                    def one(k, _):
                        at = pl.ds(aligned(k * pitch_s, 8), pitch_s)
                        ok = mask_s * row_ok(x * g.bs + k - 1, g.hs)
                        h = (r.pm[i - 1, at, lane(t)] * alpha + beta) * ok
                        r.hid[i, at, lane(t)] = h
                        r.act[i, at, lane(t)] = h * sigmoid(h)
                        return 0

                    repeat(g.rs, one, 0, UN_S)
            conv_pairs(r.act.at[i], i + 1, r.sm.at[i], x * g.bs, g.bs, g.hs,
                       pitch_s, mask_s)
            swap_start(r.sm.at[i], 1 + i)
            weight_landed(1 + i)
            part = dot(r.sm[i, :, pl.ds(mine_lanes, half)],
                       r.w[1 + i, :, pl.ds(mine_lanes, half)], (1, 1))
            swap_landed(r.sm.at[i], 1 + i)
            r.pm[i, own_rows, :] = part + dot(
                r.sm[i, :, pl.ds(their_lanes, half)],
                r.w[1 + i, :, pl.ds(their_lanes, half)], (1, 1))
            if i < 2:
                sum_start(r.ar2, 1 + i, 2 + i, moments(r.pm.at[i], 1, g.bs, pitch_s))
                edges_done = edges(r.pm.at[i], 1 + i)
                if i == 0:
                    send_cotangent()
                    weight_forward(3)
                total = sum_finish(r.ar2, 1 + i, 2 + i)
                store_moments(3 + i, total[0:1], total[1:2])
                edges_done()

        def grad_sums(gref, pref, width, first, rows):
            out = [[], []]
            for t in range(tiles):
                def one(k, carry):
                    at = pl.ds(aligned((first + k) * width, 8), width)
                    v = gref[at, lane(t)]
                    return (carry[0] + fold(v), carry[1] + fold(v * pref[at, lane(t)]))

                zero = jnp.zeros((8, LANE), F32)
                a, b = repeat(rows, one, (zero, zero), UN_S if width == pitch_s else UN_L)
                out[0].append(rowsum(a))
                out[1].append(rowsum(b))
            return [jnp.concatenate(o, axis=1) for o in out]

        for k in range(1, n_bands):
            b = other_band(k)
            landed(r.cots.at[b], r.cot_rs.at[b])
        total = 0.0
        for b in range(n_bands):
            total = total + dot(r.cots[b], r.picks[b].astype(BF16))
        r.cot[...] = total
        sum_start(r.ar4, 1, 4,
                  moments(r.pm.at[2], 1, g.bs, pitch_s)
                  + grad_sums(r.cot, r.pm.at[2], pitch_s, 1, g.bs))
        edges_done = edges(r.pm.at[2], 3)
        make_picks()
        total = sum_finish(r.ar4, 1, 4)
        store_moments(5, total[0:1], total[1:2])
        store_back(5, total[2:3], total[3:4])
        edges_done()

        def norm_back(layer, gref, pref, target, rows, width, mask, row0, height):
            for t in range(tiles):
                alpha, kappa, lam = vrow(ALPHA, layer, t), vrow(KAPPA, layer, t), vrow(LAM, layer, t)

                def one(k, _):
                    at = pl.ds(aligned(k * width, 8), width)
                    ok = mask * row_ok(row0 + k, height)
                    target[at, lane(t)] = (
                        gref[at, lane(t)] * alpha + pref[at, lane(t)] * kappa + lam) * ok
                    return 0

                repeat(rows, one, 0, UN_S if width == pitch_s else UN_L)

        def kernel_grad(aref, gref, q, rows, width):
            for t in range(tiles):
                def one(k, carry):
                    gv = gref[pl.ds(aligned((k + 1) * width, 8), width), lane(t)]
                    turned = [pltpu.roll(gv, width - 1, 0), gv, pltpu.roll(gv, 1, 0)]
                    out = []
                    for u in range(3):
                        av = aref[pl.ds(aligned((k + u) * width, 8), width), lane(t)]
                        for v in range(3):
                            out.append(carry[3 * u + v] + fold(av * turned[v]))
                    return tuple(out)

                zero = jnp.zeros((8, LANE), F32)
                sums = repeat(rows, one, (zero,) * 9, UN_S if width == pitch_s else UN_L)
                for j in range(9):
                    r.dk[q, j : j + 1, lane(t)] = rowsum(sums[j])


        def block_of(name, k):
            return getattr(r, f"{name}{k}")

        def put_units(k, value, first, cols):
            value = value[:, first : first + cols].astype(BF16)
            for b in range(n_bands):
                for t in range(cols // LANE):
                    part = value[b * shard : (b + 1) * shard, t * LANE : (t + 1) * LANE]
                    block_of("part", k)[b, t * g.tall : (t + 1) * g.tall] = (
                        part.reshape(g.tall, 16, LANE))

        def put_kernels():
            for q in range(4):
                value = r.dk[q].astype(BF16)
                for b in range(n_bands):
                    part = dot(value, r.pickb[b]).astype(BF16)
                    for t in range(g.u_dk):
                        at = g.u_in + q * g.u_dk + t
                        r.part5[b, at] = part[:, t * LANE : (t + 1) * LANE]

        def plane_send(k):
            part = g.units[k] // g.ny
            me_plane = x * g.ny + yi
            for key in range(1, g.plane):
                to = lax.rem(me_plane + key, g.plane)
                x_, y_ = to // g.ny, lax.rem(to, g.ny)
                copy_to(block_of("part", k).at[x_, pl.ds(y_ * part, part)],
                        block_of("plane", k).at[me_plane],
                        r.ra_ss.at[k, key], r.ra_rs.at[k, me_plane], zi * g.ny + y_, x_, c)

        def plane_sum_z_send(k):
            part = g.units[k] // g.ny
            me_plane = x * g.ny + yi
            total = block_of("part", k)[x, pl.ds(yi * part, part)].astype(F32)
            for key in range(1, g.plane):
                b = lax.rem(me_plane + key, g.plane)
                landed(block_of("plane", k).at[b], r.ra_rs.at[k, b])
                total = total + block_of("plane", k)[b].astype(F32)
            block_of("ys", k)[...] = total.astype(BF16)
            piece = part // g.nz
            for j in range(1, g.nz):
                to = lax.rem(zi + j, g.nz)
                copy_to(block_of("ys", k).at[pl.ds(to * piece, piece)], block_of("rzr", k).at[zi],
                        r.rz_ss.at[k, j], r.rz_rs.at[k, zi], to * g.ny + yi, x, c)

        def z_sum(k):
            part = g.units[k] // g.ny
            piece = part // g.nz
            total = block_of("ys", k)[pl.ds(zi * piece, piece)].astype(F32)
            for j in range(1, g.nz):
                b = lax.rem(zi + j, g.nz)
                landed(block_of("rzr", k).at[b], r.rz_rs.at[k, b])
                total = total + block_of("rzr", k)[b].astype(F32)
            at = pl.ds(yi * part + zi * piece, piece)
            block_of("fin", k)[at] = total.astype(BF16)
            return at

        def z_gather(k):
            at = z_sum(k)
            for j in range(1, g.nz):
                to = lax.rem(zi + j, g.nz)
                copy_to(block_of("fin", k).at[at], block_of("fin", k).at[at],
                        r.gz_ss.at[k, j], r.gz_rs.at[k, zi], to * g.ny + yi, x, c)

        def all_gather(k):
            mine = block_of("fin", k).at[z_sum(k)]
            to_images(mine, mine, r.ga_ss.at[k - 5], r.ga_rs.at[k - 5])

        def y_gather(k):
            part = g.units[k] // g.ny
            piece = part // g.nz
            for j in range(1, g.nz):
                b = lax.rem(zi + j, g.nz)
                landed(block_of("fin", k).at[pl.ds(yi * part + b * piece, piece)],
                       r.gz_rs.at[k, b])
            at = pl.ds(yi * part, part)
            for j in range(1, g.ny):
                to = lax.rem(yi + j, g.ny)
                copy_to(block_of("fin", k).at[at], block_of("fin", k).at[at],
                        r.gy_ss.at[k, j], r.gy_rs.at[k, yi], zi * g.ny + to, x, c)

        def get_units(k, cols):
            tiles_in = [
                block_of("fin", k)[t * g.tall : (t + 1) * g.tall].reshape(shard, LANE)
                for t in range(cols // LANE)
            ]
            return jnp.concatenate(tiles_in, axis=1)

        def y_landed(k):
            part = g.units[k] // g.ny
            for j in range(1, g.ny):
                b = lax.rem(yi + j, g.ny)
                landed(block_of("fin", k).at[pl.ds(b * part, part)], r.gy_rs.at[k, b])

        def finish_block(k):
            y_landed(k)
            value = dot(get_units(k, g.wide), r.place[...], (1, 1))
            r.m_dw[:, 3 - k, :] = value[0 : g.cc, 0 : g.chan]

        def finish_halves():
            y_landed(3)
            y_landed(4)
            value = jnp.concatenate(
                [get_units(3, g.wide // 2), get_units(4, g.wide // 2)], axis=1)
            value = dot(value, r.place[...], (1, 1))
            r.m_dw[:, 0, :] = value[0 : g.cc, 0 : g.chan]

        def finish_entry(k):
            piece = g.units[k] // g.n_sp
            others = block_of("fin", k).at[pl.ds(0, (g.n_sp - 1) * piece)]
            landed(others, r.ga_rs.at[k - 5])
            sends.append(lambda: landed(others, r.ga_ss.at[k - 5]))
            r.m_dwe[:, 6 - k, :] = get_units(k, g.cin).astype(F32)[0 : g.cc]
            if k == 5:
                for q in range(4):
                    at = g.u_in + q * g.u_dk
                    value = jnp.concatenate(
                        [r.fin5[at + t] for t in range(g.u_dk)], axis=1).astype(F32)
                    for j in range(9):
                        r.m_dk[j // 3, j % 3, q : q + 1, :] = value[j : j + 1, 0 : g.cc]

        def output_landed():
            for k in range(1, n_bands):
                b = other_band(k)
                landed(r.outs.at[b], r.out_rs.at[b])
            for b in range(n_bands):
                value = r.outs[b].astype(F32)
                for k in range(g.bs):
                    if b * g.bs + k < g.hs:
                        r.m_out[b * g.bs + k, :, 0, :] = value[
                            k * pitch_s : k * pitch_s + g.ws, 0 : g.cc]

        def send_output():
            for k in range(1, n_bands):
                b = other_band(k)
                copy_to(r.outx.at[b], r.outs.at[x], r.out_ss.at[k], r.out_rs.at[x], s, b, c)

        for i in (2, 1, 0):
            layer = 3 + i
            gref = r.cot if i == 2 else r.gb.at[i + 1]
            norm_back(layer, gref, r.pm.at[i], r.gt.at[i], g.rs, pitch_s, mask_s,
                      x * g.bs - 1, g.hs)
            grad = r.gt[i].astype(BF16)
            r.rsend[i] = dot(grad, r.w[1 + i, :, pl.ds(their_lanes, half)]).astype(BF16)
            copy_to(r.rsend.at[i], r.rrecv.at[i], r.r_ss.at[i], r.r_rs.at[i], s, x, 1 - c)
            part = dot(grad, r.w[1 + i, :, pl.ds(mine_lanes, half)])
            grad = r.gt[i, own_rows, :].astype(BF16)
            put_units(2 - i, dot(grad, r.sm[i], (0, 0)), 0, g.wide)
            landed(r.rrecv.at[i], r.r_rs.at[i])
            r.gs[...] = part + r.rrecv[i].astype(F32)
            rows = [[] for _ in range(4 if i == 0 else 2)]
            for t in range(tiles):
                taps = flip(taps_of(i + 1, t))

                def one(k, carry):
                    block = [
                        r.gs[pl.ds(aligned((k + u) * pitch_s, 8), pitch_s), lane(t)]
                        for u in range(3)
                    ]
                    at = pl.ds(aligned((k + 1) * pitch_s, 8), pitch_s)
                    row = x * g.bs + k
                    h = r.hid[i, at, lane(t)]
                    sig = sigmoid(h)
                    value = conv_row(block, taps) * (sig * (1.0 + h * (1.0 - sig))) * (
                        mask_s * row_ok(row, g.hs))
                    if i == 0:
                        value = value + r.cot[at, lane(t)]
                    r.gb[i, at, lane(t)] = value
                    if i == 0:
                        new = [
                            value, value * r.pside[at, lane(t)],
                            value * window_count(row),
                            value * r.poolraw[at, lane(t)] * (1.0 / 9.0)]
                    else:
                        new = [value, value * r.pm[i - 1, at, lane(t)]]
                    return tuple(a + fold(b) for a, b in zip(carry, new))

                zero = jnp.zeros((8, LANE), F32)
                sums = repeat(g.bs, one, (zero,) * len(rows), UN_S)
                for j, v in enumerate(sums):
                    rows[j].append(rowsum(v))
            rows = [jnp.concatenate(o, axis=1) for o in rows]
            buf, at_e, e = ((r.ar4, 2, 7), (r.ar2, 3, 6), (r.ar2, 4, 5))[i]
            sum_start(buf, at_e, e, rows)
            edges_done = edges(r.gb.at[i], 4 + i)
            plane_send(2 - i)
            if i < 2:
                plane_sum_z_send(1 - i)
            if i == 0:
                z_gather(0)
            kernel_grad(r.act.at[i], r.gs, i + 1, g.bs, pitch_s)
            if i == 2:
                value = []
                for t in range(tiles):
                    h = (r.pm[2, own_rows, lane(t)] * vrow(ALPHA, 5, t) + vrow(BETA, 5, t)
                         + r.hid[0, own_rows, lane(t)])
                    value.append(h.astype(BF16))
                value = jnp.concatenate(value, axis=1)
                for b in range(n_bands):
                    r.outx[b] = dot(value, r.pickb[b]).astype(BF16)
                r.outs[x] = r.outx[x]
            total = sum_finish(buf, at_e, e)
            if i > 0:
                store_back(layer - 1, total[0:1], total[1:2])
            else:
                store_back(2, total[0:1], total[1:2])
                store_back(1, total[2:3], total[3:4])
            edges_done()

        for t in range(tiles):
            alpha, kappa, lam = vrow(ALPHA, 1, t) * (1.0 / 9.0), vrow(KAPPA, 1, t), vrow(LAM, 1, t)

            def spread(v):
                r.tmp[t, pl.ds(0, pitch_s, stride=2), :] = v
                r.tmp[t, pl.ds(1, pitch_s, stride=2), :] = v + pltpu.roll(v, pitch_s - 1, 0)
                return r.tmp[t, 0:pitch, :]

            def one(k, _):
                low = r.gb[0, pl.ds(aligned(k * pitch_s, 8), pitch_s), lane(t)]
                high = r.gb[0, pl.ds(aligned((k + 1) * pitch_s, 8), pitch_s), lane(t)]
                for j, v in enumerate((low + high, high)):
                    row = x * g.bl + 2 * k + j - 1
                    ok = mask_l * row_ok(row, g.hl)
                    p = r.p2[pl.ds(aligned((2 * k + j + 2) * pitch, 8), pitch), lane(t)]
                    r.gt2[pl.ds(aligned((2 * k + j) * pitch, 8), pitch), lane(t)] = (
                        spread(v) * alpha + p * kappa + lam) * ok
                return 0

            repeat(g.bs + 1, one, 0, UN_S)
        for k in range(2):
            at = pl.ds(k * (large // 2), large // 2)
            r.rsend2[at, :] = dot(
                r.gt2[at, :].astype(BF16), r.w[0, :, pl.ds(their_lanes, half)]).astype(BF16)
        copy_to(r.rsend2, r.rrecv2, r.r_ss.at[3], r.r_rs.at[3], s, x, 1 - c)
        for k in range(2):
            at = pl.ds(k * (large // 2), large // 2)
            r.gs2[at, :] = dot(r.gt2[at, :].astype(BF16), r.w[0, :, pl.ds(mine_lanes, half)])
        grad = r.gt2[pitch : (g.bl + 1) * pitch, :].astype(BF16)
        hw = g.wide // 2
        put_units(3, dot(grad, r.s2[:, 0:hw], (0, 0)), 0, hw)
        plane_send(3)
        put_units(4, dot(grad, r.s2[:, hw:], (0, 0)), 0, hw)
        z_gather(1)
        y_gather(0)
        landed(r.rrecv2, r.r_rs.at[3])
        r.gs2[...] = r.gs2[...] + r.rrecv2[...].astype(F32)
        rows = [[], []]
        for t in range(tiles):
            taps = flip(taps_of(0, t))
            alpha, beta = vrow(ALPHA, 0, t), vrow(BETA, 0, t)

            def one(k, carry):
                block = [
                    r.gs2[pl.ds(aligned((k + u) * pitch, 8), pitch), lane(t)] for u in range(3)
                ]
                at = pl.ds(aligned((k + 1) * pitch, 8), pitch)
                p = r.p1[at, lane(t)]
                h = p * alpha + beta
                sig = sigmoid(h)
                value = conv_row(block, taps) * (sig * (1.0 + h * (1.0 - sig))) * (
                    mask_l * row_ok(x * g.bl + k, g.hl))
                r.gb1[at, lane(t)] = value
                return (carry[0] + fold(value), carry[1] + fold(value * p))

            zero = jnp.zeros((8, LANE), F32)
            sums = repeat(g.bl, one, (zero, zero), UN_L)
            for j, v in enumerate(sums):
                rows[j].append(rowsum(v))
        rows = [jnp.concatenate(o, axis=1) for o in rows]
        sum_start(r.ar2, 5, 8, rows)
        plane_sum_z_send(2)
        plane_send(4)

        def own_ok(k, width_rows):
            return jnp.where((k >= 1) & (k <= width_rows), 1.0, 0.0).astype(F32)

        for t in range(tiles):
            alpha, kappa, lam = vrow(ALPHA, 2, t), vrow(KAPPA, 2, t), vrow(LAM, 2, t)

            def one(k, _):
                out = []
                for j in range(2):
                    at = pl.ds(aligned((2 * k + j) * pitch_s, 8), pitch_s)
                    ok = mask_s * (row_ok(x * g.bs + 2 * k + j - 1, g.hs) * own_ok(2 * k + j, g.bs))
                    out.append((r.gb[0, at, lane(t)] * alpha
                                + r.pside[at, lane(t)] * kappa + lam) * ok)
                r.gside[pl.ds(aligned(2 * k * pitch_s, 16), 2 * pitch_s), lane(t)] = (
                    jnp.concatenate(out, axis=0).astype(BF16))
                return 0

            repeat(g.rs // 2, one, 0, UN_S)
        own_tiles = pl.ds(aligned(c * n_bands * LANE, LANE), n_bands * LANE)
        their_tiles = pl.ds(aligned((1 - c) * n_bands * LANE, LANE), n_bands * LANE)
        r.sdsend[...] = dot(r.gside[...], r.wp[2, :, their_tiles]).astype(BF16)
        copy_to(r.sdsend, r.sdrecv, r.es_ss.at[1], r.es_rs.at[1], s, x, 1 - c)
        part = dot(r.gside[...], r.wp[2, :, own_tiles])
        landed(r.sdrecv, r.es_rs.at[1])
        part = part + r.sdrecv[...].astype(F32)
        for b in range(n_bands):
            r.sdsum[b] = part[:, b * LANE : (b + 1) * LANE].astype(BF16)
        for k in range(1, n_bands):
            b = other_band(k)
            copy_to(r.sdsum.at[b], r.sdr.at[x], r.esx_ss.at[1, k], r.esx_rs.at[1, x], s, b, c)
        r.sdr[x] = r.sdsum[x]

        lane_at = lax.broadcasted_iota(jnp.int32, (half, g.full), 1)
        low_lanes = lax.rem(lane_at, LANE) < HALF
        both_place = r.place_in[0] + r.place_in[1]

        value = dot(r.gside[...], r.sidefull[...], (0, 0)).astype(BF16)
        put_units(5, dot(value, both_place, (1, 1)), 0, g.cin)
        kernel_grad(r.a2, r.gs2, 0, g.bl, pitch)
        put_kernels()
        plane_send(5)
        y_gather(1)
        plane_sum_z_send(3)
        total = sum_finish(r.ar2, 5, 8)
        store_back(0, total[0:1], total[1:2])

        for t in range(tiles):
            alpha, kappa, lam = vrow(ALPHA, 0, t), vrow(KAPPA, 0, t), vrow(LAM, 0, t)

            def one(k, _):
                out = []
                for j in range(2):
                    at = pl.ds(aligned((2 * k + j) * pitch, 8), pitch)
                    ok = mask_l * (row_ok(x * g.bl + 2 * k + j - 1, g.hl) * own_ok(2 * k + j, g.bl))
                    out.append((r.gb1[at, lane(t)] * alpha + r.p1[at, lane(t)] * kappa + lam) * ok)
                r.g1[pl.ds(aligned(2 * k * pitch, 16), 2 * pitch), lane(t)] = (
                    jnp.concatenate(out, axis=0).astype(BF16))
                return 0

            repeat(g.rl // 2, one, 0, UN_L)

        def entry_part(lanes):
            a = dot(r.g1[0 : g.ka, :], r.wp[0, :, lanes])
            b = dot(r.g1[g.ka : large, :], r.wp[1, :, lanes])
            if g.kb == g.ka:
                return a + b
            return jnp.concatenate([a[0 : g.kb] + b, a[g.kb :]], axis=0)

        r.essend[...] = entry_part(their_tiles).astype(BF16)
        copy_to(r.essend, r.esrecv, r.es_ss.at[0], r.es_rs.at[0], s, x, 1 - c)
        part = entry_part(own_tiles)
        grad_a = dot(r.g1[0 : g.ka, :], r.s1full[...], (0, 0))
        grad_b = dot(r.g1[g.ka : large, :], r.s1full[0 : g.kb, :], (0, 0))
        value = jnp.where(low_lanes, grad_a, grad_b).astype(BF16)
        put_units(6, dot(value, both_place, (1, 1)), 0, g.cin)
        landed(r.esrecv, r.es_rs.at[0])
        part = part + r.esrecv[...].astype(F32)
        for b in range(n_bands):
            r.essum[b] = part[:, b * LANE : (b + 1) * LANE].astype(BF16)
        for k in range(1, n_bands):
            b = other_band(k)
            copy_to(r.essum.at[b], r.esr.at[x], r.esx_ss.at[0, k], r.esx_rs.at[0, x], s, b, c)
        r.esr[x] = r.essum[x]
        older[0] = len(sends)
        plane_send(6)
        z_gather(2)
        plane_sum_z_send(4)
        z_gather(3)
        plane_sum_z_send(5)
        send_output()
        finish_block(0)
        finish_block(1)

        spot = lax.broadcasted_iota(jnp.int32, (half, 2 * LANE), 0) - x * shard
        pick_own = jnp.where(
            (spot == lax.broadcasted_iota(jnp.int32, (half, 2 * LANE), 1)) & (spot < g.cc),
            1.0, 0.0).astype(F32)
        final = dot(r.vec[0:24, :], pick_own, precision=lax.Precision.HIGHEST)
        final = final[:, 0 : g.cc]
        at_row = lax.broadcasted_iota(jnp.int32, (6, g.cc), 0)
        count = jnp.where(at_row < 2, g.count_large, g.count_small)
        bessel = count / (count - 1.0)
        r.m_means[...] = (1.0 - MOMENTUM) * r.run_means[...] + MOMENTUM * final[0:6]
        r.m_vars[...] = (1.0 - MOMENTUM) * r.run_vars[...] + MOMENTUM * (final[6:12] * bessel)
        r.m_gains[...] = final[12:18]
        r.m_biases[...] = final[18:24]

        for k in range(1, n_bands):
            b = other_band(k)
            landed(r.sdr.at[b], r.esx_rs.at[1, b])
        for b in range(n_bands):
            r.sidecp[b * g.bs * pitch_s : (b + 1) * g.bs * pitch_s, :] = (
                r.sdr[b].astype(F32)[pitch_s : (g.bs + 1) * pitch_s])
        drain()
        for k in range(1, n_bands):
            b = other_band(k)
            landed(r.esr.at[b], r.esx_rs.at[0, b])
        fill(r.gs1, 0, pitch)
        fill(r.gs1, (n_bands * g.bl + 1) * pitch, pitch)
        for b in range(n_bands):
            for k in range(g.na // 2):
                value = r.esr[b, 2 * k * pitch : (2 * k + 2) * pitch, :].astype(F32)
                for j in range(2):
                    i = 2 * k + j
                    if 1 <= i <= g.bl:
                        at = (b * g.bl + i) * pitch
                        r.gs1[at : at + pitch, :] = value[j * pitch : (j + 1) * pitch]
                if 2 * k < g.nb:
                    value = pltpu.roll(value, HALF, 1)
                    for j in range(2):
                        i = g.na + 2 * k + j
                        if 1 <= i <= g.bl:
                            at = (b * g.bl + i) * pitch
                            r.gs1[at : at + pitch, :] = value[j * pitch : (j + 1) * pitch]
        def entry_kernel(k, carry):
            gv = r.gs1[pl.ds(aligned((k + 1) * pitch, 8), pitch), :]
            turned = [pltpu.roll(gv, pitch - 1, 0), gv, pltpu.roll(gv, 1, 0)]
            out = []
            for u in range(3):
                av = r.a1[pl.ds(aligned((k + 1 + u) * pitch, 8), pitch), :]
                for v in range(3):
                    out.append(carry[3 * u + v] + fold(av * turned[v]))
            return tuple(out)

        zero = jnp.zeros((8, LANE), F32)
        sums = repeat(g.hl, entry_kernel, (zero,) * 9, UN_EK)
        for j in range(9):
            r.dke[s, j : j + 1, :] = rowsum(sums[j])

        to_images(r.dke.at[s], r.dke.at[s], r.dke_ss.at[0], r.dke_rs.at[0])

        taps = flip(taps_in)

        def in_grad(row):
            block = [r.gs1[pl.ds(aligned((row + u) * pitch, 8), pitch), :] for u in range(3)]
            h = r.x32[pl.ds(aligned((row + 1) * pitch, 8), pitch), :]
            sig = sigmoid(h)
            return conv_row(block, taps) * (sig * (1.0 + h * (1.0 - sig)))

        r.tmp[0] = jnp.zeros((48, LANE), F32)

        def in_rows(k, _):
            r.tmp[0, pl.ds(0, pitch_s, stride=2), :] = r.sidecp[
                pl.ds(aligned(k * pitch_s, 8), pitch_s), :]
            value = in_grad(2 * k) + r.tmp[0, 0:pitch, :]
            r.m_gin[2 * k, :, 0, :] = value[0 : g.wl, 0 : g.ci]
            return 0

        def in_odd_rows(k, _):
            r.m_gin[2 * k + 1, :, 0, :] = in_grad(2 * k + 1)[0 : g.wl, 0 : g.ci]
            return 0

        repeat(g.hs, in_rows, 0, UN_IR)
        repeat(g.hl // 2, in_odd_rows, 0, UN_IR)

        y_gather(2)
        plane_sum_z_send(6)
        z_gather(4)
        y_gather(3)
        all_gather(5)
        finish_block(2)
        all_gather(6)
        y_gather(4)
        output_landed()
        finish_entry(5)
        finish_halves()
        finish_entry(6)

        block = r.dke.at[pl.ds(0, g.n_sp - 1)]
        landed(block, r.dke_rs.at[0])
        sends.append(lambda: landed(block, r.dke_ss.at[0]))
        total = r.dke[0]
        for k in range(1, g.n_sp):
            total = total + r.dke[k]
        for u in range(3):
            r.m_dke[u] = total[3 * u : 3 * u + 3, 0 : g.ci]
        for wait in sends:
            wait()

    return kernel


def body(mesh_shape, *args):
    inputs, cotangent, kernel_entry, kernels, project_entry, projects = args[:6]
    g = geometry(mesh_shape, inputs, cotangent, project_entry, projects)
    operands = list(args)
    operands[3] = jnp.transpose(kernels, (1, 2, 0, 3))
    operands[4] = jnp.transpose(project_entry, (1, 0, 2))
    operands[5] = jnp.transpose(projects, (1, 0, 2))
    operands = [pltpu.with_memory_space_constraint(o, pltpu.HBM) for o in operands]
    table = scratch_table(g)
    names = list(table)
    results = [
        (g.hs, g.ws, 1, g.cc),
        (g.hl, g.wl, 1, g.ci),
        kernel_entry.shape,
        operands[3].shape,
        operands[4].shape,
        operands[5].shape,
    ] + [(6, g.cc)] * 4
    results = [jax.ShapeDtypeStruct(shape, F32) for shape in results]
    vmem = pl.BlockSpec(memory_space=pltpu.VMEM)
    parts = pl.pallas_call(
        make_kernel(g, names),
        out_shape=[pltpu.VMEM(o.shape, o.dtype) for o in results],
        in_specs=[vmem] * 10,
        out_specs=[vmem] * 10,
        scratch_shapes=list(table.values()),
        compiler_params=pltpu.CompilerParams(
            collective_id=0, has_side_effects=True, vmem_limit_bytes=54 << 20),
    )(*operands)

    def write(*refs):
        copies = [
            pltpu.make_async_copy(refs[k], refs[10 + k], refs[20].at[k]) for k in range(10)
        ]
        for copy in copies:
            copy.start()
        for copy in copies:
            copy.wait()

    out = pl.pallas_call(
        write,
        out_shape=results,
        in_specs=[vmem] * 10,
        out_specs=[pl.BlockSpec(memory_space=pl.ANY)] * 10,
        scratch_shapes=[pltpu.SemaphoreType.DMA((10,))],
        compiler_params=pltpu.CompilerParams(vmem_limit_bytes=16 << 20),
    )(*parts)
    out = list(out)
    out[0] = jnp.transpose(out[0], (2, 0, 1, 3))
    out[1] = jnp.transpose(out[1], (2, 0, 1, 3))
    out[3] = jnp.transpose(out[3], (2, 0, 1, 3))
    out[4] = jnp.transpose(out[4], (1, 0, 2))
    out[5] = jnp.transpose(out[5], (1, 0, 2))
    return tuple(out)


def solution(mesh):
    mesh_shape = dict(mesh.shape)
    wide = P("sp", None, None, "ch")
    row = P(None, "ch")
    mid = P(None, "ch", None)
    return jax.shard_map(
        lambda *args: body(mesh_shape, *args),
        mesh=mesh,
        in_specs=(wide, wide, P(None, None, "ch"), P(None, None, None, "ch"), mid, mid,
                  row, row, row, row),
        out_specs=(wide, wide, P(None, None, "ch"), P(None, None, None, "ch"), mid, mid,
                   row, row, row, row),
        check_vma=False,
    )
```
